32 devices in a mesh: section: 2 (over core), dp: 16 (over z, y, x).
Axes of the slice: x: 2, y: 2, z: 4, core: 2. Of those that a mesh axis runs over, the one named last changes fastest.
Arguments:
- tokens_in: bfloat16 [8192, 1152], P('dp'), may hold values from -6 to 6
- cotangent: bfloat16 [8192, 1152], P('dp'), may hold values from -6 to 6
- targets: bfloat16 [8192, 768], P('dp'), may hold values from -6 to 6
- buckets: int32 [32], P('dp'), may hold values from 0 to 999
- counts: int32 [16], replicated, may hold values from 1 to 2, as said below
- time_table: float32 [1000, 1152], replicated, may hold values from -6 to 6
- modulate_weight: bfloat16 [2, 1152, 6912], P('section', 'dp'), may hold values from -0.1875 to 0.1875
- modulate_bias: bfloat16 [2, 6912], P('section', 'dp'), may hold values from -3 to 3
- qkv_weight: bfloat16 [2, 1152, 3456], P('section', 'dp'), may hold values from -0.1875 to 0.1875
- qv_bias: bfloat16 [2, 2304], P('section', 'dp'), may hold values from -3 to 3
- attn_weight: bfloat16 [2, 1152, 1152], P('section', 'dp'), may hold values from -0.75 to 0.75
- attn_bias: bfloat16 [2, 1152], P('section', 'dp'), may hold values from -3 to 3
- up_weight: bfloat16 [2, 1152, 4608], P('section', 'dp'), may hold values from -0.1875 to 0.1875
- up_bias: bfloat16 [2, 4608], P('section', 'dp'), may hold values from -3 to 3
- down_weight: bfloat16 [2, 4608, 1152], P('section', 'dp'), may hold values from -0.09375 to 0.09375
- down_bias: bfloat16 [2, 1152], P('section', 'dp'), may hold values from -3 to 3
- project_in_weight: bfloat16 [1152, 2048], P('dp'), may hold values from -0.1875 to 0.1875
- project_in_bias: bfloat16 [2048], P('dp'), may hold values from -3 to 3
- project_mid_weight: bfloat16 [2048, 2048], P('dp'), may hold values from -0.125 to 0.125
- project_mid_bias: bfloat16 [2048], P('dp'), may hold values from -3 to 3
- project_out_weight: bfloat16 [2048, 768], P('dp'), may hold values from -0.125 to 0.125
- project_out_bias: bfloat16 [768], P('dp'), may hold values from -3 to 3
Outputs:
- streams: bfloat16 [2, 8192, 1152], P('section', 'dp')
- loss: float32 [], replicated
- grad_time_table: float32 [1000, 1152], replicated
- grad_modulate_weight: float32 [2, 1152, 6912], P('section', 'dp')
- grad_modulate_bias: float32 [2, 6912], P('section', 'dp')
- grad_qkv_weight: float32 [2, 1152, 3456], P('section', 'dp')
- grad_qv_bias: float32 [2, 2304], P('section', 'dp')
- grad_attn_weight: float32 [2, 1152, 1152], P('section', 'dp')
- grad_attn_bias: float32 [2, 1152], P('section', 'dp')
- grad_up_weight: float32 [2, 1152, 4608], P('section', 'dp')
- grad_up_bias: float32 [2, 4608], P('section', 'dp')
- grad_down_weight: float32 [2, 4608, 1152], P('section', 'dp')
- grad_down_bias: float32 [2, 1152], P('section', 'dp')
- grad_project_in_weight: float32 [1152, 2048], P(None, ('section', 'dp'))
- grad_project_in_bias: float32 [2048], P(('section', 'dp'))
- grad_project_mid_weight: float32 [2048, 2048], P(('section', 'dp'))
- grad_project_mid_bias: float32 [2048], P(('section', 'dp'))
- grad_project_out_weight: float32 [2048, 768], P(('section', 'dp'))
- grad_project_out_bias: float32 [768], replicated
The draws below stay inside these ranges and needn't reach their ends.
Inputs may be any that keep to these rules, and one draw needn't show every extreme that they name: The first counts[d] image slots of index d of dp are live, the others are not; some index has all 2 live.
All inputs are finite; a program needn't handle non-finite values.
Results may differ from the reference program's by a relative error of at most 0.019.
Values may be sent and summed in bfloat16 or wider, within the bound.
A program may use at most 1 GiB of HBM per device.

```python
import jax
import jax.numpy as jnp
from jax import lax

D = 1152
HEADS = 16
FF = 4608
PROJ_HID = 2048
PROJ_OUT = 768
SEQ = 256
HEAD_DIM = 72
IMG_DEV = 2
BUCKETS = 1000
IMAGES = 32
TOKENS = 8192
N_DP = 16


def draw_counts(key, part):
    first_key = jax.random.fold_in(key, 11)
    second_key = jax.random.fold_in(key, 12)
    drawn = jax.random.randint(first_key, (N_DP,), 1, IMG_DEV + 1, dtype=jnp.int32)
    chosen = jax.random.randint(second_key, (), 0, N_DP, dtype=jnp.int32)
    return jnp.where(jnp.arange(N_DP, dtype=jnp.int32) == chosen, jnp.int32(IMG_DEV), drawn)


def set_ends(array, stream_key, least, high):
    longest = array.shape.index(max(array.shape))
    spots = []
    for shift in (0, 1):
        where = [jax.random.randint(jax.random.fold_in(stream_key, axis), (), 0, length) for axis, length in enumerate(array.shape)]
        where[longest] = (where[longest] + shift) % array.shape[longest]
        spots.append(tuple(where))
    return array.at[spots[0]].set(least).at[spots[1]].set(high)


def block_scale(own_key, shape, shards, smallest, largest):
    gain, own = 1.0, jax.random.fold_in(own_key, 6)
    for dim, shards_of in shards:
        draws = jnp.exp(jax.random.uniform(jax.random.fold_in(own, dim), (shards_of,), jnp.float32, smallest / len(shards), largest / len(shards)))
        gain = gain * jnp.repeat(draws, shape[dim] // shards_of).reshape([-1 if axis == dim else 1 for axis in range(len(shape))])
    return gain


def centred(rng, shape, deviation, reach, cuts=(), held_as=jnp.bfloat16):
    values = deviation * jax.random.normal(rng, shape, jnp.float32)
    if cuts:
        values = values * block_scale(rng, shape, cuts, -0.22, 0.18)
    return jnp.clip(values, -reach, reach).astype(held_as)


def setup_inputs(seed: int = 0) -> dict:
    arg_keys = jax.random.split(jax.random.key(seed), 23)
    return {
        "tokens_in": centred(arg_keys[0], (TOKENS, D), 1.0, 6.0, ((0, 16),)),
        "cotangent": centred(arg_keys[1], (TOKENS, D), 1.0, 6.0, ((0, 16),)),
        "targets": centred(arg_keys[2], (TOKENS, PROJ_OUT), 1.0, 6.0, ((0, 16),)),
        "buckets": set_ends(jax.random.randint(arg_keys[3], (IMAGES,), 0, BUCKETS), jax.random.fold_in(arg_keys[3], 1), 0, BUCKETS - 1).astype(jnp.int32),
        "counts": draw_counts(jax.random.fold_in(arg_keys[22], 71), 0),
        "time_table": centred(arg_keys[5], (BUCKETS, D), 1.0, 6.0, (), jnp.float32),
        "modulate_weight": centred(arg_keys[6], (2, D, 6 * D), D ** -0.5, 0.1875, ((0, 2), (1, 16))),
        "modulate_bias": centred(arg_keys[7], (2, 6 * D), 0.5, 3.0, ((0, 2), (1, 16))),
        "qkv_weight": centred(arg_keys[8], (2, D, 3 * D), D ** -0.5, 0.1875, ((0, 2), (1, 16))),
        "qv_bias": centred(arg_keys[9], (2, 2 * D), 0.5, 3.0, ((0, 2), (1, 16))),
        "attn_weight": centred(arg_keys[10], (2, D, D), (D // 16) ** -0.5, 0.75, ((0, 2), (1, 16))),
        "attn_bias": centred(arg_keys[11], (2, D), 0.5, 3.0, ((0, 2), (1, 16))),
        "up_weight": centred(arg_keys[12], (2, D, FF), D ** -0.5, 0.1875, ((0, 2), (1, 16))),
        "up_bias": centred(arg_keys[13], (2, FF), 0.5, 3.0, ((0, 2), (1, 16))),
        "down_weight": centred(arg_keys[14], (2, FF, D), FF ** -0.5, 0.09375, ((0, 2), (1, 16))),
        "down_bias": centred(arg_keys[15], (2, D), 0.5, 3.0, ((0, 2), (1, 16))),
        "project_in_weight": centred(arg_keys[16], (D, PROJ_HID), D ** -0.5, 0.1875, ((0, 16),)),
        "project_in_bias": centred(arg_keys[17], (PROJ_HID,), 0.5, 3.0, ((0, 16),)),
        "project_mid_weight": centred(arg_keys[18], (PROJ_HID, PROJ_HID), PROJ_HID ** -0.5, 0.125, ((0, 16),)),
        "project_mid_bias": centred(arg_keys[19], (PROJ_HID,), 0.5, 3.0, ((0, 16),)),
        "project_out_weight": centred(arg_keys[20], (PROJ_HID, PROJ_OUT), PROJ_HID ** -0.5, 0.125, ((0, 16),)),
        "project_out_bias": centred(arg_keys[21], (PROJ_OUT,), 0.5, 3.0, ((0, 16),)),
    }


HIGHEST = lax.Precision.HIGHEST
EPSILON = 1e-06

@jax.custom_vjp
def low(v):
    return lax.optimization_barrier(v.astype(jnp.bfloat16)).astype(jnp.float32)

@jax.custom_vjp
def low_back(v):
    return v

def low_keep(v):
    return (low(v), None)

def low_pass(kept, grad):
    return (grad,)

def back_keep(v):
    return (v, None)

def back_low(kept, grad):
    return (low(grad),)
low.defvjp(low_keep, low_pass)
low_back.defvjp(back_keep, back_low)

def matmul(left_side, right_side):
    return jnp.dot(left_side, right_side, precision=HIGHEST)

def layer_norm(values):
    center = values - lax.optimization_barrier(jnp.mean(values, -1, keepdims=True))
    return center * lax.rsqrt(lax.optimization_barrier(jnp.mean(center * center, -1, keepdims=True)) + EPSILON)

def attend(packed):
    split_heads = packed.reshape(SEQ, 3, HEADS, HEAD_DIM)
    scores = jnp.einsum('qhd,khd->hqk', split_heads[:, 0], split_heads[:, 1], precision=HIGHEST) * HEAD_DIM ** (-0.5)
    probabilities = jax.nn.softmax(low_back(scores), axis=-1)
    mixed_rows = jnp.einsum('hqk,khd->qhd', low(probabilities), split_heads[:, 2], precision=HIGHEST)
    return mixed_rows.reshape(SEQ, D)

def block(hidden, silu_rows, params):
    mod_weight, mod_bias, pack_weight, pack_bias, out_weight, out_bias, first_weight, first_bias, second_weight, second_bias = params
    pieces = low_back(matmul(silu_rows, mod_weight) + mod_bias).reshape(IMAGES, 6, 1, D)
    residual = hidden.reshape(IMAGES, SEQ, D)
    attn_input = low(layer_norm(residual) * (1.0 + pieces[:, 1]) + pieces[:, 0]).reshape(TOKENS, D)
    pack_full = jnp.concatenate([pack_bias[:D], jnp.zeros((D,), jnp.float32), pack_bias[D:]])
    packed = low_back(low(matmul(attn_input, pack_weight) + pack_full))
    mixed_rows = lax.map(jax.checkpoint(attend), packed.reshape(IMAGES, SEQ, 3 * D)).reshape(TOKENS, D)
    mixed_rows = low_back(low(mixed_rows))
    attn_out = low_back(matmul(mixed_rows, out_weight) + out_bias)
    after_attn = residual + pieces[:, 2] * attn_out.reshape(IMAGES, SEQ, D)
    mlp_input = low(layer_norm(after_attn) * (1.0 + pieces[:, 4]) + pieces[:, 3]).reshape(TOKENS, D)
    pre_act = low_back(matmul(mlp_input, first_weight) + first_bias)
    activation = low(jax.nn.gelu(pre_act, approximate=True))
    mlp_out = low_back(matmul(activation, second_weight) + second_bias)
    return (after_attn + pieces[:, 5] * mlp_out.reshape(IMAGES, SEQ, D)).reshape(TOKENS, D)

def head(hidden, target_rows, token_live, params):
    in_weight, in_bias, mid_weight, mid_bias, out_weight, out_bias = params
    act_first = low(jax.nn.silu(low_back(matmul(hidden, in_weight) + in_bias)))
    act_second = low(jax.nn.silu(low_back(matmul(act_first, mid_weight) + mid_bias)))
    feature = low_back(matmul(act_second, out_weight) + out_bias)
    unit_feature = feature * lax.rsqrt(lax.optimization_barrier(jnp.sum(feature * feature, -1, keepdims=True)) + EPSILON)
    unit_target = target_rows * lax.rsqrt(lax.optimization_barrier(jnp.sum(target_rows * target_rows, -1, keepdims=True)) + EPSILON)
    cosine = lax.optimization_barrier(jnp.sum(unit_feature * unit_target, -1))
    return 0.5 * jnp.sum(token_live * (1.0 - cosine))

def reference(tokens_in, cotangent, targets, buckets, counts, time_table, modulate_weight, modulate_bias, qkv_weight, qv_bias, attn_weight, attn_bias, up_weight, up_bias, down_weight, down_bias, project_in_weight, project_in_bias, project_mid_weight, project_mid_bias, project_out_weight, project_out_bias):
    slot_index = jnp.arange(IMAGES, dtype=jnp.int32)
    image_live = (slot_index % IMG_DEV < counts[slot_index // IMG_DEV]).astype(jnp.float32)
    token_live = jnp.repeat(image_live, SEQ)
    target_rows = targets.astype(jnp.float32)
    block_params = tuple((weight.astype(jnp.float32) for weight in (modulate_weight, modulate_bias, qkv_weight, qv_bias, attn_weight, attn_bias, up_weight, up_bias, down_weight, down_bias)))
    head_params = tuple((weight.astype(jnp.float32) for weight in (project_in_weight, project_in_bias, project_mid_weight, project_mid_bias, project_out_weight, project_out_bias)))

    def forward(hidden, table, blocks_all, heads_all):
        silu_rows = low(jax.nn.silu(table[buckets]))
        first_out = low(block(hidden, silu_rows, tuple((weight[0] for weight in blocks_all))))
        second_out = block(low_back(first_out), silu_rows, tuple((weight[1] for weight in blocks_all))) * token_live[:, None]
        return (second_out, head(first_out, target_rows, token_live, heads_all))
    (second_out, loss_sum), pullback = jax.vjp(forward, tokens_in.astype(jnp.float32), time_table, block_params, head_params)
    grad_hidden, grad_table, grad_blocks, grad_heads = pullback((cotangent.astype(jnp.float32), jnp.float32(1.0)))
    streams = jnp.stack([grad_hidden.astype(jnp.bfloat16), second_out.astype(jnp.bfloat16)])
    loss_value = loss_sum / (jnp.sum(counts).astype(jnp.float32) * SEQ)
    return (streams, loss_value, grad_table, grad_blocks[0], grad_blocks[1], grad_blocks[2], grad_blocks[3], grad_blocks[4], grad_blocks[5], grad_blocks[6], grad_blocks[7], grad_blocks[8], grad_blocks[9], grad_heads[0], grad_heads[1], grad_heads[2], grad_heads[3], grad_heads[4], grad_heads[5])
```

```python
import functools
import jax
import jax.numpy as jnp
from jax import lax
from jax.experimental import pallas as pl
from jax.experimental.pallas import tpu as pltpu
from jax.sharding import PartitionSpec as P

HEADS = 16
SEQ = 256
EPSILON = 1e-06
HIGHEST = lax.Precision.HIGHEST
MESH = pl.DeviceIdType.MESH
ANY = pl.BlockSpec(memory_space=pl.ANY)
DMA = pltpu.SemaphoreType.DMA


def narrow(values):
    return values.astype(jnp.bfloat16)


def wide(values):
    return values.astype(jnp.float32)


def product(left_side, right_side):
    return jnp.dot(left_side, right_side, preferred_element_type=jnp.float32)


def product_left_t(left_side, right_side):
    return lax.dot_general(
        left_side, right_side, (((0,), (0,)), ((), ())), preferred_element_type=jnp.float32
    )


def product_right_t(left_side, right_side):
    return lax.dot_general(
        left_side, right_side, (((1,), (1,)), ((), ())), preferred_element_type=jnp.float32
    )


def ring_of(place, length):
    half, side = place // 2, place % 2
    return side * (length - 1 - half) + (1 - side) * half


def place_of(spot, length):
    side = spot // (length // 2)
    half = side * (length - 1 - spot) + (1 - side) * spot
    return 2 * half + side


def whereabouts(length):
    core = lax.axis_index("section")
    index = lax.axis_index("dp")
    place, role = index // 2, index % 2
    spot = ring_of(place, length)
    step = 1 - 2 * core

    def at(offset):
        return place_of(lax.rem(spot + step * offset + 4 * length, length), length)

    return dict(
        core=core,
        place=place,
        role=role,
        at=at,
        onward=(core, 2 * at(1) + role),
        before=(core, 2 * at(-1) + role),
        sibling=(1 - core, index),
        partner=(1 - core, 2 * place + 1 - role),
    )


def greet(devices):
    barrier = pltpu.get_barrier_semaphore()
    for device in devices:
        pl.semaphore_signal(barrier, inc=1, device_id=device, device_id_type=MESH)
    pl.semaphore_wait(barrier, len(devices))


def remote(source, target, send_sem, recv_sem, device):
    return pltpu.make_async_remote_copy(
        src_ref=source,
        dst_ref=target,
        send_sem=send_sem,
        recv_sem=recv_sem,
        device_id=device,
        device_id_type=MESH,
    )


def gather_kernel(length, count, front_only, *refs):
    shards, full = refs[:count], refs[count : 2 * count]
    own_sem, ring_send, ring_recv, side_send, side_recv = refs[2 * count :]
    me = whereabouts(length)
    core, role, place, at = me["core"], me["role"], me["place"], me["at"]
    layers = range(count)
    if front_only:
        greet([me["onward"], me["before"], me["sibling"], me["partner"]])
    else:
        greet([me["onward"], me["before"], me["sibling"], me["partner"]])

    def onward(layer, turn):
        block = full[layer].at[2 * at(-turn) + core]
        return remote(
            block, block, ring_send.at[layer, turn], ring_recv.at[layer, turn], me["onward"]
        )

    def across(layer, turn):
        block = full[layer].at[2 * at(-turn) + core]
        return remote(
            block, block, side_send.at[layer, turn], side_recv.at[layer, turn], me["sibling"]
        )

    def from_sibling(layer, turn):
        block = full[layer].at[2 * at(turn) + 1 - core]
        return remote(
            block, block, side_send.at[layer, turn], side_recv.at[layer, turn], me["sibling"]
        )

    def work():
        for layer in layers:
            onward(layer, 0).start()
            across(layer, 0).start()

        def turn_body(turn, carry):
            for layer in layers:
                block = full[layer].at[2 * at(-turn) + core]
                remote(
                    block,
                    block,
                    ring_send.at[layer, turn - 1],
                    ring_recv.at[layer, turn - 1],
                    me["onward"],
                ).wait_recv()

                @pl.when(turn < length - 1)
                def _():
                    onward(layer, turn).start()

                across(layer, turn).start()
            return carry

        lax.fori_loop(1, length, turn_body, 0)

        def end_body(turn, carry):
            for layer in layers:

                @pl.when(turn < length - 1)
                def _():
                    onward(layer, turn).wait_send()

                across(layer, turn).wait_send()
                from_sibling(layer, turn).wait_recv()
            return carry

        lax.fori_loop(0, length, end_body, 0)

    mine = 2 * place + core
    if front_only:
        @pl.when((role == 0) & (core == 0))
        def _():
            copies = [
                pltpu.make_async_copy(shards[i], full[i].at[mine], own_sem.at[i]) for i in layers
            ]
            for copy in copies:
                copy.start()
            for copy in copies:
                copy.wait()

        def crossing(layer):
            return remote(
                shards[layer],
                full[layer].at[2 * place + role],
                own_sem.at[layer],
                side_recv.at[layer, length],
                me["partner"],
            )

        @pl.when((role == 1) & (core == 0))
        def _():
            for layer in layers:
                crossing(layer).start()
            for layer in layers:
                crossing(layer).wait_send()

        @pl.when((role == 0) & (core == 1))
        def _():
            for layer in layers:
                remote(
                    shards[layer],
                    full[layer].at[mine],
                    own_sem.at[layer],
                    side_recv.at[layer, length],
                    me["partner"],
                ).wait_recv()

        @pl.when(role == 0)
        def _():
            work()

    else:

        @pl.when(core == role)
        def _():
            copies = [
                pltpu.make_async_copy(shards[i], full[i].at[mine], own_sem.at[i]) for i in layers
            ]
            for copy in copies:
                copy.start()
            for copy in copies:
                copy.wait()

        @pl.when(core != role)
        def _():
            crossings = [
                remote(
                    shards[i],
                    full[i].at[2 * place + role],
                    own_sem.at[i],
                    side_recv.at[i, length],
                    me["partner"],
                )
                for i in layers
            ]
            for copy in crossings:
                copy.start()
            for i in layers:
                remote(
                    shards[i],
                    full[i].at[mine],
                    own_sem.at[i],
                    side_recv.at[i, length],
                    me["partner"],
                ).wait()

        work()


def gather(shards, front_only, collective_id):
    members = lax.axis_size("dp")
    length, count = members // 2, len(shards)
    moved = sum(shard.size * 2 for shard in shards) * members
    return pl.pallas_call(
        functools.partial(gather_kernel, length, count, front_only),
        out_shape=[jax.ShapeDtypeStruct((members,) + s.shape, s.dtype) for s in shards],
        in_specs=[ANY] * count,
        out_specs=[ANY] * count,
        scratch_shapes=[
            DMA((count,)),
            DMA((count, length)),
            DMA((count, length)),
            DMA((count, length)),
            DMA((count, length + 1)),
        ],
        compiler_params=pltpu.CompilerParams(
            collective_id=collective_id, has_side_effects=True
        ),
        cost_estimate=pl.CostEstimate(flops=0, bytes_accessed=16 * moved, transcendentals=0),
    )(*shards)


def tile_of(columns):
    for tile in (512, 384, 256, 128):
        if columns % tile == 0:
            return tile
    return columns


def reduce_kernel(length, count, front_only, *refs):
    lefts, rights = refs[:count], refs[count : 2 * count]
    outs = refs[2 * count : 3 * count]
    scratch = refs[3 * count :]
    left_all, right_all = scratch[:count], scratch[count : 2 * count]
    arrived, leaving = scratch[2 * count : 3 * count], scratch[3 * count : 4 * count]
    own_sem, side_send, side_recv, ring_send, ring_recv, last_send, last_recv = scratch[4 * count :]
    me = whereabouts(length)
    core, role, place, at = me["core"], me["role"], me["place"], me["at"]
    layers = range(count)
    greet([me["onward"], me["before"], me["sibling"], me["partner"]] + ([(core, 2 * place + 1 - role)] if front_only else []))
    final = length % 2

    def chunk(layer, slot, turn, add):
        spot = at(-(turn + 1))
        columns = rights[layer].shape[1]
        tile = tile_of(columns)

        def body(index, carry):
            start = pl.multiple_of(index * tile, tile)
            total = product(
                left_all[layer][0, spot], right_all[layer][0, :, pl.ds(start, tile)]
            ) + product(left_all[layer][1, spot], right_all[layer][1, :, pl.ds(start, tile)])
            if add:
                total = total + wide(arrived[layer][turn - 1, :, pl.ds(start, tile)])
            leaving[layer][slot, :, pl.ds(start, tile)] = narrow(total)
            return carry

        lax.fori_loop(0, columns // tile, body, 0)

    def onward(layer, slot, turn):
        return remote(
            leaving[layer].at[slot],
            arrived[layer].at[turn],
            ring_send.at[layer, slot],
            ring_recv.at[layer, turn],
            me["onward"],
        )

    def inputs(layer):
        return [
            pltpu.make_async_copy(
                lefts[layer].at[:, core], left_all[layer].at[0], own_sem.at[layer, 0]
            ),
            pltpu.make_async_copy(rights[layer], right_all[layer].at[0], own_sem.at[layer, 1]),
            remote(
                lefts[layer].at[:, 1 - core],
                left_all[layer].at[1],
                side_send.at[layer, 0],
                side_recv.at[layer, 0],
                me["sibling"],
            ),
            remote(
                rights[layer],
                right_all[layer].at[1],
                side_send.at[layer, 1],
                side_recv.at[layer, 1],
                me["sibling"],
            ),
        ]

    def work():
        for layer in layers:
            for copy in inputs(layer):
                copy.start()
        for layer in layers:
            for copy in inputs(layer):
                copy.wait()
            chunk(layer, 0, 0, False)
            onward(layer, 0, 0).start()

        def turn_body(turn, carry):
            slot = turn % 2
            for layer in layers:
                onward(layer, slot, turn - 1).wait_recv()

                @pl.when(turn >= 2)
                def _():
                    onward(layer, slot, turn).wait_send()

                chunk(layer, slot, turn, True)
                onward(layer, slot, turn).start()
            return carry

        lax.fori_loop(1, length - 1, turn_body, 0)
        slot = (length - 1) % 2
        for layer in layers:
            onward(layer, slot, length - 2).wait_recv()
            if length >= 3:
                onward(layer, slot, length - 2).wait_send()
            chunk(layer, slot, length - 1, True)
            finish(layer, slot)
        for layer in layers:
            onward(layer, 1 - slot, length - 2).wait_send()
            finished(layer, slot)

    def local_last(layer, slot):
        return pltpu.make_async_copy(leaving[layer].at[slot], outs[layer], last_send.at[layer, 0])

    def remote_last(layer, slot):
        return remote(
            leaving[layer].at[slot],
            outs[layer],
            last_send.at[layer, 0],
            last_recv.at[layer, 0],
            me["partner"],
        )

    if not front_only:

        def finish(layer, slot):
            @pl.when(core == role)
            def _():
                local_last(layer, slot).start()

            @pl.when(core != role)
            def _():
                remote_last(layer, slot).start()

        def finished(layer, slot):
            @pl.when(core == role)
            def _():
                local_last(layer, slot).wait()

            @pl.when(core != role)
            def _():
                remote_last(layer, slot).wait()

        work()
    else:
        def part(layer, slot, half):
            rows = outs[layer].shape[0]
            return leaving[layer].at[slot, pl.ds(half * rows, rows)]

        def keep(layer, slot):
            return pltpu.make_async_copy(
                part(layer, slot, 0), outs[layer], last_send.at[layer, 0]
            )

        def hand(layer, slot, half, device):
            return remote(
                part(layer, slot, half),
                outs[layer],
                last_send.at[layer, half],
                last_recv.at[layer, 0],
                device,
            )

        def moves(layer, slot, act):
            @pl.when(core == 0)
            def _():
                act(keep(layer, slot))
                act(hand(layer, slot, 1, me["sibling"]))

            @pl.when(core == 1)
            def _():
                act(hand(layer, slot, 0, (0, 2 * place + 1)))
                act(hand(layer, slot, 1, (1, 2 * place + 1)))

        def finish(layer, slot):
            moves(layer, slot, lambda copy: copy.start())

        def finished(layer, slot):
            @pl.when(core == 0)
            def _():
                keep(layer, slot).wait()
                hand(layer, slot, 1, me["sibling"]).wait_send()

            @pl.when(core == 1)
            def _():
                hand(layer, slot, 0, (0, 2 * place + 1)).wait_send()
                hand(layer, slot, 1, (1, 2 * place + 1)).wait_send()

        @pl.when(role == 0)
        def _():
            work()

        @pl.when((role == 1) | (core == 1))
        def _():
            for layer in layers:
                hand(layer, 0, 0, me["sibling"]).wait_recv()


def reduce(lefts, rights, front_only, collective_id):
    members = lax.axis_size("dp")
    length, count = members // 2, len(lefts)
    rows = [left.shape[2] for left in lefts]
    columns = [right.shape[1] for right in rights]
    tokens = rights[0].shape[0]
    halves = 2 if front_only else 1
    bf16 = jnp.bfloat16
    work = sum(r * c for r, c in zip(rows, columns)) * length
    return pl.pallas_call(
        functools.partial(reduce_kernel, length, count, front_only),
        out_shape=[
            jax.ShapeDtypeStruct((r // halves, c), bf16) for r, c in zip(rows, columns)
        ],
        in_specs=[ANY] * (2 * count),
        out_specs=[ANY] * count,
        scratch_shapes=[pltpu.VMEM((2, length, r, tokens), bf16) for r in rows]
        + [pltpu.VMEM((2, tokens, c), bf16) for c in columns]
        + [pltpu.VMEM((length - 1, r, c), bf16) for r, c in zip(rows, columns)]
        + [pltpu.VMEM((2, r, c), bf16) for r, c in zip(rows, columns)]
        + [
            DMA((count, 2)),
            DMA((count, 2)),
            DMA((count, 2)),
            DMA((count, 2)),
            DMA((count, length)),
            DMA((count, 2)),
            DMA((count, 1)),
        ],
        compiler_params=pltpu.CompilerParams(
            collective_id=collective_id, has_side_effects=True, vmem_limit_bytes=60 * 2**20
        ),
        cost_estimate=pl.CostEstimate(
            flops=4 * work * tokens, bytes_accessed=64 * work, transcendentals=0
        ),
    )(*lefts, *rights)


def layer_norm(values):
    center = values - jnp.mean(values, -1, keepdims=True)
    inverse = lax.rsqrt(jnp.mean(center * center, -1, keepdims=True) + EPSILON)
    return (center * inverse, inverse)


def norm_back(grad_in, normed, inverse):
    return inverse * (
        grad_in
        - jnp.mean(grad_in, -1, keepdims=True)
        - normed * jnp.mean(grad_in * normed, -1, keepdims=True)
    )


def local_grad(function, primal, cotangent_in):
    return jax.vjp(function, primal)[1](cotangent_in)[0]


def gelu_tanh(values):
    return jax.nn.gelu(values, approximate=True)


def column_sums(values):
    return jnp.sum(wide(values), 0)


def blocked_t(values, members):
    tokens, features = values.shape
    return values.T.reshape(members // 2, 2, features // members, tokens)


def block_forward(hidden, pieces, weights):
    pack_weight, pack_full, out_weight, out_bias, first_weight, first_bias, second_weight, second_bias = weights
    images = pieces.shape[0]
    channels = hidden.shape[1]
    seq_len = hidden.shape[0] // images
    head_size = channels // HEADS
    scaling = head_size ** (-0.5)
    residual = wide(hidden).reshape(images, seq_len, channels)
    normed_a, _ = layer_norm(residual)
    attn_input = narrow(normed_a * (1.0 + pieces[:, 1]) + pieces[:, 0]).reshape(-1, channels)
    packed = narrow(product(attn_input, pack_weight) + pack_full)
    split_heads = packed.reshape(images, seq_len, 3, HEADS, head_size)
    queries, key_rows, values = (split_heads[:, :, 0], split_heads[:, :, 1], split_heads[:, :, 2])
    scores = (
        jnp.einsum("nqhd,nkhd->nhqk", queries, key_rows, preferred_element_type=jnp.float32)
        * scaling
    )
    scores = scores - jnp.max(scores, -1, keepdims=True)
    exponent = jnp.exp(scores)
    probabilities = narrow(exponent / jnp.sum(exponent, -1, keepdims=True))
    mixed_rows = narrow(
        jnp.einsum("nhqk,nkhd->nqhd", probabilities, values, preferred_element_type=jnp.float32)
    ).reshape(-1, channels)
    attn_out = product(mixed_rows, out_weight) + out_bias
    after_attn = residual + pieces[:, 2] * attn_out.reshape(images, seq_len, channels)
    normed_m, _ = layer_norm(after_attn)
    mlp_input = narrow(normed_m * (1.0 + pieces[:, 4]) + pieces[:, 3]).reshape(-1, channels)
    pre_act = product(mlp_input, first_weight) + first_bias
    activation = narrow(gelu_tanh(pre_act))
    mlp_out = product(activation, second_weight) + second_bias
    final_rows = after_attn + pieces[:, 5] * mlp_out.reshape(images, seq_len, channels)
    saved_state = (
        attn_input,
        packed,
        probabilities,
        mixed_rows,
        attn_out,
        after_attn,
        mlp_input,
        pre_act,
        activation,
        mlp_out,
    )
    return (final_rows.reshape(-1, channels), saved_state)


def block_backward(hidden, saved_state, pieces, weights, grad_out, members):
    pack_weight, pack_full, out_weight, out_bias, first_weight, first_bias, second_weight, second_bias = weights
    (
        attn_input,
        packed,
        probabilities,
        mixed_rows,
        attn_out,
        after_attn,
        mlp_input,
        pre_act,
        activation,
        mlp_out,
    ) = saved_state
    images = pieces.shape[0]
    channels = hidden.shape[1]
    seq_len = hidden.shape[0] // images
    head_size = channels // HEADS
    scaling = head_size ** (-0.5)
    normed_m, inverse_m = layer_norm(after_attn)
    grad_final = grad_out.reshape(images, seq_len, channels)
    grad_mlp = narrow((pieces[:, 5] * grad_final).reshape(-1, channels))
    gate_m_grad = jnp.sum(grad_final * mlp_out.reshape(images, seq_len, channels), 1)
    second_b_grad = column_sums(grad_mlp)
    grad_pre = narrow(local_grad(gelu_tanh, pre_act, product_right_t(grad_mlp, second_weight)))
    first_b_grad = column_sums(grad_pre)
    grad_min = product_right_t(grad_pre, first_weight).reshape(images, seq_len, channels)
    shift_m_grad = jnp.sum(grad_min, 1)
    scale_m_grad = jnp.sum(grad_min * normed_m, 1)
    grad_after = grad_final + norm_back(grad_min * (1.0 + pieces[:, 4]), normed_m, inverse_m)
    grad_attn = narrow((pieces[:, 2] * grad_after).reshape(-1, channels))
    gate_a_grad = jnp.sum(grad_after * attn_out.reshape(images, seq_len, channels), 1)
    out_b_grad = column_sums(grad_attn)
    grad_mixed = narrow(product_right_t(grad_attn, out_weight)).reshape(
        images, seq_len, HEADS, head_size
    )
    split_heads = packed.reshape(images, seq_len, 3, HEADS, head_size)
    queries, key_rows, values = (split_heads[:, :, 0], split_heads[:, :, 1], split_heads[:, :, 2])
    grad_probs = jnp.einsum(
        "nqhd,nkhd->nhqk", grad_mixed, values, preferred_element_type=jnp.float32
    )
    grad_values = jnp.einsum(
        "nhqk,nqhd->nkhd", probabilities, grad_mixed, preferred_element_type=jnp.float32
    )
    probs_wide = wide(probabilities)
    grad_scores = narrow(
        probs_wide * (grad_probs - jnp.sum(grad_probs * probs_wide, -1, keepdims=True))
    )
    grad_queries = (
        jnp.einsum("nhqk,nkhd->nqhd", grad_scores, key_rows, preferred_element_type=jnp.float32)
        * scaling
    )
    grad_keys = (
        jnp.einsum("nhqk,nqhd->nkhd", grad_scores, queries, preferred_element_type=jnp.float32)
        * scaling
    )
    grad_packed = narrow(
        jnp.stack([grad_queries, grad_keys, grad_values], 2).reshape(-1, 3 * channels)
    )
    pack_sums = column_sums(grad_packed)
    pack_b_grad = jnp.concatenate([pack_sums[:channels], pack_sums[2 * channels :]])
    grad_ain = product_right_t(grad_packed, pack_weight).reshape(images, seq_len, channels)
    normed_a, inverse_a = layer_norm(wide(hidden).reshape(images, seq_len, channels))
    shift_a_grad = jnp.sum(grad_ain, 1)
    scale_a_grad = jnp.sum(grad_ain * normed_a, 1)
    grad_input = grad_after + norm_back(grad_ain * (1.0 + pieces[:, 1]), normed_a, inverse_a)
    grad_mod = narrow(
        jnp.stack(
            [shift_a_grad, scale_a_grad, gate_a_grad, shift_m_grad, scale_m_grad, gate_m_grad], 1
        ).reshape(images, 6 * channels)
    )
    lefts = tuple(blocked_t(v, members) for v in (activation, mlp_input, mixed_rows, attn_input))
    rights = (grad_mlp, grad_pre, grad_attn, grad_packed)
    bias_grads = (pack_b_grad, out_b_grad, first_b_grad, second_b_grad)
    return (grad_input.reshape(-1, channels), lefts, rights, bias_grads, grad_mod)


def head_pass(hidden_rows, target_rows, live_rows, head_weights, members):
    in_weight, in_bias, mid_weight, mid_bias, out_weight, out_bias = head_weights
    pre_first = product(hidden_rows, in_weight) + in_bias
    act_first = narrow(jax.nn.silu(pre_first))
    pre_second = product(act_first, mid_weight) + mid_bias
    act_second = narrow(jax.nn.silu(pre_second))
    feature = product(act_second, out_weight) + out_bias
    inverse_feature = lax.rsqrt(jnp.sum(feature * feature, -1, keepdims=True) + EPSILON)
    unit_feature = feature * inverse_feature
    target_float = wide(target_rows)
    unit_target = target_float * lax.rsqrt(
        jnp.sum(target_float * target_float, -1, keepdims=True) + EPSILON
    )
    cosine = jnp.sum(unit_feature * unit_target, -1)
    loss_part = 0.5 * jnp.sum(live_rows * (1.0 - cosine))
    grad_unit = -0.5 * live_rows[:, None] * unit_target
    grad_feature = narrow(
        inverse_feature
        * (grad_unit - unit_feature * jnp.sum(grad_unit * unit_feature, -1, keepdims=True))
    )
    grad_second = narrow(
        local_grad(jax.nn.silu, pre_second, product_right_t(grad_feature, out_weight))
    )
    grad_first = narrow(
        local_grad(jax.nn.silu, pre_first, product_right_t(grad_second, mid_weight))
    )
    grad_hidden = product_right_t(grad_first, in_weight)

    def in_halves(values):
        tokens, features = values.shape
        rows = features // (2 * members)
        cut = values.T.reshape(2, members, rows, tokens)
        return jnp.swapaxes(cut, 0, 1).reshape(members // 2, 2, 2 * rows, tokens)

    lefts = (in_halves(act_second), in_halves(act_first), in_halves(grad_first))
    rights = (grad_feature, grad_second, hidden_rows)
    sums = (column_sums(grad_first), column_sums(grad_second), column_sums(grad_feature))
    return (grad_hidden, loss_part, lefts, rights, sums)


def either(first_function, second_function, is_first, operands):
    shapes = jax.eval_shape(first_function or second_function, *operands)

    def zeros(*operands_in):
        return jax.tree.map(lambda leaf: jnp.zeros(leaf.shape, leaf.dtype), shapes)

    return lax.cond(is_first, first_function or zeros, second_function or zeros, *operands)


def on_device(
    tokens_in,
    cotangent,
    targets,
    buckets,
    counts,
    time_table,
    modulate_weight,
    modulate_bias,
    qkv_weight,
    qv_bias,
    attn_weight,
    attn_bias,
    up_weight,
    up_bias,
    down_weight,
    down_bias,
    project_in_weight,
    project_in_bias,
    project_mid_weight,
    project_mid_bias,
    project_out_weight,
    project_out_bias,
):
    members = lax.axis_size("dp")
    core = lax.axis_index("section")
    index = lax.axis_index("dp")
    place, role = index // 2, index % 2
    is_first = role == 0
    own = 2 * place + core
    channels = tokens_in.shape[1]
    images = tokens_in.shape[0] // SEQ
    pairs_swap, pairs_up, pairs_back = [], [], []
    for pair in range(members // 2):
        low, high = 2 * pair, 2 * pair + 1
        pairs_swap += [(low, low), (members + low, high), (high, members + low), (members + high, members + high)]
        pairs_up += [(low, high), (members + low, members + high)]
        pairs_back += [(high, low), (members + high, members + low)]
    axes = ("section", "dp")

    def swap(values):
        return lax.ppermute(values, axes, pairs_swap)

    section_biases = (qv_bias[0], attn_bias[0], up_bias[0], down_bias[0])
    head_biases = (project_in_bias, project_mid_bias, project_out_bias)
    parts = section_biases + head_biases
    widths = [part.shape[0] for part in parts]
    lanes = 16 * 128
    packed_bias = jnp.concatenate(
        list(parts) + [jnp.zeros((lanes - sum(widths),), jnp.bfloat16)]
    ).reshape(16, 128)
    all_bias, pack_weight, out_weight, first_weight, second_weight = gather(
        (packed_bias, qkv_weight[0], attn_weight[0], up_weight[0], down_weight[0]), False, 0
    )
    all_bias = all_bias.reshape(members, lanes)
    biases, offset = [], 0
    for width in widths:
        biases.append(wide(all_bias[:, offset : offset + width].reshape(-1)))
        offset += width
    pack_full = jnp.concatenate(
        [biases[0][:channels], jnp.zeros((channels,), jnp.float32), biases[0][channels:]]
    )

    def whole(values):
        return values.reshape(-1, values.shape[-1])

    block_weights = (
        whole(pack_weight),
        pack_full,
        whole(out_weight),
        biases[1],
        whole(first_weight),
        biases[2],
        whole(second_weight),
        biases[3],
    )

    all_buckets = lax.all_gather(buckets, "dp", axis=0, tiled=True)
    one_hot = (
        all_buckets[:, None] == jnp.arange(time_table.shape[0], dtype=jnp.int32)[None, :]
    ).astype(jnp.float32)
    conditioning = jnp.dot(one_hot, time_table, precision=HIGHEST)
    silu_all = narrow(jax.nn.silu(conditioning))
    depth = modulate_weight.shape[1]
    silu_depth = lax.dynamic_slice_in_dim(silu_all, index * depth, depth, 1)
    mod_part = product(silu_depth, modulate_weight[0])
    share = modulate_bias.shape[1]
    bias_row = lax.dynamic_update_slice_in_dim(
        jnp.zeros((mod_part.shape[1],), jnp.float32), wide(modulate_bias[0]), index * share, 0
    )
    mod_own = lax.psum_scatter(mod_part + bias_row[None], "dp", scatter_dimension=0, tiled=True)
    pieces = swap(mod_own).reshape(images, 6, 1, channels)

    own_counts = counts[own]
    image_live = (jnp.arange(images, dtype=jnp.int32) < own_counts).astype(jnp.float32)
    token_live = jnp.repeat(image_live, SEQ)
    total_live = wide(jnp.sum(counts)) * SEQ
    payload = swap(jnp.where(is_first, cotangent, tokens_in))
    crossed = core != role
    hidden_first = jnp.where(crossed, payload, tokens_in)
    outer = jnp.where(crossed, payload, cotangent)
    own_targets = swap(targets)

    final_rows, saved_state = either(
        lambda h, m, *w: block_forward(h, m, w),
        None,
        is_first,
        (hidden_first, pieces) + block_weights,
    )
    first_out = narrow(final_rows)
    hidden_second = lax.ppermute(first_out, axes, pairs_up)

    head_full = gather((project_in_weight, project_mid_weight, project_out_weight), True, 1)
    head_weights = (
        whole(head_full[0]),
        biases[4],
        whole(head_full[1]),
        biases[5],
        whole(head_full[2]),
        biases[6],
    )

    def back(first, second, mod, grad, target, live, block, head):
        final, state = block_forward(second, mod, block)
        outer_grad = wide(grad) * live[:, None]
        grad_input, lefts, rights, bias_grads, grad_mod = block_backward(
            second, state, mod, block, outer_grad, members
        )
        return (narrow(grad_input), narrow(final * live[:, None]), lefts, rights, bias_grads, grad_mod)

    def zeros_like_of(function, *operands):
        shapes = jax.eval_shape(function, *operands)
        return jax.tree.map(lambda leaf: jnp.zeros(leaf.shape, leaf.dtype), shapes)

    def do_head(first, target, live, head):
        return head_pass(first, target, live, head, members)

    def do_second(second, mod, grad, live, block):
        return back(None, second, mod, grad, None, live, block, None)

    operands = (first_out, hidden_second, pieces, outer, own_targets, token_live, block_weights, head_weights)

    def at_front(first, second, mod, grad, target, live, block, head):
        return (
            do_head(first, target, live, head),
            zeros_like_of(do_second, second, mod, grad, live, block),
        )

    def at_back(first, second, mod, grad, target, live, block, head):
        return (
            zeros_like_of(do_head, first, target, live, head),
            do_second(second, mod, grad, live, block),
        )

    head_result, second_result = lax.cond(is_first, at_front, at_back, *operands)
    grad_hidden, loss_part, head_lefts, head_rights, head_sums = head_result
    arrived_back = lax.ppermute(second_result[0], axes, pairs_back)
    head_grads = reduce(head_lefts, head_rights, True, 2)

    def do_first(hidden, state, mod, extra, back_grad, block, other):
        grad_input, lefts, rights, bias_grads, grad_mod = block_backward(
            hidden, state, mod, block, wide(back_grad) + extra, members
        )
        return (narrow(grad_input),) + (lefts, rights, bias_grads, grad_mod)

    def keep_second(hidden, state, mod, extra, back_grad, block, other):
        return other

    stream, lefts, rights, bias_grads, grad_mod = lax.cond(
        is_first,
        do_first,
        keep_second,
        hidden_first,
        saved_state,
        pieces,
        grad_hidden,
        arrived_back,
        block_weights,
        second_result[1:],
    )
    down_grad, up_grad, attn_grad, qkv_grad = reduce(lefts, rights, False, 3)
    stream_own = swap(stream)
    mod_grad_all = lax.all_gather(swap(grad_mod), "dp", axis=0, tiled=True)
    mod_w_grad = product_left_t(silu_depth, mod_grad_all)
    mod_b_grad = lax.dynamic_slice_in_dim(column_sums(mod_grad_all), index * share, share, 0)
    silu_part = product_right_t(mod_grad_all, modulate_weight[0])
    silu_parts = lax.all_gather(silu_part, axes, axis=0, tiled=False)
    silu_total = jnp.sum(silu_parts.reshape((2, members) + silu_part.shape), 0)
    silu_total = jnp.swapaxes(silu_total, 0, 1).reshape(silu_part.shape[0], channels)
    cond_grad = local_grad(jax.nn.silu, conditioning, silu_total)
    table_grad = jnp.dot(one_hot.T, cond_grad, precision=HIGHEST)

    block_sums = jnp.concatenate(bias_grads)
    mine = (jnp.arange(2) == role).astype(jnp.float32)[:, None] * block_sums[None]
    sums = lax.psum((mine, head_sums, loss_part), axes)
    section_sums = sums[0][core]
    in_sums, mid_sums, out_sums = sums[1]
    bias_outs, offset = [], 0
    for part, grads in zip(section_biases, bias_grads):
        width = part.shape[0]
        bias_outs.append(
            lax.dynamic_slice_in_dim(section_sums, offset + index * width, width, 0)[None]
        )
        offset += grads.shape[0]
    device = core * members + index
    head_share = in_sums.shape[0] // (2 * members)
    loss_value = sums[2] / total_live
    return (
        stream_own[None],
        loss_value,
        table_grad,
        mod_w_grad[None],
        mod_b_grad[None],
        wide(qkv_grad)[None],
        bias_outs[0],
        wide(attn_grad)[None],
        bias_outs[1],
        wide(up_grad)[None],
        bias_outs[2],
        wide(down_grad)[None],
        bias_outs[3],
        wide(head_grads[2]).T,
        lax.dynamic_slice_in_dim(in_sums, device * head_share, head_share, 0),
        wide(head_grads[1]),
        lax.dynamic_slice_in_dim(mid_sums, device * head_share, head_share, 0),
        wide(head_grads[0]),
        out_sums,
    )


def solution(mesh):
    in_specs = (
        P("dp", None),
        P("dp", None),
        P("dp", None),
        P("dp"),
        P(),
        P(),
        P("section", "dp", None),
        P("section", "dp"),
        P("section", "dp", None),
        P("section", "dp"),
        P("section", "dp", None),
        P("section", "dp"),
        P("section", "dp", None),
        P("section", "dp"),
        P("section", "dp", None),
        P("section", "dp"),
        P("dp", None),
        P("dp"),
        P("dp", None),
        P("dp"),
        P("dp", None),
        P("dp"),
    )
    out_specs = (
        P("section", "dp", None),
        P(),
        P(),
        P("section", "dp", None),
        P("section", "dp"),
        P("section", "dp", None),
        P("section", "dp"),
        P("section", "dp", None),
        P("section", "dp"),
        P("section", "dp", None),
        P("section", "dp"),
        P("section", "dp", None),
        P("section", "dp"),
        P(None, ("section", "dp")),
        P(("section", "dp")),
        P(("section", "dp"), None),
        P(("section", "dp")),
        P(("section", "dp"), None),
        P(),
    )
    return jax.shard_map(
        on_device, mesh=mesh, in_specs=in_specs, out_specs=out_specs, check_vma=False
    )
```

```python
import functools
import jax
import jax.numpy as jnp
from jax import lax
from jax.experimental import pallas as pl
from jax.experimental.pallas import tpu as pltpu
from jax.sharding import PartitionSpec as P

HEADS = 16
SEQ = 256
EPSILON = 1e-06
HIGHEST = lax.Precision.HIGHEST
MESH = pl.DeviceIdType.MESH
ANY = pl.BlockSpec(memory_space=pl.ANY)
DMA = pltpu.SemaphoreType.DMA
VMEM_BYTES = 60 * 2**20


def narrow(values):
    return values.astype(jnp.bfloat16)


def wide(values):
    return values.astype(jnp.float32)


def product(left_side, right_side):
    return jnp.dot(left_side, right_side, preferred_element_type=jnp.float32)


def product_left_t(left_side, right_side):
    return lax.dot_general(
        left_side, right_side, (((0,), (0,)), ((), ())), preferred_element_type=jnp.float32
    )


def product_right_t(left_side, right_side):
    return lax.dot_general(
        left_side, right_side, (((1,), (1,)), ((), ())), preferred_element_type=jnp.float32
    )


def ring_of(place, length):
    half, side = place // 2, place % 2
    return side * (length - 1 - half) + (1 - side) * half


def place_of(spot, length):
    side = spot // (length // 2)
    half = side * (length - 1 - spot) + (1 - side) * spot
    return 2 * half + side


def whereabouts(length):
    core = lax.axis_index("section")
    index = lax.axis_index("dp")
    place, role = index // 2, index % 2
    spot = ring_of(place, length)
    step = 1 - 2 * core

    def at(offset):
        return place_of(lax.rem(spot + step * offset + 4 * length, length), length)

    return dict(
        core=core,
        place=place,
        role=role,
        at=at,
        onward=(core, 2 * at(1) + role),
        before=(core, 2 * at(-1) + role),
        sibling=(1 - core, index),
        partner=(1 - core, 2 * place + 1 - role),
    )


def greet(devices):
    barrier = pltpu.get_barrier_semaphore()
    for device in devices:
        pl.semaphore_signal(barrier, inc=1, device_id=device, device_id_type=MESH)
    pl.semaphore_wait(barrier, len(devices))


def remote(source, target, send_sem, recv_sem, device):
    return pltpu.make_async_remote_copy(
        src_ref=source,
        dst_ref=target,
        send_sem=send_sem,
        recv_sem=recv_sem,
        device_id=device,
        device_id_type=MESH,
    )


def each(first, last, body):
    def step(index, carry):
        body(index)
        return carry

    lax.fori_loop(first, last, step, 0)


def gather_kernel(length, count, heads, *refs):
    total = count + heads
    shards, mod_part = refs[:total], refs[total]
    full, mod_all = refs[total + 1 : 2 * total + 1], refs[2 * total + 1]
    (
        own_sem, swap_send, swap_recv, ring_send, ring_recv, side_send, side_recv,
        cross_send, cross_recv, mod_send, mod_recv, mod_sem,
    ) = refs[2 * total + 2 :]
    me = whereabouts(length)
    core, role, place, at = me["core"], me["role"], me["place"], me["at"]
    members = 2 * length
    index = 2 * place + role
    neighbour = (core, 2 * place + 1 - role)
    mine = 2 * place + core
    layers, head_layers = range(count), range(count, total)

    barrier = pltpu.get_barrier_semaphore()

    def signal(device):
        pl.semaphore_signal(barrier, inc=1, device_id=device, device_id_type=MESH)

    def greet_all(peer):
        other = (peer // members, lax.rem(peer, members))

        @pl.when((other[0] != core) | (other[1] != index))
        def _():
            signal(other)

    each(0, 2 * members, greet_all)
    pl.semaphore_wait(barrier, 2 * members - 1)

    def block(layer, turn):
        return full[layer].at[2 * at(-turn) + core]

    def onward(layer, turn):
        part = block(layer, turn)
        return remote(
            part, part, ring_send.at[layer, turn], ring_recv.at[layer, turn], me["onward"]
        )

    def across(layer, turn):
        part = block(layer, turn)
        return remote(
            part, part, side_send.at[layer, turn], side_recv.at[layer, turn], me["sibling"]
        )

    def from_sibling(layer, turn):
        part = full[layer].at[2 * at(turn) + 1 - core]
        return remote(
            part, part, side_send.at[layer, turn], side_recv.at[layer, turn], me["sibling"]
        )

    def own(layer):
        return pltpu.make_async_copy(shards[layer], full[layer].at[mine], own_sem.at[layer])

    def swap_out(layer):
        return remote(
            shards[layer], full[layer].at[index], swap_send.at[layer], swap_recv.at[layer],
            me["partner"],
        )

    def swap_in(layer):
        return remote(
            shards[layer], full[layer].at[mine], swap_send.at[layer], swap_recv.at[layer],
            me["partner"],
        )

    def lend(layer):
        return remote(
            shards[layer], full[layer].at[2 * place], swap_send.at[layer], swap_recv.at[layer],
            neighbour,
        )

    def cross(layer, turn):
        part = block(layer, turn)
        return remote(
            part, part, cross_send.at[layer - count, turn], cross_recv.at[layer - count, turn],
            neighbour,
        )

    @pl.when(core == role)
    def _():
        for layer in layers:
            own(layer).start()

    @pl.when(core != role)
    def _():
        for layer in layers:
            swap_out(layer).start()

    @pl.when(core == role)
    def _():
        for layer in head_layers:
            own(layer).start()

    @pl.when((core == 0) & (role == 0))
    def _():
        for layer in head_layers:
            lend(layer).start()

    def mod_target(peer):
        return (lax.rem(peer, 2), 2 * (peer // 2) + core)

    def mod_copy(peer):
        return remote(
            mod_part.at[peer], mod_all.at[index], mod_send.at[peer], mod_recv.at[index],
            mod_target(peer),
        )

    def mod_is_own(peer):
        return (core == role) & (peer == mine)

    mod_own = pltpu.make_async_copy(mod_part.at[mine], mod_all.at[index], mod_sem)

    def spread_mod():
        def start(peer):
            @pl.when(jnp.logical_not(mod_is_own(peer)))
            def _():
                mod_copy(peer).start()

        each(0, members, start)

        @pl.when(core == role)
        def _():
            mod_own.start()

    def gathered_mod():
        @pl.when(core == role)
        def _():
            mod_own.wait()

        def sent(peer):
            @pl.when(jnp.logical_not(mod_is_own(peer)))
            def _():
                mod_copy(peer).wait_send()

        each(0, members, sent)

        def came(source):
            @pl.when(jnp.logical_not((core == role) & (source == index)))
            def _():
                remote(
                    mod_part.at[0], mod_all.at[source], mod_send.at[0], mod_recv.at[source],
                    me["sibling"],
                ).wait_recv()

        each(0, members, came)

    def begin(layer):
        @pl.when(core == role)
        def _():
            own(layer).wait()

        @pl.when(core != role)
        def _():
            swap_in(layer).wait_recv()

        onward(layer, 0).start()
        across(layer, 0).start()

    def ring_turn(turn, more):
        for layer in layers:
            onward(layer, turn - 1).wait_recv()
            if more:
                onward(layer, turn).start()
            across(layer, turn).start()

    def ring_end():
        def end(turn):
            for layer in layers:
                onward(layer, turn).wait_send()
                across(layer, turn).wait_send()
                from_sibling(layer, turn).wait_recv()

        each(0, length - 1, end)
        for layer in layers:
            across(layer, length - 1).wait_send()
            from_sibling(layer, length - 1).wait_recv()

    def front_head(turn, first):
        for layer in head_layers:
            if first:

                @pl.when(core == 0)
                def _():
                    own(layer).wait()

                @pl.when(core == 1)
                def _():
                    cross(layer, turn).wait_recv()

            else:
                cross(layer, turn).wait_recv()
            across(layer, turn).start()

    @pl.when(role == 0)
    def _():
        for layer in layers:
            begin(layer)
        spread_mod()
        front_head(0, True)
        ring_turn(1, True)
        late = 2

        def turn_body(turn):
            ring_turn(turn, True)

            @pl.when(turn > late)
            def _():
                front_head(turn - late, False)

        each(2, length - 1, turn_body)
        ring_turn(length - 1, False)
        each(length - 1 - late, length, lambda turn: front_head(turn, False))
        ring_end()
        gathered_mod()

        def head_end(turn):
            for layer in head_layers:
                across(layer, turn).wait_send()
                from_sibling(layer, turn).wait_recv()

        each(0, length, head_end)

        @pl.when(core == 0)
        def _():
            for layer in head_layers:
                lend(layer).wait_send()

    @pl.when(role == 1)
    def _():
        spread_mod()
        for layer in head_layers:

            @pl.when(core == 1)
            def _():
                own(layer).wait()
                cross(layer, 0).start()

            @pl.when(core == 0)
            def _():
                lend(layer).wait_recv()

            onward(layer, 0).start()

        def head_turn(turn):
            for layer in head_layers:
                onward(layer, turn - 1).wait_recv()

                @pl.when(turn < length - 1)
                def _():
                    onward(layer, turn).start()

                cross(layer, turn).start()

        each(1, length, head_turn)
        for layer in layers:
            begin(layer)
        each(1, length - 1, lambda turn: ring_turn(turn, True))
        ring_turn(length - 1, False)
        ring_end()
        gathered_mod()

        def head_end(turn):
            for layer in head_layers:

                @pl.when(turn < length - 1)
                def _():
                    onward(layer, turn).wait_send()

                @pl.when((turn > 0) | (core == 1))
                def _():
                    cross(layer, turn).wait_send()

        each(0, length, head_end)

    @pl.when(core != role)
    def _():
        for layer in layers:
            swap_out(layer).wait_send()


def gather(shards, head_shards, mod_part, collective_id):
    members = lax.axis_size("dp")
    length, count, heads = members // 2, len(shards), len(head_shards)
    total = count + heads
    everything = list(shards) + list(head_shards)
    moved = sum(shard.size * 2 for shard in everything) * members
    inside = pl.BlockSpec(memory_space=pltpu.VMEM)
    results = pl.pallas_call(
        functools.partial(gather_kernel, length, count, heads),
        name="gather",
        out_shape=[jax.ShapeDtypeStruct((members,) + s.shape, s.dtype) for s in everything]
        + [jax.ShapeDtypeStruct((members,) + mod_part.shape[1:], mod_part.dtype)],
        in_specs=[inside] * (total + 1),
        out_specs=[ANY] * (total + 1),
        scratch_shapes=[
            DMA((total,)),
            DMA((total,)),
            DMA((total,)),
            DMA((total, length)),
            DMA((total, length)),
            DMA((total, length)),
            DMA((total, length)),
            DMA((heads, length)),
            DMA((heads, length)),
            DMA((members,)),
            DMA((members,)),
            DMA(()),
        ],
        compiler_params=pltpu.CompilerParams(
            collective_id=collective_id, has_side_effects=True, vmem_limit_bytes=VMEM_BYTES
        ),
        cost_estimate=pl.CostEstimate(flops=0, bytes_accessed=16 * moved, transcendentals=0),
    )(*everything, mod_part)
    return results[:count], results[count:total], results[total]


def tile_of(columns):
    for tile in (512, 384, 256, 128):
        if columns % tile == 0:
            return tile
    return columns


class Ring:
    def __init__(self, me, length, lefts, rights, scratch):
        count = len(lefts)
        self.me, self.length, self.layers = me, length, range(count)
        self.lefts, self.rights = lefts, rights
        self.left_all, self.right_all = scratch[:count], scratch[count : 2 * count]
        self.arrived, self.leaving = scratch[2 * count : 3 * count], scratch[3 * count : 4 * count]
        (
            self.own_sem, self.side_send, self.side_recv, self.ring_send, self.ring_recv,
        ) = scratch[4 * count : 4 * count + 5]

    @staticmethod
    def scratch(length, rows, columns, tokens):
        bf16, count = jnp.bfloat16, len(rows)
        return (
            [pltpu.VMEM((2, length, r, tokens), bf16) for r in rows]
            + [pltpu.VMEM((2, tokens, c), bf16) for c in columns]
            + [pltpu.VMEM((length - 1, r, c), bf16) for r, c in zip(rows, columns)]
            + [pltpu.VMEM((2, r, c), bf16) for r, c in zip(rows, columns)]
            + [
                DMA((count, 2)),
                DMA((count, 2)),
                DMA((count, 2)),
                DMA((count, 2)),
                DMA((count, length)),
            ]
        )

    def chunk(self, layer, slot, turn, add):
        spot = self.me["at"](-(turn + 1))
        columns = self.rights[layer].shape[1]
        tile = tile_of(columns)
        left, right = self.left_all[layer], self.right_all[layer]

        def body(index):
            start = pl.multiple_of(index * tile, tile)
            total = product(left[0, spot], right[0, :, pl.ds(start, tile)]) + product(
                left[1, spot], right[1, :, pl.ds(start, tile)]
            )
            if add:
                total = total + wide(self.arrived[layer][turn - 1, :, pl.ds(start, tile)])
            self.leaving[layer][slot, :, pl.ds(start, tile)] = narrow(total)

        each(0, columns // tile, body)

    def onward(self, layer, slot, turn):
        return remote(
            self.leaving[layer].at[slot],
            self.arrived[layer].at[turn],
            self.ring_send.at[layer, slot],
            self.ring_recv.at[layer, turn],
            self.me["onward"],
        )

    def inputs(self, layer):
        core, sibling = self.me["core"], self.me["sibling"]
        return [
            pltpu.make_async_copy(
                self.lefts[layer].at[:, core], self.left_all[layer].at[0], self.own_sem.at[layer, 0]
            ),
            pltpu.make_async_copy(
                self.rights[layer], self.right_all[layer].at[0], self.own_sem.at[layer, 1]
            ),
            remote(
                self.lefts[layer].at[:, 1 - core],
                self.left_all[layer].at[1],
                self.side_send.at[layer, 0],
                self.side_recv.at[layer, 0],
                sibling,
            ),
            remote(
                self.rights[layer],
                self.right_all[layer].at[1],
                self.side_send.at[layer, 1],
                self.side_recv.at[layer, 1],
                sibling,
            ),
        ]

    def run(self, finish):
        length = self.length
        for layer in self.layers:
            for copy in self.inputs(layer):
                copy.start()
        for layer in self.layers:
            for copy in self.inputs(layer):
                copy.wait()
            self.chunk(layer, 0, 0, False)
            self.onward(layer, 0, 0).start()

        def turn_body(turn):
            slot = lax.rem(turn, 2)
            for layer in self.layers:
                self.onward(layer, slot, turn - 1).wait_recv()

                @pl.when(turn >= 2)
                def _():
                    self.onward(layer, slot, turn).wait_send()

                self.chunk(layer, slot, turn, True)
                self.onward(layer, slot, turn).start()

        each(1, length - 1, turn_body)
        slot = (length - 1) % 2
        for layer in self.layers:
            self.onward(layer, slot, length - 2).wait_recv()
            if length >= 3:
                self.onward(layer, slot, length - 2).wait_send()
            self.chunk(layer, slot, length - 1, True)
            finish(layer, slot)
        for layer in self.layers:
            self.onward(layer, 1 - slot, length - 2).wait_send()


def ring_cost(length, rows, columns, tokens):
    work = sum(r * c for r, c in zip(rows, columns)) * length
    return pl.CostEstimate(flops=4 * work * tokens, bytes_accessed=64 * work, transcendentals=0)


def head_reduce_kernel(length, count, *refs):
    lefts, rights, outs = refs[:count], refs[count : 2 * count], refs[2 * count : 3 * count]
    scratch = refs[3 * count :]
    last_sem = scratch[-1]
    me = whereabouts(length)

    @pl.when(me["role"] == 0)
    def _():
        greet([me["onward"], me["before"], me["sibling"]])
        ring = Ring(me, length, lefts, rights, scratch[:-1])

        def last(layer, slot):
            return pltpu.make_async_copy(
                ring.leaving[layer].at[slot], outs[layer], last_sem.at[layer]
            )

        ring.run(lambda layer, slot: last(layer, slot).start())
        for layer in ring.layers:
            last(layer, (length - 1) % 2).wait()


def head_reduce(lefts, rights, collective_id):
    length, count = lax.axis_size("dp") // 2, len(lefts)
    rows = [left.shape[2] for left in lefts]
    columns = [right.shape[1] for right in rights]
    tokens = rights[0].shape[0]
    return pl.pallas_call(
        functools.partial(head_reduce_kernel, length, count),
        name="head_reduce",
        out_shape=[jax.ShapeDtypeStruct((r, c), jnp.bfloat16) for r, c in zip(rows, columns)],
        in_specs=[ANY] * (2 * count),
        out_specs=[ANY] * count,
        scratch_shapes=Ring.scratch(length, rows, columns, tokens) + [DMA((count,))],
        compiler_params=pltpu.CompilerParams(
            collective_id=collective_id, has_side_effects=True, vmem_limit_bytes=VMEM_BYTES
        ),
        cost_estimate=ring_cost(length, rows, columns, tokens),
    )(*lefts, *rights)


def reduce_kernel(length, count, heads, *refs):
    lefts, rights = refs[:count], refs[count : 2 * count]
    head_parts = refs[2 * count : 2 * count + heads]
    stream, mod, bias, head_sums = refs[2 * count + heads : 2 * count + heads + 4]
    refs = refs[2 * count + heads + 4 :]
    outs, head_outs = refs[:count], refs[count : count + heads]
    stream_out, mod_all, bias_all, head_all = refs[count + heads : count + heads + 4]
    scratch = refs[count + heads + 4 :]
    (
        last_send, last_recv, part_send, part_recv, stream_send, stream_recv, small_send,
        mod_recv, bias_recv, head_recv, keep_sem,
    ) = scratch[-11:]
    me = whereabouts(length)
    core, role, place = me["core"], me["role"], me["place"]
    members = 2 * length
    index, mine = 2 * place + role, 2 * place + core
    barrier = pltpu.get_barrier_semaphore()

    def greet_all(peer):
        other = (peer // members, lax.rem(peer, members))

        @pl.when((other[0] != core) | (other[1] != index))
        def _():
            pl.semaphore_signal(barrier, inc=1, device_id=other, device_id_type=MESH)

    each(0, 2 * members, greet_all)
    pl.semaphore_wait(barrier, 2 * members - 1)

    stream_copy = remote(stream, stream_out, stream_send, stream_recv, me["partner"])

    @pl.when(core != role)
    def _():
        stream_copy.start()

    def small(source, target, send, recv, device):
        return remote(source, target, send, recv, device)

    def mod_copy(peer):
        return small(
            mod, mod_all.at[mine], small_send.at[0, peer], mod_recv.at[mine], (role, peer)
        )

    def bias_copy(peer):
        return small(
            bias.at[peer], bias_all.at[mine], small_send.at[1, peer], bias_recv.at[mine],
            (role, peer),
        )

    def head_copy(peer):
        return small(
            head_sums.at[peer], head_all.at[mine], small_send.at[2, peer], head_recv.at[mine],
            (peer // members, lax.rem(peer, members)),
        )

    own_mod = pltpu.make_async_copy(mod, mod_all.at[mine], keep_sem.at[0])
    own_bias = pltpu.make_async_copy(bias.at[index], bias_all.at[mine], keep_sem.at[1])
    own_head = pltpu.make_async_copy(
        head_sums.at[core * members + index], head_all.at[mine], keep_sem.at[2]
    )

    def smalls(act_mod, act_head, act_own):
        def to_section(peer):
            @pl.when((core != role) | (peer != index))
            def _():
                act_mod(mod_copy(peer))
                act_mod(bias_copy(peer))

        each(0, members, to_section)

        @pl.when(core == role)
        def _():
            act_own(own_mod)
            act_own(own_bias)

        @pl.when(role == 0)
        def _():
            def to_all(peer):
                @pl.when(peer != core * members + index)
                def _():
                    act_head(head_copy(peer))

            each(0, 2 * members, to_all)
            act_own(own_head)

    def start(copy):
        copy.start()

    smalls(start, start, start)

    def part(layer, half):
        rows = head_outs[layer].shape[0]
        return head_parts[layer].at[pl.ds(half * rows, rows)]

    def kept(layer):
        return pltpu.make_async_copy(part(layer, 0), head_outs[layer], part_send.at[layer, 0])

    def handed(layer, half, device):
        return remote(
            part(layer, half), head_outs[layer], part_send.at[layer, half], part_recv.at[layer],
            device,
        )

    @pl.when((role == 0) & (core == 0))
    def _():
        for layer in range(heads):
            kept(layer).start()
            handed(layer, 1, me["sibling"]).start()

    @pl.when((role == 0) & (core == 1))
    def _():
        for layer in range(heads):
            handed(layer, 0, (0, 2 * place + 1)).start()
            handed(layer, 1, (1, 2 * place + 1)).start()

    ring = Ring(me, length, lefts, rights, scratch[:-11])

    def local_last(layer, slot):
        return pltpu.make_async_copy(ring.leaving[layer].at[slot], outs[layer], last_send.at[layer])

    def remote_last(layer, slot):
        return remote(
            ring.leaving[layer].at[slot], outs[layer], last_send.at[layer], last_recv.at[layer],
            me["partner"],
        )

    def finish(layer, slot):
        @pl.when(core == role)
        def _():
            local_last(layer, slot).start()

        @pl.when(core != role)
        def _():
            remote_last(layer, slot).start()

    ring.run(finish)

    @pl.when((role == 0) & (core == 0))
    def _():
        for layer in range(heads):
            kept(layer).wait()
            handed(layer, 1, me["sibling"]).wait_send()

    @pl.when((role == 0) & (core == 1))
    def _():
        for layer in range(heads):
            handed(layer, 0, (0, 2 * place + 1)).wait_send()
            handed(layer, 1, (1, 2 * place + 1)).wait_send()

    @pl.when((role == 1) | (core == 1))
    def _():
        for layer in range(heads):
            handed(layer, 0, me["sibling"]).wait_recv()

    @pl.when(core != role)
    def _():
        stream_copy.wait()

    smalls(lambda copy: copy.wait_send(), lambda copy: copy.wait_send(), lambda copy: copy.wait())

    def came(source):
        @pl.when((core != role) | (source != mine))
        def _():
            small(
                mod, mod_all.at[source], small_send.at[0, 0], mod_recv.at[source], me["sibling"]
            ).wait_recv()
            small(
                bias.at[0], bias_all.at[source], small_send.at[1, 0], bias_recv.at[source],
                me["sibling"],
            ).wait_recv()

        @pl.when((role != 0) | (source != mine))
        def _():
            small(
                head_sums.at[0], head_all.at[source], small_send.at[2, 0], head_recv.at[source],
                me["sibling"],
            ).wait_recv()

    each(0, members, came)
    slot = (length - 1) % 2
    for layer in ring.layers:

        @pl.when(core == role)
        def _():
            local_last(layer, slot).wait()

        @pl.when(core != role)
        def _():
            remote_last(layer, slot).wait()


def reduce(lefts, rights, head_parts, stream, mod, bias, head_sums, collective_id):
    members = lax.axis_size("dp")
    length, count, heads = members // 2, len(lefts), len(head_parts)
    rows = [left.shape[2] for left in lefts]
    columns = [right.shape[1] for right in rights]
    tokens = rights[0].shape[0]
    bf16 = jnp.bfloat16
    inside = pl.BlockSpec(memory_space=pltpu.VMEM)
    small = [mod.shape, bias.shape[1:], head_sums.shape[1:]]
    results = pl.pallas_call(
        functools.partial(reduce_kernel, length, count, heads),
        name="reduce",
        out_shape=[jax.ShapeDtypeStruct((r, c), bf16) for r, c in zip(rows, columns)]
        + [jax.ShapeDtypeStruct((h.shape[0] // 2, h.shape[1]), bf16) for h in head_parts]
        + [jax.ShapeDtypeStruct(stream.shape, stream.dtype)]
        + [
            jax.ShapeDtypeStruct((members,) + shape, array.dtype)
            for shape, array in zip(small, (mod, bias, head_sums))
        ],
        in_specs=[ANY] * (2 * count) + [inside] * heads + [ANY] + [inside] * 3,
        out_specs=[ANY] * (count + heads + 4),
        scratch_shapes=Ring.scratch(length, rows, columns, tokens)
        + [
            DMA((count,)),
            DMA((count,)),
            DMA((heads, 2)),
            DMA((heads,)),
            DMA(()),
            DMA(()),
            DMA((3, 2 * members)),
            DMA((members,)),
            DMA((members,)),
            DMA((members,)),
            DMA((3,)),
        ],
        compiler_params=pltpu.CompilerParams(
            collective_id=collective_id, has_side_effects=True, vmem_limit_bytes=VMEM_BYTES
        ),
        cost_estimate=ring_cost(length, rows, columns, tokens),
    )(*lefts, *rights, *head_parts, stream, mod, bias, head_sums)
    return (results[:count], results[count : count + heads]) + tuple(results[count + heads :])


def spread_kernel(members, given, taken, keep_sem, send_sem, recv_sem):
    core, index = lax.axis_index("section"), lax.axis_index("dp")
    here = core * members + index
    barrier = pltpu.get_barrier_semaphore()

    def others(act):
        def body(peer):
            @pl.when(peer != here)
            def _():
                act(peer, (peer // members, lax.rem(peer, members)))

        each(0, 2 * members, body)

    def copy(peer, device):
        return remote(given, taken.at[here], send_sem.at[peer], recv_sem.at[here], device)

    own = pltpu.make_async_copy(given, taken.at[here], keep_sem)
    own.start()
    others(
        lambda peer, device: pl.semaphore_signal(
            barrier, inc=1, device_id=device, device_id_type=MESH
        )
    )
    pl.semaphore_wait(barrier, 2 * members - 1)
    others(lambda peer, device: copy(peer, device).start())
    others(lambda peer, device: copy(peer, device).wait_send())
    others(
        lambda peer, device: remote(
            given, taken.at[peer], send_sem.at[peer], recv_sem.at[peer], device
        ).wait_recv()
    )
    own.wait()


def spread(block, collective_id):
    members = lax.axis_size("dp")
    return pl.pallas_call(
        functools.partial(spread_kernel, members),
        name="spread",
        out_shape=jax.ShapeDtypeStruct((2 * members,) + block.shape, block.dtype),
        in_specs=[pl.BlockSpec(memory_space=pltpu.VMEM)],
        out_specs=ANY,
        scratch_shapes=[DMA(()), DMA((2 * members,)), DMA((2 * members,))],
        compiler_params=pltpu.CompilerParams(collective_id=collective_id, has_side_effects=True),
    )(block)


def local_grad(function, primal, cotangent_in):
    return jax.vjp(function, primal)[1](cotangent_in)[0]


def column_sums(values):
    return jnp.sum(wide(values), 0)


def blocked_t(values, members):
    tokens, features = values.shape
    return values.T.reshape(members // 2, 2, features // members, tokens)


def normed_of(values):
    center = values - jnp.mean(values, -1, keepdims=True)
    inverse = lax.rsqrt(jnp.mean(center * center, -1, keepdims=True) + EPSILON)
    return center * inverse, inverse


def lane_window(head, head_size):
    start = head * head_size
    base = start // 128 * 128
    width = -(-(start + head_size - base) // 128) * 128
    return base, width, start - base


def head_only(block, inside, head_size):
    lanes = lax.broadcasted_iota(jnp.int32, block.shape, 1)
    keep = (lanes >= inside) & (lanes < inside + head_size)
    return jnp.where(keep, block, jnp.zeros_like(block))


def attend_kernel(
    head_count, hidden, pieces, pack_w, pack_b, out_w, out_b,
    input_out, packed_out, probs_out, mixed_out, attn_out, after_out, mixed_acc,
):
    channels = hidden.shape[1]
    head_size = channels // head_count
    scaling = head_size ** (-0.5)
    residual = wide(hidden[...])
    normed, _ = normed_of(residual)
    attn_input = narrow(normed * (1.0 + pieces[0, 1:2]) + pieces[0, 0:1])
    input_out[...] = attn_input
    packed_out[...] = narrow(product(attn_input, pack_w[...]) + pack_b[...])
    mixed_acc[...] = jnp.zeros_like(mixed_acc)
    for head in range(head_count):
        base, width, inside = lane_window(head, head_size)
        queries = packed_out[:, base : base + width]
        keys = head_only(packed_out[:, channels + base : channels + base + width], inside, head_size)
        values = head_only(
            packed_out[:, 2 * channels + base : 2 * channels + base + width], inside, head_size
        )
        scores = product_right_t(queries, keys) * scaling
        exponent = jnp.exp(scores - jnp.max(scores, -1, keepdims=True))
        probs = narrow(exponent * (1.0 / jnp.sum(exponent, -1, keepdims=True)))
        probs_out[0, head] = probs
        mixed_acc[:, base : base + width] += product(probs, values)
    mixed = narrow(mixed_acc[...])
    mixed_out[...] = mixed
    out = product(mixed, out_w[...]) + out_b[...]
    attn_out[...] = narrow(out)
    after_out[...] = residual + pieces[0, 2:3] * out


def rows_spec(seq_len, columns):
    return pl.BlockSpec((seq_len, columns), lambda i: (i, 0))


def fixed_spec(shape):
    zeros = (0,) * len(shape)
    return pl.BlockSpec(shape, lambda i: zeros, pipeline_mode=pl.Buffered(1))


def attend(hidden, pieces, pack_w, pack_b, out_w, out_b):
    tokens, channels = hidden.shape
    images = pieces.shape[0]
    seq = tokens // images
    bf16, f32 = jnp.bfloat16, jnp.float32
    work = tokens * channels * (4 * channels + 2 * seq)
    return pl.pallas_call(
        functools.partial(attend_kernel, HEADS),
        grid=(images,),
        name="attend",
        in_specs=[
            rows_spec(seq, channels),
            pl.BlockSpec((1,) + pieces.shape[1:], lambda i: (i, 0, 0)),
            fixed_spec(pack_w.shape),
            fixed_spec(pack_b.shape),
            fixed_spec(out_w.shape),
            fixed_spec(out_b.shape),
        ],
        out_specs=[
            rows_spec(seq, channels),
            rows_spec(seq, 3 * channels),
            pl.BlockSpec((1, HEADS, seq, seq), lambda i: (i, 0, 0, 0)),
            rows_spec(seq, channels),
            rows_spec(seq, channels),
            rows_spec(seq, channels),
        ],
        out_shape=[
            jax.ShapeDtypeStruct((tokens, channels), bf16),
            jax.ShapeDtypeStruct((tokens, 3 * channels), bf16),
            jax.ShapeDtypeStruct((images, HEADS, seq, seq), bf16),
            jax.ShapeDtypeStruct((tokens, channels), bf16),
            jax.ShapeDtypeStruct((tokens, channels), bf16),
            jax.ShapeDtypeStruct((tokens, channels), f32),
        ],
        scratch_shapes=[pltpu.VMEM((seq, channels), f32)],
        compiler_params=pltpu.CompilerParams(vmem_limit_bytes=VMEM_BYTES),
        cost_estimate=pl.CostEstimate(
            flops=2 * work, bytes_accessed=40 * 2**20, transcendentals=0
        ),
    )(hidden, pieces, pack_w, pack_b, out_w, out_b)


def per_image(values, images):
    return values.reshape(images, values.shape[0] // images, values.shape[1])


GELU_A, GELU_B = 0.7978845608028654, 0.044715


def mlp_kernel(
    after, pieces, up_w, up_b, down_w, down_b,
    input_out, act_out, slope_out, mlp_out, final_out, input_keep, total,
):
    step, steps = pl.program_id(0), pl.num_programs(0)
    images = pieces.shape[0]

    @pl.when(step == 0)
    def _():
        normed, _ = normed_of(per_image(after[...], images))
        rows = narrow(normed * (1.0 + pieces[:, 4:5]) + pieces[:, 3:4]).reshape(after.shape)
        input_keep[...] = rows
        input_out[...] = rows
        total[...] = jnp.zeros_like(total)

    pre = product(input_keep[...], up_w[...]) + up_b[...]
    square = pre * pre
    tanh = jnp.tanh(GELU_A * pre * (1.0 + GELU_B * square))
    half = 0.5 + 0.5 * tanh
    act = narrow(pre * half)
    act_out[...] = act
    slope_out[...] = narrow(
        half + pre * (0.5 - 0.5 * tanh * tanh) * (GELU_A + (3.0 * GELU_A * GELU_B) * square)
    )
    total[...] += product(act, down_w[...])

    @pl.when(step == steps - 1)
    def _():
        out = total[...] + down_b[...]
        mlp_out[...] = narrow(out)
        final = per_image(after[...], images) + pieces[:, 5:6] * per_image(out, images)
        final_out[...] = narrow(final * pieces[:, 6:7]).reshape(after.shape)


def feed_tile(width):
    return 1152 if width % 1152 == 0 else width


def mlp(after, pieces, up_w, up_b, down_w, down_b):
    tokens, channels = after.shape
    width = up_w.shape[1]
    tile = feed_tile(width)
    bf16, f32 = jnp.bfloat16, jnp.float32
    columns = pl.BlockSpec((tokens, tile), lambda i: (0, i))
    return pl.pallas_call(
        mlp_kernel,
        grid=(width // tile,),
        name="mlp",
        in_specs=[
            fixed_spec(after.shape),
            fixed_spec(pieces.shape),
            pl.BlockSpec((channels, tile), lambda i: (0, i)),
            pl.BlockSpec((1, tile), lambda i: (0, i)),
            pl.BlockSpec((tile, channels), lambda i: (i, 0)),
            fixed_spec(down_b.shape),
        ],
        out_specs=[
            fixed_spec((tokens, channels)),
            columns,
            columns,
            fixed_spec((tokens, channels)),
            fixed_spec((tokens, channels)),
        ],
        out_shape=[
            jax.ShapeDtypeStruct((tokens, channels), bf16),
            jax.ShapeDtypeStruct((tokens, width), bf16),
            jax.ShapeDtypeStruct((tokens, width), bf16),
            jax.ShapeDtypeStruct((tokens, channels), bf16),
            jax.ShapeDtypeStruct((tokens, channels), bf16),
        ],
        scratch_shapes=[pltpu.VMEM((tokens, channels), bf16), pltpu.VMEM((tokens, channels), f32)],
        compiler_params=pltpu.CompilerParams(vmem_limit_bytes=VMEM_BYTES),
        cost_estimate=pl.CostEstimate(
            flops=4 * tokens * channels * width, bytes_accessed=40 * 2**20, transcendentals=0
        ),
    )(after, pieces, up_w, up_b, down_w, down_b)


def sum_rows(values):
    return product(jnp.ones((8, values.shape[0]), jnp.bfloat16), values)


def layer_norm_back(grad_in, normed, inverse):
    return inverse * (
        grad_in
        - jnp.mean(grad_in, -1, keepdims=True)
        - normed * jnp.mean(grad_in * normed, -1, keepdims=True)
    )


def mlp_back_kernel(
    grad, after, pieces, slope, mlp_out, attn_out, up_w, down_w,
    grad_mlp_out, grad_pre_out, grad_after_out, grad_attn_out, sums_out, pre_sums, out_sums,
    total,
):
    step, steps = pl.program_id(0), pl.num_programs(0)
    images = pieces.shape[0]

    @pl.when(step == 0)
    def _():
        given = per_image(grad[...], images)
        rows = narrow(pieces[:, 5:6] * given).reshape(grad.shape)
        grad_mlp_out[...] = rows
        sums_out[:, 5] = jnp.sum(given * per_image(wide(mlp_out[...]), images), 1)
        out_sums[0] = sum_rows(rows)
        total[...] = jnp.zeros_like(total)

    grad_pre = narrow(wide(slope[...]) * product_right_t(grad_mlp_out[...], down_w[...]))
    grad_pre_out[...] = grad_pre
    pre_sums[...] = sum_rows(grad_pre)
    total[...] += product_right_t(grad_pre, up_w[...])

    @pl.when(step == steps - 1)
    def _():
        normed, inverse = normed_of(per_image(after[...], images))
        grad_min = per_image(total[...], images)
        sums_out[:, 3] = jnp.sum(grad_min, 1)
        sums_out[:, 4] = jnp.sum(grad_min * normed, 1)
        grad_after = per_image(grad[...], images) + layer_norm_back(
            grad_min * (1.0 + pieces[:, 4:5]), normed, inverse
        )
        grad_after_out[...] = grad_after.reshape(grad.shape)
        rows = narrow(pieces[:, 2:3] * grad_after).reshape(grad.shape)
        grad_attn_out[...] = rows
        sums_out[:, 2] = jnp.sum(grad_after * per_image(wide(attn_out[...]), images), 1)
        out_sums[1] = sum_rows(rows)


def mlp_back(grad, after, pieces, slope, mlp_out, attn_out, up_w, down_w):
    tokens, channels = after.shape
    images = pieces.shape[0]
    width = up_w.shape[1]
    tile = feed_tile(width)
    bf16, f32 = jnp.bfloat16, jnp.float32
    columns = pl.BlockSpec((tokens, tile), lambda i: (0, i))
    rows = fixed_spec((tokens, channels))
    return pl.pallas_call(
        mlp_back_kernel,
        grid=(width // tile,),
        name="mlp_back",
        in_specs=[
            rows,
            rows,
            fixed_spec(pieces.shape),
            columns,
            rows,
            rows,
            pl.BlockSpec((channels, tile), lambda i: (0, i)),
            pl.BlockSpec((tile, channels), lambda i: (i, 0)),
        ],
        out_specs=[
            rows,
            columns,
            rows,
            rows,
            fixed_spec((images, 8, channels)),
            pl.BlockSpec((8, tile), lambda i: (0, i)),
            fixed_spec((2, 8, channels)),
        ],
        out_shape=[
            jax.ShapeDtypeStruct((tokens, channels), bf16),
            jax.ShapeDtypeStruct((tokens, width), bf16),
            jax.ShapeDtypeStruct((tokens, channels), f32),
            jax.ShapeDtypeStruct((tokens, channels), bf16),
            jax.ShapeDtypeStruct((images, 8, channels), f32),
            jax.ShapeDtypeStruct((8, width), f32),
            jax.ShapeDtypeStruct((2, 8, channels), f32),
        ],
        scratch_shapes=[pltpu.VMEM((tokens, channels), f32)],
        compiler_params=pltpu.CompilerParams(vmem_limit_bytes=VMEM_BYTES),
        cost_estimate=pl.CostEstimate(
            flops=4 * tokens * channels * width, bytes_accessed=40 * 2**20, transcendentals=0
        ),
    )(grad, after, pieces, slope, mlp_out, attn_out, up_w, down_w)


def attend_back_kernel(
    head_count, hidden, pieces, packed, probs_in, grad_attn, grad_after, pack_w, out_w,
    grad_packed_out, grad_hidden_out, sums_out, pack_sums, acc, grad_mixed_keep,
):
    image = pl.program_id(0)
    channels = hidden.shape[1]
    head_size = channels // head_count
    scaling = head_size ** (-0.5)
    grad_mixed_keep[...] = narrow(product_right_t(grad_attn[...], out_w[...]))
    acc[...] = jnp.zeros_like(acc)
    for head in range(head_count):
        base, width, inside = lane_window(head, head_size)
        q_at, k_at, v_at = (slice(j * channels + base, j * channels + base + width) for j in range(3))
        queries = head_only(packed[:, q_at], inside, head_size)
        keys = head_only(packed[:, k_at], inside, head_size)
        grad_mixed = head_only(grad_mixed_keep[:, q_at], inside, head_size)
        probs = probs_in[0, head]
        grad_probs = product_right_t(grad_mixed, packed[:, v_at])
        probs_wide = wide(probs)
        weighted = probs_wide * grad_probs
        grad_scores = narrow(weighted - probs_wide * jnp.sum(weighted, -1, keepdims=True))
        acc[:, v_at] += product_left_t(probs, grad_mixed)
        acc[:, q_at] += product(grad_scores, keys) * scaling
        acc[:, k_at] += product_left_t(grad_scores, queries) * scaling
    grad_packed = narrow(acc[...])
    grad_packed_out[...] = grad_packed
    column_totals = sum_rows(grad_packed)

    @pl.when(image == 0)
    def _():
        pack_sums[...] = column_totals

    @pl.when(image > 0)
    def _():
        pack_sums[...] += column_totals

    grad_ain = product_right_t(grad_packed, pack_w[...])
    normed, inverse = normed_of(wide(hidden[...]))
    sums_out[0, 0:1] = jnp.sum(grad_ain, 0, keepdims=True)
    sums_out[0, 1:2] = jnp.sum(grad_ain * normed, 0, keepdims=True)
    grad_hidden_out[...] = narrow(
        grad_after[...] + layer_norm_back(grad_ain * (1.0 + pieces[0, 1:2]), normed, inverse)
    )


def attend_back(hidden, pieces, packed, probs, grad_attn, grad_after, pack_w, out_w):
    tokens, channels = hidden.shape
    images = pieces.shape[0]
    seq = tokens // images
    bf16, f32 = jnp.bfloat16, jnp.float32
    work = tokens * channels * (4 * channels + 5 * seq)
    rows = rows_spec(seq, channels)
    return pl.pallas_call(
        functools.partial(attend_back_kernel, HEADS),
        grid=(images,),
        name="attend_back",
        in_specs=[
            rows,
            pl.BlockSpec((1,) + pieces.shape[1:], lambda i: (i, 0, 0)),
            rows_spec(seq, 3 * channels),
            pl.BlockSpec((1, HEADS, seq, seq), lambda i: (i, 0, 0, 0)),
            rows,
            rows,
            fixed_spec(pack_w.shape),
            fixed_spec(out_w.shape),
        ],
        out_specs=[
            rows_spec(seq, 3 * channels),
            rows,
            pl.BlockSpec((1, 8, channels), lambda i: (i, 0, 0)),
            fixed_spec((8, 3 * channels)),
        ],
        out_shape=[
            jax.ShapeDtypeStruct((tokens, 3 * channels), bf16),
            jax.ShapeDtypeStruct((tokens, channels), bf16),
            jax.ShapeDtypeStruct((images, 8, channels), f32),
            jax.ShapeDtypeStruct((8, 3 * channels), f32),
        ],
        scratch_shapes=[
            pltpu.VMEM((seq, 3 * channels), f32),
            pltpu.VMEM((seq, channels), bf16),
        ],
        compiler_params=pltpu.CompilerParams(vmem_limit_bytes=VMEM_BYTES),
        cost_estimate=pl.CostEstimate(
            flops=2 * work, bytes_accessed=40 * 2**20, transcendentals=0
        ),
    )(hidden, pieces, packed, probs, grad_attn, grad_after, pack_w, out_w)


def block_forward(hidden, pieces, weights):
    pack_w, pack_b, out_w, out_b, up_w, up_b, down_w, down_b = weights
    attn_input, packed, probs, mixed, attn_out, after = attend(
        hidden, pieces, pack_w, pack_b, out_w, out_b
    )
    mlp_input, act, slope, mlp_out, final = mlp(after, pieces, up_w, up_b, down_w, down_b)
    return final, (attn_input, packed, probs, mixed, attn_out, after, mlp_input, act, slope, mlp_out)


def block_backward(hidden, saved_state, pieces, weights, grad):
    pack_w, pack_b, out_w, out_b, up_w, up_b, down_w, down_b = weights
    attn_input, packed, probs, mixed, attn_out, after, mlp_input, act, slope, mlp_out = saved_state
    grad_mlp, grad_pre, grad_after, grad_attn, high_sums, pre_sums, out_sums = mlp_back(
        grad, after, pieces, slope, mlp_out, attn_out, up_w, down_w
    )
    grad_packed, grad_hidden, low_sums, pack_sums = attend_back(
        hidden, pieces, packed, probs, grad_attn, grad_after, pack_w, out_w
    )
    images, channels = pieces.shape[0], hidden.shape[1]
    grad_mod = narrow(
        jnp.concatenate([low_sums[:, 0:2], high_sums[:, 2:6]], 1).reshape(images, 6 * channels)
    )
    pack_row = pack_sums[0]
    bias_grads = (
        jnp.concatenate([pack_row[:channels], pack_row[2 * channels :]]),
        out_sums[1, 0],
        pre_sums[0],
        out_sums[0, 0],
    )
    return grad_hidden, (grad_mlp, grad_pre, grad_attn, grad_packed), bias_grads, grad_mod


def head_pass(hidden_rows, target_rows, live_rows, head_weights, members):
    in_weight, in_bias, mid_weight, mid_bias, out_weight, out_bias = head_weights
    pre_first = product(hidden_rows, in_weight) + in_bias
    act_first = narrow(jax.nn.silu(pre_first))
    pre_second = product(act_first, mid_weight) + mid_bias
    act_second = narrow(jax.nn.silu(pre_second))
    feature = product(act_second, out_weight) + out_bias
    inverse_feature = lax.rsqrt(jnp.sum(feature * feature, -1, keepdims=True) + EPSILON)
    unit_feature = feature * inverse_feature
    target_float = wide(target_rows)
    unit_target = target_float * lax.rsqrt(
        jnp.sum(target_float * target_float, -1, keepdims=True) + EPSILON
    )
    cosine = jnp.sum(unit_feature * unit_target, -1)
    loss_part = 0.5 * jnp.sum(live_rows * (1.0 - cosine))
    grad_unit = -0.5 * live_rows[:, None] * unit_target
    grad_feature = narrow(
        inverse_feature
        * (grad_unit - unit_feature * jnp.sum(grad_unit * unit_feature, -1, keepdims=True))
    )
    grad_second = narrow(
        local_grad(jax.nn.silu, pre_second, product_right_t(grad_feature, out_weight))
    )
    grad_first = narrow(
        local_grad(jax.nn.silu, pre_first, product_right_t(grad_second, mid_weight))
    )
    grad_hidden = product_right_t(grad_first, in_weight)

    def in_halves(values):
        tokens, features = values.shape
        rows = features // (2 * members)
        cut = values.T.reshape(2, members, rows, tokens)
        return jnp.swapaxes(cut, 0, 1).reshape(members // 2, 2, 2 * rows, tokens)

    lefts = (in_halves(act_second), in_halves(act_first), in_halves(grad_first))
    rights = (grad_feature, grad_second, hidden_rows)
    sums = (column_sums(grad_first), column_sums(grad_second), column_sums(grad_feature))
    return (grad_hidden, loss_part, lefts, rights, sums)


def on_device(
    tokens_in,
    cotangent,
    targets,
    buckets,
    counts,
    time_table,
    modulate_weight,
    modulate_bias,
    qkv_weight,
    qv_bias,
    attn_weight,
    attn_bias,
    up_weight,
    up_bias,
    down_weight,
    down_bias,
    project_in_weight,
    project_in_bias,
    project_mid_weight,
    project_mid_bias,
    project_out_weight,
    project_out_bias,
):
    members = lax.axis_size("dp")
    core = lax.axis_index("section")
    index = lax.axis_index("dp")
    place, role = index // 2, index % 2
    is_first = role == 0
    own = 2 * place + core
    channels = tokens_in.shape[1]
    images = tokens_in.shape[0] // SEQ
    pairs_swap, pairs_up, pairs_back = [], [], []
    for pair in range(members // 2):
        low, high = 2 * pair, 2 * pair + 1
        pairs_swap += [(low, low), (members + low, high), (high, members + low), (members + high, members + high)]
        pairs_up += [(low, high), (members + low, members + high)]
        pairs_back += [(high, low), (members + high, members + low)]
    axes = ("section", "dp")

    def swap(values):
        return lax.ppermute(values, axes, pairs_swap)

    all_buckets = lax.all_gather(buckets, "dp", axis=0, tiled=True)
    one_hot = (
        all_buckets[:, None] == jnp.arange(time_table.shape[0], dtype=jnp.int32)[None, :]
    ).astype(jnp.float32)
    conditioning = jnp.dot(one_hot, time_table, precision=HIGHEST)
    silu_all = narrow(jax.nn.silu(conditioning))
    depth = modulate_weight.shape[1]
    silu_depth = lax.dynamic_slice_in_dim(silu_all, index * depth, depth, 1)
    mod_part = product(silu_depth, modulate_weight[0])
    share = modulate_bias.shape[1]
    bias_row = lax.dynamic_update_slice_in_dim(
        jnp.zeros((mod_part.shape[1],), jnp.float32), wide(modulate_bias[0]), index * share, 0
    )
    mod_part = (mod_part + bias_row[None]).reshape(members, images, 6 * channels)

    section_biases = (qv_bias[0], attn_bias[0], up_bias[0], down_bias[0])
    head_biases = (project_in_bias, project_mid_bias, project_out_bias)
    parts = section_biases + head_biases
    widths = [part.shape[0] for part in parts]
    lanes = 16 * 128
    packed_bias = jnp.concatenate(
        list(parts) + [jnp.zeros((lanes - sum(widths),), jnp.bfloat16)]
    ).reshape(16, 128)
    block_full, head_full, mod_all = gather(
        (packed_bias, qkv_weight[0], attn_weight[0], up_weight[0], down_weight[0], project_out_weight),
        (project_in_weight, project_mid_weight),
        mod_part,
        0,
    )
    all_bias, pack_weight, out_weight, first_weight, second_weight, head_last = block_full
    all_bias = all_bias.reshape(members, lanes)
    biases, offset = [], 0
    for width in widths:
        biases.append(wide(all_bias[:, offset : offset + width].reshape(-1)))
        offset += width
    pack_full = jnp.concatenate(
        [biases[0][:channels], jnp.zeros((channels,), jnp.float32), biases[0][channels:]]
    )

    def whole(values):
        return values.reshape(-1, values.shape[-1])

    block_weights = (
        whole(pack_weight),
        pack_full[None],
        whole(out_weight),
        biases[1][None],
        whole(first_weight),
        biases[2][None],
        whole(second_weight),
        biases[3][None],
    )
    head_weights = (
        whole(head_full[0]),
        biases[4],
        whole(head_full[1]),
        biases[5],
        whole(head_last),
        biases[6],
    )
    pieces = jnp.sum(mod_all, 0).reshape(images, 6, channels)

    own_counts = counts[own]
    image_live = (jnp.arange(images, dtype=jnp.int32) < own_counts).astype(jnp.float32)
    token_live = jnp.repeat(image_live, SEQ)
    out_scale = jnp.where(is_first, 1.0, image_live)
    scale_rows = jnp.broadcast_to(out_scale[:, None, None], (images, 2, channels))
    pieces = jnp.concatenate([pieces, scale_rows], 1)
    total_live = wide(jnp.sum(counts)) * SEQ
    payload = swap(jnp.where(is_first, cotangent, tokens_in))
    crossed = core != role
    hidden_first = jnp.where(crossed, payload, tokens_in)
    outer = jnp.where(crossed, payload, cotangent)
    own_targets = swap(targets)

    def zeros_of(function, *operands_in):
        shapes = jax.eval_shape(function, *operands_in)
        return jax.tree.map(lambda leaf: jnp.zeros(leaf.shape, leaf.dtype), shapes)

    def lefts_of(state):
        attn_input, mixed, mlp_input, act = state[0], state[3], state[6], state[7]
        return tuple(blocked_t(v, members) for v in (act, mlp_input, mixed, attn_input))

    first_out, saved_state = lax.cond(
        is_first,
        block_forward,
        lambda *operands_in: zeros_of(block_forward, *operands_in),
        hidden_first,
        pieces,
        block_weights,
    )
    hidden_second = lax.ppermute(first_out, axes, pairs_up)

    def do_head(first, target, live, state, head):
        return head_pass(first, target, live, head, members) + (lefts_of(state),)

    def do_second(second, mod, grad, live, block):
        final, state = block_forward(second, mod, block)
        outer_grad = wide(grad) * live[:, None]
        grad_input, rights, bias_grads, grad_mod = block_backward(
            second, state, mod, block, outer_grad
        )
        keep = (state[0], state[3], state[6], state[7])
        return grad_input, final, rights, bias_grads, grad_mod, keep

    def at_front(first, second, mod, grad, target, live, state, block, head):
        return (
            do_head(first, target, live, state, head),
            zeros_of(do_second, second, mod, grad, live, block),
        )

    def at_back(first, second, mod, grad, target, live, state, block, head):
        return (
            zeros_of(do_head, first, target, live, state, head),
            do_second(second, mod, grad, live, block),
        )

    head_result, second_result = lax.cond(
        is_first,
        at_front,
        at_back,
        first_out,
        hidden_second,
        pieces,
        outer,
        own_targets,
        token_live,
        saved_state,
        block_weights,
        head_weights,
    )
    grad_hidden, loss_part, head_lefts, head_rights, head_sums, first_lefts = head_result
    arrived_back = lax.ppermute(second_result[0], axes, pairs_back)
    head_parts = head_reduce(head_lefts, head_rights, 2)

    def do_first(hidden, state, mod, extra, back_grad, block, lefts, other):
        grad_input, rights, bias_grads, grad_mod = block_backward(
            hidden, state, mod, block, wide(back_grad) + extra
        )
        return grad_input, rights, bias_grads, grad_mod, lefts

    def keep_second(hidden, state, mod, extra, back_grad, block, lefts, other):
        attn_input, mixed, mlp_input, act = other[-1]
        return other[:-1] + (
            tuple(blocked_t(v, members) for v in (act, mlp_input, mixed, attn_input)),
        )

    stream, rights, bias_grads, grad_mod, lefts = lax.cond(
        is_first,
        do_first,
        keep_second,
        hidden_first,
        saved_state,
        pieces,
        grad_hidden,
        arrived_back,
        block_weights,
        first_lefts,
        second_result[1:],
    )
    bias_rows = jnp.concatenate([grads.reshape(members, -1) for grads in bias_grads], 1)
    bias_width = bias_rows.shape[1]
    bias_rows = jnp.pad(bias_rows, ((0, 0), (0, 1024 - bias_width))).reshape(members, 8, 128)
    in_sums, mid_sums, out_sums = head_sums
    devices = 2 * members
    out_width = out_sums.shape[0]
    head_rows = jnp.concatenate(
        [
            in_sums.reshape(devices, -1),
            mid_sums.reshape(devices, -1),
            jnp.broadcast_to(out_sums[None], (devices, out_width)),
            jnp.broadcast_to(loss_part[None, None], (devices, 1)),
        ],
        1,
    )
    head_width = head_rows.shape[1]
    head_rows = jnp.pad(head_rows, ((0, 0), (0, 1024 - head_width))).reshape(devices, 8, 128)
    mod_width = images * 6 * channels
    mod_lines = -(-mod_width // 2048) * 16
    mod_rows = jnp.pad(grad_mod.reshape(-1), (0, mod_lines * 128 - mod_width)).reshape(-1, 128)
    block_grads, head_grads, stream_in, mod_grads, bias_all, head_all = reduce(
        lefts, rights, head_parts, stream, mod_rows, bias_rows, head_rows, 3
    )
    down_grad, up_grad, attn_grad, qkv_grad = block_grads
    stream_own = jnp.where(crossed, stream_in, stream)
    mod_grad_all = mod_grads.reshape(members, -1)[:, :mod_width].reshape(-1, 6 * channels)
    silu_part = product_right_t(mod_grad_all, modulate_weight[0])
    lines = silu_part.shape[0]
    padded = jnp.pad(silu_part, ((0, 0), (0, 128 - depth)))
    silu_parts = spread(padded, 4)[:, :, :depth].reshape(2, members, lines, depth)
    mod_w_grad = product_left_t(silu_depth, mod_grad_all)
    mod_b_grad = lax.dynamic_slice_in_dim(column_sums(mod_grad_all), index * share, share, 0)
    silu_total = jnp.swapaxes(jnp.sum(silu_parts, 0), 0, 1).reshape(lines, channels)
    cond_grad = local_grad(jax.nn.silu, conditioning, silu_total)
    table_grad = jnp.dot(one_hot.T, cond_grad, precision=HIGHEST)

    bias_sums = jnp.sum(bias_all, 0).reshape(-1)
    bias_outs, offset = [], 0
    for part in section_biases:
        width = part.shape[0]
        bias_outs.append(bias_sums[offset : offset + width][None])
        offset += width
    sums = jnp.sum(head_all, 0).reshape(-1)
    head_share = in_sums.shape[0] // devices
    loss_value = sums[head_width - 1] / total_live
    return (
        stream_own[None],
        loss_value,
        table_grad,
        mod_w_grad[None],
        mod_b_grad[None],
        wide(qkv_grad)[None],
        bias_outs[0],
        wide(attn_grad)[None],
        bias_outs[1],
        wide(up_grad)[None],
        bias_outs[2],
        wide(down_grad)[None],
        bias_outs[3],
        wide(head_grads[2]).T,
        sums[:head_share],
        wide(head_grads[1]),
        sums[head_share : 2 * head_share],
        wide(head_grads[0]),
        sums[2 * head_share : 2 * head_share + out_width],
    )


def solution(mesh):
    in_specs = (
        P("dp", None),
        P("dp", None),
        P("dp", None),
        P("dp"),
        P(),
        P(),
        P("section", "dp", None),
        P("section", "dp"),
        P("section", "dp", None),
        P("section", "dp"),
        P("section", "dp", None),
        P("section", "dp"),
        P("section", "dp", None),
        P("section", "dp"),
        P("section", "dp", None),
        P("section", "dp"),
        P("dp", None),
        P("dp"),
        P("dp", None),
        P("dp"),
        P("dp", None),
        P("dp"),
    )
    out_specs = (
        P("section", "dp", None),
        P(),
        P(),
        P("section", "dp", None),
        P("section", "dp"),
        P("section", "dp", None),
        P("section", "dp"),
        P("section", "dp", None),
        P("section", "dp"),
        P("section", "dp", None),
        P("section", "dp"),
        P("section", "dp", None),
        P("section", "dp"),
        P(None, ("section", "dp")),
        P(("section", "dp")),
        P(("section", "dp"), None),
        P(("section", "dp")),
        P(("section", "dp"), None),
        P(),
    )
    return jax.shard_map(
        on_device, mesh=mesh, in_specs=in_specs, out_specs=out_specs, check_vma=False
    )
```

```python
import functools
import jax
import jax.numpy as jnp
from jax import lax
from jax.experimental import pallas as pl
from jax.experimental.pallas import tpu as pltpu
from jax.sharding import PartitionSpec as P

HEADS = 16
SEQ = 256
EPSILON = 1e-06
HIGHEST = lax.Precision.HIGHEST
MESH = pl.DeviceIdType.MESH
ANY = pl.BlockSpec(memory_space=pl.ANY)
DMA = pltpu.SemaphoreType.DMA
VMEM_BYTES = 60 * 2**20


def narrow(values):
    return values.astype(jnp.bfloat16)


def wide(values):
    return values.astype(jnp.float32)


def product(left_side, right_side):
    return jnp.dot(left_side, right_side, preferred_element_type=jnp.float32)


def product_left_t(left_side, right_side):
    return lax.dot_general(
        left_side, right_side, (((0,), (0,)), ((), ())), preferred_element_type=jnp.float32
    )


def product_right_t(left_side, right_side):
    return lax.dot_general(
        left_side, right_side, (((1,), (1,)), ((), ())), preferred_element_type=jnp.float32
    )


def ring_of(place, length):
    half, side = place // 2, place % 2
    return side * (length - 1 - half) + (1 - side) * half


def place_of(spot, length):
    side = spot // (length // 2)
    half = side * (length - 1 - spot) + (1 - side) * spot
    return 2 * half + side


def whereabouts(length):
    core = lax.axis_index("section")
    index = lax.axis_index("dp")
    place, role = index // 2, index % 2
    spot = ring_of(place, length)
    step = 1 - 2 * core

    def at(offset):
        return place_of(lax.rem(spot + step * offset + 4 * length, length), length)

    return dict(
        core=core,
        place=place,
        role=role,
        at=at,
        onward=(core, 2 * at(1) + role),
        before=(core, 2 * at(-1) + role),
        sibling=(1 - core, index),
        partner=(1 - core, 2 * place + 1 - role),
    )


def greet(devices):
    barrier = pltpu.get_barrier_semaphore()
    for device in devices:
        pl.semaphore_signal(barrier, inc=1, device_id=device, device_id_type=MESH)
    pl.semaphore_wait(barrier, len(devices))


def remote(source, target, send_sem, recv_sem, device):
    return pltpu.make_async_remote_copy(
        src_ref=source,
        dst_ref=target,
        send_sem=send_sem,
        recv_sem=recv_sem,
        device_id=device,
        device_id_type=MESH,
    )


def each(first, last, body):
    def step(index, carry):
        body(index)
        return carry

    lax.fori_loop(first, last, step, 0)


def gather_kernel(length, count, heads, *refs):
    total = count + heads
    shards, (mod_part, tokens, cotangent) = refs[:total], refs[total : total + 3]
    refs = refs[total + 3 :]
    full, (mod_all, rows_in) = refs[:total], refs[total : total + 2]
    (
        own_sem, swap_send, swap_recv, ring_send, ring_recv, side_send, side_recv,
        cross_send, cross_recv, mod_send, mod_recv, mod_sem, rows_send, rows_recv, mod_pair, mod_in,
        mod_sum,
    ) = refs[total + 2 :]
    me = whereabouts(length)
    core, role, place, at = me["core"], me["role"], me["place"], me["at"]
    members = 2 * length
    index = 2 * place + role
    neighbour = (core, 2 * place + 1 - role)
    mine = 2 * place + core
    layers, shared, head_layers = range(count), range(count - 1), range(count, total)

    barrier = pltpu.get_barrier_semaphore()

    def signal(device):
        pl.semaphore_signal(barrier, inc=1, device_id=device, device_id_type=MESH)

    def greet_all(peer):
        other = (peer // members, lax.rem(peer, members))

        @pl.when((other[0] != core) | (other[1] != index))
        def _():
            signal(other)

    each(0, 2 * members, greet_all)
    pl.semaphore_wait(barrier, 2 * members - 1)

    def block(layer, turn):
        return full[layer].at[2 * at(-turn) + core]

    def onward(layer, turn):
        part = block(layer, turn)
        return remote(
            part, part, ring_send.at[layer, turn], ring_recv.at[layer, turn], me["onward"]
        )

    def across(layer, turn):
        part = block(layer, turn)
        return remote(
            part, part, side_send.at[layer, turn], side_recv.at[layer, turn], me["sibling"]
        )

    def from_sibling(layer, turn):
        part = full[layer].at[2 * at(turn) + 1 - core]
        return remote(
            part, part, side_send.at[layer, turn], side_recv.at[layer, turn], me["sibling"]
        )

    def own(layer):
        return pltpu.make_async_copy(shards[layer], full[layer].at[mine], own_sem.at[layer])

    def swap_out(layer):
        return remote(
            shards[layer], full[layer].at[index], swap_send.at[layer], swap_recv.at[layer],
            me["partner"],
        )

    def swap_in(layer):
        return remote(
            shards[layer], full[layer].at[mine], swap_send.at[layer], swap_recv.at[layer],
            me["partner"],
        )

    def lend(layer):
        return remote(
            shards[layer], full[layer].at[2 * place], swap_send.at[layer], swap_recv.at[layer],
            neighbour,
        )

    def cross(layer, turn):
        part = block(layer, turn)
        return remote(
            part, part, cross_send.at[layer - count, turn], cross_recv.at[layer - count, turn],
            neighbour,
        )

    @pl.when(core == role)
    def _():
        for layer in shared:
            own(layer).start()

    @pl.when((core == 0) & (role == 0))
    def _():
        own(count - 1).start()

    def rows_move(source):
        return remote(source, rows_in, rows_send, rows_recv, me["partner"])

    @pl.when(core != role)
    def _():
        for layer in shared:
            swap_out(layer).start()

    @pl.when((core == 0) & (role == 1))
    def _():
        swap_out(count - 1).start()

    @pl.when(core == role)
    def _():
        for layer in head_layers:
            own(layer).start()

    @pl.when((core == 0) & (role == 0))
    def _():
        for layer in head_layers:
            lend(layer).start()

    mod_move = remote(mod_part, mod_in, mod_pair.at[0], mod_pair.at[1], neighbour)

    def mod_copy(peer):
        return remote(
            mod_sum.at[peer], mod_all.at[place], mod_send.at[peer], mod_recv.at[place],
            (lax.rem(peer, 2), 2 * (peer // 2) + core),
        )

    mod_own = pltpu.make_async_copy(mod_sum.at[mine], mod_all.at[place], mod_sem)

    def others(act):
        def body(peer):
            @pl.when(peer != mine)
            def _():
                act(mod_copy(peer))

        each(0, members, body)

    @pl.when(core != role)
    def _():
        mod_move.start()

    def spread_mod():
        @pl.when(core == role)
        def _():
            mod_move.wait_recv()
            mod_sum[...] = mod_part[...] + mod_in[...]
            others(lambda copy: copy.start())
            mod_own.start()

    def gathered_mod():
        @pl.when(core == role)
        def _():
            mod_own.wait()
            others(lambda copy: copy.wait_send())

        @pl.when(core != role)
        def _():
            mod_move.wait_send()

        def came(source):
            @pl.when(jnp.logical_not((core == role) & (source == place)))
            def _():
                remote(
                    mod_sum.at[0], mod_all.at[source], mod_send.at[0], mod_recv.at[source],
                    me["sibling"],
                ).wait_recv()

        each(0, length, came)

    def begin(layer):
        @pl.when(core == role)
        def _():
            own(layer).wait()

        @pl.when(core != role)
        def _():
            swap_in(layer).wait_recv()

        onward(layer, 0).start()
        across(layer, 0).start()

    def ring_turn(turn, more, which):
        for layer in which:
            onward(layer, turn - 1).wait_recv()
            if more:
                onward(layer, turn).start()
            across(layer, turn).start()

    def ring_end(which):
        def end(turn):
            for layer in which:
                onward(layer, turn).wait_send()
                across(layer, turn).wait_send()
                from_sibling(layer, turn).wait_recv()

        each(0, length - 1, end)
        for layer in which:
            across(layer, length - 1).wait_send()
            from_sibling(layer, length - 1).wait_recv()

    def front_head(turn, first):
        for layer in head_layers:
            if first:

                @pl.when(core == 0)
                def _():
                    own(layer).wait()

                @pl.when(core == 1)
                def _():
                    cross(layer, turn).wait_recv()

            else:
                cross(layer, turn).wait_recv()
            across(layer, turn).start()

    @pl.when(role == 0)
    def _():
        for layer in layers:
            begin(layer)

        @pl.when(core == 1)
        def _():
            rows_move(cotangent).start()

        front_head(0, True)
        ring_turn(1, True, layers)
        spread_mod()
        late = 2

        def turn_body(turn):
            ring_turn(turn, True, layers)

            @pl.when(turn > late)
            def _():
                front_head(turn - late, False)

        each(2, length - 1, turn_body)
        ring_turn(length - 1, False, layers)
        each(length - 1 - late, length, lambda turn: front_head(turn, False))
        ring_end(layers)
        gathered_mod()

        def head_end(turn):
            for layer in head_layers:
                across(layer, turn).wait_send()
                from_sibling(layer, turn).wait_recv()

        each(0, length, head_end)

        @pl.when(core == 0)
        def _():
            for layer in head_layers:
                lend(layer).wait_send()

    @pl.when(role == 1)
    def _():
        lag = 3

        def cross_start(turn):
            @pl.when((turn > 0) | (core == 1))
            def _():
                for layer in head_layers:
                    cross(layer, turn).start()

        for layer in head_layers:

            @pl.when(core == 1)
            def _():
                own(layer).wait()

            @pl.when(core == 0)
            def _():
                lend(layer).wait_recv()

            onward(layer, 0).start()

        def head_turn(turn):
            for layer in head_layers:
                onward(layer, turn - 1).wait_recv()

                @pl.when(turn < length - 1)
                def _():
                    onward(layer, turn).start()

            @pl.when(turn >= lag)
            def _():
                cross_start(turn - lag)

        each(1, length, head_turn)
        @pl.when(core == 0)
        def _():
            rows_move(tokens).start()

        each(length - lag, length, cross_start)
        spread_mod()
        for layer in shared:
            begin(layer)
        each(1, length - 1, lambda turn: ring_turn(turn, True, shared))
        ring_turn(length - 1, False, shared)
        ring_end(shared)
        gathered_mod()

        def head_end(turn):
            for layer in head_layers:

                @pl.when(turn < length - 1)
                def _():
                    onward(layer, turn).wait_send()

                @pl.when((turn > 0) | (core == 1))
                def _():
                    cross(layer, turn).wait_send()

        each(0, length, head_end)

    @pl.when((core == 0) & (role == 1))
    def _():
        swap_out(count - 1).wait_send()

    @pl.when(core != role)
    def _():
        for layer in shared:
            swap_out(layer).wait_send()
        rows_move(tokens).wait()


def gather(shards, head_shards, mod_part, tokens, cotangent, collective_id):
    members = lax.axis_size("dp")
    length, count, heads = members // 2, len(shards), len(head_shards)
    total = count + heads
    everything = list(shards) + list(head_shards)
    moved = sum(shard.size * 2 for shard in everything) * members
    inside = pl.BlockSpec(memory_space=pltpu.VMEM)
    results = pl.pallas_call(
        functools.partial(gather_kernel, length, count, heads),
        name="gather",
        out_shape=[jax.ShapeDtypeStruct((members,) + s.shape, s.dtype) for s in everything]
        + [jax.ShapeDtypeStruct((length,) + mod_part.shape[1:], mod_part.dtype)]
        + [jax.ShapeDtypeStruct(tokens.shape, tokens.dtype)],
        in_specs=[inside] * (total + 1) + [ANY] * 2,
        out_specs=[ANY] * (total + 2),
        scratch_shapes=[
            DMA((total,)),
            DMA((total,)),
            DMA((total,)),
            DMA((total, length)),
            DMA((total, length)),
            DMA((total, length)),
            DMA((total, length)),
            DMA((heads, length)),
            DMA((heads, length)),
            DMA((members,)),
            DMA((members,)),
            DMA(()),
            DMA(()),
            DMA(()),
            DMA((2,)),
            pltpu.VMEM(mod_part.shape, mod_part.dtype),
            pltpu.VMEM(mod_part.shape, mod_part.dtype),
        ],
        compiler_params=pltpu.CompilerParams(
            collective_id=collective_id, has_side_effects=True, vmem_limit_bytes=VMEM_BYTES
        ),
        cost_estimate=pl.CostEstimate(flops=0, bytes_accessed=16 * moved, transcendentals=0),
    )(*everything, mod_part, tokens, cotangent)
    return (results[:count], results[count:total]) + tuple(results[total:])


def tile_of(columns):
    for tile in (512, 384, 256, 128):
        if columns % tile == 0:
            return tile
    return columns


class Ring:
    def __init__(self, me, length, lefts, rights, scratch):
        count = len(lefts)
        self.me, self.length, self.layers = me, length, range(count)
        self.lefts, self.rights = lefts, rights
        self.left_all, self.right_all = scratch[:count], scratch[count : 2 * count]
        self.arrived, self.leaving = scratch[2 * count : 3 * count], scratch[3 * count : 4 * count]
        (
            self.own_sem, self.side_send, self.side_recv, self.ring_send, self.ring_recv,
        ) = scratch[4 * count : 4 * count + 5]

    @staticmethod
    def scratch(length, rows, columns, tokens):
        bf16, count = jnp.bfloat16, len(rows)
        return (
            [pltpu.VMEM((2, length, r, tokens), bf16) for r in rows]
            + [pltpu.VMEM((2, tokens, c), bf16) for c in columns]
            + [pltpu.VMEM((length - 1, r, c), bf16) for r, c in zip(rows, columns)]
            + [pltpu.VMEM((2, r, c), bf16) for r, c in zip(rows, columns)]
            + [
                DMA((count, 2)),
                DMA((count, 2)),
                DMA((count, 2)),
                DMA((count, 2)),
                DMA((count, length)),
            ]
        )

    def chunk(self, layer, slot, turn, add):
        spot = self.me["at"](-(turn + 1))
        columns = self.rights[layer].shape[1]
        tile = tile_of(columns)
        left, right = self.left_all[layer], self.right_all[layer]

        def body(index):
            start = pl.multiple_of(index * tile, tile)
            total = product(left[0, spot], right[0, :, pl.ds(start, tile)]) + product(
                left[1, spot], right[1, :, pl.ds(start, tile)]
            )
            if add:
                total = total + wide(self.arrived[layer][turn - 1, :, pl.ds(start, tile)])
            self.leaving[layer][slot, :, pl.ds(start, tile)] = narrow(total)

        each(0, columns // tile, body)

    def onward(self, layer, slot, turn):
        return remote(
            self.leaving[layer].at[slot],
            self.arrived[layer].at[turn],
            self.ring_send.at[layer, slot],
            self.ring_recv.at[layer, turn],
            self.me["onward"],
        )

    def inputs(self, layer):
        core, sibling = self.me["core"], self.me["sibling"]
        return [
            pltpu.make_async_copy(
                self.lefts[layer].at[:, core], self.left_all[layer].at[0], self.own_sem.at[layer, 0]
            ),
            pltpu.make_async_copy(
                self.rights[layer], self.right_all[layer].at[0], self.own_sem.at[layer, 1]
            ),
            remote(
                self.lefts[layer].at[:, 1 - core],
                self.left_all[layer].at[1],
                self.side_send.at[layer, 0],
                self.side_recv.at[layer, 0],
                sibling,
            ),
            remote(
                self.rights[layer],
                self.right_all[layer].at[1],
                self.side_send.at[layer, 1],
                self.side_recv.at[layer, 1],
                sibling,
            ),
        ]

    def run(self, finish, midway=None, late=None):
        length = self.length
        for layer in self.layers:
            for copy in self.inputs(layer):
                copy.start()
        for layer in self.layers:
            for copy in self.inputs(layer):
                copy.wait()
            self.chunk(layer, 0, 0, False)
            self.onward(layer, 0, 0).start()

        def turn_body(turn):
            slot = lax.rem(turn, 2)
            for layer in self.layers:
                self.onward(layer, slot, turn - 1).wait_recv()

                @pl.when(turn >= 2)
                def _():
                    self.onward(layer, slot, turn).wait_send()

                self.chunk(layer, slot, turn, True)
                self.onward(layer, slot, turn).start()

        first, second = min(3, length - 1), max(min(3, length - 1), length - 2)
        each(1, first, turn_body)
        if midway:
            midway()
        each(first, second, turn_body)
        if late:
            late()
        each(second, length - 1, turn_body)
        slot = (length - 1) % 2
        for layer in self.layers:
            self.onward(layer, slot, length - 2).wait_recv()
            if length >= 3:
                self.onward(layer, slot, length - 2).wait_send()
            self.chunk(layer, slot, length - 1, True)
            finish(layer, slot)
        for layer in self.layers:
            self.onward(layer, 1 - slot, length - 2).wait_send()


def ring_cost(length, rows, columns, tokens):
    work = sum(r * c for r, c in zip(rows, columns)) * length
    return pl.CostEstimate(flops=4 * work * tokens, bytes_accessed=64 * work, transcendentals=0)


def head_reduce_kernel(length, count, *refs):
    lefts, rights, outs = refs[:count], refs[count : 2 * count], refs[2 * count : 3 * count]
    scratch = refs[3 * count :]
    last_sem = scratch[-1]
    me = whereabouts(length)

    @pl.when(me["role"] == 0)
    def _():
        greet([me["onward"], me["before"], me["sibling"]])
        ring = Ring(me, length, lefts, rights, scratch[:-1])

        def last(layer, slot):
            return pltpu.make_async_copy(
                ring.leaving[layer].at[slot], outs[layer], last_sem.at[layer]
            )

        ring.run(lambda layer, slot: last(layer, slot).start())
        for layer in ring.layers:
            last(layer, (length - 1) % 2).wait()


def head_reduce(lefts, rights, collective_id):
    length, count = lax.axis_size("dp") // 2, len(lefts)
    rows = [left.shape[2] for left in lefts]
    columns = [right.shape[1] for right in rights]
    tokens = rights[0].shape[0]
    return pl.pallas_call(
        functools.partial(head_reduce_kernel, length, count),
        name="head_reduce",
        out_shape=[jax.ShapeDtypeStruct((r, c), jnp.bfloat16) for r, c in zip(rows, columns)],
        in_specs=[ANY] * (2 * count),
        out_specs=[ANY] * count,
        scratch_shapes=Ring.scratch(length, rows, columns, tokens) + [DMA((count,))],
        compiler_params=pltpu.CompilerParams(
            collective_id=collective_id, has_side_effects=True, vmem_limit_bytes=VMEM_BYTES
        ),
        cost_estimate=ring_cost(length, rows, columns, tokens),
    )(*lefts, *rights)


def reduce_kernel(length, count, heads, *refs):
    lefts, rights = refs[:count], refs[count : 2 * count]
    head_parts = refs[2 * count : 2 * count + heads]
    stream, mod, bias, head_sums, mod_weight = refs[2 * count + heads : 2 * count + heads + 5]
    refs = refs[2 * count + heads + 5 :]
    outs, head_outs = refs[:count], refs[count : count + heads]
    stream_out, bias_all, head_all, mod_rows, silu_all = refs[count + heads : count + heads + 5]
    scratch = refs[count + heads + 5 :]
    mod_all, silu_own, silu_keep, silu_send, silu_recv, silu_side = scratch[-6:]
    scratch = scratch[:-6]
    (
        last_send, last_recv, part_send, part_recv, stream_send, stream_recv, small_send,
        mod_recv, bias_recv, head_recv, keep_sem,
    ) = scratch[-11:]
    me = whereabouts(length)
    core, role, place = me["core"], me["role"], me["place"]
    members = 2 * length
    index, mine = 2 * place + role, 2 * place + core
    barrier = pltpu.get_barrier_semaphore()

    def greet_all(peer):
        other = (peer // members, lax.rem(peer, members))

        @pl.when((other[0] != core) | (other[1] != index))
        def _():
            pl.semaphore_signal(barrier, inc=1, device_id=other, device_id_type=MESH)

    each(0, 2 * members, greet_all)
    pl.semaphore_wait(barrier, 2 * members - 1)

    stream_copy = remote(stream, stream_out, stream_send, stream_recv, me["partner"])

    @pl.when(core != role)
    def _():
        stream_copy.start()

    def small(source, target, send, recv, device):
        return remote(source, target, send, recv, device)

    def mod_copy(peer):
        return small(
            mod, mod_all.at[mine], small_send.at[0, peer], mod_recv.at[mine], (role, peer)
        )

    def bias_copy(peer):
        return small(
            bias.at[peer], bias_all.at[mine], small_send.at[1, peer], bias_recv.at[mine],
            (role, peer),
        )

    def head_copy(peer):
        return small(
            head_sums.at[peer], head_all.at[mine], small_send.at[2, peer], head_recv.at[mine],
            (peer // members, lax.rem(peer, members)),
        )

    own_mod = pltpu.make_async_copy(mod, mod_all.at[mine], keep_sem.at[0])
    own_bias = pltpu.make_async_copy(bias.at[index], bias_all.at[mine], keep_sem.at[1])
    own_head = pltpu.make_async_copy(
        head_sums.at[core * members + index], head_all.at[mine], keep_sem.at[2]
    )

    def smalls(act_mod, act_head, act_own):
        def to_section(peer):
            @pl.when((core != role) | (peer != index))
            def _():
                act_mod(mod_copy(peer))
                act_mod(bias_copy(peer))

        each(0, members, to_section)

        @pl.when(core == role)
        def _():
            act_own(own_mod)
            act_own(own_bias)

        @pl.when(role == 0)
        def _():
            def to_all(peer):
                @pl.when(peer != core * members + index)
                def _():
                    act_head(head_copy(peer))

            each(0, 2 * members, to_all)
            act_own(own_head)

    def start(copy):
        copy.start()

    smalls(start, start, start)

    def part(layer, half):
        rows = head_outs[layer].shape[0]
        return head_parts[layer].at[pl.ds(half * rows, rows)]

    def kept(layer):
        return pltpu.make_async_copy(part(layer, 0), head_outs[layer], part_send.at[layer, 0])

    def handed(layer, half, device):
        return remote(
            part(layer, half), head_outs[layer], part_send.at[layer, half], part_recv.at[layer],
            device,
        )

    @pl.when((role == 0) & (core == 0))
    def _():
        for layer in range(heads):
            kept(layer).start()
            handed(layer, 1, me["sibling"]).start()

    @pl.when((role == 0) & (core == 1))
    def _():
        for layer in range(heads):
            handed(layer, 0, (0, 2 * place + 1)).start()
            handed(layer, 1, (1, 2 * place + 1)).start()

    ring = Ring(me, length, lefts, rights, scratch[:-11])

    def local_last(layer, slot):
        return pltpu.make_async_copy(ring.leaving[layer].at[slot], outs[layer], last_send.at[layer])

    def remote_last(layer, slot):
        return remote(
            ring.leaving[layer].at[slot], outs[layer], last_send.at[layer], last_recv.at[layer],
            me["partner"],
        )

    def finish(layer, slot):
        @pl.when(core == role)
        def _():
            local_last(layer, slot).start()

        @pl.when(core != role)
        def _():
            remote_last(layer, slot).start()

    def silu_copy(peer):
        return remote(
            silu_own, silu_all.at[core, index], silu_send.at[peer], silu_recv.at[index],
            (core, peer),
        )

    silu_kept = pltpu.make_async_copy(silu_own, silu_all.at[core, index], silu_keep)

    def others(act):
        def body(peer):
            @pl.when(peer != index)
            def _():
                act(peer)

        each(0, members, body)

    def midway():
        def mod_came(source):
            @pl.when((core != role) | (source != mine))
            def _():
                small(
                    mod, mod_all.at[source], small_send.at[0, 0], mod_recv.at[source],
                    me["sibling"],
                ).wait_recv()

        each(0, members, mod_came)

        @pl.when(core == role)
        def _():
            own_mod.wait()

        images, depth = mod.shape[0], mod_weight.shape[0]
        for source in range(members):
            mod_rows[source * images : (source + 1) * images, :] = wide(mod_all[source])
        silu_own[...] = jnp.zeros_like(silu_own)
        silu_own[:, 0:depth] = product_right_t(narrow(mod_rows[...]), mod_weight[...])
        silu_kept.start()
        others(lambda peer: silu_copy(peer).start())

    across = remote(
        silu_all.at[core], silu_all.at[core], silu_side.at[0], silu_side.at[1], me["sibling"]
    )

    def late():
        others(
            lambda peer: remote(
                silu_own, silu_all.at[core, peer], silu_send.at[peer], silu_recv.at[peer],
                (core, peer),
            ).wait_recv()
        )
        silu_kept.wait()
        across.start()

    ring.run(finish, midway, late)
    others(lambda peer: silu_copy(peer).wait_send())
    across.wait_send()
    remote(
        silu_all.at[1 - core], silu_all.at[1 - core], silu_side.at[0], silu_side.at[1],
        me["sibling"],
    ).wait_recv()

    @pl.when((role == 0) & (core == 0))
    def _():
        for layer in range(heads):
            kept(layer).wait()
            handed(layer, 1, me["sibling"]).wait_send()

    @pl.when((role == 0) & (core == 1))
    def _():
        for layer in range(heads):
            handed(layer, 0, (0, 2 * place + 1)).wait_send()
            handed(layer, 1, (1, 2 * place + 1)).wait_send()

    @pl.when((role == 1) | (core == 1))
    def _():
        for layer in range(heads):
            handed(layer, 0, me["sibling"]).wait_recv()

    @pl.when(core != role)
    def _():
        stream_copy.wait()

    smalls(
        lambda copy: copy.wait_send(),
        lambda copy: copy.wait_send(),
        lambda copy: None if copy is own_mod else copy.wait(),
    )

    def came(source):
        @pl.when((core != role) | (source != mine))
        def _():
            small(
                bias.at[0], bias_all.at[source], small_send.at[1, 0], bias_recv.at[source],
                me["sibling"],
            ).wait_recv()

        @pl.when((role != 0) | (source != mine))
        def _():
            small(
                head_sums.at[0], head_all.at[source], small_send.at[2, 0], head_recv.at[source],
                me["sibling"],
            ).wait_recv()

    each(0, members, came)
    slot = (length - 1) % 2
    for layer in ring.layers:

        @pl.when(core == role)
        def _():
            local_last(layer, slot).wait()

        @pl.when(core != role)
        def _():
            remote_last(layer, slot).wait()


def reduce(lefts, rights, head_parts, stream, mod, bias, head_sums, mod_weight, collective_id):
    members = lax.axis_size("dp")
    length, count, heads = members // 2, len(lefts), len(head_parts)
    rows = [left.shape[2] for left in lefts]
    columns = [right.shape[1] for right in rights]
    tokens = rights[0].shape[0]
    bf16 = jnp.bfloat16
    inside = pl.BlockSpec(memory_space=pltpu.VMEM)
    f32 = jnp.float32
    lines = members * mod.shape[0]
    results = pl.pallas_call(
        functools.partial(reduce_kernel, length, count, heads),
        name="reduce",
        out_shape=[jax.ShapeDtypeStruct((r, c), bf16) for r, c in zip(rows, columns)]
        + [jax.ShapeDtypeStruct((h.shape[0] // 2, h.shape[1]), bf16) for h in head_parts]
        + [jax.ShapeDtypeStruct(stream.shape, stream.dtype)]
        + [
            jax.ShapeDtypeStruct((members,) + array.shape[1:], array.dtype)
            for array in (bias, head_sums)
        ]
        + [
            jax.ShapeDtypeStruct((lines, mod.shape[1]), f32),
            jax.ShapeDtypeStruct((2, members, lines, 128), f32),
        ],
        in_specs=[ANY] * (2 * count) + [inside] * heads + [ANY] + [inside] * 4,
        out_specs=[ANY] * (count + heads + 3) + [inside, ANY],
        scratch_shapes=Ring.scratch(length, rows, columns, tokens)
        + [
            DMA((count,)),
            DMA((count,)),
            DMA((heads, 2)),
            DMA((heads,)),
            DMA(()),
            DMA(()),
            DMA((3, 2 * members)),
            DMA((members,)),
            DMA((members,)),
            DMA((members,)),
            DMA((3,)),
            pltpu.VMEM((members,) + mod.shape, mod.dtype),
            pltpu.VMEM((lines, 128), f32),
            DMA(()),
            DMA((members,)),
            DMA((members,)),
            DMA((2,)),
        ],
        compiler_params=pltpu.CompilerParams(
            collective_id=collective_id, has_side_effects=True, vmem_limit_bytes=VMEM_BYTES
        ),
        cost_estimate=ring_cost(length, rows, columns, tokens),
    )(*lefts, *rights, *head_parts, stream, mod, bias, head_sums, mod_weight)
    return (results[:count], results[count : count + heads]) + tuple(results[count + heads :])


def local_grad(function, primal, cotangent_in):
    return jax.vjp(function, primal)[1](cotangent_in)[0]


def column_sums(values):
    return jnp.sum(wide(values), 0)


def normed_of(values):
    center = values - jnp.mean(values, -1, keepdims=True)
    inverse = lax.rsqrt(jnp.mean(center * center, -1, keepdims=True) + EPSILON)
    return center * inverse, inverse


def lane_window(head, head_size):
    start = head * head_size
    base = start // 128 * 128
    width = -(-(start + head_size - base) // 128) * 128
    return base, width, start - base


def head_only(block, inside, head_size):
    lanes = lax.broadcasted_iota(jnp.int32, block.shape, 1)
    keep = (lanes >= inside) & (lanes < inside + head_size)
    return jnp.where(keep, block, jnp.zeros_like(block))


def lay_shards(left, values):
    rows = left.shape[2]
    turned = values.T
    for shard in range(values.shape[1] // rows):
        left[shard // 2, shard % 2] = turned[shard * rows : (shard + 1) * rows]


def attend_kernel(
    head_count, hidden, pieces, pack_w, pack_b, out_w, out_b,
    input_left, packed_out, probs_out, mixed_left, attn_out, after_out, mixed_acc,
):
    channels = hidden.shape[1]
    head_size = channels // head_count
    scaling = head_size ** (-0.5)
    residual = wide(hidden[...])
    normed, _ = normed_of(residual)
    attn_input = narrow(normed * (1.0 + pieces[0, 1:2]) + pieces[0, 0:1])
    lay_shards(input_left, attn_input)
    packed_out[...] = narrow(product(attn_input, pack_w[...]) + pack_b[...])
    mixed_acc[...] = jnp.zeros_like(mixed_acc)
    for head in range(head_count):
        base, width, inside = lane_window(head, head_size)
        queries = packed_out[:, base : base + width]
        keys = head_only(packed_out[:, channels + base : channels + base + width], inside, head_size)
        values = head_only(
            packed_out[:, 2 * channels + base : 2 * channels + base + width], inside, head_size
        )
        scores = product_right_t(queries, keys) * scaling
        exponent = jnp.exp(scores - jnp.max(scores, -1, keepdims=True))
        probs = narrow(exponent * (1.0 / jnp.sum(exponent, -1, keepdims=True)))
        probs_out[0, head] = probs
        mixed_acc[:, base : base + width] += product(probs, values)
    mixed = narrow(mixed_acc[...])
    lay_shards(mixed_left, mixed)
    out = product(mixed, out_w[...]) + out_b[...]
    attn_out[...] = narrow(out)
    after_out[...] = residual + pieces[0, 2:3] * out


def rows_spec(seq_len, columns):
    return pl.BlockSpec((seq_len, columns), lambda i: (i, 0))


def fixed_spec(shape):
    zeros = (0,) * len(shape)
    return pl.BlockSpec(shape, lambda i: zeros, pipeline_mode=pl.Buffered(1))


def attend(hidden, pieces, pack_w, pack_b, out_w, out_b, members):
    tokens, channels = hidden.shape
    left = (members // 2, 2, channels // members)
    images = pieces.shape[0]
    seq = tokens // images
    bf16, f32 = jnp.bfloat16, jnp.float32
    work = tokens * channels * (4 * channels + 2 * seq)
    return pl.pallas_call(
        functools.partial(attend_kernel, HEADS),
        grid=(images,),
        name="attend",
        in_specs=[
            rows_spec(seq, channels),
            pl.BlockSpec((1,) + pieces.shape[1:], lambda i: (i, 0, 0)),
            fixed_spec(pack_w.shape),
            fixed_spec(pack_b.shape),
            fixed_spec(out_w.shape),
            fixed_spec(out_b.shape),
        ],
        out_specs=[
            pl.BlockSpec(left + (seq,), lambda i: (0, 0, 0, i)),
            rows_spec(seq, 3 * channels),
            pl.BlockSpec((1, HEADS, seq, seq), lambda i: (i, 0, 0, 0)),
            pl.BlockSpec(left + (seq,), lambda i: (0, 0, 0, i)),
            rows_spec(seq, channels),
            rows_spec(seq, channels),
        ],
        out_shape=[
            jax.ShapeDtypeStruct(left + (tokens,), bf16),
            jax.ShapeDtypeStruct((tokens, 3 * channels), bf16),
            jax.ShapeDtypeStruct((images, HEADS, seq, seq), bf16),
            jax.ShapeDtypeStruct(left + (tokens,), bf16),
            jax.ShapeDtypeStruct((tokens, channels), bf16),
            jax.ShapeDtypeStruct((tokens, channels), f32),
        ],
        scratch_shapes=[pltpu.VMEM((seq, channels), f32)],
        compiler_params=pltpu.CompilerParams(vmem_limit_bytes=VMEM_BYTES),
        cost_estimate=pl.CostEstimate(
            flops=2 * work, bytes_accessed=40 * 2**20, transcendentals=0
        ),
    )(hidden, pieces, pack_w, pack_b, out_w, out_b)


def per_image(values, images):
    return values.reshape(images, values.shape[0] // images, values.shape[1])


GELU_A, GELU_B = 0.7978845608028654, 0.044715


def mlp_kernel(
    after, pieces, up_w, up_b, down_w, down_b,
    input_left, act_left, slope_out, mlp_out, final_out, input_keep, total,
):
    step, steps = pl.program_id(0), pl.num_programs(0)
    images = pieces.shape[0]

    @pl.when(step == 0)
    def _():
        normed, _ = normed_of(per_image(after[...], images))
        rows = narrow(normed * (1.0 + pieces[:, 4:5]) + pieces[:, 3:4]).reshape(after.shape)
        input_keep[...] = rows
        lay_shards(input_left, rows)
        total[...] = jnp.zeros_like(total)

    pre = product(input_keep[...], up_w[...]) + up_b[...]
    square = pre * pre
    tanh = jnp.tanh(GELU_A * pre * (1.0 + GELU_B * square))
    half = 0.5 + 0.5 * tanh
    act = narrow(pre * half)
    lay_shards(act_left, act)
    slope_out[...] = narrow(
        half + pre * (0.5 - 0.5 * tanh * tanh) * (GELU_A + (3.0 * GELU_A * GELU_B) * square)
    )
    total[...] += product(act, down_w[...])

    @pl.when(step == steps - 1)
    def _():
        out = total[...] + down_b[...]
        mlp_out[...] = narrow(out)
        final = per_image(after[...], images) + pieces[:, 5:6] * per_image(out, images)
        final_out[...] = narrow(final * pieces[:, 6:7]).reshape(after.shape)


def feed_tile(width):
    return 1152 if width % 1152 == 0 else width


def mlp(after, pieces, up_w, up_b, down_w, down_b, members):
    tokens, channels = after.shape
    width = up_w.shape[1]
    tile = feed_tile(width)
    bf16, f32 = jnp.bfloat16, jnp.float32
    columns = pl.BlockSpec((tokens, tile), lambda i: (0, i))
    left = (members // 2, 2, channels // members, tokens)
    rows = width // members
    act_block = (tile // (2 * rows), 2, rows, tokens)
    return pl.pallas_call(
        mlp_kernel,
        grid=(width // tile,),
        name="mlp",
        in_specs=[
            fixed_spec(after.shape),
            fixed_spec(pieces.shape),
            pl.BlockSpec((channels, tile), lambda i: (0, i)),
            pl.BlockSpec((1, tile), lambda i: (0, i)),
            pl.BlockSpec((tile, channels), lambda i: (i, 0)),
            fixed_spec(down_b.shape),
        ],
        out_specs=[
            fixed_spec(left),
            pl.BlockSpec(act_block, lambda i: (i, 0, 0, 0)),
            columns,
            fixed_spec((tokens, channels)),
            fixed_spec((tokens, channels)),
        ],
        out_shape=[
            jax.ShapeDtypeStruct(left, bf16),
            jax.ShapeDtypeStruct((members // 2, 2, rows, tokens), bf16),
            jax.ShapeDtypeStruct((tokens, width), bf16),
            jax.ShapeDtypeStruct((tokens, channels), bf16),
            jax.ShapeDtypeStruct((tokens, channels), bf16),
        ],
        scratch_shapes=[pltpu.VMEM((tokens, channels), bf16), pltpu.VMEM((tokens, channels), f32)],
        compiler_params=pltpu.CompilerParams(vmem_limit_bytes=VMEM_BYTES),
        cost_estimate=pl.CostEstimate(
            flops=4 * tokens * channels * width, bytes_accessed=40 * 2**20, transcendentals=0
        ),
    )(after, pieces, up_w, up_b, down_w, down_b)


def sum_rows(values):
    return product(jnp.ones((8, values.shape[0]), jnp.bfloat16), values)


def layer_norm_back(grad_in, normed, inverse):
    return inverse * (
        grad_in
        - jnp.mean(grad_in, -1, keepdims=True)
        - normed * jnp.mean(grad_in * normed, -1, keepdims=True)
    )


def mlp_back_kernel(
    grad, after, pieces, slope, mlp_out, attn_out, up_w, down_w,
    grad_mlp_out, grad_pre_out, grad_after_out, grad_attn_out, sums_out, pre_sums, out_sums,
    total,
):
    step, steps = pl.program_id(0), pl.num_programs(0)
    images = pieces.shape[0]

    @pl.when(step == 0)
    def _():
        given = per_image(grad[...], images)
        rows = narrow(pieces[:, 5:6] * given).reshape(grad.shape)
        grad_mlp_out[...] = rows
        sums_out[:, 5] = jnp.sum(given * per_image(wide(mlp_out[...]), images), 1)
        out_sums[0] = sum_rows(rows)
        total[...] = jnp.zeros_like(total)

    grad_pre = narrow(wide(slope[...]) * product_right_t(grad_mlp_out[...], down_w[...]))
    grad_pre_out[...] = grad_pre
    pre_sums[...] = sum_rows(grad_pre)
    total[...] += product_right_t(grad_pre, up_w[...])

    @pl.when(step == steps - 1)
    def _():
        normed, inverse = normed_of(per_image(after[...], images))
        grad_min = per_image(total[...], images)
        sums_out[:, 3] = jnp.sum(grad_min, 1)
        sums_out[:, 4] = jnp.sum(grad_min * normed, 1)
        grad_after = per_image(grad[...], images) + layer_norm_back(
            grad_min * (1.0 + pieces[:, 4:5]), normed, inverse
        )
        grad_after_out[...] = grad_after.reshape(grad.shape)
        rows = narrow(pieces[:, 2:3] * grad_after).reshape(grad.shape)
        grad_attn_out[...] = rows
        sums_out[:, 2] = jnp.sum(grad_after * per_image(wide(attn_out[...]), images), 1)
        out_sums[1] = sum_rows(rows)


def mlp_back(grad, after, pieces, slope, mlp_out, attn_out, up_w, down_w):
    tokens, channels = after.shape
    images = pieces.shape[0]
    width = up_w.shape[1]
    tile = feed_tile(width)
    bf16, f32 = jnp.bfloat16, jnp.float32
    columns = pl.BlockSpec((tokens, tile), lambda i: (0, i))
    rows = fixed_spec((tokens, channels))
    return pl.pallas_call(
        mlp_back_kernel,
        grid=(width // tile,),
        name="mlp_back",
        in_specs=[
            rows,
            rows,
            fixed_spec(pieces.shape),
            columns,
            rows,
            rows,
            pl.BlockSpec((channels, tile), lambda i: (0, i)),
            pl.BlockSpec((tile, channels), lambda i: (i, 0)),
        ],
        out_specs=[
            rows,
            columns,
            rows,
            rows,
            fixed_spec((images, 8, channels)),
            pl.BlockSpec((8, tile), lambda i: (0, i)),
            fixed_spec((2, 8, channels)),
        ],
        out_shape=[
            jax.ShapeDtypeStruct((tokens, channels), bf16),
            jax.ShapeDtypeStruct((tokens, width), bf16),
            jax.ShapeDtypeStruct((tokens, channels), f32),
            jax.ShapeDtypeStruct((tokens, channels), bf16),
            jax.ShapeDtypeStruct((images, 8, channels), f32),
            jax.ShapeDtypeStruct((8, width), f32),
            jax.ShapeDtypeStruct((2, 8, channels), f32),
        ],
        scratch_shapes=[pltpu.VMEM((tokens, channels), f32)],
        compiler_params=pltpu.CompilerParams(vmem_limit_bytes=VMEM_BYTES),
        cost_estimate=pl.CostEstimate(
            flops=4 * tokens * channels * width, bytes_accessed=40 * 2**20, transcendentals=0
        ),
    )(grad, after, pieces, slope, mlp_out, attn_out, up_w, down_w)


def attend_back_kernel(
    head_count, hidden, pieces, packed, probs_in, grad_attn, grad_after, pack_w, out_w,
    grad_packed_out, grad_hidden_out, sums_out, pack_sums, acc, grad_mixed_keep,
):
    image = pl.program_id(0)
    channels = hidden.shape[1]
    head_size = channels // head_count
    scaling = head_size ** (-0.5)
    grad_mixed_keep[...] = narrow(product_right_t(grad_attn[...], out_w[...]))
    acc[...] = jnp.zeros_like(acc)
    for head in range(head_count):
        base, width, inside = lane_window(head, head_size)
        q_at, k_at, v_at = (slice(j * channels + base, j * channels + base + width) for j in range(3))
        queries = head_only(packed[:, q_at], inside, head_size)
        keys = head_only(packed[:, k_at], inside, head_size)
        grad_mixed = head_only(grad_mixed_keep[:, q_at], inside, head_size)
        probs = probs_in[0, head]
        grad_probs = product_right_t(grad_mixed, packed[:, v_at])
        probs_wide = wide(probs)
        weighted = probs_wide * grad_probs
        grad_scores = narrow(weighted - probs_wide * jnp.sum(weighted, -1, keepdims=True))
        acc[:, v_at] += product_left_t(probs, grad_mixed)
        acc[:, q_at] += product(grad_scores, keys) * scaling
        acc[:, k_at] += product_left_t(grad_scores, queries) * scaling
    grad_packed = narrow(acc[...])
    grad_packed_out[...] = grad_packed
    column_totals = sum_rows(grad_packed)

    @pl.when(image == 0)
    def _():
        pack_sums[...] = column_totals

    @pl.when(image > 0)
    def _():
        pack_sums[...] += column_totals

    grad_ain = product_right_t(grad_packed, pack_w[...])
    normed, inverse = normed_of(wide(hidden[...]))
    sums_out[0, 0:1] = jnp.sum(grad_ain, 0, keepdims=True)
    sums_out[0, 1:2] = jnp.sum(grad_ain * normed, 0, keepdims=True)
    grad_hidden_out[...] = narrow(
        grad_after[...] + layer_norm_back(grad_ain * (1.0 + pieces[0, 1:2]), normed, inverse)
    )


def attend_back(hidden, pieces, packed, probs, grad_attn, grad_after, pack_w, out_w):
    tokens, channels = hidden.shape
    images = pieces.shape[0]
    seq = tokens // images
    bf16, f32 = jnp.bfloat16, jnp.float32
    work = tokens * channels * (4 * channels + 5 * seq)
    rows = rows_spec(seq, channels)
    return pl.pallas_call(
        functools.partial(attend_back_kernel, HEADS),
        grid=(images,),
        name="attend_back",
        in_specs=[
            rows,
            pl.BlockSpec((1,) + pieces.shape[1:], lambda i: (i, 0, 0)),
            rows_spec(seq, 3 * channels),
            pl.BlockSpec((1, HEADS, seq, seq), lambda i: (i, 0, 0, 0)),
            rows,
            rows,
            fixed_spec(pack_w.shape),
            fixed_spec(out_w.shape),
        ],
        out_specs=[
            rows_spec(seq, 3 * channels),
            rows,
            pl.BlockSpec((1, 8, channels), lambda i: (i, 0, 0)),
            fixed_spec((8, 3 * channels)),
        ],
        out_shape=[
            jax.ShapeDtypeStruct((tokens, 3 * channels), bf16),
            jax.ShapeDtypeStruct((tokens, channels), bf16),
            jax.ShapeDtypeStruct((images, 8, channels), f32),
            jax.ShapeDtypeStruct((8, 3 * channels), f32),
        ],
        scratch_shapes=[
            pltpu.VMEM((seq, 3 * channels), f32),
            pltpu.VMEM((seq, channels), bf16),
        ],
        compiler_params=pltpu.CompilerParams(vmem_limit_bytes=VMEM_BYTES),
        cost_estimate=pl.CostEstimate(
            flops=2 * work, bytes_accessed=40 * 2**20, transcendentals=0
        ),
    )(hidden, pieces, packed, probs, grad_attn, grad_after, pack_w, out_w)


def block_forward(hidden, pieces, weights, members):
    pack_w, pack_b, out_w, out_b, up_w, up_b, down_w, down_b = weights
    input_left, packed, probs, mixed_left, attn_out, after = attend(
        hidden, pieces, pack_w, pack_b, out_w, out_b, members
    )
    rows_left, act_left, slope, mlp_out, final = mlp(
        after, pieces, up_w, up_b, down_w, down_b, members
    )
    return (
        final,
        (packed, probs, attn_out, after, slope, mlp_out),
        (act_left, rows_left, mixed_left, input_left),
    )


def block_backward(hidden, saved_state, pieces, weights, grad):
    pack_w, pack_b, out_w, out_b, up_w, up_b, down_w, down_b = weights
    packed, probs, attn_out, after, slope, mlp_out = saved_state
    grad_mlp, grad_pre, grad_after, grad_attn, high_sums, pre_sums, out_sums = mlp_back(
        grad, after, pieces, slope, mlp_out, attn_out, up_w, down_w
    )
    grad_packed, grad_hidden, low_sums, pack_sums = attend_back(
        hidden, pieces, packed, probs, grad_attn, grad_after, pack_w, out_w
    )
    images, channels = pieces.shape[0], hidden.shape[1]
    grad_mod = narrow(
        jnp.concatenate([low_sums[:, 0:2], high_sums[:, 2:6]], 1).reshape(images, 6 * channels)
    )
    pack_row = pack_sums[0:1]
    bias_grads = (
        jnp.concatenate([pack_row[:, :channels], pack_row[:, 2 * channels :]], 1),
        out_sums[1, 0:1],
        pre_sums[0:1],
        out_sums[0, 0:1],
    )
    return grad_hidden, (grad_mlp, grad_pre, grad_attn, grad_packed), bias_grads, grad_mod


def silu_parts(values):
    gate = 0.5 + 0.5 * jnp.tanh(0.5 * values)
    return values * gate, gate * (1.0 + values * (1.0 - gate))


def head_kernel(
    members, hidden_at, target_at, live, in_w_at, in_b, mid_w_at, mid_b, out_w_at, out_b,
    grad_hidden_at, last_left_at, mid_left_at, in_left_at, grad_feature_at, grad_second_at,
    in_sums, mid_sums, out_sums, loss_out,
    hidden, target, in_w, mid_w, out_w,
    grad_hidden_out, last_left, mid_left, in_left, grad_feature_out, grad_second_out,
    act_first, slope_first, act_second, slope_second, grad_first_keep, come_sem, go_sem,
):
    width = in_w.shape[1]
    tile = 512 if width % 512 == 0 else width
    tiles = [slice(start, start + tile) for start in range(0, width, tile)]
    rows = width // (2 * members)
    pairs_in = ((hidden_at, hidden), (in_w_at, in_w), (mid_w_at, mid_w), (out_w_at, out_w), (target_at, target))
    come = [
        pltpu.make_async_copy(there, here, come_sem.at[i]) for i, (there, here) in enumerate(pairs_in)
    ]
    pairs_out = (
        (grad_hidden_out, grad_hidden_at),
        (last_left, last_left_at),
        (mid_left, mid_left_at),
        (in_left, in_left_at),
        (grad_feature_out, grad_feature_at),
        (grad_second_out, grad_second_at),
    )
    go = [
        pltpu.make_async_copy(here, there, go_sem.at[i]) for i, (here, there) in enumerate(pairs_out)
    ]

    def lay(left, values, start):
        turned = values.T
        for offset in range(0, values.shape[1], rows):
            shard = (start + offset) // rows
            half, index = shard // members, shard % members
            left[index // 2, index % 2, half * rows : (half + 1) * rows] = turned[
                offset : offset + rows
            ]

    @pl.when(lax.rem(lax.axis_index("dp"), 2) == 0)
    def _():
        for copy in come:
            copy.start()
        come[0].wait()
        come[1].wait()
        for at in tiles:
            act, slope = silu_parts(product(hidden[...], in_w[:, at]) + in_b[:, at])
            act_first[:, at] = narrow(act)
            slope_first[:, at] = narrow(slope)
        come[2].wait()
        for at in tiles:
            act, slope = silu_parts(product(act_first[...], mid_w[:, at]) + mid_b[:, at])
            act_second[:, at] = narrow(act)
            slope_second[:, at] = narrow(slope)
            lay(mid_left, act_first[:, at], at.start)
        go[2].start()
        come[3].wait()
        come[4].wait()
        feature = product(act_second[...], out_w[...]) + out_b[...]
        inverse = lax.rsqrt(jnp.sum(feature * feature, -1, keepdims=True) + EPSILON)
        unit = feature * inverse
        aim = wide(target[...])
        aim = aim * lax.rsqrt(jnp.sum(aim * aim, -1, keepdims=True) + EPSILON)
        alive = live[:, 0:1]
        cosine = jnp.sum(unit * aim, -1, keepdims=True)
        loss_out[...] = jnp.broadcast_to(
            0.5 * jnp.sum(alive * (1.0 - cosine), axis=(0, 1), keepdims=True), loss_out.shape
        )
        grad_unit = (-0.5 * alive) * aim
        grad_feature = narrow(
            inverse * (grad_unit - unit * jnp.sum(grad_unit * unit, -1, keepdims=True))
        )
        grad_feature_out[...] = grad_feature
        go[4].start()
        out_sums[...] = sum_rows(grad_feature)
        for at in tiles:
            grad_second = narrow(
                wide(slope_second[:, at]) * product_right_t(grad_feature, out_w[at, :])
            )
            grad_second_out[:, at] = grad_second
            mid_sums[:, at] = sum_rows(grad_second)
            lay(last_left, act_second[:, at], at.start)
        go[1].start()
        go[5].start()
        for at in tiles:
            grad_first = narrow(
                wide(slope_first[:, at]) * product_right_t(grad_second_out[...], mid_w[at, :])
            )
            grad_first_keep[:, at] = grad_first
            in_sums[:, at] = sum_rows(grad_first)
            part = product_right_t(grad_first, in_w[:, at])
            if at.start == 0:
                grad_hidden_out[...] = part
            else:
                grad_hidden_out[...] += part
            lay(in_left, grad_first_keep[:, at], at.start)
        go[0].start()
        go[3].start()
        for copy in go:
            copy.wait()


def head_pass(hidden, target, live, head_weights, members):
    tokens, channels = hidden.shape
    width, features = head_weights[2].shape[0], target.shape[1]
    bf16, f32 = jnp.bfloat16, jnp.float32
    left = ((members // 2, 2, width // members, tokens), bf16)
    live_lanes = jnp.broadcast_to(live[:, None], (tokens, 128))
    in_w, in_b, mid_w, mid_b, out_w, out_b = head_weights
    inside = pl.BlockSpec(memory_space=pltpu.VMEM)
    work = tokens * (channels * width + width * width + width * features)
    big = [
        ((tokens, channels), f32),
        left,
        left,
        left,
        ((tokens, features), bf16),
        ((tokens, width), bf16),
    ]
    small = [((8, width), f32), ((8, width), f32), ((8, features), f32), ((8, 128), f32)]
    results = pl.pallas_call(
        functools.partial(head_kernel, members),
        name="head",
        in_specs=[ANY, ANY, inside, ANY, inside, ANY, inside, ANY, inside],
        out_specs=[ANY] * 6 + [inside] * 4,
        out_shape=[jax.ShapeDtypeStruct(*leaf) for leaf in big + small],
        scratch_shapes=[
            pltpu.VMEM(array.shape, array.dtype) for array in (hidden, target, in_w, mid_w, out_w)
        ]
        + [pltpu.VMEM(*leaf) for leaf in big]
        + [pltpu.VMEM((tokens, width), bf16)] * 5
        + [DMA((5,)), DMA((6,))],
        compiler_params=pltpu.CompilerParams(vmem_limit_bytes=VMEM_BYTES),
        cost_estimate=pl.CostEstimate(
            flops=4 * work, bytes_accessed=40 * 2**20, transcendentals=0
        ),
    )(hidden, target, live_lanes, in_w, in_b[None], mid_w, mid_b[None], out_w, out_b[None])
    grad_hidden, last_left, mid_left, in_left, grad_feature, grad_second = results[:6]
    in_sums, mid_sums, out_sums, loss = results[6:]
    return (
        grad_hidden,
        loss[0:1],
        (last_left, mid_left, in_left),
        (grad_feature, grad_second),
        (in_sums[0:1], mid_sums[0:1], out_sums[0:1]),
    )


def hollow(shapes):
    leaves, form = jax.tree.flatten(shapes)
    results = pl.pallas_call(
        lambda *refs: None,
        name="hollow",
        out_shape=[jax.ShapeDtypeStruct(leaf.shape, leaf.dtype) for leaf in leaves],
        out_specs=[ANY if leaf.ndim else pl.BlockSpec(memory_space=pltpu.SMEM) for leaf in leaves],
    )()
    return jax.tree.unflatten(form, list(results))


def on_device(
    tokens_in,
    cotangent,
    targets,
    buckets,
    counts,
    time_table,
    modulate_weight,
    modulate_bias,
    qkv_weight,
    qv_bias,
    attn_weight,
    attn_bias,
    up_weight,
    up_bias,
    down_weight,
    down_bias,
    project_in_weight,
    project_in_bias,
    project_mid_weight,
    project_mid_bias,
    project_out_weight,
    project_out_bias,
):
    members = lax.axis_size("dp")
    core = lax.axis_index("section")
    index = lax.axis_index("dp")
    place, role = index // 2, index % 2
    is_first = role == 0
    own = 2 * place + core
    channels = tokens_in.shape[1]
    images = tokens_in.shape[0] // SEQ
    pairs_up, pairs_back, pairs_swap = [], [], []
    for pair in range(members // 2):
        low, high = 2 * pair, 2 * pair + 1
        pairs_swap += [(high, members + low)]
        pairs_up += [(low, high), (members + low, members + high)]
        pairs_back += [(high, low), (members + high, members + low)]
    axes = ("section", "dp")

    all_buckets = lax.all_gather(buckets, "dp", axis=0, tiled=True)
    one_hot = (
        all_buckets[:, None] == jnp.arange(time_table.shape[0], dtype=jnp.int32)[None, :]
    ).astype(jnp.float32)
    conditioning = jnp.dot(one_hot, time_table, precision=HIGHEST)
    silu_all = narrow(jax.nn.silu(conditioning))
    depth = modulate_weight.shape[1]
    silu_depth = lax.dynamic_slice_in_dim(silu_all, index * depth, depth, 1)
    mod_part = product(silu_depth, modulate_weight[0])
    share = modulate_bias.shape[1]
    bias_row = lax.dynamic_update_slice_in_dim(
        jnp.zeros((mod_part.shape[1],), jnp.float32), wide(modulate_bias[0]), index * share, 0
    )
    mod_part = (mod_part + bias_row[None]).reshape(members, images, 6 * channels)

    section_biases = (qv_bias[0], attn_bias[0], up_bias[0], down_bias[0])
    head_biases = (project_in_bias, project_mid_bias, project_out_bias)
    parts = section_biases + head_biases
    widths = [part.shape[0] for part in parts]
    lanes = 16 * 128
    packed_bias = jnp.concatenate(
        list(parts) + [jnp.zeros((lanes - sum(widths),), jnp.bfloat16)]
    ).reshape(16, 128)
    block_full, head_full, mod_all, rows_in = gather(
        (
            packed_bias,
            qkv_weight[0],
            attn_weight[0],
            up_weight[0],
            down_weight[0],
            project_out_weight,
        ),
        (project_in_weight, project_mid_weight),
        mod_part,
        tokens_in,
        cotangent,
        0,
    )
    all_bias, pack_weight, out_weight, first_weight, second_weight, head_last = block_full
    all_bias = all_bias.reshape(members, lanes)
    biases, offset = [], 0
    for width in widths:
        biases.append(wide(all_bias[:, offset : offset + width].reshape(-1)))
        offset += width
    pack_full = jnp.concatenate(
        [biases[0][:channels], jnp.zeros((channels,), jnp.float32), biases[0][channels:]]
    )

    def whole(values):
        return values.reshape(-1, values.shape[-1])

    block_weights = (
        whole(pack_weight),
        pack_full[None],
        whole(out_weight),
        biases[1][None],
        whole(first_weight),
        biases[2][None],
        whole(second_weight),
        biases[3][None],
    )
    head_weights = (
        whole(head_full[0]),
        biases[4],
        whole(head_full[1]),
        biases[5],
        whole(head_last),
        biases[6],
    )
    pieces = jnp.sum(mod_all, 0).reshape(images, 6, channels)

    own_counts = counts[own]
    image_live = (jnp.arange(images, dtype=jnp.int32) < own_counts).astype(jnp.float32)
    token_live = jnp.repeat(image_live, SEQ)
    out_scale = jnp.where(is_first, 1.0, image_live)
    scale_rows = jnp.broadcast_to(out_scale[:, None, None], (images, 2, channels))
    pieces = jnp.concatenate([pieces, scale_rows], 1)
    total_live = wide(jnp.sum(counts)) * SEQ
    crossed = core != role
    targets_out, rows_in = lax.optimization_barrier((targets, rows_in))
    hidden_first = jnp.where(crossed, rows_in, tokens_in)
    outer = jnp.where(crossed, rows_in, cotangent)
    own_targets = jnp.where(crossed, lax.ppermute(targets_out, axes, pairs_swap), targets)

    def unused(function, *operands_in):
        return hollow(jax.eval_shape(function, *operands_in))

    def forward(hidden, mod, block):
        return block_forward(hidden, mod, block, members)

    first_out, saved_state, first_lefts = lax.cond(
        is_first,
        forward,
        lambda *operands_in: unused(forward, *operands_in),
        hidden_first,
        pieces,
        block_weights,
    )
    hidden_second = lax.ppermute(first_out, axes, pairs_up)

    def do_second(second, mod, grad, live, block):
        final, state, lefts = forward(second, mod, block)
        outer_grad = wide(grad) * live[:, None]
        grad_input, rights, bias_grads, grad_mod = block_backward(
            second, state, mod, block, outer_grad
        )
        return grad_input, final, rights, bias_grads, grad_mod, lefts

    head_result = head_pass(first_out, own_targets, token_live, head_weights, members)
    head_lefts, head_rights = head_result[2:4]
    head_parts = head_reduce(head_lefts, head_rights + (first_out,), 2)
    hidden_second, head_result, head_parts = lax.optimization_barrier(
        (hidden_second, head_result, head_parts)
    )
    grad_hidden, loss_part, head_lefts, head_rights, head_sums = head_result
    second_result = lax.cond(
        is_first,
        lambda *operands_in: unused(do_second, *operands_in),
        do_second,
        hidden_second,
        pieces,
        outer,
        token_live,
        block_weights,
    )
    send_back = second_result[0]
    arrived_back = lax.ppermute(send_back, axes, pairs_back)
    lefts = lax.cond(
        is_first,
        lambda one, other: one,
        lambda one, other: other,
        first_lefts,
        second_result[-1],
    )
    arrived_back, lefts = lax.optimization_barrier((arrived_back, lefts))

    def do_first(hidden, state, mod, extra, back_grad, block, other):
        return block_backward(hidden, state, mod, block, wide(back_grad) + extra)

    def keep_second(hidden, state, mod, extra, back_grad, block, other):
        return other

    stream, rights, bias_grads, grad_mod = lax.cond(
        is_first,
        do_first,
        keep_second,
        hidden_first,
        saved_state,
        pieces,
        grad_hidden,
        arrived_back,
        block_weights,
        second_result[1:-1],
    )
    bias_rows = jnp.concatenate([grads.reshape(members, -1) for grads in bias_grads], 1)
    bias_width = bias_rows.shape[1]
    bias_rows = jnp.pad(bias_rows, ((0, 0), (0, 1024 - bias_width))).reshape(members, 8, 128)
    in_sums, mid_sums, out_sums = head_sums
    devices = 2 * members
    out_width = out_sums.shape[1]
    head_rows = jnp.concatenate(
        [
            in_sums.reshape(devices, -1),
            mid_sums.reshape(devices, -1),
            jnp.broadcast_to(out_sums, (devices, out_width)),
            jnp.broadcast_to(loss_part[:, 0:1], (devices, 1)),
        ],
        1,
    )
    head_width = head_rows.shape[1]
    head_rows = jnp.pad(head_rows, ((0, 0), (0, 1024 - head_width))).reshape(devices, 8, 128)
    block_grads, head_grads, stream_in, bias_all, head_all, mod_wide, silu_all_terms = reduce(
        lefts,
        rights,
        head_parts,
        stream,
        grad_mod,
        bias_rows,
        head_rows,
        modulate_weight[0],
        3,
    )
    down_grad, up_grad, attn_grad, qkv_grad = block_grads
    stream_own = jnp.where(crossed, stream_in, stream)
    mod_w_grad = product_left_t(silu_depth, narrow(mod_wide))
    mod_b_grad = lax.dynamic_slice_in_dim(jnp.sum(mod_wide, 0), index * share, share, 0)
    silu_total = jnp.sum(silu_all_terms[:, :, :, :depth], 0)
    silu_total = jnp.swapaxes(silu_total, 0, 1).reshape(-1, channels)
    cond_grad = local_grad(jax.nn.silu, conditioning, silu_total)
    table_grad = jnp.dot(one_hot.T, cond_grad, precision=HIGHEST)

    bias_sums = jnp.sum(bias_all, 0).reshape(-1)
    bias_outs, offset = [], 0
    for part in section_biases:
        width = part.shape[0]
        bias_outs.append(bias_sums[offset : offset + width][None])
        offset += width
    sums = jnp.sum(head_all, 0).reshape(-1)
    head_share = in_sums.shape[1] // devices
    loss_value = sums[head_width - 1] / total_live
    return (
        stream_own[None],
        loss_value,
        table_grad,
        mod_w_grad[None],
        mod_b_grad[None],
        wide(qkv_grad)[None],
        bias_outs[0],
        wide(attn_grad)[None],
        bias_outs[1],
        wide(up_grad)[None],
        bias_outs[2],
        wide(down_grad)[None],
        bias_outs[3],
        wide(head_grads[2]).T,
        sums[:head_share],
        wide(head_grads[1]),
        sums[head_share : 2 * head_share],
        wide(head_grads[0]),
        sums[2 * head_share : 2 * head_share + out_width],
    )


def solution(mesh):
    in_specs = (
        P("dp", None),
        P("dp", None),
        P("dp", None),
        P("dp"),
        P(),
        P(),
        P("section", "dp", None),
        P("section", "dp"),
        P("section", "dp", None),
        P("section", "dp"),
        P("section", "dp", None),
        P("section", "dp"),
        P("section", "dp", None),
        P("section", "dp"),
        P("section", "dp", None),
        P("section", "dp"),
        P("dp", None),
        P("dp"),
        P("dp", None),
        P("dp"),
        P("dp", None),
        P("dp"),
    )
    out_specs = (
        P("section", "dp", None),
        P(),
        P(),
        P("section", "dp", None),
        P("section", "dp"),
        P("section", "dp", None),
        P("section", "dp"),
        P("section", "dp", None),
        P("section", "dp"),
        P("section", "dp", None),
        P("section", "dp"),
        P("section", "dp", None),
        P("section", "dp"),
        P(None, ("section", "dp")),
        P(("section", "dp")),
        P(("section", "dp"), None),
        P(("section", "dp")),
        P(("section", "dp"), None),
        P(),
    )
    return jax.shard_map(
        on_device, mesh=mesh, in_specs=in_specs, out_specs=out_specs, check_vma=False
    )
```

```python
import functools
import jax
import jax.numpy as jnp
from jax import lax
from jax.experimental import pallas as pl
from jax.experimental.pallas import tpu as pltpu
from jax.sharding import PartitionSpec as P

HEADS = 16
SEQ = 256
EPSILON = 1e-06
HIGHEST = lax.Precision.HIGHEST
MESH = pl.DeviceIdType.MESH
ANY = pl.BlockSpec(memory_space=pl.ANY)
DMA = pltpu.SemaphoreType.DMA
VMEM_BYTES = 60 * 2**20


def narrow(values):
    return values.astype(jnp.bfloat16)


def wide(values):
    return values.astype(jnp.float32)


def product(left_side, right_side):
    return jnp.dot(left_side, right_side, preferred_element_type=jnp.float32)


def product_left_t(left_side, right_side):
    return lax.dot_general(
        left_side, right_side, (((0,), (0,)), ((), ())), preferred_element_type=jnp.float32
    )


def product_right_t(left_side, right_side):
    return lax.dot_general(
        left_side, right_side, (((1,), (1,)), ((), ())), preferred_element_type=jnp.float32
    )


def ring_of(place, length):
    half, side = place // 2, place % 2
    return side * (length - 1 - half) + (1 - side) * half


def place_of(spot, length):
    side = spot // (length // 2)
    half = side * (length - 1 - spot) + (1 - side) * spot
    return 2 * half + side


def whereabouts(length):
    core = lax.axis_index("section")
    index = lax.axis_index("dp")
    place, role = index // 2, index % 2
    spot = ring_of(place, length)
    step = 1 - 2 * core

    def at(offset):
        return place_of(lax.rem(spot + step * offset + 4 * length, length), length)

    return dict(
        core=core,
        place=place,
        role=role,
        at=at,
        onward=(core, 2 * at(1) + role),
        before=(core, 2 * at(-1) + role),
        sibling=(1 - core, index),
        partner=(1 - core, 2 * place + 1 - role),
    )


def greet(devices):
    barrier = pltpu.get_barrier_semaphore()
    for device in devices:
        pl.semaphore_signal(barrier, inc=1, device_id=device, device_id_type=MESH)
    pl.semaphore_wait(barrier, len(devices))


def remote(source, target, send_sem, recv_sem, device):
    return pltpu.make_async_remote_copy(
        src_ref=source,
        dst_ref=target,
        send_sem=send_sem,
        recv_sem=recv_sem,
        device_id=device,
        device_id_type=MESH,
    )


def each(first, last, body):
    def step(index, carry):
        body(index)
        return carry

    lax.fori_loop(first, last, step, 0)


def gather_kernel(length, count, heads, widths, *refs):
    total = count + heads
    shards, (mod_part, tokens, cotangent) = refs[:total], refs[total : total + 3]
    refs = refs[total + 3 :]
    full, (mod_all, rows_in, block_bias, head_bias) = refs[:total], refs[total : total + 4]
    (
        own_sem, swap_send, swap_recv, ring_send, ring_recv, side_send, side_recv,
        cross_send, cross_recv, mod_send, mod_recv, mod_sem, rows_send, rows_recv, mod_pair, mod_in,
        mod_sum,
        bias_in, bias_sem,
    ) = refs[total + 4 :]
    me = whereabouts(length)
    core, role, place, at = me["core"], me["role"], me["place"], me["at"]
    members = 2 * length
    index = 2 * place + role
    neighbour = (core, 2 * place + 1 - role)
    mine = 2 * place + core
    layers, shared, head_layers = range(count), range(count - 1), range(count, total)

    barrier = pltpu.get_barrier_semaphore()

    def signal(device):
        pl.semaphore_signal(barrier, inc=1, device_id=device, device_id_type=MESH)

    def greet_all(peer):
        other = (peer // members, lax.rem(peer, members))

        @pl.when((other[0] != core) | (other[1] != index))
        def _():
            signal(other)

    each(0, 2 * members, greet_all)
    pl.semaphore_wait(barrier, 2 * members - 1)

    def block(layer, turn):
        return full[layer].at[2 * at(-turn) + core]

    def onward(layer, turn):
        part = block(layer, turn)
        return remote(
            part, part, ring_send.at[layer, turn], ring_recv.at[layer, turn], me["onward"]
        )

    def across(layer, turn):
        part = block(layer, turn)
        return remote(
            part, part, side_send.at[layer, turn], side_recv.at[layer, turn], me["sibling"]
        )

    def from_sibling(layer, turn):
        part = full[layer].at[2 * at(turn) + 1 - core]
        return remote(
            part, part, side_send.at[layer, turn], side_recv.at[layer, turn], me["sibling"]
        )

    def own(layer):
        return pltpu.make_async_copy(shards[layer], full[layer].at[mine], own_sem.at[layer])

    def swap_out(layer):
        return remote(
            shards[layer], full[layer].at[index], swap_send.at[layer], swap_recv.at[layer],
            me["partner"],
        )

    def swap_in(layer):
        return remote(
            shards[layer], full[layer].at[mine], swap_send.at[layer], swap_recv.at[layer],
            me["partner"],
        )

    def lend(layer):
        return remote(
            shards[layer], full[layer].at[2 * place], swap_send.at[layer], swap_recv.at[layer],
            neighbour,
        )

    def cross(layer, turn):
        part = block(layer, turn)
        return remote(
            part, part, cross_send.at[layer - count, turn], cross_recv.at[layer - count, turn],
            neighbour,
        )

    @pl.when(core == role)
    def _():
        for layer in shared:
            own(layer).start()

    @pl.when((core == 0) & (role == 0))
    def _():
        own(count - 1).start()

    def rows_move(source):
        return remote(source, rows_in, rows_send, rows_recv, me["partner"])

    @pl.when(core != role)
    def _():
        for layer in shared:
            swap_out(layer).start()

    @pl.when((core == 0) & (role == 1))
    def _():
        swap_out(count - 1).start()

    @pl.when(core == role)
    def _():
        for layer in head_layers:
            own(layer).start()

    @pl.when((core == 0) & (role == 0))
    def _():
        for layer in head_layers:
            lend(layer).start()

    mod_move = remote(mod_part, mod_in, mod_pair.at[0], mod_pair.at[1], neighbour)

    def mod_copy(peer):
        return remote(
            mod_sum.at[peer], mod_all.at[place], mod_send.at[peer], mod_recv.at[place],
            (lax.rem(peer, 2), 2 * (peer // 2) + core),
        )

    mod_own = pltpu.make_async_copy(mod_sum.at[mine], mod_all.at[place], mod_sem)

    def others(act):
        def body(peer):
            @pl.when(peer != mine)
            def _():
                act(mod_copy(peer))

        each(0, members, body)

    @pl.when(core != role)
    def _():
        mod_move.start()

    def spread_mod():
        @pl.when(core == role)
        def _():
            mod_move.wait_recv()
            mod_sum[...] = mod_part[...] + mod_in[...]
            others(lambda copy: copy.start())
            mod_own.start()

    def gathered_mod():
        @pl.when(core == role)
        def _():
            mod_own.wait()
            others(lambda copy: copy.wait_send())

        @pl.when(core != role)
        def _():
            mod_move.wait_send()

        def came(source):
            @pl.when(jnp.logical_not((core == role) & (source == place)))
            def _():
                remote(
                    mod_sum.at[0], mod_all.at[source], mod_send.at[0], mod_recv.at[source],
                    me["sibling"],
                ).wait_recv()

        each(0, length, came)

    def begin(layer):
        @pl.when(core == role)
        def _():
            own(layer).wait()

        @pl.when(core != role)
        def _():
            swap_in(layer).wait_recv()

        onward(layer, 0).start()
        across(layer, 0).start()

    def ring_turn(turn, more, which):
        for layer in which:
            onward(layer, turn - 1).wait_recv()
            if more:
                onward(layer, turn).start()
            across(layer, turn).start()

    def ring_end(which):
        def end(turn):
            for layer in which:
                onward(layer, turn).wait_send()
                across(layer, turn).wait_send()
                from_sibling(layer, turn).wait_recv()

        each(0, length - 1, end)
        for layer in which:
            across(layer, length - 1).wait_send()
            from_sibling(layer, length - 1).wait_recv()

    def front_head(turn, first):
        for layer in head_layers:
            if first:

                @pl.when(core == 0)
                def _():
                    own(layer).wait()

                @pl.when(core == 1)
                def _():
                    cross(layer, turn).wait_recv()

            else:
                cross(layer, turn).wait_recv()
            across(layer, turn).start()

    @pl.when(role == 0)
    def _():
        for layer in layers:
            begin(layer)

        @pl.when(core == 1)
        def _():
            rows_move(cotangent).start()

        front_head(0, True)
        ring_turn(1, True, layers)
        spread_mod()
        late = 2

        def turn_body(turn):
            ring_turn(turn, True, layers)

            @pl.when(turn > late)
            def _():
                front_head(turn - late, False)

        each(2, length - 1, turn_body)
        ring_turn(length - 1, False, layers)
        each(length - 1 - late, length, lambda turn: front_head(turn, False))
        ring_end(layers)
        gathered_mod()

        def head_end(turn):
            for layer in head_layers:
                across(layer, turn).wait_send()
                from_sibling(layer, turn).wait_recv()

        each(0, length, head_end)

        @pl.when(core == 0)
        def _():
            for layer in head_layers:
                lend(layer).wait_send()

    @pl.when(role == 1)
    def _():
        lag = 3

        def cross_start(turn):
            @pl.when((turn > 0) | (core == 1))
            def _():
                for layer in head_layers:
                    cross(layer, turn).start()

        for layer in head_layers:

            @pl.when(core == 1)
            def _():
                own(layer).wait()

            @pl.when(core == 0)
            def _():
                lend(layer).wait_recv()

            onward(layer, 0).start()

        def head_turn(turn):
            for layer in head_layers:
                onward(layer, turn - 1).wait_recv()

                @pl.when(turn < length - 1)
                def _():
                    onward(layer, turn).start()

            @pl.when(turn >= lag)
            def _():
                cross_start(turn - lag)

        each(1, length, head_turn)
        @pl.when(core == 0)
        def _():
            rows_move(tokens).start()

        each(length - lag, length, cross_start)
        spread_mod()
        for layer in shared:
            begin(layer)
        each(1, length - 1, lambda turn: ring_turn(turn, True, shared))
        ring_turn(length - 1, False, shared)
        ring_end(shared)
        gathered_mod()

        def head_end(turn):
            for layer in head_layers:

                @pl.when(turn < length - 1)
                def _():
                    onward(layer, turn).wait_send()

                @pl.when((turn > 0) | (core == 1))
                def _():
                    cross(layer, turn).wait_send()

        each(0, length, head_end)

    fetch = pltpu.make_async_copy(full[0], bias_in, bias_sem)
    fetch.start()
    fetch.wait()
    block_bias[...] = jnp.zeros_like(block_bias)
    channels = tokens.shape[1]
    for shard in range(members):
        block = wide(bias_in[shard])
        line, start = 0, 0
        for part, width in enumerate(widths):
            if part == 4:
                start = 0
            target = block_bias if part < 4 else head_bias
            first = start + shard * width
            if part == 0 and first >= channels:
                first += channels
            for offset in range(0, width, 128):
                size = min(128, width - offset)
                target[:, first + offset : first + offset + size] = block[line : line + 1, :size]
                line += 1
            start += members * width + (channels if part == 0 else 0)

    @pl.when((core == 0) & (role == 1))
    def _():
        swap_out(count - 1).wait_send()

    @pl.when(core != role)
    def _():
        for layer in shared:
            swap_out(layer).wait_send()
        rows_move(tokens).wait()


def gather(shards, head_shards, mod_part, tokens, cotangent, widths, collective_id):
    members = lax.axis_size("dp")
    length, count, heads = members // 2, len(shards), len(head_shards)
    total = count + heads
    everything = list(shards) + list(head_shards)
    moved = sum(shard.size * 2 for shard in everything) * members
    inside = pl.BlockSpec(memory_space=pltpu.VMEM)
    results = pl.pallas_call(
        functools.partial(gather_kernel, length, count, heads, widths),
        name="gather",
        out_shape=[jax.ShapeDtypeStruct((members,) + s.shape, s.dtype) for s in everything]
        + [jax.ShapeDtypeStruct((length,) + mod_part.shape[1:], mod_part.dtype)]
        + [
            jax.ShapeDtypeStruct(tokens.shape, tokens.dtype),
            jax.ShapeDtypeStruct((1, members * sum(widths[:4]) + tokens.shape[1]), jnp.float32),
            jax.ShapeDtypeStruct((1, members * sum(widths[4:])), jnp.float32),
        ],
        in_specs=[inside] * (total + 1) + [ANY] * 2,
        out_specs=[ANY] * (total + 2) + [inside] * 2,
        scratch_shapes=[
            DMA((total,)),
            DMA((total,)),
            DMA((total,)),
            DMA((total, length)),
            DMA((total, length)),
            DMA((total, length)),
            DMA((total, length)),
            DMA((heads, length)),
            DMA((heads, length)),
            DMA((members,)),
            DMA((members,)),
            DMA(()),
            DMA(()),
            DMA(()),
            DMA((2,)),
            pltpu.VMEM(mod_part.shape, mod_part.dtype),
            pltpu.VMEM(mod_part.shape, mod_part.dtype),
            pltpu.VMEM((members,) + shards[0].shape, shards[0].dtype),
            DMA(()),
        ],
        compiler_params=pltpu.CompilerParams(
            collective_id=collective_id, has_side_effects=True, vmem_limit_bytes=VMEM_BYTES
        ),
        cost_estimate=pl.CostEstimate(flops=0, bytes_accessed=16 * moved, transcendentals=0),
    )(*everything, mod_part, tokens, cotangent)
    return (results[:count], results[count:total]) + tuple(results[total:])


def tile_of(columns):
    for tile in (512, 384, 256, 128):
        if columns % tile == 0:
            return tile
    return columns


class Ring:
    def __init__(self, me, length, variants, scratch):
        count = len(variants[0][1])
        self.me, self.length, self.layers = me, length, range(count)
        self.variants = variants
        self.left_all, self.right_all = scratch[:count], scratch[count : 2 * count]
        self.arrived, self.leaving = scratch[2 * count : 3 * count], scratch[3 * count : 4 * count]
        (
            self.own_sem, self.side_send, self.side_recv, self.ring_send, self.ring_recv,
        ) = scratch[4 * count : 4 * count + 5]

    @staticmethod
    def scratch(length, rows, columns, tokens, parts):
        bf16, count = jnp.bfloat16, len(rows)
        return (
            [pltpu.VMEM((2, length, r, tokens), bf16) for r in rows]
            + [pltpu.VMEM((2, tokens, c), bf16) for c in columns]
            + [pltpu.VMEM((length - 1, r, c), bf16) for r, c in zip(rows, columns)]
            + [pltpu.VMEM((2, r, c), bf16) for r, c in zip(rows, columns)]
            + [
                DMA((count, 2 * parts)),
                DMA((count, 2 * parts)),
                DMA((count, 2 * parts)),
                DMA((count, 2)),
                DMA((count, length)),
            ]
        )

    def chunk(self, layer, slot, turn, add):
        spot = self.me["at"](-(turn + 1))
        left, right = self.left_all[layer], self.right_all[layer]
        columns = right.shape[2]
        tile = tile_of(columns)

        def body(index):
            start = pl.multiple_of(index * tile, tile)
            total = product(left[0, spot], right[0, :, pl.ds(start, tile)]) + product(
                left[1, spot], right[1, :, pl.ds(start, tile)]
            )
            if add:
                total = total + wide(self.arrived[layer][turn - 1, :, pl.ds(start, tile)])
            self.leaving[layer][slot, :, pl.ds(start, tile)] = narrow(total)

        each(0, columns // tile, body)

    def onward(self, layer, slot, turn):
        return remote(
            self.leaving[layer].at[slot],
            self.arrived[layer].at[turn],
            self.ring_send.at[layer, slot],
            self.ring_recv.at[layer, turn],
            self.me["onward"],
        )

    def inputs(self, layer, lefts, rights):
        core, sibling = self.me["core"], self.me["sibling"]
        left_all, right_all = self.left_all[layer], self.right_all[layer]
        copies, sem, start = [], 0, 0

        def both(mine, own_to, other, other_to):
            nonlocal sem
            at = (layer, sem)
            sem += 1
            copies.append(pltpu.make_async_copy(mine, own_to, self.own_sem.at[at]))
            copies.append(
                remote(other, other_to, self.side_send.at[at], self.side_recv.at[at], sibling)
            )

        for part in lefts[layer]:
            lanes = pl.ds(start, part.shape[3])
            both(
                part.at[:, core],
                left_all.at[0, :, :, lanes],
                part.at[:, 1 - core],
                left_all.at[1, :, :, lanes],
            )
            start += part.shape[3]
        start = 0
        for part in rights[layer]:
            rows = pl.ds(start, part.shape[0])
            both(part, right_all.at[0, rows], part, right_all.at[1, rows])
            start += part.shape[0]
        return copies

    def fetch(self, layer, act):
        for predicate, lefts, rights in self.variants:

            def body():
                for copy in self.inputs(layer, lefts, rights):
                    act(copy)

            if predicate is None:
                body()
            else:
                pl.when(predicate)(body)

    def run(self, finish, midway=None, late=None):
        length = self.length
        for layer in self.layers:
            self.fetch(layer, lambda copy: copy.start())
        for layer in self.layers:
            self.fetch(layer, lambda copy: copy.wait())
            self.chunk(layer, 0, 0, False)
            self.onward(layer, 0, 0).start()

        def turn_body(turn):
            slot = lax.rem(turn, 2)
            for layer in self.layers:
                self.onward(layer, slot, turn - 1).wait_recv()

                @pl.when(turn >= 2)
                def _():
                    self.onward(layer, slot, turn).wait_send()

                self.chunk(layer, slot, turn, True)
                self.onward(layer, slot, turn).start()

        first, second = min(3, length - 1), max(min(3, length - 1), length - 2)
        each(1, first, turn_body)
        if midway:
            midway()
        each(first, second, turn_body)
        if late:
            late()
        each(second, length - 1, turn_body)
        slot = (length - 1) % 2
        for layer in self.layers:
            self.onward(layer, slot, length - 2).wait_recv()
            if length >= 3:
                self.onward(layer, slot, length - 2).wait_send()
            self.chunk(layer, slot, length - 1, True)
            finish(layer, slot)
        for layer in self.layers:
            self.onward(layer, 1 - slot, length - 2).wait_send()


def ring_cost(length, rows, columns, tokens):
    work = sum(r * c for r, c in zip(rows, columns)) * length
    return pl.CostEstimate(flops=4 * work * tokens, bytes_accessed=64 * work, transcendentals=0)


def head_reduce_kernel(length, count, *refs):
    lefts, rights, outs = refs[:count], refs[count : 2 * count], refs[2 * count : 3 * count]
    scratch = refs[3 * count :]
    last_sem = scratch[-1]
    me = whereabouts(length)

    @pl.when(me["role"] == 0)
    def _():
        greet([me["onward"], me["before"], me["sibling"]])
        ring = Ring(me, length, [(None, [[v] for v in lefts], [[v] for v in rights])], scratch[:-1])

        def last(layer, slot):
            return pltpu.make_async_copy(
                ring.leaving[layer].at[slot], outs[layer], last_sem.at[layer]
            )

        ring.run(lambda layer, slot: last(layer, slot).start())
        for layer in ring.layers:
            last(layer, (length - 1) % 2).wait()


def head_reduce(lefts, rights, collective_id):
    length, count = lax.axis_size("dp") // 2, len(lefts)
    rows = [left.shape[2] for left in lefts]
    columns = [right.shape[1] for right in rights]
    tokens = rights[0].shape[0]
    return pl.pallas_call(
        functools.partial(head_reduce_kernel, length, count),
        name="head_reduce",
        out_shape=[jax.ShapeDtypeStruct((r, c), jnp.bfloat16) for r, c in zip(rows, columns)],
        in_specs=[ANY] * (2 * count),
        out_specs=[ANY] * count,
        scratch_shapes=Ring.scratch(length, rows, columns, tokens, 1) + [DMA((count,))],
        compiler_params=pltpu.CompilerParams(
            collective_id=collective_id, has_side_effects=True, vmem_limit_bytes=VMEM_BYTES
        ),
        cost_estimate=ring_cost(length, rows, columns, tokens),
    )(*lefts, *rights)


def reduce_kernel(length, form, count, heads, *refs):
    operands = form.num_leaves
    fronts, backs, head_parts, mod, bias, head_sums, mod_weight = jax.tree.unflatten(
        form, refs[:operands]
    )
    refs = refs[operands:]
    outs, head_outs = refs[:count], refs[count : count + heads]
    stream_out, bias_all, head_all, mod_rows, silu_all = refs[count + heads : count + heads + 5]
    scratch = refs[count + heads + 5 :]
    mod_all, silu_own, silu_keep, silu_send, silu_recv, silu_side = scratch[-6:]
    scratch = scratch[:-6]
    (
        last_send, last_recv, part_send, part_recv, stream_send, stream_recv, small_send,
        mod_recv, bias_recv, head_recv, keep_sem,
    ) = scratch[-11:]
    me = whereabouts(length)
    core, role, place = me["core"], me["role"], me["place"]
    members = 2 * length
    index, mine = 2 * place + role, 2 * place + core
    barrier = pltpu.get_barrier_semaphore()

    def greet_all(peer):
        other = (peer // members, lax.rem(peer, members))

        @pl.when((other[0] != core) | (other[1] != index))
        def _():
            pl.semaphore_signal(barrier, inc=1, device_id=other, device_id_type=MESH)

    each(0, 2 * members, greet_all)
    pl.semaphore_wait(barrier, 2 * members - 1)

    unit = fronts[2][0].shape[0]

    def streams(act):
        for there, parts in ((0, fronts[2]), (1, backs[2])):

            @pl.when((role == there) & (core != role))
            def _():
                cuts = [
                    part.at[pl.ds(start, unit)]
                    for part in parts
                    for start in range(0, part.shape[0], unit)
                ]
                for i, cut in enumerate(cuts):
                    act(
                        remote(
                            cut,
                            stream_out.at[pl.ds(i * unit, unit)],
                            stream_send.at[i],
                            stream_recv.at[i],
                            me["partner"],
                        )
                    )

    streams(lambda copy: copy.start())

    def small(source, target, send, recv, device):
        return remote(source, target, send, recv, device)

    def mod_copy(peer):
        return small(
            mod, mod_all.at[mine], small_send.at[0, peer], mod_recv.at[mine], (role, peer)
        )

    def bias_copy(peer):
        return small(
            bias.at[peer], bias_all.at[mine], small_send.at[1, peer], bias_recv.at[mine],
            (role, peer),
        )

    def head_copy(peer):
        return small(
            head_sums.at[peer], head_all.at[mine], small_send.at[2, peer], head_recv.at[mine],
            (peer // members, lax.rem(peer, members)),
        )

    own_mod = pltpu.make_async_copy(mod, mod_all.at[mine], keep_sem.at[0])
    own_bias = pltpu.make_async_copy(bias.at[index], bias_all.at[mine], keep_sem.at[1])
    own_head = pltpu.make_async_copy(
        head_sums.at[core * members + index], head_all.at[mine], keep_sem.at[2]
    )

    def smalls(act_mod, act_head, act_own):
        def to_section(peer):
            @pl.when((core != role) | (peer != index))
            def _():
                act_mod(mod_copy(peer))
                act_mod(bias_copy(peer))

        each(0, members, to_section)

        @pl.when(core == role)
        def _():
            act_own(own_mod)
            act_own(own_bias)

        @pl.when(role == 0)
        def _():
            def to_all(peer):
                @pl.when(peer != core * members + index)
                def _():
                    act_head(head_copy(peer))

            each(0, 2 * members, to_all)
            act_own(own_head)

    def start(copy):
        copy.start()

    smalls(start, start, start)

    def part(layer, half):
        rows = head_outs[layer].shape[0]
        return head_parts[layer].at[pl.ds(half * rows, rows)]

    def kept(layer):
        return pltpu.make_async_copy(part(layer, 0), head_outs[layer], part_send.at[layer, 0])

    def handed(layer, half, device):
        return remote(
            part(layer, half), head_outs[layer], part_send.at[layer, half], part_recv.at[layer],
            device,
        )

    @pl.when((role == 0) & (core == 0))
    def _():
        for layer in range(heads):
            kept(layer).start()
            handed(layer, 1, me["sibling"]).start()

    @pl.when((role == 0) & (core == 1))
    def _():
        for layer in range(heads):
            handed(layer, 0, (0, 2 * place + 1)).start()
            handed(layer, 1, (1, 2 * place + 1)).start()

    variants = [(role == 0,) + tuple(fronts[:2]), (role == 1,) + tuple(backs[:2])]
    ring = Ring(me, length, variants, scratch[:-11])

    def local_last(layer, slot):
        return pltpu.make_async_copy(ring.leaving[layer].at[slot], outs[layer], last_send.at[layer])

    def remote_last(layer, slot):
        return remote(
            ring.leaving[layer].at[slot], outs[layer], last_send.at[layer], last_recv.at[layer],
            me["partner"],
        )

    def finish(layer, slot):
        @pl.when(core == role)
        def _():
            local_last(layer, slot).start()

        @pl.when(core != role)
        def _():
            remote_last(layer, slot).start()

    def silu_copy(peer):
        return remote(
            silu_own, silu_all.at[core, index], silu_send.at[peer], silu_recv.at[index],
            (core, peer),
        )

    silu_kept = pltpu.make_async_copy(silu_own, silu_all.at[core, index], silu_keep)

    def others(act):
        def body(peer):
            @pl.when(peer != index)
            def _():
                act(peer)

        each(0, members, body)

    def midway():
        def mod_came(source):
            @pl.when((core != role) | (source != mine))
            def _():
                small(
                    mod, mod_all.at[source], small_send.at[0, 0], mod_recv.at[source],
                    me["sibling"],
                ).wait_recv()

        each(0, members, mod_came)

        @pl.when(core == role)
        def _():
            own_mod.wait()

        images, depth = mod.shape[0], mod_weight.shape[0]
        for source in range(members):
            mod_rows[source * images : (source + 1) * images, :] = wide(mod_all[source])
        silu_own[...] = jnp.zeros_like(silu_own)
        silu_own[:, 0:depth] = product_right_t(narrow(mod_rows[...]), mod_weight[...])
        silu_kept.start()
        others(lambda peer: silu_copy(peer).start())

    across = remote(
        silu_all.at[core], silu_all.at[core], silu_side.at[0], silu_side.at[1], me["sibling"]
    )

    def late():
        others(
            lambda peer: remote(
                silu_own, silu_all.at[core, peer], silu_send.at[peer], silu_recv.at[peer],
                (core, peer),
            ).wait_recv()
        )
        silu_kept.wait()
        across.start()

    ring.run(finish, midway, late)
    others(lambda peer: silu_copy(peer).wait_send())
    across.wait_send()
    remote(
        silu_all.at[1 - core], silu_all.at[1 - core], silu_side.at[0], silu_side.at[1],
        me["sibling"],
    ).wait_recv()

    @pl.when((role == 0) & (core == 0))
    def _():
        for layer in range(heads):
            kept(layer).wait()
            handed(layer, 1, me["sibling"]).wait_send()

    @pl.when((role == 0) & (core == 1))
    def _():
        for layer in range(heads):
            handed(layer, 0, (0, 2 * place + 1)).wait_send()
            handed(layer, 1, (1, 2 * place + 1)).wait_send()

    @pl.when((role == 1) | (core == 1))
    def _():
        for layer in range(heads):
            handed(layer, 0, me["sibling"]).wait_recv()

    streams(lambda copy: copy.wait())
    smalls(
        lambda copy: copy.wait_send(),
        lambda copy: copy.wait_send(),
        lambda copy: None if copy is own_mod else copy.wait(),
    )

    def came(source):
        @pl.when((core != role) | (source != mine))
        def _():
            small(
                bias.at[0], bias_all.at[source], small_send.at[1, 0], bias_recv.at[source],
                me["sibling"],
            ).wait_recv()

        @pl.when((role != 0) | (source != mine))
        def _():
            small(
                head_sums.at[0], head_all.at[source], small_send.at[2, 0], head_recv.at[source],
                me["sibling"],
            ).wait_recv()

    each(0, members, came)
    slot = (length - 1) % 2
    for layer in ring.layers:

        @pl.when(core == role)
        def _():
            local_last(layer, slot).wait()

        @pl.when(core != role)
        def _():
            remote_last(layer, slot).wait()


def reduce(fronts, backs, head_parts, mod, bias, head_sums, mod_weight, collective_id):
    members = lax.axis_size("dp")
    lefts, rights, streams = fronts
    length, count, heads = members // 2, len(lefts), len(head_parts)
    rows = [left[0].shape[2] for left in lefts]
    columns = [right[0].shape[1] for right in rights]
    parts = len(rights[0])
    tokens = parts * rights[0][0].shape[0]
    bf16 = jnp.bfloat16
    inside = pl.BlockSpec(memory_space=pltpu.VMEM)
    stream_shape = (tokens, streams[0].shape[1])
    operands, form = jax.tree.flatten(
        (fronts, backs, head_parts, mod, bias, head_sums, mod_weight)
    )
    outer = len(operands) - heads - 4
    f32 = jnp.float32
    lines = members * mod.shape[0]
    results = pl.pallas_call(
        functools.partial(reduce_kernel, length, form, count, heads),
        name="reduce",
        out_shape=[jax.ShapeDtypeStruct((r, c), bf16) for r, c in zip(rows, columns)]
        + [jax.ShapeDtypeStruct((h.shape[0] // 2, h.shape[1]), bf16) for h in head_parts]
        + [jax.ShapeDtypeStruct(stream_shape, bf16)]
        + [
            jax.ShapeDtypeStruct((members,) + array.shape[1:], array.dtype)
            for array in (bias, head_sums)
        ]
        + [
            jax.ShapeDtypeStruct((lines, mod.shape[1]), f32),
            jax.ShapeDtypeStruct((2, members, lines, 128), f32),
        ],
        in_specs=[ANY] * outer + [inside] * (heads + 4),
        out_specs=[ANY] * (count + heads + 3) + [inside, ANY],
        scratch_shapes=Ring.scratch(length, rows, columns, tokens, parts)
        + [
            DMA((count,)),
            DMA((count,)),
            DMA((heads, 2)),
            DMA((heads,)),
            DMA((parts,)),
            DMA((parts,)),
            DMA((3, 2 * members)),
            DMA((members,)),
            DMA((members,)),
            DMA((members,)),
            DMA((3,)),
            pltpu.VMEM((members,) + mod.shape, mod.dtype),
            pltpu.VMEM((lines, 128), f32),
            DMA(()),
            DMA((members,)),
            DMA((members,)),
            DMA((2,)),
        ],
        compiler_params=pltpu.CompilerParams(
            collective_id=collective_id, has_side_effects=True, vmem_limit_bytes=VMEM_BYTES
        ),
        cost_estimate=ring_cost(length, rows, columns, tokens),
    )(*operands)
    return (results[:count], results[count : count + heads]) + tuple(results[count + heads :])


def local_grad(function, primal, cotangent_in):
    return jax.vjp(function, primal)[1](cotangent_in)[0]


def column_sums(values):
    return jnp.sum(wide(values), 0)


def normed_of(values):
    center = values - jnp.mean(values, -1, keepdims=True)
    inverse = lax.rsqrt(jnp.mean(center * center, -1, keepdims=True) + EPSILON)
    return center * inverse, inverse


def lane_window(head, head_size):
    start = head * head_size
    base = start // 128 * 128
    width = -(-(start + head_size - base) // 128) * 128
    return base, width, start - base


def head_only(block, inside, head_size):
    lanes = lax.broadcasted_iota(jnp.int32, block.shape, 1)
    keep = (lanes >= inside) & (lanes < inside + head_size)
    return jnp.where(keep, block, jnp.zeros_like(block))


def lay_shards(left, values):
    rows = left.shape[2]
    turned = values.T
    for shard in range(values.shape[1] // rows):
        left[shard // 2, shard % 2] = turned[shard * rows : (shard + 1) * rows]


def attend_kernel(
    head_count, hidden, pieces, pack_w, pack_b, out_w, out_b,
    input_left, packed_out, probs_out, mixed_left, attn_out, after_out, mixed_acc,
):
    channels = hidden.shape[1]
    head_size = channels // head_count
    scaling = head_size ** (-0.5)
    residual = wide(hidden[...])
    normed, _ = normed_of(residual)
    attn_input = narrow(normed * (1.0 + pieces[0, 1:2]) + pieces[0, 0:1])
    lay_shards(input_left, attn_input)
    packed_out[...] = narrow(product(attn_input, pack_w[...]) + pack_b[...])
    mixed_acc[...] = jnp.zeros_like(mixed_acc)
    for head in range(head_count):
        base, width, inside = lane_window(head, head_size)
        queries = packed_out[:, base : base + width]
        keys = head_only(packed_out[:, channels + base : channels + base + width], inside, head_size)
        values = head_only(
            packed_out[:, 2 * channels + base : 2 * channels + base + width], inside, head_size
        )
        scores = product_right_t(queries, keys) * scaling
        exponent = jnp.exp(scores - jnp.max(scores, -1, keepdims=True))
        probs = narrow(exponent * (1.0 / jnp.sum(exponent, -1, keepdims=True)))
        probs_out[0, head] = probs
        mixed_acc[:, base : base + width] += product(probs, values)
    mixed = narrow(mixed_acc[...])
    lay_shards(mixed_left, mixed)
    out = product(mixed, out_w[...]) + out_b[...]
    attn_out[...] = narrow(out)
    after_out[...] = residual + pieces[0, 2:3] * out


def rows_spec(seq_len, columns):
    return pl.BlockSpec((seq_len, columns), lambda i: (i, 0))


def block_at(shape, index):
    return pl.BlockSpec(shape, lambda i: index, pipeline_mode=pl.Buffered(1))


def fixed_spec(shape):
    return block_at(shape, (0,) * len(shape))


def image_rows(array, image):
    if image is None:
        return fixed_spec(array.shape)
    return block_at((SEQ, array.shape[1]), (image if array.shape[0] > SEQ else 0, 0))


def image_steps(array, image):
    base = 0 if image is None or array.shape[0] <= SEQ else image
    return pl.BlockSpec((SEQ, array.shape[1]), lambda i: (base + i, 0))


def attend(hidden, pieces, pack_w, out_w, bias, members, image):
    tokens, channels = hidden.shape
    left = (members // 2, 2, channels // members)
    images, seq = tokens // SEQ, SEQ
    lowest = image or 0
    bf16, f32 = jnp.bfloat16, jnp.float32
    work = tokens * channels * (4 * channels + 2 * seq)
    return pl.pallas_call(
        functools.partial(attend_kernel, HEADS),
        grid=(images,),
        name="attend",
        in_specs=[
            rows_spec(seq, channels),
            pl.BlockSpec((1,) + pieces.shape[1:], lambda i: (lowest + i, 0, 0)),
            fixed_spec(pack_w.shape),
            block_at((1, 3 * channels), (0, 0)),
            fixed_spec(out_w.shape),
            block_at((1, channels), (0, 3)),
        ],
        out_specs=[
            pl.BlockSpec(left + (seq,), lambda i: (0, 0, 0, i)),
            rows_spec(seq, 3 * channels),
            pl.BlockSpec((1, HEADS, seq, seq), lambda i: (i, 0, 0, 0)),
            pl.BlockSpec(left + (seq,), lambda i: (0, 0, 0, i)),
            rows_spec(seq, channels),
            rows_spec(seq, channels),
        ],
        out_shape=[
            jax.ShapeDtypeStruct(left + (tokens,), bf16),
            jax.ShapeDtypeStruct((tokens, 3 * channels), bf16),
            jax.ShapeDtypeStruct((images, HEADS, seq, seq), bf16),
            jax.ShapeDtypeStruct(left + (tokens,), bf16),
            jax.ShapeDtypeStruct((tokens, channels), bf16),
            jax.ShapeDtypeStruct((tokens, channels), f32),
        ],
        scratch_shapes=[pltpu.VMEM((seq, channels), f32)],
        compiler_params=pltpu.CompilerParams(vmem_limit_bytes=VMEM_BYTES),
        cost_estimate=pl.CostEstimate(
            flops=2 * work, bytes_accessed=40 * 2**20, transcendentals=0
        ),
    )(hidden, pieces, pack_w, bias, out_w, bias)


def per_image(values, images):
    return values.reshape(images, values.shape[0] // images, values.shape[1])


GELU_A, GELU_B = 0.7978845608028654, 0.044715


def mlp_kernel(
    after, pieces, up_w, up_b, down_w, down_b,
    input_left, act_left, slope_out, mlp_out, final_out, input_keep, total,
):
    step, steps = pl.program_id(0), pl.num_programs(0)
    images = pieces.shape[0]

    @pl.when(step == 0)
    def _():
        normed, _ = normed_of(per_image(after[...], images))
        rows = narrow(normed * (1.0 + pieces[:, 4:5]) + pieces[:, 3:4]).reshape(after.shape)
        input_keep[...] = rows
        lay_shards(input_left, rows)
        total[...] = jnp.zeros_like(total)

    pre = product(input_keep[...], up_w[...]) + up_b[...]
    square = pre * pre
    tanh = jnp.tanh(GELU_A * pre * (1.0 + GELU_B * square))
    half = 0.5 + 0.5 * tanh
    act = narrow(pre * half)
    lay_shards(act_left, act)
    slope_out[...] = narrow(
        half + pre * (0.5 - 0.5 * tanh * tanh) * (GELU_A + (3.0 * GELU_A * GELU_B) * square)
    )
    total[...] += product(act, down_w[...])

    @pl.when(step == steps - 1)
    def _():
        out = total[...] + down_b[...]
        mlp_out[...] = narrow(out)
        final = per_image(after[...], images) + pieces[:, 5:6] * per_image(out, images)
        final_out[...] = narrow(final * pieces[:, 6:7]).reshape(after.shape)


def feed_tile(width):
    return 1152 if width % 1152 == 0 else width


def mlp(after, pieces, up_w, down_w, bias, members, image):
    tokens, channels = after.shape
    width = up_w.shape[1]
    tile = feed_tile(width)
    bf16, f32 = jnp.bfloat16, jnp.float32
    columns = pl.BlockSpec((tokens, tile), lambda i: (0, i))
    left = (members // 2, 2, channels // members, tokens)
    rows = width // members
    act_block = (tile // (2 * rows), 2, rows, tokens)
    return pl.pallas_call(
        mlp_kernel,
        grid=(width // tile,),
        name="mlp",
        in_specs=[
            fixed_spec(after.shape),
            block_at((tokens // SEQ,) + pieces.shape[1:], (image or 0, 0, 0)),
            pl.BlockSpec((channels, tile), lambda i: (0, i)),
            pl.BlockSpec((1, tile), lambda i: (0, 4 * channels // tile + i)),
            pl.BlockSpec((tile, channels), lambda i: (i, 0)),
            block_at((1, channels), (0, 4 + width // channels)),
        ],
        out_specs=[
            fixed_spec(left),
            pl.BlockSpec(act_block, lambda i: (i, 0, 0, 0)),
            columns,
            fixed_spec((tokens, channels)),
            fixed_spec((tokens, channels)),
        ],
        out_shape=[
            jax.ShapeDtypeStruct(left, bf16),
            jax.ShapeDtypeStruct((members // 2, 2, rows, tokens), bf16),
            jax.ShapeDtypeStruct((tokens, width), bf16),
            jax.ShapeDtypeStruct((tokens, channels), bf16),
            jax.ShapeDtypeStruct((tokens, channels), bf16),
        ],
        scratch_shapes=[pltpu.VMEM((tokens, channels), bf16), pltpu.VMEM((tokens, channels), f32)],
        compiler_params=pltpu.CompilerParams(vmem_limit_bytes=VMEM_BYTES),
        cost_estimate=pl.CostEstimate(
            flops=4 * tokens * channels * width, bytes_accessed=40 * 2**20, transcendentals=0
        ),
    )(after, pieces, up_w, bias, down_w, bias)


def sum_rows(values):
    return product(jnp.ones((8, values.shape[0]), jnp.bfloat16), values)


def layer_norm_back(grad_in, normed, inverse):
    return inverse * (
        grad_in
        - jnp.mean(grad_in, -1, keepdims=True)
        - normed * jnp.mean(grad_in * normed, -1, keepdims=True)
    )


def added_grad(grad, extra, pieces):
    return per_image(wide(grad[...]) + extra[...], pieces.shape[0])


def scaled_grad(grad, extra, pieces):
    return per_image(wide(grad[...]), pieces.shape[0]) * pieces[:, 6:7]


def mlp_back_kernel(
    given_grad, grad, extra, after, pieces, slope, mlp_out, attn_out, up_w, down_w,
    grad_mlp_out, grad_pre_out, grad_after_out, grad_attn_out, sums_out, pre_sums, out_sums,
    total,
):
    step, steps = pl.program_id(0), pl.num_programs(0)
    images = pieces.shape[0]

    @pl.when(step == 0)
    def _():
        given = given_grad(grad, extra, pieces)
        rows = narrow(pieces[:, 5:6] * given).reshape(grad.shape)
        grad_mlp_out[...] = rows
        sums_out[:, 5] = jnp.sum(given * per_image(wide(mlp_out[...]), images), 1)
        out_sums[0] = sum_rows(rows)
        total[...] = jnp.zeros_like(total)

    grad_pre = narrow(wide(slope[...]) * product_right_t(grad_mlp_out[...], down_w[...]))
    grad_pre_out[...] = grad_pre
    pre_sums[...] = sum_rows(grad_pre)
    total[...] += product_right_t(grad_pre, up_w[...])

    @pl.when(step == steps - 1)
    def _():
        normed, inverse = normed_of(per_image(after[...], images))
        grad_min = per_image(total[...], images)
        sums_out[:, 3] = jnp.sum(grad_min, 1)
        sums_out[:, 4] = jnp.sum(grad_min * normed, 1)
        grad_after = given_grad(grad, extra, pieces) + layer_norm_back(
            grad_min * (1.0 + pieces[:, 4:5]), normed, inverse
        )
        grad_after_out[...] = grad_after.reshape(grad.shape)
        rows = narrow(pieces[:, 2:3] * grad_after).reshape(grad.shape)
        grad_attn_out[...] = rows
        sums_out[:, 2] = jnp.sum(grad_after * per_image(wide(attn_out[...]), images), 1)
        out_sums[1] = sum_rows(rows)


def mlp_back(given_grad, grad, extra, after, pieces, slope, mlp_out, attn_out, up_w, down_w, image):
    tokens = after.shape[0] if image is None else SEQ
    images, channels, width = tokens // SEQ, after.shape[1], up_w.shape[1]
    tile = feed_tile(width)
    bf16, f32 = jnp.bfloat16, jnp.float32
    columns = pl.BlockSpec((tokens, tile), lambda i: (0, i))
    slope_row = image if image and slope.shape[0] > SEQ else 0
    rows = fixed_spec((tokens, channels))
    return pl.pallas_call(
        functools.partial(mlp_back_kernel, given_grad),
        grid=(width // tile,),
        name="mlp_back",
        in_specs=[
            image_rows(grad, image),
            image_rows(extra, image),
            image_rows(after, image),
            block_at((images,) + pieces.shape[1:], (image or 0, 0, 0)),
            pl.BlockSpec((tokens, tile), lambda i: (slope_row, i)),
            image_rows(mlp_out, image),
            image_rows(attn_out, image),
            pl.BlockSpec((channels, tile), lambda i: (0, i)),
            pl.BlockSpec((tile, channels), lambda i: (i, 0)),
        ],
        out_specs=[
            rows,
            columns,
            rows,
            rows,
            fixed_spec((images, 8, channels)),
            pl.BlockSpec((8, tile), lambda i: (0, i)),
            fixed_spec((2, 8, channels)),
        ],
        out_shape=[
            jax.ShapeDtypeStruct((tokens, channels), bf16),
            jax.ShapeDtypeStruct((tokens, width), bf16),
            jax.ShapeDtypeStruct((tokens, channels), f32),
            jax.ShapeDtypeStruct((tokens, channels), bf16),
            jax.ShapeDtypeStruct((images, 8, channels), f32),
            jax.ShapeDtypeStruct((8, width), f32),
            jax.ShapeDtypeStruct((2, 8, channels), f32),
        ],
        scratch_shapes=[pltpu.VMEM((tokens, channels), f32)],
        compiler_params=pltpu.CompilerParams(vmem_limit_bytes=VMEM_BYTES),
        cost_estimate=pl.CostEstimate(
            flops=4 * tokens * channels * width, bytes_accessed=40 * 2**20, transcendentals=0
        ),
    )(grad, extra, after, pieces, slope, mlp_out, attn_out, up_w, down_w)


def attend_back_kernel(
    head_count, hidden, pieces, packed, probs_in, grad_attn, grad_after, pack_w, out_w,
    grad_packed_out, grad_hidden_out, sums_out, pack_sums, acc, grad_mixed_keep,
):
    channels = hidden.shape[1]
    head_size = channels // head_count
    scaling = head_size ** (-0.5)
    grad_mixed_keep[...] = narrow(product_right_t(grad_attn[...], out_w[...]))
    acc[...] = jnp.zeros_like(acc)
    for head in range(head_count):
        base, width, inside = lane_window(head, head_size)
        q_at, k_at, v_at = (slice(j * channels + base, j * channels + base + width) for j in range(3))
        queries = head_only(packed[:, q_at], inside, head_size)
        keys = head_only(packed[:, k_at], inside, head_size)
        grad_mixed = head_only(grad_mixed_keep[:, q_at], inside, head_size)
        probs = probs_in[0, head]
        grad_probs = product_right_t(grad_mixed, packed[:, v_at])
        probs_wide = wide(probs)
        weighted = probs_wide * grad_probs
        grad_scores = narrow(weighted - probs_wide * jnp.sum(weighted, -1, keepdims=True))
        acc[:, v_at] += product_left_t(probs, grad_mixed)
        acc[:, q_at] += product(grad_scores, keys) * scaling
        acc[:, k_at] += product_left_t(grad_scores, queries) * scaling
    grad_packed = narrow(acc[...])
    grad_packed_out[...] = grad_packed
    column_totals = sum_rows(grad_packed)

    @pl.when(pl.program_id(0) == 0)
    def _():
        pack_sums[...] = column_totals

    @pl.when(pl.program_id(0) > 0)
    def _():
        pack_sums[...] += column_totals

    grad_ain = product_right_t(grad_packed, pack_w[...])
    normed, inverse = normed_of(wide(hidden[...]))
    sums_out[0, 0:1] = jnp.sum(grad_ain, 0, keepdims=True)
    sums_out[0, 1:2] = jnp.sum(grad_ain * normed, 0, keepdims=True)
    grad_hidden_out[...] = narrow(
        grad_after[...] + layer_norm_back(grad_ain * (1.0 + pieces[0, 1:2]), normed, inverse)
    )


def attend_back(hidden, pieces, packed, probs, grad_attn, grad_after, pack_w, out_w, image):
    tokens = hidden.shape[0] if image is None else SEQ
    images, channels, seq = tokens // SEQ, hidden.shape[1], SEQ
    lowest = image or 0
    probs_at = lowest if probs.shape[0] > 1 else 0
    bf16, f32 = jnp.bfloat16, jnp.float32
    work = tokens * channels * (4 * channels + 5 * seq)
    return pl.pallas_call(
        functools.partial(attend_back_kernel, HEADS),
        grid=(images,),
        name="attend_back",
        in_specs=[
            image_steps(hidden, image),
            pl.BlockSpec((1,) + pieces.shape[1:], lambda i: (lowest + i, 0, 0)),
            image_steps(packed, image),
            pl.BlockSpec((1, HEADS, seq, seq), lambda i: (probs_at + i, 0, 0, 0)),
            image_steps(grad_attn, image),
            image_steps(grad_after, image),
            fixed_spec(pack_w.shape),
            fixed_spec(out_w.shape),
        ],
        out_specs=[
            rows_spec(seq, 3 * channels),
            rows_spec(seq, channels),
            pl.BlockSpec((1, 8, channels), lambda i: (i, 0, 0)),
            fixed_spec((8, 3 * channels)),
        ],
        out_shape=[
            jax.ShapeDtypeStruct((tokens, 3 * channels), bf16),
            jax.ShapeDtypeStruct((tokens, channels), bf16),
            jax.ShapeDtypeStruct((images, 8, channels), f32),
            jax.ShapeDtypeStruct((8, 3 * channels), f32),
        ],
        scratch_shapes=[
            pltpu.VMEM((seq, 3 * channels), f32),
            pltpu.VMEM((seq, channels), bf16),
        ],
        compiler_params=pltpu.CompilerParams(vmem_limit_bytes=VMEM_BYTES),
        cost_estimate=pl.CostEstimate(
            flops=2 * work, bytes_accessed=40 * 2**20, transcendentals=0
        ),
    )(hidden, pieces, packed, probs, grad_attn, grad_after, pack_w, out_w)


def block_forward(hidden, pieces, weights, members, image=None):
    pack_w, out_w, up_w, down_w, bias = weights
    input_left, packed, probs, mixed_left, attn_out, after = attend(
        hidden, pieces, pack_w, out_w, bias, members, image
    )
    rows_left, act_left, slope, mlp_out, final = mlp(
        after, pieces, up_w, down_w, bias, members, image
    )
    return (
        final,
        (packed, probs, attn_out, after, slope, mlp_out),
        (act_left, rows_left, mixed_left, input_left),
    )


def block_backward(hidden, saved_state, pieces, weights, given_grad, grad, extra, image):
    pack_w, out_w, up_w, down_w, _ = weights
    packed, probs, attn_out, after, slope, mlp_out = saved_state
    grad_mlp, grad_pre, grad_after, grad_attn, high_sums, pre_sums, out_sums = mlp_back(
        given_grad, grad, extra, after, pieces, slope, mlp_out, attn_out, up_w, down_w, image
    )
    grad_packed, grad_hidden, low_sums, pack_sums = attend_back(
        hidden, pieces, packed, probs, grad_attn, grad_after, pack_w, out_w, image
    )
    rights = (grad_mlp, grad_pre, grad_attn, grad_packed)
    return grad_hidden, rights, (low_sums, high_sums, pack_sums, pre_sums, out_sums)


def silu_parts(values):
    gate = 0.5 + 0.5 * jnp.tanh(0.5 * values)
    return values * gate, gate * (1.0 + values * (1.0 - gate))


def head_kernel(
    members, hidden_at, target_at, live, in_w_at, in_b, mid_w_at, mid_b, out_w_at, out_b,
    grad_hidden_at, last_left_at, mid_left_at, in_left_at, grad_feature_at, grad_second_at,
    in_sums, mid_sums, out_sums, loss_out,
    hidden, target, in_w, mid_w, out_w,
    grad_hidden_out, last_left, mid_left, in_left, grad_feature_out, grad_second_out,
    act_first, slope_first, act_second, slope_second, grad_first_keep, come_sem, go_sem,
):
    width = in_w.shape[1]
    tile = 512 if width % 512 == 0 else width
    tiles = [slice(start, start + tile) for start in range(0, width, tile)]
    rows = width // (2 * members)
    pairs_in = ((hidden_at, hidden), (in_w_at, in_w), (mid_w_at, mid_w), (out_w_at, out_w), (target_at, target))
    come = [
        pltpu.make_async_copy(there, here, come_sem.at[i]) for i, (there, here) in enumerate(pairs_in)
    ]
    pairs_out = (
        (grad_hidden_out, grad_hidden_at),
        (last_left, last_left_at),
        (mid_left, mid_left_at),
        (in_left, in_left_at),
        (grad_feature_out, grad_feature_at),
        (grad_second_out, grad_second_at),
    )
    go = [
        pltpu.make_async_copy(here, there, go_sem.at[i]) for i, (here, there) in enumerate(pairs_out)
    ]

    def lay(left, values, start):
        turned = values.T
        for offset in range(0, values.shape[1], rows):
            shard = (start + offset) // rows
            half, index = shard // members, shard % members
            left[index // 2, index % 2, half * rows : (half + 1) * rows] = turned[
                offset : offset + rows
            ]

    @pl.when(lax.rem(lax.axis_index("dp"), 2) == 0)
    def _():
        for copy in come:
            copy.start()
        come[0].wait()
        come[1].wait()
        for at in tiles:
            act, slope = silu_parts(product(hidden[...], in_w[:, at]) + in_b[:, at])
            act_first[:, at] = narrow(act)
            slope_first[:, at] = narrow(slope)
        come[2].wait()
        for at in tiles:
            act, slope = silu_parts(product(act_first[...], mid_w[:, at]) + mid_b[:, at])
            act_second[:, at] = narrow(act)
            slope_second[:, at] = narrow(slope)
            lay(mid_left, act_first[:, at], at.start)
        go[2].start()
        come[3].wait()
        come[4].wait()
        feature = product(act_second[...], out_w[...]) + out_b[...]
        inverse = lax.rsqrt(jnp.sum(feature * feature, -1, keepdims=True) + EPSILON)
        unit = feature * inverse
        aim = wide(target[...])
        aim = aim * lax.rsqrt(jnp.sum(aim * aim, -1, keepdims=True) + EPSILON)
        alive = live[:, 0:1]
        cosine = jnp.sum(unit * aim, -1, keepdims=True)
        loss_out[...] = jnp.broadcast_to(
            0.5 * jnp.sum(alive * (1.0 - cosine), axis=(0, 1), keepdims=True), loss_out.shape
        )
        grad_unit = (-0.5 * alive) * aim
        grad_feature = narrow(
            inverse * (grad_unit - unit * jnp.sum(grad_unit * unit, -1, keepdims=True))
        )
        grad_feature_out[...] = grad_feature
        go[4].start()
        out_sums[...] = sum_rows(grad_feature)
        for at in tiles:
            grad_second = narrow(
                wide(slope_second[:, at]) * product_right_t(grad_feature, out_w[at, :])
            )
            grad_second_out[:, at] = grad_second
            mid_sums[:, at] = sum_rows(grad_second)
            lay(last_left, act_second[:, at], at.start)
        go[1].start()
        go[5].start()
        for at in tiles:
            grad_first = narrow(
                wide(slope_first[:, at]) * product_right_t(grad_second_out[...], mid_w[at, :])
            )
            grad_first_keep[:, at] = grad_first
            in_sums[:, at] = sum_rows(grad_first)
            part = product_right_t(grad_first, in_w[:, at])
            if at.start == 0:
                grad_hidden_out[...] = part
            else:
                grad_hidden_out[...] += part
            lay(in_left, grad_first_keep[:, at], at.start)
        go[0].start()
        go[3].start()
        for copy in go:
            copy.wait()


def head_pass(hidden, target, live, head_weights, members):
    tokens, channels = hidden.shape
    width, features = head_weights[2].shape[0], target.shape[1]
    bf16, f32 = jnp.bfloat16, jnp.float32
    left = ((members // 2, 2, width // members, tokens), bf16)
    live_lanes = jnp.broadcast_to(live[:, None], (tokens, 128))
    in_w, in_b, mid_w, mid_b, out_w, out_b = head_weights
    inside = pl.BlockSpec(memory_space=pltpu.VMEM)
    work = tokens * (channels * width + width * width + width * features)
    big = [
        ((tokens, channels), f32),
        left,
        left,
        left,
        ((tokens, features), bf16),
        ((tokens, width), bf16),
    ]
    small = [((8, width), f32), ((8, width), f32), ((8, features), f32), ((8, 128), f32)]
    results = pl.pallas_call(
        functools.partial(head_kernel, members),
        name="head",
        in_specs=[ANY, ANY, inside, ANY, inside, ANY, inside, ANY, inside],
        out_specs=[ANY] * 6 + [inside] * 4,
        out_shape=[jax.ShapeDtypeStruct(*leaf) for leaf in big + small],
        scratch_shapes=[
            pltpu.VMEM(array.shape, array.dtype) for array in (hidden, target, in_w, mid_w, out_w)
        ]
        + [pltpu.VMEM(*leaf) for leaf in big]
        + [pltpu.VMEM((tokens, width), bf16)] * 5
        + [DMA((5,)), DMA((6,))],
        compiler_params=pltpu.CompilerParams(vmem_limit_bytes=VMEM_BYTES),
        cost_estimate=pl.CostEstimate(
            flops=4 * work, bytes_accessed=40 * 2**20, transcendentals=0
        ),
    )(hidden, target, live_lanes, in_w, in_b[None], mid_w, mid_b[None], out_w, out_b[None])
    grad_hidden, last_left, mid_left, in_left, grad_feature, grad_second = results[:6]
    in_sums, mid_sums, out_sums, loss = results[6:]
    return (
        grad_hidden,
        loss[0:1],
        (last_left, mid_left, in_left),
        (grad_feature, grad_second),
        (in_sums[0:1], mid_sums[0:1], out_sums[0:1]),
    )


def hollow(shapes):
    leaves, form = jax.tree.flatten(shapes)
    results = pl.pallas_call(
        lambda *refs: None,
        name="hollow",
        out_shape=[jax.ShapeDtypeStruct(leaf.shape, leaf.dtype) for leaf in leaves],
        out_specs=[ANY if leaf.ndim else pl.BlockSpec(memory_space=pltpu.SMEM) for leaf in leaves],
    )()
    return jax.tree.unflatten(form, list(results))


def on_device(
    tokens_in,
    cotangent,
    targets,
    buckets,
    counts,
    time_table,
    modulate_weight,
    modulate_bias,
    qkv_weight,
    qv_bias,
    attn_weight,
    attn_bias,
    up_weight,
    up_bias,
    down_weight,
    down_bias,
    project_in_weight,
    project_in_bias,
    project_mid_weight,
    project_mid_bias,
    project_out_weight,
    project_out_bias,
):
    members = lax.axis_size("dp")
    core = lax.axis_index("section")
    index = lax.axis_index("dp")
    place, role = index // 2, index % 2
    is_first = role == 0
    own = 2 * place + core
    channels = tokens_in.shape[1]
    images = tokens_in.shape[0] // SEQ
    pairs_up, pairs_back, pairs_swap = [], [], []
    for pair in range(members // 2):
        low, high = 2 * pair, 2 * pair + 1
        pairs_swap += [(high, members + low)]
        pairs_up += [(low, high), (members + low, members + high)]
        pairs_back += [(high, low), (members + high, members + low)]
    axes = ("section", "dp")

    all_buckets = lax.all_gather(buckets, "dp", axis=0, tiled=True)
    one_hot = (
        all_buckets[:, None] == jnp.arange(time_table.shape[0], dtype=jnp.int32)[None, :]
    ).astype(jnp.float32)
    conditioning = jnp.dot(one_hot, time_table, precision=HIGHEST)
    silu_all = narrow(jax.nn.silu(conditioning))
    depth = modulate_weight.shape[1]
    silu_depth = lax.dynamic_slice_in_dim(silu_all, index * depth, depth, 1)
    mod_part = product(silu_depth, modulate_weight[0])
    share = modulate_bias.shape[1]
    bias_row = lax.dynamic_update_slice_in_dim(
        jnp.zeros((mod_part.shape[1],), jnp.float32), wide(modulate_bias[0]), index * share, 0
    )
    mod_part = (mod_part + bias_row[None]).reshape(members, images, 6 * channels)

    section_biases = (qv_bias[0], attn_bias[0], up_bias[0], down_bias[0])
    biases = section_biases + (project_in_bias, project_mid_bias, project_out_bias)
    widths = [part.shape[0] for part in biases]
    lines = [
        jnp.pad(part, (0, -part.shape[0] % 128)).reshape(-1, 128) for part in biases
    ]
    bias_block = jnp.concatenate(lines)
    bias_block = jnp.pad(bias_block, ((0, -bias_block.shape[0] % 16), (0, 0)))
    block_full, head_full, mod_all, rows_in, block_bias, head_bias = gather(
        (
            bias_block,
            qkv_weight[0],
            attn_weight[0],
            up_weight[0],
            down_weight[0],
            project_out_weight,
        ),
        (project_in_weight, project_mid_weight),
        mod_part,
        tokens_in,
        cotangent,
        widths,
        0,
    )
    _, pack_weight, out_weight, first_weight, second_weight, head_last = block_full
    head_ends = [members * width for width in widths[4:]]
    head_bias = [
        head_bias[0, sum(head_ends[:i]) : sum(head_ends[: i + 1])] for i in range(len(head_ends))
    ]

    def whole(values):
        return values.reshape(-1, values.shape[-1])

    block_weights = (
        whole(pack_weight),
        whole(out_weight),
        whole(first_weight),
        whole(second_weight),
        block_bias,
    )
    head_weights = (
        whole(head_full[0]),
        head_bias[0],
        whole(head_full[1]),
        head_bias[1],
        whole(head_last),
        head_bias[2],
    )
    pieces = jnp.sum(mod_all, 0).reshape(images, 6, channels)

    own_counts = counts[own]
    image_live = (jnp.arange(images, dtype=jnp.int32) < own_counts).astype(jnp.float32)
    token_live = jnp.repeat(image_live, SEQ)
    out_scale = jnp.where(is_first, 1.0, image_live)
    scale_rows = jnp.broadcast_to(out_scale[:, None, None], (images, 2, channels))
    pieces = jnp.concatenate([pieces, scale_rows], 1)
    total_live = wide(jnp.sum(counts)) * SEQ
    crossed = core != role
    targets_out, rows_in = lax.optimization_barrier((targets, rows_in))
    hidden_first = jnp.where(crossed, rows_in, tokens_in)
    outer = jnp.where(crossed, rows_in, cotangent)
    own_targets = jnp.where(crossed, lax.ppermute(targets_out, axes, pairs_swap), targets)

    def unused(function, *operands_in):
        return hollow(jax.eval_shape(function, *operands_in))

    def forward(hidden, mod, block):
        return block_forward(hidden, mod, block, members)

    first_out, saved_state, first_lefts = lax.cond(
        is_first,
        forward,
        lambda *operands_in: unused(forward, *operands_in),
        hidden_first,
        pieces,
        block_weights,
    )
    hidden_second = lax.ppermute(first_out, axes, pairs_up)

    head_result = head_pass(first_out, own_targets, token_live, head_weights, members)
    hidden_second, head_result = lax.optimization_barrier((hidden_second, head_result))
    grad_hidden, loss_part, head_lefts, head_rights, head_sums = head_result

    def do_second(rows, mod, grad, block):
        final, state, lefts = block_forward(rows, mod, block, members)
        grad_rows, rights, sums_of = block_backward(
            rows, state, mod, block, scaled_grad, grad, grad, None
        )
        cut = tuple(grad_rows[i * SEQ : (i + 1) * SEQ] for i in range(images))
        return cut, final, rights, sums_of, lefts

    second = lax.cond(
        is_first,
        lambda *operands_in: unused(do_second, *operands_in),
        do_second,
        hidden_second,
        pieces,
        outer,
        block_weights,
    )
    returning = [lax.ppermute(rows, axes, pairs_back) for rows in second[0]]
    head_lefts, head_rights, kept = lax.optimization_barrier((head_lefts, head_rights, second[1]))
    second = (second[0], kept) + second[2:]
    head_parts = head_reduce(head_lefts, head_rights + (first_out,), 2)
    returning[0], head_parts = lax.optimization_barrier((returning[0], head_parts))
    first = []
    for i in range(images):

        def do_first(rows, state, mod, extra, grad, block, i=i):
            return block_backward(rows, state, mod, block, added_grad, grad, extra, i)

        if i:
            returning[i], gone = lax.optimization_barrier((returning[i], first[i - 1][0]))
            first[i - 1] = (gone,) + first[i - 1][1:]
        first.append(
            lax.cond(
                is_first,
                do_first,
                lambda *operands_in: unused(do_first, *operands_in),
                hidden_first,
                saved_state,
                pieces,
                grad_hidden,
                returning[i],
                block_weights,
            )
        )
    sums_first = [result[2] for result in first]
    low_sums, high_sums = (
        jnp.where(is_first, jnp.concatenate([sums_of[j] for sums_of in sums_first]), second[3][j])
        for j in range(2)
    )
    pack_row, pre_row, out_rows = (
        jnp.where(is_first, sum(sums_of[j] for sums_of in sums_first), second[3][j])[..., 0:1, :]
        for j in range(2, 5)
    )
    grad_mod = narrow(
        jnp.concatenate([low_sums[:, 0:2], high_sums[:, 2:6]], 1).reshape(images, 6 * channels)
    )
    bias_grads = (
        jnp.concatenate([pack_row[:, :channels], pack_row[:, 2 * channels :]], 1),
        out_rows[1],
        pre_row,
        out_rows[0],
    )

    def by_layer(results):
        return [list(parts_of) for parts_of in zip(*results)]

    fronts = (
        [[left] for left in first_lefts],
        by_layer([result[1] for result in first]),
        [result[0] for result in first],
    )
    backs = ([[left] for left in second[4]], [[right] for right in second[2]], [second[1]])
    bias_rows = jnp.concatenate([grads.reshape(members, -1) for grads in bias_grads], 1)
    bias_width = bias_rows.shape[1]
    bias_rows = jnp.pad(bias_rows, ((0, 0), (0, 1024 - bias_width))).reshape(members, 8, 128)
    in_sums, mid_sums, out_sums = head_sums
    devices = 2 * members
    out_width = out_sums.shape[1]
    head_rows = jnp.concatenate(
        [
            in_sums.reshape(devices, -1),
            mid_sums.reshape(devices, -1),
            jnp.broadcast_to(out_sums, (devices, out_width)),
            jnp.broadcast_to(loss_part[:, 0:1], (devices, 1)),
        ],
        1,
    )
    head_width = head_rows.shape[1]
    head_rows = jnp.pad(head_rows, ((0, 0), (0, 1024 - head_width))).reshape(devices, 8, 128)
    block_grads, head_grads, stream_in, bias_all, head_all, mod_wide, silu_all_terms = reduce(
        fronts,
        backs,
        head_parts,
        grad_mod,
        bias_rows,
        head_rows,
        modulate_weight[0],
        3,
    )
    down_grad, up_grad, attn_grad, qkv_grad = block_grads
    stream = jnp.where(is_first, jnp.concatenate(fronts[2]), jnp.concatenate(backs[2]))
    stream_own = jnp.where(crossed, stream_in, stream)
    mod_w_grad = product_left_t(silu_depth, narrow(mod_wide))
    mod_b_grad = lax.dynamic_slice_in_dim(jnp.sum(mod_wide, 0), index * share, share, 0)
    silu_total = jnp.sum(silu_all_terms[:, :, :, :depth], 0)
    silu_total = jnp.swapaxes(silu_total, 0, 1).reshape(-1, channels)
    cond_grad = local_grad(jax.nn.silu, conditioning, silu_total)
    table_grad = jnp.dot(one_hot.T, cond_grad, precision=HIGHEST)

    bias_sums = jnp.sum(bias_all, 0).reshape(-1)
    bias_outs, offset = [], 0
    for part in section_biases:
        width = part.shape[0]
        bias_outs.append(bias_sums[offset : offset + width][None])
        offset += width
    sums = jnp.sum(head_all, 0).reshape(-1)
    head_share = in_sums.shape[1] // devices
    loss_value = sums[head_width - 1] / total_live
    return (
        stream_own[None],
        loss_value,
        table_grad,
        mod_w_grad[None],
        mod_b_grad[None],
        wide(qkv_grad)[None],
        bias_outs[0],
        wide(attn_grad)[None],
        bias_outs[1],
        wide(up_grad)[None],
        bias_outs[2],
        wide(down_grad)[None],
        bias_outs[3],
        wide(head_grads[2]).T,
        sums[:head_share],
        wide(head_grads[1]),
        sums[head_share : 2 * head_share],
        wide(head_grads[0]),
        sums[2 * head_share : 2 * head_share + out_width],
    )


def solution(mesh):
    in_specs = (
        P("dp", None),
        P("dp", None),
        P("dp", None),
        P("dp"),
        P(),
        P(),
        P("section", "dp", None),
        P("section", "dp"),
        P("section", "dp", None),
        P("section", "dp"),
        P("section", "dp", None),
        P("section", "dp"),
        P("section", "dp", None),
        P("section", "dp"),
        P("section", "dp", None),
        P("section", "dp"),
        P("dp", None),
        P("dp"),
        P("dp", None),
        P("dp"),
        P("dp", None),
        P("dp"),
    )
    out_specs = (
        P("section", "dp", None),
        P(),
        P(),
        P("section", "dp", None),
        P("section", "dp"),
        P("section", "dp", None),
        P("section", "dp"),
        P("section", "dp", None),
        P("section", "dp"),
        P("section", "dp", None),
        P("section", "dp"),
        P("section", "dp", None),
        P("section", "dp"),
        P(None, ("section", "dp")),
        P(("section", "dp")),
        P(("section", "dp"), None),
        P(("section", "dp")),
        P(("section", "dp"), None),
        P(),
    )
    return jax.shard_map(
        on_device, mesh=mesh, in_specs=in_specs, out_specs=out_specs, check_vma=False
    )
```

```python
import functools
import jax
import jax.numpy as jnp
from jax import lax
from jax.experimental import pallas as pl
from jax.experimental.pallas import tpu as pltpu
from jax.sharding import PartitionSpec as P

HEADS = 16
SEQ = 256
EPSILON = 1e-06
HIGHEST = lax.Precision.HIGHEST
MESH = pl.DeviceIdType.MESH
ANY = pl.BlockSpec(memory_space=pl.ANY)
DMA = pltpu.SemaphoreType.DMA
VMEM_BYTES = 60 * 2**20


def narrow(values):
    return values.astype(jnp.bfloat16)


def wide(values):
    return values.astype(jnp.float32)


def product(left_side, right_side):
    return jnp.dot(left_side, right_side, preferred_element_type=jnp.float32)


def product_left_t(left_side, right_side):
    return lax.dot_general(
        left_side, right_side, (((0,), (0,)), ((), ())), preferred_element_type=jnp.float32
    )


def product_right_t(left_side, right_side):
    return lax.dot_general(
        left_side, right_side, (((1,), (1,)), ((), ())), preferred_element_type=jnp.float32
    )


def ring_of(place, length):
    half, side = place // 2, place % 2
    return side * (length - 1 - half) + (1 - side) * half


def place_of(spot, length):
    side = spot // (length // 2)
    half = side * (length - 1 - spot) + (1 - side) * spot
    return 2 * half + side


def whereabouts(length):
    core = lax.axis_index("section")
    index = lax.axis_index("dp")
    place, role = index // 2, index % 2
    spot = ring_of(place, length)
    step = 1 - 2 * core

    def at(offset):
        return place_of(lax.rem(spot + step * offset + 4 * length, length), length)

    return dict(
        core=core,
        place=place,
        role=role,
        at=at,
        onward=(core, 2 * at(1) + role),
        before=(core, 2 * at(-1) + role),
        sibling=(1 - core, index),
        partner=(1 - core, 2 * place + 1 - role),
    )


def greet(devices):
    barrier = pltpu.get_barrier_semaphore()
    for device in devices:
        pl.semaphore_signal(barrier, inc=1, device_id=device, device_id_type=MESH)
    pl.semaphore_wait(barrier, len(devices))


def remote(source, target, send_sem, recv_sem, device):
    return pltpu.make_async_remote_copy(
        src_ref=source,
        dst_ref=target,
        send_sem=send_sem,
        recv_sem=recv_sem,
        device_id=device,
        device_id_type=MESH,
    )


def each(first, last, body):
    def step(index, carry):
        body(index)
        return carry

    lax.fori_loop(first, last, step, 0)


def gather_kernel(length, count, heads, widths, *refs):
    total = count + heads
    shards, (mod_part, tokens, cotangent) = refs[:total], refs[total : total + 3]
    refs = refs[total + 3 :]
    full, (mod_all, rows_in, block_bias, head_bias) = refs[:total], refs[total : total + 4]
    (
        own_sem, swap_send, swap_recv, ring_send, ring_recv, side_send, side_recv,
        cross_send, cross_recv, mod_send, mod_recv, mod_sem, rows_send, rows_recv, mod_pair, mod_in,
        mod_sum,
        bias_in, bias_sem,
    ) = refs[total + 4 :]
    me = whereabouts(length)
    core, role, place, at = me["core"], me["role"], me["place"], me["at"]
    members = 2 * length
    index = 2 * place + role
    neighbour = (core, 2 * place + 1 - role)
    mine = 2 * place + core
    layers, shared, head_layers = range(count), range(count - 1), range(count, total)

    barrier = pltpu.get_barrier_semaphore()

    def signal(device):
        pl.semaphore_signal(barrier, inc=1, device_id=device, device_id_type=MESH)

    def greet_all(peer):
        other = (peer // members, lax.rem(peer, members))

        @pl.when((other[0] != core) | (other[1] != index))
        def _():
            signal(other)

    each(0, 2 * members, greet_all)
    pl.semaphore_wait(barrier, 2 * members - 1)

    def block(layer, turn):
        return full[layer].at[2 * at(-turn) + core]

    def onward(layer, turn):
        part = block(layer, turn)
        return remote(
            part, part, ring_send.at[layer, turn], ring_recv.at[layer, turn], me["onward"]
        )

    def across(layer, turn):
        part = block(layer, turn)
        return remote(
            part, part, side_send.at[layer, turn], side_recv.at[layer, turn], me["sibling"]
        )

    def from_sibling(layer, turn):
        part = full[layer].at[2 * at(turn) + 1 - core]
        return remote(
            part, part, side_send.at[layer, turn], side_recv.at[layer, turn], me["sibling"]
        )

    def own(layer):
        return pltpu.make_async_copy(shards[layer], full[layer].at[mine], own_sem.at[layer])

    def swap_out(layer):
        return remote(
            shards[layer], full[layer].at[index], swap_send.at[layer], swap_recv.at[layer],
            me["partner"],
        )

    def swap_in(layer):
        return remote(
            shards[layer], full[layer].at[mine], swap_send.at[layer], swap_recv.at[layer],
            me["partner"],
        )

    def lend(layer):
        return remote(
            shards[layer], full[layer].at[2 * place], swap_send.at[layer], swap_recv.at[layer],
            neighbour,
        )

    def cross(layer, turn):
        part = block(layer, turn)
        return remote(
            part, part, cross_send.at[layer - count, turn], cross_recv.at[layer - count, turn],
            neighbour,
        )

    @pl.when(core == role)
    def _():
        for layer in shared:
            own(layer).start()

    @pl.when((core == 0) & (role == 0))
    def _():
        own(count - 1).start()

    def rows_move(source):
        return remote(source, rows_in, rows_send, rows_recv, me["partner"])

    @pl.when(core != role)
    def _():
        for layer in shared:
            swap_out(layer).start()

    @pl.when((core == 0) & (role == 1))
    def _():
        swap_out(count - 1).start()

    @pl.when(core == role)
    def _():
        for layer in head_layers:
            own(layer).start()

    @pl.when((core == 0) & (role == 0))
    def _():
        for layer in head_layers:
            lend(layer).start()

    mod_move = remote(mod_part, mod_in, mod_pair.at[0], mod_pair.at[1], neighbour)

    def mod_copy(peer):
        return remote(
            mod_sum.at[peer], mod_all.at[place], mod_send.at[peer], mod_recv.at[place],
            (lax.rem(peer, 2), 2 * (peer // 2) + core),
        )

    mod_own = pltpu.make_async_copy(mod_sum.at[mine], mod_all.at[place], mod_sem)

    def others(act):
        def body(peer):
            @pl.when(peer != mine)
            def _():
                act(mod_copy(peer))

        each(0, members, body)

    @pl.when(core != role)
    def _():
        mod_move.start()

    def spread_mod():
        @pl.when(core == role)
        def _():
            mod_move.wait_recv()
            mod_sum[...] = mod_part[...] + mod_in[...]
            others(lambda copy: copy.start())
            mod_own.start()

    def gathered_mod():
        @pl.when(core == role)
        def _():
            mod_own.wait()
            others(lambda copy: copy.wait_send())

        @pl.when(core != role)
        def _():
            mod_move.wait_send()

        def came(source):
            @pl.when(jnp.logical_not((core == role) & (source == place)))
            def _():
                remote(
                    mod_sum.at[0], mod_all.at[source], mod_send.at[0], mod_recv.at[source],
                    me["sibling"],
                ).wait_recv()

        each(0, length, came)

    def begin(layer):
        @pl.when(core == role)
        def _():
            own(layer).wait()

        @pl.when(core != role)
        def _():
            swap_in(layer).wait_recv()

        onward(layer, 0).start()
        across(layer, 0).start()

    def ring_turn(turn, more, which):
        for layer in which:
            onward(layer, turn - 1).wait_recv()
            if more:
                onward(layer, turn).start()
            across(layer, turn).start()

    def ring_end(which):
        def end(turn):
            for layer in which:
                onward(layer, turn).wait_send()
                across(layer, turn).wait_send()
                from_sibling(layer, turn).wait_recv()

        each(0, length - 1, end)
        for layer in which:
            across(layer, length - 1).wait_send()
            from_sibling(layer, length - 1).wait_recv()

    def front_head(turn, first):
        for layer in head_layers:
            if first:

                @pl.when(core == 0)
                def _():
                    own(layer).wait()

                @pl.when(core == 1)
                def _():
                    cross(layer, turn).wait_recv()

            else:
                cross(layer, turn).wait_recv()
            across(layer, turn).start()

    @pl.when(role == 0)
    def _():
        for layer in layers:
            begin(layer)

        @pl.when(core == 1)
        def _():
            rows_move(cotangent).start()

        front_head(0, True)
        ring_turn(1, True, layers)
        spread_mod()
        late = 2

        def turn_body(turn):
            ring_turn(turn, True, layers)

            @pl.when(turn > late)
            def _():
                front_head(turn - late, False)

        each(2, length - 1, turn_body)
        ring_turn(length - 1, False, layers)
        each(length - 1 - late, length, lambda turn: front_head(turn, False))
        ring_end(layers)
        gathered_mod()

        def head_end(turn):
            for layer in head_layers:
                across(layer, turn).wait_send()
                from_sibling(layer, turn).wait_recv()

        each(0, length, head_end)

        @pl.when(core == 0)
        def _():
            for layer in head_layers:
                lend(layer).wait_send()

    @pl.when(role == 1)
    def _():
        lag = 3

        def cross_start(turn):
            @pl.when((turn > 0) | (core == 1))
            def _():
                for layer in head_layers:
                    cross(layer, turn).start()

        for layer in head_layers:

            @pl.when(core == 1)
            def _():
                own(layer).wait()

            @pl.when(core == 0)
            def _():
                lend(layer).wait_recv()

            onward(layer, 0).start()

        def head_turn(turn):
            for layer in head_layers:
                onward(layer, turn - 1).wait_recv()

                @pl.when(turn < length - 1)
                def _():
                    onward(layer, turn).start()

            @pl.when(turn >= lag)
            def _():
                cross_start(turn - lag)

        each(1, length, head_turn)
        @pl.when(core == 0)
        def _():
            rows_move(tokens).start()

        each(length - lag, length, cross_start)
        spread_mod()
        for layer in shared:
            begin(layer)
        each(1, length - 1, lambda turn: ring_turn(turn, True, shared))
        ring_turn(length - 1, False, shared)
        ring_end(shared)
        gathered_mod()

        def head_end(turn):
            for layer in head_layers:

                @pl.when(turn < length - 1)
                def _():
                    onward(layer, turn).wait_send()

                @pl.when((turn > 0) | (core == 1))
                def _():
                    cross(layer, turn).wait_send()

        each(0, length, head_end)

    fetch = pltpu.make_async_copy(full[0], bias_in, bias_sem)
    fetch.start()
    fetch.wait()
    block_bias[...] = jnp.zeros_like(block_bias)
    channels = tokens.shape[1]
    for shard in range(members):
        block = wide(bias_in[shard])
        line, start = 0, 0
        for part, width in enumerate(widths):
            if part == 4:
                start = 0
            target = block_bias if part < 4 else head_bias
            first = start + shard * width
            if part == 0 and first >= channels:
                first += channels
            for offset in range(0, width, 128):
                size = min(128, width - offset)
                target[:, first + offset : first + offset + size] = block[line : line + 1, :size]
                line += 1
            start += members * width + (channels if part == 0 else 0)

    @pl.when((core == 0) & (role == 1))
    def _():
        swap_out(count - 1).wait_send()

    @pl.when(core != role)
    def _():
        for layer in shared:
            swap_out(layer).wait_send()
        rows_move(tokens).wait()


def gather(shards, head_shards, mod_part, tokens, cotangent, widths, collective_id):
    members = lax.axis_size("dp")
    length, count, heads = members // 2, len(shards), len(head_shards)
    total = count + heads
    everything = list(shards) + list(head_shards)
    moved = sum(shard.size * 2 for shard in everything) * members
    inside = pl.BlockSpec(memory_space=pltpu.VMEM)
    results = pl.pallas_call(
        functools.partial(gather_kernel, length, count, heads, widths),
        name="gather",
        out_shape=[jax.ShapeDtypeStruct((members,) + s.shape, s.dtype) for s in everything]
        + [jax.ShapeDtypeStruct((length,) + mod_part.shape[1:], mod_part.dtype)]
        + [
            jax.ShapeDtypeStruct(tokens.shape, tokens.dtype),
            jax.ShapeDtypeStruct((1, members * sum(widths[:4]) + tokens.shape[1]), jnp.float32),
            jax.ShapeDtypeStruct((1, members * sum(widths[4:])), jnp.float32),
        ],
        in_specs=[inside] * (total + 1) + [ANY] * 2,
        out_specs=[ANY] * (total + 2) + [inside] * 2,
        scratch_shapes=[
            DMA((total,)),
            DMA((total,)),
            DMA((total,)),
            DMA((total, length)),
            DMA((total, length)),
            DMA((total, length)),
            DMA((total, length)),
            DMA((heads, length)),
            DMA((heads, length)),
            DMA((members,)),
            DMA((members,)),
            DMA(()),
            DMA(()),
            DMA(()),
            DMA((2,)),
            pltpu.VMEM(mod_part.shape, mod_part.dtype),
            pltpu.VMEM(mod_part.shape, mod_part.dtype),
            pltpu.VMEM((members,) + shards[0].shape, shards[0].dtype),
            DMA(()),
        ],
        compiler_params=pltpu.CompilerParams(
            collective_id=collective_id, has_side_effects=True, vmem_limit_bytes=VMEM_BYTES
        ),
        cost_estimate=pl.CostEstimate(flops=0, bytes_accessed=16 * moved, transcendentals=0),
    )(*everything, mod_part, tokens, cotangent)
    return (results[:count], results[count:total]) + tuple(results[total:])


def tile_of(columns):
    for tile in (512, 384, 256, 128):
        if columns % tile == 0:
            return tile
    return columns


class Ring:
    def __init__(self, me, length, variants, scratch):
        count = len(variants[0][1])
        self.me, self.length, self.layers = me, length, range(count)
        self.variants = variants
        self.left_all, self.right_all = scratch[:count], scratch[count : 2 * count]
        self.arrived, self.leaving = scratch[2 * count : 3 * count], scratch[3 * count : 4 * count]
        (
            self.own_sem, self.side_send, self.side_recv, self.ring_send, self.ring_recv,
        ) = scratch[4 * count : 4 * count + 5]

    @staticmethod
    def scratch(length, rows, columns, tokens, parts):
        bf16, count = jnp.bfloat16, len(rows)
        return (
            [pltpu.VMEM((2, length, r, tokens), bf16) for r in rows]
            + [pltpu.VMEM((2, tokens, c), bf16) for c in columns]
            + [pltpu.VMEM((length - 1, r, c), bf16) for r, c in zip(rows, columns)]
            + [pltpu.VMEM((2, r, c), bf16) for r, c in zip(rows, columns)]
            + [
                DMA((count, 2 * parts)),
                DMA((count, 2 * parts)),
                DMA((count, 2 * parts)),
                DMA((count, 2)),
                DMA((count, length)),
            ]
        )

    def chunk(self, layer, slot, turn, add):
        spot = self.me["at"](-(turn + 1))
        left, right = self.left_all[layer], self.right_all[layer]
        columns = right.shape[2]
        tile = tile_of(columns)

        def body(index):
            start = pl.multiple_of(index * tile, tile)
            total = product(left[0, spot], right[0, :, pl.ds(start, tile)]) + product(
                left[1, spot], right[1, :, pl.ds(start, tile)]
            )
            if add:
                total = total + wide(self.arrived[layer][turn - 1, :, pl.ds(start, tile)])
            self.leaving[layer][slot, :, pl.ds(start, tile)] = narrow(total)

        each(0, columns // tile, body)

    def onward(self, layer, slot, turn):
        return remote(
            self.leaving[layer].at[slot],
            self.arrived[layer].at[turn],
            self.ring_send.at[layer, slot],
            self.ring_recv.at[layer, turn],
            self.me["onward"],
        )

    def inputs(self, layer, lefts, rights):
        core, sibling = self.me["core"], self.me["sibling"]
        left_all, right_all = self.left_all[layer], self.right_all[layer]
        copies, sem, start = [], 0, 0

        def both(mine, own_to, other, other_to):
            nonlocal sem
            at = (layer, sem)
            sem += 1
            copies.append(pltpu.make_async_copy(mine, own_to, self.own_sem.at[at]))
            copies.append(
                remote(other, other_to, self.side_send.at[at], self.side_recv.at[at], sibling)
            )

        for part in lefts[layer]:
            lanes = pl.ds(start, part.shape[3])
            both(
                part.at[:, core],
                left_all.at[0, :, :, lanes],
                part.at[:, 1 - core],
                left_all.at[1, :, :, lanes],
            )
            start += part.shape[3]
        start = 0
        for part in rights[layer]:
            rows = pl.ds(start, part.shape[0])
            both(part, right_all.at[0, rows], part, right_all.at[1, rows])
            start += part.shape[0]
        return copies

    def fetch(self, layer, act):
        for predicate, lefts, rights in self.variants:

            def body():
                for copy in self.inputs(layer, lefts, rights):
                    act(copy)

            if predicate is None:
                body()
            else:
                pl.when(predicate)(body)

    def run(self, finish, early=None, midway=None, late=None):
        length = self.length
        for layer in self.layers:
            self.fetch(layer, lambda copy: copy.start())
        if early:
            early()
        for layer in self.layers:
            self.fetch(layer, lambda copy: copy.wait())
            self.chunk(layer, 0, 0, False)
            self.onward(layer, 0, 0).start()

        def turn_body(turn):
            slot = lax.rem(turn, 2)
            for layer in self.layers:
                self.onward(layer, slot, turn - 1).wait_recv()

                @pl.when(turn >= 2)
                def _():
                    self.onward(layer, slot, turn).wait_send()

                self.chunk(layer, slot, turn, True)
                self.onward(layer, slot, turn).start()

        first, second = min(3, length - 1), max(min(3, length - 1), length - 2)
        each(1, first, turn_body)
        if midway:
            midway()
        each(first, second, turn_body)
        if late:
            late()
        each(second, length - 1, turn_body)
        slot = (length - 1) % 2
        for layer in self.layers:
            self.onward(layer, slot, length - 2).wait_recv()
            if length >= 3:
                self.onward(layer, slot, length - 2).wait_send()
            self.chunk(layer, slot, length - 1, True)
            finish(layer, slot)
        for layer in self.layers:
            self.onward(layer, 1 - slot, length - 2).wait_send()


def ring_cost(length, rows, columns, tokens):
    work = sum(r * c for r, c in zip(rows, columns)) * length
    return pl.CostEstimate(flops=4 * work * tokens, bytes_accessed=64 * work, transcendentals=0)


def head_reduce_kernel(length, count, *refs):
    lefts, rights, outs = refs[:count], refs[count : 2 * count], refs[2 * count : 3 * count]
    scratch = refs[3 * count :]
    last_sem = scratch[-1]
    me = whereabouts(length)

    @pl.when(me["role"] == 0)
    def _():
        greet([me["onward"], me["before"], me["sibling"]])
        ring = Ring(me, length, [(None, [[v] for v in lefts], [[v] for v in rights])], scratch[:-1])

        def last(layer, slot):
            return pltpu.make_async_copy(
                ring.leaving[layer].at[slot], outs[layer], last_sem.at[layer]
            )

        ring.run(lambda layer, slot: last(layer, slot).start())
        for layer in ring.layers:
            last(layer, (length - 1) % 2).wait()


def head_reduce(lefts, rights, collective_id):
    length, count = lax.axis_size("dp") // 2, len(lefts)
    rows = [left.shape[2] for left in lefts]
    columns = [right.shape[1] for right in rights]
    tokens = rights[0].shape[0]
    return pl.pallas_call(
        functools.partial(head_reduce_kernel, length, count),
        name="head_reduce",
        out_shape=[jax.ShapeDtypeStruct((r, c), jnp.bfloat16) for r, c in zip(rows, columns)],
        in_specs=[ANY] * (2 * count),
        out_specs=[ANY] * count,
        scratch_shapes=Ring.scratch(length, rows, columns, tokens, 1) + [DMA((count,))],
        compiler_params=pltpu.CompilerParams(
            collective_id=collective_id, has_side_effects=True, vmem_limit_bytes=VMEM_BYTES
        ),
        cost_estimate=ring_cost(length, rows, columns, tokens),
    )(*lefts, *rights)


def reduce_kernel(length, form, count, heads, widths, *refs):
    operands = form.num_leaves
    fronts, backs, head_parts, head_sums, mod_weight = jax.tree.unflatten(form, refs[:operands])
    refs = refs[operands:]
    outs, head_outs = refs[:count], refs[count : count + heads]
    stream_out, bias_all, head_all, mod_rows, silu_all = refs[count + heads : count + heads + 5]
    scratch = refs[count + heads + 5 :]
    mod_all, silu_own, silu_keep, silu_send, silu_recv, silu_side = scratch[-6:]
    mod, bias, bias_line = scratch[-9:-6]
    scratch = scratch[:-9]
    (
        last_send, last_recv, part_send, part_recv, stream_send, stream_recv, small_send,
        mod_recv, bias_recv, head_recv, keep_sem,
    ) = scratch[-11:]
    me = whereabouts(length)
    core, role, place = me["core"], me["role"], me["place"]
    members = 2 * length
    index, mine = 2 * place + role, 2 * place + core
    barrier = pltpu.get_barrier_semaphore()

    def greet_all(peer):
        other = (peer // members, lax.rem(peer, members))

        @pl.when((other[0] != core) | (other[1] != index))
        def _():
            pl.semaphore_signal(barrier, inc=1, device_id=other, device_id_type=MESH)

    each(0, 2 * members, greet_all)
    pl.semaphore_wait(barrier, 2 * members - 1)

    unit = fronts[2][0].shape[0]

    def streams(act):
        for there, parts in ((0, fronts[2]), (1, backs[2])):

            @pl.when((role == there) & (core != role))
            def _():
                cuts = [
                    part.at[pl.ds(start, unit)]
                    for part in parts
                    for start in range(0, part.shape[0], unit)
                ]
                for i, cut in enumerate(cuts):
                    act(
                        remote(
                            cut,
                            stream_out.at[pl.ds(i * unit, unit)],
                            stream_send.at[i],
                            stream_recv.at[i],
                            me["partner"],
                        )
                    )

    streams(lambda copy: copy.start())

    def small(source, target, send, recv, device):
        return remote(source, target, send, recv, device)

    def mod_copy(peer):
        return small(
            mod, mod_all.at[mine], small_send.at[0, peer], mod_recv.at[mine], (role, peer)
        )

    def bias_copy(peer):
        return small(
            bias.at[peer], bias_all.at[mine], small_send.at[1, peer], bias_recv.at[mine],
            (role, peer),
        )

    def head_copy(peer):
        return small(
            head_sums.at[peer], head_all.at[mine], small_send.at[2, peer], head_recv.at[mine],
            (peer // members, lax.rem(peer, members)),
        )

    own_mod = pltpu.make_async_copy(mod, mod_all.at[mine], keep_sem.at[0])
    own_bias = pltpu.make_async_copy(bias.at[index], bias_all.at[mine], keep_sem.at[1])
    own_head = pltpu.make_async_copy(
        head_sums.at[core * members + index], head_all.at[mine], keep_sem.at[2]
    )

    def smalls(act_mod, act_head, act_own):
        def to_section(peer):
            @pl.when((core != role) | (peer != index))
            def _():
                act_mod(mod_copy(peer))
                act_mod(bias_copy(peer))

        each(0, members, to_section)

        @pl.when(core == role)
        def _():
            act_own(own_mod)
            act_own(own_bias)

        @pl.when(role == 0)
        def _():
            def to_all(peer):
                @pl.when(peer != core * members + index)
                def _():
                    act_head(head_copy(peer))

            each(0, 2 * members, to_all)
            act_own(own_head)

    def start(copy):
        copy.start()

    def gather_sums(entries):
        lows = [low[i] for low, *_ in entries for i in range(low.shape[0])]
        highs = [high[i] for _, high, *_ in entries for i in range(high.shape[0])]
        channels = lows[0].shape[1]
        for piece in range(6):
            rows = [v[piece : piece + 1] for v in (lows if piece < 2 else highs)]
            mod[:, piece * channels : (piece + 1) * channels] = narrow(jnp.concatenate(rows, 0))

        def total(read):
            return sum(read(entry) for entry in entries)

        wide_pre = entries[0][3].shape[1]
        bias_line[:, 0:channels] = total(lambda e: e[2][0:1, 0:channels])
        bias_line[:, channels : 2 * channels] = total(lambda e: e[2][0:1, 2 * channels :])
        bias_line[:, 2 * channels : 3 * channels] = total(lambda e: e[4][1, 0:1])
        bias_line[:, 3 * channels : 3 * channels + wide_pre] = total(lambda e: e[3][0:1])
        bias_line[:, 3 * channels + wide_pre :] = total(lambda e: e[4][0, 0:1])

    def early():
        @pl.when(role == 0)
        def _():
            gather_sums(fronts[3])

        @pl.when(role == 1)
        def _():
            gather_sums(backs[3])

        for shard in range(members):
            line, start_at = 0, 0
            for width in widths:
                for offset in range(0, width, 128):
                    size = min(128, width - offset)
                    first = start_at + shard * width + offset
                    bias[shard, line : line + 1, 0:size] = bias_line[:, first : first + size]
                    line += 1
                start_at += members * width
        smalls(start, start, start)

    def part(layer, half):
        rows = head_outs[layer].shape[0]
        return head_parts[layer].at[pl.ds(half * rows, rows)]

    def kept(layer):
        return pltpu.make_async_copy(part(layer, 0), head_outs[layer], part_send.at[layer, 0])

    def handed(layer, half, device):
        return remote(
            part(layer, half), head_outs[layer], part_send.at[layer, half], part_recv.at[layer],
            device,
        )

    @pl.when((role == 0) & (core == 0))
    def _():
        for layer in range(heads):
            kept(layer).start()
            handed(layer, 1, me["sibling"]).start()

    @pl.when((role == 0) & (core == 1))
    def _():
        for layer in range(heads):
            handed(layer, 0, (0, 2 * place + 1)).start()
            handed(layer, 1, (1, 2 * place + 1)).start()

    variants = [(role == 0,) + tuple(fronts[:2]), (role == 1,) + tuple(backs[:2])]
    ring = Ring(me, length, variants, scratch[:-11])

    def local_last(layer, slot):
        return pltpu.make_async_copy(ring.leaving[layer].at[slot], outs[layer], last_send.at[layer])

    def remote_last(layer, slot):
        return remote(
            ring.leaving[layer].at[slot], outs[layer], last_send.at[layer], last_recv.at[layer],
            me["partner"],
        )

    def finish(layer, slot):
        @pl.when(core == role)
        def _():
            local_last(layer, slot).start()

        @pl.when(core != role)
        def _():
            remote_last(layer, slot).start()

    def silu_copy(peer):
        return remote(
            silu_own, silu_all.at[core, index], silu_send.at[peer], silu_recv.at[index],
            (core, peer),
        )

    silu_kept = pltpu.make_async_copy(silu_own, silu_all.at[core, index], silu_keep)

    def others(act):
        def body(peer):
            @pl.when(peer != index)
            def _():
                act(peer)

        each(0, members, body)

    def midway():
        def mod_came(source):
            @pl.when((core != role) | (source != mine))
            def _():
                small(
                    mod, mod_all.at[source], small_send.at[0, 0], mod_recv.at[source],
                    me["sibling"],
                ).wait_recv()

        each(0, members, mod_came)

        @pl.when(core == role)
        def _():
            own_mod.wait()

        images, depth = mod.shape[0], mod_weight.shape[0]
        for source in range(members):
            mod_rows[source * images : (source + 1) * images, :] = wide(mod_all[source])
        silu_own[...] = jnp.zeros_like(silu_own)
        silu_own[:, 0:depth] = product_right_t(narrow(mod_rows[...]), mod_weight[...])
        silu_kept.start()
        others(lambda peer: silu_copy(peer).start())

    across = remote(
        silu_all.at[core], silu_all.at[core], silu_side.at[0], silu_side.at[1], me["sibling"]
    )

    def late():
        others(
            lambda peer: remote(
                silu_own, silu_all.at[core, peer], silu_send.at[peer], silu_recv.at[peer],
                (core, peer),
            ).wait_recv()
        )
        silu_kept.wait()
        across.start()

    ring.run(finish, early, midway, late)
    others(lambda peer: silu_copy(peer).wait_send())
    across.wait_send()
    remote(
        silu_all.at[1 - core], silu_all.at[1 - core], silu_side.at[0], silu_side.at[1],
        me["sibling"],
    ).wait_recv()

    @pl.when((role == 0) & (core == 0))
    def _():
        for layer in range(heads):
            kept(layer).wait()
            handed(layer, 1, me["sibling"]).wait_send()

    @pl.when((role == 0) & (core == 1))
    def _():
        for layer in range(heads):
            handed(layer, 0, (0, 2 * place + 1)).wait_send()
            handed(layer, 1, (1, 2 * place + 1)).wait_send()

    @pl.when((role == 1) | (core == 1))
    def _():
        for layer in range(heads):
            handed(layer, 0, me["sibling"]).wait_recv()

    streams(lambda copy: copy.wait())
    smalls(
        lambda copy: copy.wait_send(),
        lambda copy: copy.wait_send(),
        lambda copy: None if copy is own_mod else copy.wait(),
    )

    def came(source):
        @pl.when((core != role) | (source != mine))
        def _():
            small(
                bias.at[0], bias_all.at[source], small_send.at[1, 0], bias_recv.at[source],
                me["sibling"],
            ).wait_recv()

        @pl.when((role != 0) | (source != mine))
        def _():
            small(
                head_sums.at[0], head_all.at[source], small_send.at[2, 0], head_recv.at[source],
                me["sibling"],
            ).wait_recv()

    each(0, members, came)
    slot = (length - 1) % 2
    for layer in ring.layers:

        @pl.when(core == role)
        def _():
            local_last(layer, slot).wait()

        @pl.when(core != role)
        def _():
            remote_last(layer, slot).wait()


def reduce(fronts, backs, head_parts, head_sums, mod_weight, widths, collective_id):
    members = lax.axis_size("dp")
    lefts, rights, streams, image_sums = fronts
    length, count, heads = members // 2, len(lefts), len(head_parts)
    rows = [left[0].shape[2] for left in lefts]
    columns = [right[0].shape[1] for right in rights]
    parts = len(rights[0])
    tokens = parts * rights[0][0].shape[0]
    bf16 = jnp.bfloat16
    inside = pl.BlockSpec(memory_space=pltpu.VMEM)
    stream_shape = (tokens, streams[0].shape[1])
    operands, form = jax.tree.flatten((fronts, backs, head_parts, head_sums, mod_weight))

    def side_specs(side):
        return jax.tree.map(lambda _: ANY, side[:3]) + (jax.tree.map(lambda _: inside, side[3]),)

    specs = side_specs(fronts) + side_specs(backs)
    specs = jax.tree.leaves(specs, is_leaf=lambda leaf: isinstance(leaf, pl.BlockSpec))
    images = sum(sums_of[0].shape[0] for sums_of in image_sums)
    mod_shape = (images, 6 * image_sums[0][0].shape[2])
    bias_shape = (members, 8, 128)
    f32 = jnp.float32
    lines = members * images
    results = pl.pallas_call(
        functools.partial(reduce_kernel, length, form, count, heads, widths),
        name="reduce",
        out_shape=[jax.ShapeDtypeStruct((r, c), bf16) for r, c in zip(rows, columns)]
        + [jax.ShapeDtypeStruct((h.shape[0] // 2, h.shape[1]), bf16) for h in head_parts]
        + [jax.ShapeDtypeStruct(stream_shape, bf16)]
        + [
            jax.ShapeDtypeStruct(bias_shape, f32),
            jax.ShapeDtypeStruct((members,) + head_sums.shape[1:], f32),
        ]
        + [
            jax.ShapeDtypeStruct((lines, mod_shape[1]), f32),
            jax.ShapeDtypeStruct((2, members, lines, 128), f32),
        ],
        in_specs=specs + [inside] * (heads + 2),
        out_specs=[ANY] * (count + heads + 3) + [inside, ANY],
        scratch_shapes=Ring.scratch(length, rows, columns, tokens, parts)
        + [
            DMA((count,)),
            DMA((count,)),
            DMA((heads, 2)),
            DMA((heads,)),
            DMA((parts,)),
            DMA((parts,)),
            DMA((3, 2 * members)),
            DMA((members,)),
            DMA((members,)),
            DMA((members,)),
            DMA((3,)),
            pltpu.VMEM(mod_shape, bf16),
            pltpu.VMEM(bias_shape, f32),
            pltpu.VMEM((1, members * sum(widths)), f32),
            pltpu.VMEM((members,) + mod_shape, bf16),
            pltpu.VMEM((lines, 128), f32),
            DMA(()),
            DMA((members,)),
            DMA((members,)),
            DMA((2,)),
        ],
        compiler_params=pltpu.CompilerParams(
            collective_id=collective_id, has_side_effects=True, vmem_limit_bytes=VMEM_BYTES
        ),
        cost_estimate=ring_cost(length, rows, columns, tokens),
    )(*operands)
    return (results[:count], results[count : count + heads]) + tuple(results[count + heads :])


def local_grad(function, primal, cotangent_in):
    return jax.vjp(function, primal)[1](cotangent_in)[0]


def column_sums(values):
    return jnp.sum(wide(values), 0)


def normed_of(values):
    center = values - jnp.mean(values, -1, keepdims=True)
    inverse = lax.rsqrt(jnp.mean(center * center, -1, keepdims=True) + EPSILON)
    return center * inverse, inverse


def lane_window(head, head_size):
    start = head * head_size
    base = start // 128 * 128
    width = -(-(start + head_size - base) // 128) * 128
    return base, width, start - base


def head_only(block, inside, head_size):
    lanes = lax.broadcasted_iota(jnp.int32, block.shape, 1)
    keep = (lanes >= inside) & (lanes < inside + head_size)
    return jnp.where(keep, block, jnp.zeros_like(block))


def lay_shards(left, values):
    rows = left.shape[2]
    turned = values.T
    for shard in range(values.shape[1] // rows):
        left[shard // 2, shard % 2] = turned[shard * rows : (shard + 1) * rows]


def attend_kernel(
    head_count, hidden, pieces, pack_w, pack_b, out_w, out_b,
    input_left, packed_out, probs_out, mixed_left, attn_out, after_out, mixed_acc,
):
    channels = hidden.shape[1]
    head_size = channels // head_count
    scaling = head_size ** (-0.5)
    residual = wide(hidden[...])
    normed, _ = normed_of(residual)
    attn_input = narrow(normed * (1.0 + pieces[0, 1:2]) + pieces[0, 0:1])
    lay_shards(input_left, attn_input)
    packed_out[...] = narrow(product(attn_input, pack_w[...]) + pack_b[...])
    mixed_acc[...] = jnp.zeros_like(mixed_acc)
    for head in range(head_count):
        base, width, inside = lane_window(head, head_size)
        queries = packed_out[:, base : base + width]
        keys = head_only(packed_out[:, channels + base : channels + base + width], inside, head_size)
        values = head_only(
            packed_out[:, 2 * channels + base : 2 * channels + base + width], inside, head_size
        )
        scores = product_right_t(queries, keys) * scaling
        exponent = jnp.exp(scores - jnp.max(scores, -1, keepdims=True))
        probs = narrow(exponent * (1.0 / jnp.sum(exponent, -1, keepdims=True)))
        probs_out[0, head] = probs
        mixed_acc[:, base : base + width] += product(probs, values)
    mixed = narrow(mixed_acc[...])
    lay_shards(mixed_left, mixed)
    out = product(mixed, out_w[...]) + out_b[...]
    attn_out[...] = narrow(out)
    after_out[...] = residual + pieces[0, 2:3] * out


def rows_spec(seq_len, columns):
    return pl.BlockSpec((seq_len, columns), lambda i: (i, 0))


def block_at(shape, index):
    return pl.BlockSpec(shape, lambda i: index, pipeline_mode=pl.Buffered(1))


def fixed_spec(shape):
    return block_at(shape, (0,) * len(shape))


def image_rows(array, image):
    if image is None:
        return fixed_spec(array.shape)
    return block_at((SEQ, array.shape[1]), (image if array.shape[0] > SEQ else 0, 0))


def image_steps(array, image):
    base = 0 if image is None or array.shape[0] <= SEQ else image
    return pl.BlockSpec((SEQ, array.shape[1]), lambda i: (base + i, 0))


def attend(hidden, pieces, pack_w, out_w, bias, members, image):
    tokens, channels = hidden.shape
    left = (members // 2, 2, channels // members)
    images, seq = tokens // SEQ, SEQ
    lowest = image or 0
    bf16, f32 = jnp.bfloat16, jnp.float32
    work = tokens * channels * (4 * channels + 2 * seq)
    return pl.pallas_call(
        functools.partial(attend_kernel, HEADS),
        grid=(images,),
        name="attend",
        in_specs=[
            rows_spec(seq, channels),
            pl.BlockSpec((1,) + pieces.shape[1:], lambda i: (lowest + i, 0, 0)),
            fixed_spec(pack_w.shape),
            block_at((1, 3 * channels), (0, 0)),
            fixed_spec(out_w.shape),
            block_at((1, channels), (0, 3)),
        ],
        out_specs=[
            pl.BlockSpec(left + (seq,), lambda i: (0, 0, 0, i)),
            rows_spec(seq, 3 * channels),
            pl.BlockSpec((1, HEADS, seq, seq), lambda i: (i, 0, 0, 0)),
            pl.BlockSpec(left + (seq,), lambda i: (0, 0, 0, i)),
            rows_spec(seq, channels),
            rows_spec(seq, channels),
        ],
        out_shape=[
            jax.ShapeDtypeStruct(left + (tokens,), bf16),
            jax.ShapeDtypeStruct((tokens, 3 * channels), bf16),
            jax.ShapeDtypeStruct((images, HEADS, seq, seq), bf16),
            jax.ShapeDtypeStruct(left + (tokens,), bf16),
            jax.ShapeDtypeStruct((tokens, channels), bf16),
            jax.ShapeDtypeStruct((tokens, channels), f32),
        ],
        scratch_shapes=[pltpu.VMEM((seq, channels), f32)],
        compiler_params=pltpu.CompilerParams(vmem_limit_bytes=VMEM_BYTES),
        cost_estimate=pl.CostEstimate(
            flops=2 * work, bytes_accessed=40 * 2**20, transcendentals=0
        ),
    )(hidden, pieces, pack_w, bias, out_w, bias)


def per_image(values, images):
    return values.reshape(images, values.shape[0] // images, values.shape[1])


GELU_A, GELU_B = 0.7978845608028654, 0.044715


def mlp_kernel(
    after, pieces, up_w, up_b, down_w, down_b,
    input_left, act_left, slope_out, mlp_out, final_out, input_keep, total,
):
    step, steps = pl.program_id(0), pl.num_programs(0)
    images = pieces.shape[0]

    @pl.when(step == 0)
    def _():
        normed, _ = normed_of(per_image(after[...], images))
        rows = narrow(normed * (1.0 + pieces[:, 4:5]) + pieces[:, 3:4]).reshape(after.shape)
        input_keep[...] = rows
        lay_shards(input_left, rows)
        total[...] = jnp.zeros_like(total)

    pre = product(input_keep[...], up_w[...]) + up_b[...]
    square = pre * pre
    tanh = jnp.tanh(GELU_A * pre * (1.0 + GELU_B * square))
    half = 0.5 + 0.5 * tanh
    act = narrow(pre * half)
    lay_shards(act_left, act)
    slope_out[...] = narrow(
        half + pre * (0.5 - 0.5 * tanh * tanh) * (GELU_A + (3.0 * GELU_A * GELU_B) * square)
    )
    total[...] += product(act, down_w[...])

    @pl.when(step == steps - 1)
    def _():
        out = total[...] + down_b[...]
        mlp_out[...] = narrow(out)
        final = per_image(after[...], images) + pieces[:, 5:6] * per_image(out, images)
        final_out[...] = narrow(final * pieces[:, 6:7]).reshape(after.shape)


def feed_tile(width):
    return 1152 if width % 1152 == 0 else width


def mlp(after, pieces, up_w, down_w, bias, members, image):
    tokens, channels = after.shape
    width = up_w.shape[1]
    tile = feed_tile(width)
    bf16, f32 = jnp.bfloat16, jnp.float32
    columns = pl.BlockSpec((tokens, tile), lambda i: (0, i))
    left = (members // 2, 2, channels // members, tokens)
    rows = width // members
    act_block = (tile // (2 * rows), 2, rows, tokens)
    return pl.pallas_call(
        mlp_kernel,
        grid=(width // tile,),
        name="mlp",
        in_specs=[
            fixed_spec(after.shape),
            block_at((tokens // SEQ,) + pieces.shape[1:], (image or 0, 0, 0)),
            pl.BlockSpec((channels, tile), lambda i: (0, i)),
            pl.BlockSpec((1, tile), lambda i: (0, 4 * channels // tile + i)),
            pl.BlockSpec((tile, channels), lambda i: (i, 0)),
            block_at((1, channels), (0, 4 + width // channels)),
        ],
        out_specs=[
            fixed_spec(left),
            pl.BlockSpec(act_block, lambda i: (i, 0, 0, 0)),
            columns,
            fixed_spec((tokens, channels)),
            fixed_spec((tokens, channels)),
        ],
        out_shape=[
            jax.ShapeDtypeStruct(left, bf16),
            jax.ShapeDtypeStruct((members // 2, 2, rows, tokens), bf16),
            jax.ShapeDtypeStruct((tokens, width), bf16),
            jax.ShapeDtypeStruct((tokens, channels), bf16),
            jax.ShapeDtypeStruct((tokens, channels), bf16),
        ],
        scratch_shapes=[pltpu.VMEM((tokens, channels), bf16), pltpu.VMEM((tokens, channels), f32)],
        compiler_params=pltpu.CompilerParams(vmem_limit_bytes=VMEM_BYTES),
        cost_estimate=pl.CostEstimate(
            flops=4 * tokens * channels * width, bytes_accessed=40 * 2**20, transcendentals=0
        ),
    )(after, pieces, up_w, bias, down_w, bias)


def sum_rows(values):
    return product(jnp.ones((8, values.shape[0]), jnp.bfloat16), values)


def layer_norm_back(grad_in, normed, inverse):
    return inverse * (
        grad_in
        - jnp.mean(grad_in, -1, keepdims=True)
        - normed * jnp.mean(grad_in * normed, -1, keepdims=True)
    )


def added_grad(grad, extra, pieces):
    return per_image(wide(grad[...]) + extra[...], pieces.shape[0])


def scaled_grad(grad, extra, pieces):
    return per_image(wide(grad[...]), pieces.shape[0]) * pieces[:, 6:7]


def mlp_back_kernel(
    given_grad, grad, extra, after, pieces, slope, mlp_out, attn_out, up_w, down_w,
    grad_mlp_out, grad_pre_out, grad_after_out, grad_attn_out, sums_out, pre_sums, out_sums,
    total,
):
    step, steps = pl.program_id(0), pl.num_programs(0)
    images = pieces.shape[0]

    @pl.when(step == 0)
    def _():
        given = given_grad(grad, extra, pieces)
        rows = narrow(pieces[:, 5:6] * given).reshape(grad.shape)
        grad_mlp_out[...] = rows
        sums_out[:, 5] = jnp.sum(given * per_image(wide(mlp_out[...]), images), 1)
        out_sums[0] = sum_rows(rows)
        total[...] = jnp.zeros_like(total)

    grad_pre = narrow(wide(slope[...]) * product_right_t(grad_mlp_out[...], down_w[...]))
    grad_pre_out[...] = grad_pre
    pre_sums[...] = sum_rows(grad_pre)
    total[...] += product_right_t(grad_pre, up_w[...])

    @pl.when(step == steps - 1)
    def _():
        normed, inverse = normed_of(per_image(after[...], images))
        grad_min = per_image(total[...], images)
        sums_out[:, 3] = jnp.sum(grad_min, 1)
        sums_out[:, 4] = jnp.sum(grad_min * normed, 1)
        grad_after = given_grad(grad, extra, pieces) + layer_norm_back(
            grad_min * (1.0 + pieces[:, 4:5]), normed, inverse
        )
        grad_after_out[...] = grad_after.reshape(grad.shape)
        rows = narrow(pieces[:, 2:3] * grad_after).reshape(grad.shape)
        grad_attn_out[...] = rows
        sums_out[:, 2] = jnp.sum(grad_after * per_image(wide(attn_out[...]), images), 1)
        out_sums[1] = sum_rows(rows)


def mlp_back(given_grad, grad, extra, after, pieces, slope, mlp_out, attn_out, up_w, down_w, image):
    tokens = after.shape[0] if image is None else SEQ
    images, channels, width = tokens // SEQ, after.shape[1], up_w.shape[1]
    tile = feed_tile(width)
    bf16, f32 = jnp.bfloat16, jnp.float32
    columns = pl.BlockSpec((tokens, tile), lambda i: (0, i))
    slope_row = image if image and slope.shape[0] > SEQ else 0
    rows = fixed_spec((tokens, channels))
    return pl.pallas_call(
        functools.partial(mlp_back_kernel, given_grad),
        grid=(width // tile,),
        name="mlp_back",
        in_specs=[
            image_rows(grad, image),
            image_rows(extra, image),
            image_rows(after, image),
            block_at((images,) + pieces.shape[1:], (image or 0, 0, 0)),
            pl.BlockSpec((tokens, tile), lambda i: (slope_row, i)),
            image_rows(mlp_out, image),
            image_rows(attn_out, image),
            pl.BlockSpec((channels, tile), lambda i: (0, i)),
            pl.BlockSpec((tile, channels), lambda i: (i, 0)),
        ],
        out_specs=[
            rows,
            columns,
            rows,
            rows,
            fixed_spec((images, 8, channels)),
            pl.BlockSpec((8, tile), lambda i: (0, i)),
            fixed_spec((2, 8, channels)),
        ],
        out_shape=[
            jax.ShapeDtypeStruct((tokens, channels), bf16),
            jax.ShapeDtypeStruct((tokens, width), bf16),
            jax.ShapeDtypeStruct((tokens, channels), f32),
            jax.ShapeDtypeStruct((tokens, channels), bf16),
            jax.ShapeDtypeStruct((images, 8, channels), f32),
            jax.ShapeDtypeStruct((8, width), f32),
            jax.ShapeDtypeStruct((2, 8, channels), f32),
        ],
        scratch_shapes=[pltpu.VMEM((tokens, channels), f32)],
        compiler_params=pltpu.CompilerParams(vmem_limit_bytes=VMEM_BYTES),
        cost_estimate=pl.CostEstimate(
            flops=4 * tokens * channels * width, bytes_accessed=40 * 2**20, transcendentals=0
        ),
    )(grad, extra, after, pieces, slope, mlp_out, attn_out, up_w, down_w)


def attend_back_kernel(
    head_count, hidden, pieces, packed, probs_in, grad_attn, grad_after, pack_w, out_w,
    grad_packed_out, grad_hidden_out, sums_out, pack_sums, acc, grad_mixed_keep,
):
    channels = hidden.shape[1]
    head_size = channels // head_count
    scaling = head_size ** (-0.5)
    grad_mixed_keep[...] = narrow(product_right_t(grad_attn[...], out_w[...]))
    acc[...] = jnp.zeros_like(acc)
    for head in range(head_count):
        base, width, inside = lane_window(head, head_size)
        q_at, k_at, v_at = (slice(j * channels + base, j * channels + base + width) for j in range(3))
        queries = head_only(packed[:, q_at], inside, head_size)
        keys = head_only(packed[:, k_at], inside, head_size)
        grad_mixed = head_only(grad_mixed_keep[:, q_at], inside, head_size)
        probs = probs_in[0, head]
        grad_probs = product_right_t(grad_mixed, packed[:, v_at])
        probs_wide = wide(probs)
        weighted = probs_wide * grad_probs
        grad_scores = narrow(weighted - probs_wide * jnp.sum(weighted, -1, keepdims=True))
        acc[:, v_at] += product_left_t(probs, grad_mixed)
        acc[:, q_at] += product(grad_scores, keys) * scaling
        acc[:, k_at] += product_left_t(grad_scores, queries) * scaling
    grad_packed = narrow(acc[...])
    grad_packed_out[...] = grad_packed
    column_totals = sum_rows(grad_packed)

    @pl.when(pl.program_id(0) == 0)
    def _():
        pack_sums[...] = column_totals

    @pl.when(pl.program_id(0) > 0)
    def _():
        pack_sums[...] += column_totals

    grad_ain = product_right_t(grad_packed, pack_w[...])
    normed, inverse = normed_of(wide(hidden[...]))
    sums_out[0, 0:1] = jnp.sum(grad_ain, 0, keepdims=True)
    sums_out[0, 1:2] = jnp.sum(grad_ain * normed, 0, keepdims=True)
    grad_hidden_out[...] = narrow(
        grad_after[...] + layer_norm_back(grad_ain * (1.0 + pieces[0, 1:2]), normed, inverse)
    )


def attend_back(hidden, pieces, packed, probs, grad_attn, grad_after, pack_w, out_w, image):
    tokens = hidden.shape[0] if image is None else SEQ
    images, channels, seq = tokens // SEQ, hidden.shape[1], SEQ
    lowest = image or 0
    probs_at = lowest if probs.shape[0] > 1 else 0
    bf16, f32 = jnp.bfloat16, jnp.float32
    work = tokens * channels * (4 * channels + 5 * seq)
    return pl.pallas_call(
        functools.partial(attend_back_kernel, HEADS),
        grid=(images,),
        name="attend_back",
        in_specs=[
            image_steps(hidden, image),
            pl.BlockSpec((1,) + pieces.shape[1:], lambda i: (lowest + i, 0, 0)),
            image_steps(packed, image),
            pl.BlockSpec((1, HEADS, seq, seq), lambda i: (probs_at + i, 0, 0, 0)),
            image_steps(grad_attn, image),
            image_steps(grad_after, image),
            fixed_spec(pack_w.shape),
            fixed_spec(out_w.shape),
        ],
        out_specs=[
            rows_spec(seq, 3 * channels),
            rows_spec(seq, channels),
            pl.BlockSpec((1, 8, channels), lambda i: (i, 0, 0)),
            fixed_spec((8, 3 * channels)),
        ],
        out_shape=[
            jax.ShapeDtypeStruct((tokens, 3 * channels), bf16),
            jax.ShapeDtypeStruct((tokens, channels), bf16),
            jax.ShapeDtypeStruct((images, 8, channels), f32),
            jax.ShapeDtypeStruct((8, 3 * channels), f32),
        ],
        scratch_shapes=[
            pltpu.VMEM((seq, 3 * channels), f32),
            pltpu.VMEM((seq, channels), bf16),
        ],
        compiler_params=pltpu.CompilerParams(vmem_limit_bytes=VMEM_BYTES),
        cost_estimate=pl.CostEstimate(
            flops=2 * work, bytes_accessed=40 * 2**20, transcendentals=0
        ),
    )(hidden, pieces, packed, probs, grad_attn, grad_after, pack_w, out_w)


def block_forward(hidden, pieces, weights, members, image=None):
    pack_w, out_w, up_w, down_w, bias = weights
    input_left, packed, probs, mixed_left, attn_out, after = attend(
        hidden, pieces, pack_w, out_w, bias, members, image
    )
    rows_left, act_left, slope, mlp_out, final = mlp(
        after, pieces, up_w, down_w, bias, members, image
    )
    return (
        final,
        (packed, probs, attn_out, after, slope, mlp_out),
        (act_left, rows_left, mixed_left, input_left),
    )


def block_backward(hidden, saved_state, pieces, weights, given_grad, grad, extra, image):
    pack_w, out_w, up_w, down_w, _ = weights
    packed, probs, attn_out, after, slope, mlp_out = saved_state
    grad_mlp, grad_pre, grad_after, grad_attn, high_sums, pre_sums, out_sums = mlp_back(
        given_grad, grad, extra, after, pieces, slope, mlp_out, attn_out, up_w, down_w, image
    )
    grad_packed, grad_hidden, low_sums, pack_sums = attend_back(
        hidden, pieces, packed, probs, grad_attn, grad_after, pack_w, out_w, image
    )
    rights = (grad_mlp, grad_pre, grad_attn, grad_packed)
    return grad_hidden, rights, (low_sums, high_sums, pack_sums, pre_sums, out_sums)


def silu_parts(values):
    gate = 0.5 + 0.5 * jnp.tanh(0.5 * values)
    return values * gate, gate * (1.0 + values * (1.0 - gate))


def head_kernel(
    members, hidden_at, target_at, live, in_w_at, in_b, mid_w_at, mid_b, out_w_at, out_b,
    grad_hidden_at, last_left_at, mid_left_at, in_left_at, grad_feature_at, grad_second_at,
    device_rows,
    hidden, target, in_w, mid_w, out_w,
    grad_hidden_out, last_left, mid_left, in_left, grad_feature_out, grad_second_out,
    act_first, slope_first, act_second, slope_second, grad_first_keep, in_sums, mid_sums,
    come_sem, go_sem,
):
    width = in_w.shape[1]
    tile = 512 if width % 512 == 0 else width
    tiles = [slice(start, start + tile) for start in range(0, width, tile)]
    rows = width // (2 * members)
    pairs_in = ((hidden_at, hidden), (in_w_at, in_w), (mid_w_at, mid_w), (out_w_at, out_w), (target_at, target))
    come = [
        pltpu.make_async_copy(there, here, come_sem.at[i]) for i, (there, here) in enumerate(pairs_in)
    ]
    pairs_out = (
        (grad_hidden_out, grad_hidden_at),
        (last_left, last_left_at),
        (mid_left, mid_left_at),
        (in_left, in_left_at),
        (grad_feature_out, grad_feature_at),
        (grad_second_out, grad_second_at),
    )
    go = [
        pltpu.make_async_copy(here, there, go_sem.at[i]) for i, (here, there) in enumerate(pairs_out)
    ]

    def lay(left, values, start):
        turned = values.T
        for offset in range(0, values.shape[1], rows):
            shard = (start + offset) // rows
            half, index = shard // members, shard % members
            left[index // 2, index % 2, half * rows : (half + 1) * rows] = turned[
                offset : offset + rows
            ]

    @pl.when(lax.rem(lax.axis_index("dp"), 2) == 0)
    def _():
        for copy in come:
            copy.start()
        come[0].wait()
        come[1].wait()
        for at in tiles:
            act, slope = silu_parts(product(hidden[...], in_w[:, at]) + in_b[:, at])
            act_first[:, at] = narrow(act)
            slope_first[:, at] = narrow(slope)
        come[2].wait()
        for at in tiles:
            act, slope = silu_parts(product(act_first[...], mid_w[:, at]) + mid_b[:, at])
            act_second[:, at] = narrow(act)
            slope_second[:, at] = narrow(slope)
            lay(mid_left, act_first[:, at], at.start)
        go[2].start()
        come[3].wait()
        come[4].wait()
        feature = product(act_second[...], out_w[...]) + out_b[...]
        inverse = lax.rsqrt(jnp.sum(feature * feature, -1, keepdims=True) + EPSILON)
        unit = feature * inverse
        aim = wide(target[...])
        aim = aim * lax.rsqrt(jnp.sum(aim * aim, -1, keepdims=True) + EPSILON)
        alive = live[:, 0:1]
        cosine = jnp.sum(unit * aim, -1, keepdims=True)
        loss = 0.5 * jnp.sum(alive * (1.0 - cosine), axis=(0, 1), keepdims=True)
        grad_unit = (-0.5 * alive) * aim
        grad_feature = narrow(
            inverse * (grad_unit - unit * jnp.sum(grad_unit * unit, -1, keepdims=True))
        )
        grad_feature_out[...] = grad_feature
        go[4].start()
        out_sums = sum_rows(grad_feature)
        for at in tiles:
            grad_second = narrow(
                wide(slope_second[:, at]) * product_right_t(grad_feature, out_w[at, :])
            )
            grad_second_out[:, at] = grad_second
            mid_sums[:, at] = sum_rows(grad_second)
            lay(last_left, act_second[:, at], at.start)
        go[1].start()
        go[5].start()
        for at in tiles:
            grad_first = narrow(
                wide(slope_first[:, at]) * product_right_t(grad_second_out[...], mid_w[at, :])
            )
            grad_first_keep[:, at] = grad_first
            in_sums[:, at] = sum_rows(grad_first)
            part = product_right_t(grad_first, in_w[:, at])
            if at.start == 0:
                grad_hidden_out[...] = part
            else:
                grad_hidden_out[...] += part
            lay(in_left, grad_first_keep[:, at], at.start)
        go[0].start()
        go[3].start()
        share, devices = width // (2 * members), 2 * members
        device_rows[...] = jnp.zeros_like(device_rows)
        for device in range(devices):
            lanes = slice(device * share, (device + 1) * share)
            device_rows[device, 0:1, 0:share] = in_sums[0:1, lanes]
            device_rows[device, 0:1, share : 2 * share] = mid_sums[0:1, lanes]
        count = out_sums.shape[1] // 128
        for line in range(count):
            device_rows[:, 1 + line, :] = jnp.broadcast_to(
                out_sums[0:1, line * 128 : (line + 1) * 128], (devices, 128)
            )
        device_rows[:, 1 + count, :] = jnp.broadcast_to(loss, (devices, 128))
        for copy in go:
            copy.wait()


def head_pass(hidden, target, live, head_weights, members):
    tokens, channels = hidden.shape
    width, features = head_weights[2].shape[0], target.shape[1]
    bf16, f32 = jnp.bfloat16, jnp.float32
    left = ((members // 2, 2, width // members, tokens), bf16)
    live_lanes = jnp.broadcast_to(live[:, None], (tokens, 128))
    in_w, in_b, mid_w, mid_b, out_w, out_b = head_weights
    inside = pl.BlockSpec(memory_space=pltpu.VMEM)
    work = tokens * (channels * width + width * width + width * features)
    big = [
        ((tokens, channels), f32),
        left,
        left,
        left,
        ((tokens, features), bf16),
        ((tokens, width), bf16),
    ]
    small = [((2 * members, 2 + features // 128, 128), f32)]
    results = pl.pallas_call(
        functools.partial(head_kernel, members),
        name="head",
        in_specs=[ANY, ANY, inside, ANY, inside, ANY, inside, ANY, inside],
        out_specs=[ANY] * 6 + [inside],
        out_shape=[jax.ShapeDtypeStruct(*leaf) for leaf in big + small],
        scratch_shapes=[
            pltpu.VMEM(array.shape, array.dtype) for array in (hidden, target, in_w, mid_w, out_w)
        ]
        + [pltpu.VMEM(*leaf) for leaf in big]
        + [pltpu.VMEM((tokens, width), bf16)] * 5
        + [pltpu.VMEM((8, width), f32)] * 2
        + [DMA((5,)), DMA((6,))],
        compiler_params=pltpu.CompilerParams(vmem_limit_bytes=VMEM_BYTES),
        cost_estimate=pl.CostEstimate(
            flops=4 * work, bytes_accessed=40 * 2**20, transcendentals=0
        ),
    )(hidden, target, live_lanes, in_w, in_b[None], mid_w, mid_b[None], out_w, out_b[None])
    grad_hidden, last_left, mid_left, in_left, grad_feature, grad_second, device_rows = results
    return (
        grad_hidden,
        (last_left, mid_left, in_left),
        (grad_feature, grad_second),
        device_rows,
    )


def trade_kernel(members, given, taken, send_sem, recv_sem):
    core, index = lax.axis_index("section"), lax.axis_index("dp")
    barrier = pltpu.get_barrier_semaphore()

    def others(act):
        def body(peer):
            @pl.when(peer != index)
            def _():
                act(peer)

        each(0, members, body)

    def copy(peer):
        return remote(given, taken.at[index], send_sem.at[peer], recv_sem.at[index], (core, peer))

    others(
        lambda peer: pl.semaphore_signal(
            barrier, inc=1, device_id=(core, peer), device_id_type=MESH
        )
    )
    pl.semaphore_wait(barrier, members - 1)
    others(lambda peer: copy(peer).start())
    taken[index] = given[...]
    others(
        lambda peer: remote(
            given, taken.at[peer], send_sem.at[peer], recv_sem.at[peer], (core, peer)
        ).wait_recv()
    )
    others(lambda peer: copy(peer).wait_send())


def trade(block, collective_id):
    members = lax.axis_size("dp")
    inside = pl.BlockSpec(memory_space=pltpu.VMEM)
    return pl.pallas_call(
        functools.partial(trade_kernel, members),
        name="trade",
        out_shape=jax.ShapeDtypeStruct((members,) + block.shape, block.dtype),
        in_specs=[inside],
        out_specs=inside,
        scratch_shapes=[DMA((members,)), DMA((members,))],
        compiler_params=pltpu.CompilerParams(collective_id=collective_id, has_side_effects=True),
    )(block)


def hollow(shapes):
    leaves, form = jax.tree.flatten(shapes)
    results = pl.pallas_call(
        lambda *refs: None,
        name="hollow",
        out_shape=[jax.ShapeDtypeStruct(leaf.shape, leaf.dtype) for leaf in leaves],
        out_specs=[ANY if leaf.ndim else pl.BlockSpec(memory_space=pltpu.SMEM) for leaf in leaves],
    )()
    return jax.tree.unflatten(form, list(results))


def on_device(
    tokens_in,
    cotangent,
    targets,
    buckets,
    counts,
    time_table,
    modulate_weight,
    modulate_bias,
    qkv_weight,
    qv_bias,
    attn_weight,
    attn_bias,
    up_weight,
    up_bias,
    down_weight,
    down_bias,
    project_in_weight,
    project_in_bias,
    project_mid_weight,
    project_mid_bias,
    project_out_weight,
    project_out_bias,
):
    members = lax.axis_size("dp")
    core = lax.axis_index("section")
    index = lax.axis_index("dp")
    place, role = index // 2, index % 2
    is_first = role == 0
    own = 2 * place + core
    channels = tokens_in.shape[1]
    images = tokens_in.shape[0] // SEQ
    pairs_up, pairs_back, pairs_swap = [], [], []
    for pair in range(members // 2):
        low, high = 2 * pair, 2 * pair + 1
        pairs_swap += [(high, members + low)]
        pairs_up += [(low, high), (members + low, members + high)]
        pairs_back += [(high, low), (members + high, members + low)]
    axes = ("section", "dp")

    bucket_block = jnp.broadcast_to(jnp.pad(buckets, (0, 128 - images))[None], (8, 128))
    all_buckets = trade(bucket_block, 1)[:, 0, :images].reshape(-1)
    one_hot = (
        all_buckets[:, None] == jnp.arange(time_table.shape[0], dtype=jnp.int32)[None, :]
    ).astype(jnp.float32)
    conditioning = jnp.dot(one_hot, time_table, precision=HIGHEST)
    silu_all = narrow(jax.nn.silu(conditioning))
    depth = modulate_weight.shape[1]
    silu_depth = lax.dynamic_slice_in_dim(silu_all, index * depth, depth, 1)
    mod_part = product(silu_depth, modulate_weight[0])
    share = modulate_bias.shape[1]
    bias_row = lax.dynamic_update_slice_in_dim(
        jnp.zeros((mod_part.shape[1],), jnp.float32), wide(modulate_bias[0]), index * share, 0
    )
    mod_part = (mod_part + bias_row[None]).reshape(members, images, 6 * channels)

    section_biases = (qv_bias[0], attn_bias[0], up_bias[0], down_bias[0])
    biases = section_biases + (project_in_bias, project_mid_bias, project_out_bias)
    widths = [part.shape[0] for part in biases]
    lines = [
        jnp.pad(part, (0, -part.shape[0] % 128)).reshape(-1, 128) for part in biases
    ]
    bias_block = jnp.concatenate(lines)
    bias_block = jnp.pad(bias_block, ((0, -bias_block.shape[0] % 16), (0, 0)))
    block_full, head_full, mod_all, rows_in, block_bias, head_bias = gather(
        (
            bias_block,
            qkv_weight[0],
            attn_weight[0],
            up_weight[0],
            down_weight[0],
            project_out_weight,
        ),
        (project_in_weight, project_mid_weight),
        mod_part,
        tokens_in,
        cotangent,
        widths,
        0,
    )
    _, pack_weight, out_weight, first_weight, second_weight, head_last = block_full
    head_ends = [members * width for width in widths[4:]]
    head_bias = [
        head_bias[0, sum(head_ends[:i]) : sum(head_ends[: i + 1])] for i in range(len(head_ends))
    ]

    def whole(values):
        return values.reshape(-1, values.shape[-1])

    block_weights = (
        whole(pack_weight),
        whole(out_weight),
        whole(first_weight),
        whole(second_weight),
        block_bias,
    )
    head_weights = (
        whole(head_full[0]),
        head_bias[0],
        whole(head_full[1]),
        head_bias[1],
        whole(head_last),
        head_bias[2],
    )
    pieces = jnp.sum(mod_all, 0).reshape(images, 6, channels)

    own_counts = counts[own]
    image_live = (jnp.arange(images, dtype=jnp.int32) < own_counts).astype(jnp.float32)
    token_live = jnp.repeat(image_live, SEQ)
    out_scale = jnp.where(is_first, 1.0, image_live)
    scale_rows = jnp.broadcast_to(out_scale[:, None, None], (images, 2, channels))
    pieces = jnp.concatenate([pieces, scale_rows], 1)
    total_live = wide(jnp.sum(counts)) * SEQ
    crossed = core != role
    targets_out, rows_in = lax.optimization_barrier((targets, rows_in))
    hidden_first = jnp.where(crossed, rows_in, tokens_in)
    outer = jnp.where(crossed, rows_in, cotangent)
    outer = lax.optimization_barrier(outer)
    own_targets = jnp.where(crossed, lax.ppermute(targets_out, axes, pairs_swap), targets)

    def unused(function, *operands_in):
        return hollow(jax.eval_shape(function, *operands_in))

    def forward(hidden, mod, block):
        return block_forward(hidden, mod, block, members)

    first_out, saved_state, first_lefts = lax.cond(
        is_first,
        forward,
        lambda *operands_in: unused(forward, *operands_in),
        hidden_first,
        pieces,
        block_weights,
    )
    hidden_second = lax.ppermute(first_out, axes, pairs_up)

    head_result = head_pass(first_out, own_targets, token_live, head_weights, members)
    hidden_second, head_result = lax.optimization_barrier((hidden_second, head_result))
    grad_hidden, head_lefts, head_rights, head_rows = head_result

    def do_second(rows, mod, grad, block):
        final, state, lefts = block_forward(rows, mod, block, members)
        grad_rows, rights, sums_of = block_backward(
            rows, state, mod, block, scaled_grad, grad, grad, None
        )
        cut = tuple(grad_rows[i * SEQ : (i + 1) * SEQ] for i in range(images))
        return cut, final, rights, sums_of, lefts

    second = lax.cond(
        is_first,
        lambda *operands_in: unused(do_second, *operands_in),
        do_second,
        hidden_second,
        pieces,
        outer,
        block_weights,
    )
    returning = [lax.ppermute(rows, axes, pairs_back) for rows in second[0]]
    head_lefts, head_rights, kept = lax.optimization_barrier((head_lefts, head_rights, second[1]))
    second = (second[0], kept) + second[2:]
    head_parts = head_reduce(head_lefts, head_rights + (first_out,), 2)
    returning[0], head_parts = lax.optimization_barrier((returning[0], head_parts))
    first = []
    for i in range(images):

        def do_first(rows, state, mod, extra, grad, block, i=i):
            return block_backward(rows, state, mod, block, added_grad, grad, extra, i)

        if i:
            returning[i], gone = lax.optimization_barrier((returning[i], first[i - 1][0]))
            first[i - 1] = (gone,) + first[i - 1][1:]
        first.append(
            lax.cond(
                is_first,
                do_first,
                lambda *operands_in: unused(do_first, *operands_in),
                hidden_first,
                saved_state,
                pieces,
                grad_hidden,
                returning[i],
                block_weights,
            )
        )
    def by_layer(results):
        return [list(parts_of) for parts_of in zip(*results)]

    fronts = (
        [[left] for left in first_lefts],
        by_layer([result[1] for result in first]),
        [result[0] for result in first],
        [result[2] for result in first],
    )
    backs = (
        [[left] for left in second[4]],
        [[right] for right in second[2]],
        [second[1]],
        [second[3]],
    )
    block_grads, head_grads, stream_in, bias_all, head_all, mod_wide, silu_all_terms = reduce(
        fronts,
        backs,
        head_parts,
        head_rows,
        modulate_weight[0],
        widths[:4],
        3,
    )
    down_grad, up_grad, attn_grad, qkv_grad = block_grads
    stream = jnp.where(is_first, jnp.concatenate(fronts[2]), jnp.concatenate(backs[2]))
    stream_own = jnp.where(crossed, stream_in, stream)
    mod_w_grad = product_left_t(silu_depth, narrow(mod_wide))
    mod_b_grad = lax.dynamic_slice_in_dim(jnp.sum(mod_wide, 0), index * share, share, 0)
    silu_total = jnp.sum(silu_all_terms[:, :, :, :depth], 0)
    silu_total = jnp.swapaxes(silu_total, 0, 1).reshape(-1, channels)
    cond_grad = local_grad(jax.nn.silu, conditioning, silu_total)
    table_grad = jnp.dot(one_hot.T, cond_grad, precision=HIGHEST)

    bias_sums = jnp.sum(bias_all, 0)
    bias_outs, line = [], 0
    for width in widths[:4]:
        count = -(-width // 128)
        bias_outs.append(bias_sums[line : line + count].reshape(1, -1)[:, :width])
        line += count
    sums = jnp.sum(head_all, 0)
    head_share = head_grads[1].shape[0]
    loss_value = sums[-1, 0] / total_live
    return (
        stream_own[None],
        loss_value,
        table_grad,
        mod_w_grad[None],
        mod_b_grad[None],
        wide(qkv_grad)[None],
        bias_outs[0],
        wide(attn_grad)[None],
        bias_outs[1],
        wide(up_grad)[None],
        bias_outs[2],
        wide(down_grad)[None],
        bias_outs[3],
        wide(head_grads[2]).T,
        sums[0, :head_share],
        wide(head_grads[1]),
        sums[0, head_share : 2 * head_share],
        wide(head_grads[0]),
        sums[1:-1].reshape(-1),
    )


def solution(mesh):
    in_specs = (
        P("dp", None),
        P("dp", None),
        P("dp", None),
        P("dp"),
        P(),
        P(),
        P("section", "dp", None),
        P("section", "dp"),
        P("section", "dp", None),
        P("section", "dp"),
        P("section", "dp", None),
        P("section", "dp"),
        P("section", "dp", None),
        P("section", "dp"),
        P("section", "dp", None),
        P("section", "dp"),
        P("dp", None),
        P("dp"),
        P("dp", None),
        P("dp"),
        P("dp", None),
        P("dp"),
    )
    out_specs = (
        P("section", "dp", None),
        P(),
        P(),
        P("section", "dp", None),
        P("section", "dp"),
        P("section", "dp", None),
        P("section", "dp"),
        P("section", "dp", None),
        P("section", "dp"),
        P("section", "dp", None),
        P("section", "dp"),
        P("section", "dp", None),
        P("section", "dp"),
        P(None, ("section", "dp")),
        P(("section", "dp")),
        P(("section", "dp"), None),
        P(("section", "dp")),
        P(("section", "dp"), None),
        P(),
    )
    return jax.shard_map(
        on_device, mesh=mesh, in_specs=in_specs, out_specs=out_specs, check_vma=False
    )
```

```python
import functools
import jax
import jax.numpy as jnp
from jax import lax
from jax.experimental import pallas as pl
from jax.experimental.pallas import tpu as pltpu
from jax.sharding import PartitionSpec as P

HEADS = 16
SEQ = 256
EPSILON = 1e-06
HIGHEST = lax.Precision.HIGHEST
MESH = pl.DeviceIdType.MESH
ANY = pl.BlockSpec(memory_space=pl.ANY)
DMA = pltpu.SemaphoreType.DMA
VMEM_BYTES = 60 * 2**20


def narrow(values):
    return values.astype(jnp.bfloat16)


def wide(values):
    return values.astype(jnp.float32)


def product(left_side, right_side):
    return jnp.dot(left_side, right_side, preferred_element_type=jnp.float32)


def product_left_t(left_side, right_side):
    return lax.dot_general(
        left_side, right_side, (((0,), (0,)), ((), ())), preferred_element_type=jnp.float32
    )


def product_right_t(left_side, right_side):
    return lax.dot_general(
        left_side, right_side, (((1,), (1,)), ((), ())), preferred_element_type=jnp.float32
    )


def ring_of(place, length):
    half, side = place // 2, place % 2
    return side * (length - 1 - half) + (1 - side) * half


def place_of(spot, length):
    side = spot // (length // 2)
    half = side * (length - 1 - spot) + (1 - side) * spot
    return 2 * half + side


def whereabouts(length):
    core = lax.axis_index("section")
    index = lax.axis_index("dp")
    place, role = index // 2, index % 2
    spot = ring_of(place, length)
    step = 1 - 2 * core

    def at(offset):
        return place_of(lax.rem(spot + step * offset + 4 * length, length), length)

    return dict(
        core=core,
        place=place,
        role=role,
        at=at,
        onward=(core, 2 * at(1) + role),
        before=(core, 2 * at(-1) + role),
        sibling=(1 - core, index),
        partner=(1 - core, 2 * place + 1 - role),
    )


def greet(devices):
    barrier = pltpu.get_barrier_semaphore()
    for device in devices:
        pl.semaphore_signal(barrier, inc=1, device_id=device, device_id_type=MESH)
    pl.semaphore_wait(barrier, len(devices))


def remote(source, target, send_sem, recv_sem, device):
    return pltpu.make_async_remote_copy(
        src_ref=source,
        dst_ref=target,
        send_sem=send_sem,
        recv_sem=recv_sem,
        device_id=device,
        device_id_type=MESH,
    )


def each(first, last, body):
    def step(index, carry):
        body(index)
        return carry

    lax.fori_loop(first, last, step, 0)


def gather_kernel(length, count, heads, widths, *refs):
    total = count + heads
    shards, (mod_part, tokens, cotangent) = refs[:total], refs[total : total + 3]
    refs = refs[total + 3 :]
    full, (mod_all, rows_in, block_bias, head_bias) = refs[:total], refs[total : total + 4]
    (
        own_sem, swap_send, swap_recv, ring_send, ring_recv, side_send, side_recv,
        cross_send, cross_recv, mod_send, mod_recv, mod_sem, rows_send, rows_recv, mod_pair, mod_in,
        mod_sum,
        bias_in, bias_sem,
    ) = refs[total + 4 :]
    me = whereabouts(length)
    core, role, place, at = me["core"], me["role"], me["place"], me["at"]
    members = 2 * length
    index = 2 * place + role
    neighbour = (core, 2 * place + 1 - role)
    mine = 2 * place + core
    layers, shared, head_layers = range(count), range(count - 1), range(count, total)

    barrier = pltpu.get_barrier_semaphore()

    def signal(device):
        pl.semaphore_signal(barrier, inc=1, device_id=device, device_id_type=MESH)

    def greet_all(peer):
        other = (peer // members, lax.rem(peer, members))

        @pl.when((other[0] != core) | (other[1] != index))
        def _():
            signal(other)

    each(0, 2 * members, greet_all)
    pl.semaphore_wait(barrier, 2 * members - 1)

    def block(layer, turn):
        return full[layer].at[2 * at(-turn) + core]

    def onward(layer, turn):
        part = block(layer, turn)
        return remote(
            part, part, ring_send.at[layer, turn], ring_recv.at[layer, turn], me["onward"]
        )

    def across(layer, turn):
        part = block(layer, turn)
        return remote(
            part, part, side_send.at[layer, turn], side_recv.at[layer, turn], me["sibling"]
        )

    def from_sibling(layer, turn):
        part = full[layer].at[2 * at(turn) + 1 - core]
        return remote(
            part, part, side_send.at[layer, turn], side_recv.at[layer, turn], me["sibling"]
        )

    def own(layer):
        return pltpu.make_async_copy(shards[layer], full[layer].at[mine], own_sem.at[layer])

    def swap_out(layer):
        return remote(
            shards[layer], full[layer].at[index], swap_send.at[layer], swap_recv.at[layer],
            me["partner"],
        )

    def swap_in(layer):
        return remote(
            shards[layer], full[layer].at[mine], swap_send.at[layer], swap_recv.at[layer],
            me["partner"],
        )

    def lend(layer):
        return remote(
            shards[layer], full[layer].at[2 * place], swap_send.at[layer], swap_recv.at[layer],
            neighbour,
        )

    def cross(layer, turn):
        part = block(layer, turn)
        return remote(
            part, part, cross_send.at[layer - count, turn], cross_recv.at[layer - count, turn],
            neighbour,
        )

    @pl.when(core == role)
    def _():
        for layer in shared:
            own(layer).start()

    @pl.when((core == 0) & (role == 0))
    def _():
        own(count - 1).start()

    def rows_move(source):
        return remote(source, rows_in, rows_send, rows_recv, me["partner"])

    @pl.when(core != role)
    def _():
        for layer in shared:
            swap_out(layer).start()

    @pl.when((core == 0) & (role == 1))
    def _():
        swap_out(count - 1).start()

    @pl.when(core == role)
    def _():
        for layer in head_layers:
            own(layer).start()

    @pl.when((core == 0) & (role == 0))
    def _():
        for layer in head_layers:
            lend(layer).start()

    mod_move = remote(mod_part, mod_in, mod_pair.at[0], mod_pair.at[1], neighbour)

    def mod_copy(peer):
        return remote(
            mod_sum.at[peer], mod_all.at[place], mod_send.at[peer], mod_recv.at[place],
            (lax.rem(peer, 2), 2 * (peer // 2) + core),
        )

    mod_own = pltpu.make_async_copy(mod_sum.at[mine], mod_all.at[place], mod_sem)

    def others(act):
        def body(peer):
            @pl.when(peer != mine)
            def _():
                act(mod_copy(peer))

        each(0, members, body)

    @pl.when(core != role)
    def _():
        mod_move.start()

    def spread_mod():
        @pl.when(core == role)
        def _():
            mod_move.wait_recv()
            mod_sum[...] = mod_part[...] + mod_in[...]
            others(lambda copy: copy.start())
            mod_own.start()

    def gathered_mod():
        @pl.when(core == role)
        def _():
            mod_own.wait()
            others(lambda copy: copy.wait_send())

        @pl.when(core != role)
        def _():
            mod_move.wait_send()

        def came(source):
            @pl.when(jnp.logical_not((core == role) & (source == place)))
            def _():
                remote(
                    mod_sum.at[0], mod_all.at[source], mod_send.at[0], mod_recv.at[source],
                    me["sibling"],
                ).wait_recv()

        each(0, length, came)

    def begin(layer):
        @pl.when(core == role)
        def _():
            own(layer).wait()

        @pl.when(core != role)
        def _():
            swap_in(layer).wait_recv()

        onward(layer, 0).start()
        across(layer, 0).start()

    def ring_turn(turn, more, which):
        for layer in which:
            onward(layer, turn - 1).wait_recv()
            if more:
                onward(layer, turn).start()
            across(layer, turn).start()

    def ring_end(which):
        def end(turn):
            for layer in which:
                onward(layer, turn).wait_send()
                across(layer, turn).wait_send()
                from_sibling(layer, turn).wait_recv()

        each(0, length - 1, end)
        for layer in which:
            across(layer, length - 1).wait_send()
            from_sibling(layer, length - 1).wait_recv()

    def front_head(turn, first):
        for layer in head_layers:
            if first:

                @pl.when(core == 0)
                def _():
                    own(layer).wait()

                @pl.when(core == 1)
                def _():
                    cross(layer, turn).wait_recv()

            else:
                cross(layer, turn).wait_recv()
            across(layer, turn).start()

    @pl.when(role == 0)
    def _():
        for layer in layers:
            begin(layer)

        @pl.when(core == 1)
        def _():
            rows_move(cotangent).start()

        front_head(0, True)
        ring_turn(1, True, layers)
        spread_mod()
        late = 2

        def turn_body(turn):
            ring_turn(turn, True, layers)

            @pl.when(turn > late)
            def _():
                front_head(turn - late, False)

        each(2, length - 1, turn_body)
        ring_turn(length - 1, False, layers)
        each(length - 1 - late, length, lambda turn: front_head(turn, False))
        ring_end(layers)
        gathered_mod()

        def head_end(turn):
            for layer in head_layers:
                across(layer, turn).wait_send()
                from_sibling(layer, turn).wait_recv()

        each(0, length, head_end)

        @pl.when(core == 0)
        def _():
            for layer in head_layers:
                lend(layer).wait_send()

    @pl.when(role == 1)
    def _():
        lag = 3

        def cross_start(turn):
            @pl.when((turn > 0) | (core == 1))
            def _():
                for layer in head_layers:
                    cross(layer, turn).start()

        for layer in head_layers:

            @pl.when(core == 1)
            def _():
                own(layer).wait()

            @pl.when(core == 0)
            def _():
                lend(layer).wait_recv()

            onward(layer, 0).start()

        def head_turn(turn):
            for layer in head_layers:
                onward(layer, turn - 1).wait_recv()

                @pl.when(turn < length - 1)
                def _():
                    onward(layer, turn).start()

            @pl.when(turn >= lag)
            def _():
                cross_start(turn - lag)

        each(1, length, head_turn)
        @pl.when(core == 0)
        def _():
            rows_move(tokens).start()

        each(length - lag, length, cross_start)
        spread_mod()
        for layer in shared:
            begin(layer)
        each(1, length - 1, lambda turn: ring_turn(turn, True, shared))
        ring_turn(length - 1, False, shared)
        ring_end(shared)
        gathered_mod()

        def head_end(turn):
            for layer in head_layers:

                @pl.when(turn < length - 1)
                def _():
                    onward(layer, turn).wait_send()

                @pl.when((turn > 0) | (core == 1))
                def _():
                    cross(layer, turn).wait_send()

        each(0, length, head_end)

    fetch = pltpu.make_async_copy(full[0], bias_in, bias_sem)
    fetch.start()
    fetch.wait()
    block_bias[...] = jnp.zeros_like(block_bias)
    channels = tokens.shape[1]
    for shard in range(members):
        block = wide(bias_in[shard])
        line, start = 0, 0
        for part, width in enumerate(widths):
            if part == 4:
                start = 0
            target = block_bias if part < 4 else head_bias
            first = start + shard * width
            if part == 0 and first >= channels:
                first += channels
            for offset in range(0, width, 128):
                size = min(128, width - offset)
                target[:, first + offset : first + offset + size] = block[line : line + 1, :size]
                line += 1
            start += members * width + (channels if part == 0 else 0)

    @pl.when((core == 0) & (role == 1))
    def _():
        swap_out(count - 1).wait_send()

    @pl.when(core != role)
    def _():
        for layer in shared:
            swap_out(layer).wait_send()
        rows_move(tokens).wait()


def gather(shards, head_shards, mod_part, tokens, cotangent, widths, collective_id):
    members = lax.axis_size("dp")
    length, count, heads = members // 2, len(shards), len(head_shards)
    total = count + heads
    everything = list(shards) + list(head_shards)
    moved = sum(shard.size * 2 for shard in everything) * members
    inside = pl.BlockSpec(memory_space=pltpu.VMEM)
    results = pl.pallas_call(
        functools.partial(gather_kernel, length, count, heads, widths),
        name="gather",
        out_shape=[jax.ShapeDtypeStruct((members,) + s.shape, s.dtype) for s in everything]
        + [jax.ShapeDtypeStruct((length,) + mod_part.shape[1:], mod_part.dtype)]
        + [
            jax.ShapeDtypeStruct(tokens.shape, tokens.dtype),
            jax.ShapeDtypeStruct((1, members * sum(widths[:4]) + tokens.shape[1]), jnp.float32),
            jax.ShapeDtypeStruct((1, members * sum(widths[4:])), jnp.float32),
        ],
        in_specs=[inside] * (total + 1) + [ANY] * 2,
        out_specs=[ANY] * (total + 2) + [inside] * 2,
        scratch_shapes=[
            DMA((total,)),
            DMA((total,)),
            DMA((total,)),
            DMA((total, length)),
            DMA((total, length)),
            DMA((total, length)),
            DMA((total, length)),
            DMA((heads, length)),
            DMA((heads, length)),
            DMA((members,)),
            DMA((members,)),
            DMA(()),
            DMA(()),
            DMA(()),
            DMA((2,)),
            pltpu.VMEM(mod_part.shape, mod_part.dtype),
            pltpu.VMEM(mod_part.shape, mod_part.dtype),
            pltpu.VMEM((members,) + shards[0].shape, shards[0].dtype),
            DMA(()),
        ],
        compiler_params=pltpu.CompilerParams(
            collective_id=collective_id, has_side_effects=True, vmem_limit_bytes=VMEM_BYTES
        ),
        cost_estimate=pl.CostEstimate(flops=0, bytes_accessed=16 * moved, transcendentals=0),
    )(*everything, mod_part, tokens, cotangent)
    return (results[:count], results[count:total]) + tuple(results[total:])


def tile_of(columns):
    for tile in (512, 384, 256, 128):
        if columns % tile == 0:
            return tile
    return columns


class Ring:
    def __init__(self, me, length, variants, scratch):
        count = len(variants[0][1])
        self.me, self.length, self.layers = me, length, range(count)
        self.variants = variants
        self.left_all, self.right_all = scratch[:count], scratch[count : 2 * count]
        self.arrived, self.leaving = scratch[2 * count : 3 * count], scratch[3 * count : 4 * count]
        (
            self.own_sem, self.side_send, self.side_recv, self.ring_send, self.ring_recv,
        ) = scratch[4 * count : 4 * count + 5]

    @staticmethod
    def scratch(length, rows, columns, tokens, parts):
        bf16, count = jnp.bfloat16, len(rows)
        return (
            [pltpu.VMEM((2, length, r, tokens), bf16) for r in rows]
            + [pltpu.VMEM((2, tokens, c), bf16) for c in columns]
            + [pltpu.VMEM((length - 1, r, c), bf16) for r, c in zip(rows, columns)]
            + [pltpu.VMEM((2, r, c), bf16) for r, c in zip(rows, columns)]
            + [
                DMA((count, 2 * parts)),
                DMA((count, 2 * parts)),
                DMA((count, 2 * parts)),
                DMA((count, 2)),
                DMA((count, length)),
            ]
        )

    def chunk(self, layer, slot, turn, add):
        spot = self.me["at"](-(turn + 1))
        left, right = self.left_all[layer], self.right_all[layer]
        columns = right.shape[2]
        tile = tile_of(columns)

        def body(index):
            start = pl.multiple_of(index * tile, tile)
            total = product(left[0, spot], right[0, :, pl.ds(start, tile)]) + product(
                left[1, spot], right[1, :, pl.ds(start, tile)]
            )
            if add:
                total = total + wide(self.arrived[layer][turn - 1, :, pl.ds(start, tile)])
            self.leaving[layer][slot, :, pl.ds(start, tile)] = narrow(total)

        each(0, columns // tile, body)

    def onward(self, layer, slot, turn):
        return remote(
            self.leaving[layer].at[slot],
            self.arrived[layer].at[turn],
            self.ring_send.at[layer, slot],
            self.ring_recv.at[layer, turn],
            self.me["onward"],
        )

    def inputs(self, layer, lefts, rights):
        core, sibling = self.me["core"], self.me["sibling"]
        left_all, right_all = self.left_all[layer], self.right_all[layer]
        copies, sem, start = [], 0, 0

        def both(mine, own_to, other, other_to):
            nonlocal sem
            at = (layer, sem)
            sem += 1
            copies.append(pltpu.make_async_copy(mine, own_to, self.own_sem.at[at]))
            copies.append(
                remote(other, other_to, self.side_send.at[at], self.side_recv.at[at], sibling)
            )

        for part in lefts[layer]:
            lanes = pl.ds(start, part.shape[3])
            both(
                part.at[:, core],
                left_all.at[0, :, :, lanes],
                part.at[:, 1 - core],
                left_all.at[1, :, :, lanes],
            )
            start += part.shape[3]
        start = 0
        for part in rights[layer]:
            rows = pl.ds(start, part.shape[0])
            both(part, right_all.at[0, rows], part, right_all.at[1, rows])
            start += part.shape[0]
        return copies

    def fetch(self, layer, act):
        for predicate, lefts, rights in self.variants:

            def body():
                for copy in self.inputs(layer, lefts, rights):
                    act(copy)

            if predicate is None:
                body()
            else:
                pl.when(predicate)(body)

    def run(self, finish, early=None, midway=None, late=None):
        length = self.length
        for layer in self.layers:
            self.fetch(layer, lambda copy: copy.start())
        if early:
            early()
        for layer in self.layers:
            self.fetch(layer, lambda copy: copy.wait())
            self.chunk(layer, 0, 0, False)
            self.onward(layer, 0, 0).start()

        def turn_body(turn):
            slot = lax.rem(turn, 2)
            for layer in self.layers:
                self.onward(layer, slot, turn - 1).wait_recv()

                @pl.when(turn >= 2)
                def _():
                    self.onward(layer, slot, turn).wait_send()

                self.chunk(layer, slot, turn, True)
                self.onward(layer, slot, turn).start()

        first, second = min(3, length - 1), max(min(3, length - 1), length - 2)
        each(1, first, turn_body)
        if midway:
            midway()
        each(first, second, turn_body)
        if late:
            late()
        each(second, length - 1, turn_body)
        slot = (length - 1) % 2
        for layer in self.layers:
            self.onward(layer, slot, length - 2).wait_recv()
            if length >= 3:
                self.onward(layer, slot, length - 2).wait_send()
            self.chunk(layer, slot, length - 1, True)
            finish(layer, slot)
        for layer in self.layers:
            self.onward(layer, 1 - slot, length - 2).wait_send()


def ring_cost(length, rows, columns, tokens):
    work = sum(r * c for r, c in zip(rows, columns)) * length
    return pl.CostEstimate(flops=4 * work * tokens, bytes_accessed=64 * work, transcendentals=0)


def head_reduce_kernel(length, count, *refs):
    lefts, rights, outs = refs[:count], refs[count : 2 * count], refs[2 * count : 3 * count]
    scratch = refs[3 * count :]
    last_sem = scratch[-1]
    me = whereabouts(length)

    @pl.when(me["role"] == 0)
    def _():
        greet([me["onward"], me["before"], me["sibling"]])
        ring = Ring(me, length, [(None, [[v] for v in lefts], [[v] for v in rights])], scratch[:-1])

        def last(layer, slot):
            return pltpu.make_async_copy(
                ring.leaving[layer].at[slot], outs[layer], last_sem.at[layer]
            )

        ring.run(lambda layer, slot: last(layer, slot).start())
        for layer in ring.layers:
            last(layer, (length - 1) % 2).wait()


def head_reduce(lefts, rights, collective_id):
    length, count = lax.axis_size("dp") // 2, len(lefts)
    rows = [left.shape[2] for left in lefts]
    columns = [right.shape[1] for right in rights]
    tokens = rights[0].shape[0]
    return pl.pallas_call(
        functools.partial(head_reduce_kernel, length, count),
        name="head_reduce",
        out_shape=[jax.ShapeDtypeStruct((r, c), jnp.bfloat16) for r, c in zip(rows, columns)],
        in_specs=[ANY] * (2 * count),
        out_specs=[ANY] * count,
        scratch_shapes=Ring.scratch(length, rows, columns, tokens, 1) + [DMA((count,))],
        compiler_params=pltpu.CompilerParams(
            collective_id=collective_id, has_side_effects=True, vmem_limit_bytes=VMEM_BYTES
        ),
        cost_estimate=ring_cost(length, rows, columns, tokens),
    )(*lefts, *rights)


def reduce_kernel(length, form, count, heads, widths, *refs):
    operands = form.num_leaves
    fronts, backs, head_parts, head_sums, mod_weight = jax.tree.unflatten(form, refs[:operands])
    refs = refs[operands:]
    outs, head_outs = refs[:count], refs[count : count + heads]
    stream_out, bias_all, head_all, mod_rows, silu_all = refs[count + heads : count + heads + 5]
    scratch = refs[count + heads + 5 :]
    mod_all, silu_own, silu_keep, silu_send, silu_recv, silu_side = scratch[-6:]
    mod, bias, bias_line = scratch[-9:-6]
    scratch = scratch[:-9]
    (
        last_send, last_recv, part_send, part_recv, stream_send, stream_recv, small_send,
        mod_recv, bias_recv, head_recv, keep_sem,
    ) = scratch[-11:]
    me = whereabouts(length)
    core, role, place = me["core"], me["role"], me["place"]
    members = 2 * length
    index, mine = 2 * place + role, 2 * place + core
    barrier = pltpu.get_barrier_semaphore()

    def greet_all(peer):
        other = (peer // members, lax.rem(peer, members))

        @pl.when((other[0] != core) | (other[1] != index))
        def _():
            pl.semaphore_signal(barrier, inc=1, device_id=other, device_id_type=MESH)

    each(0, 2 * members, greet_all)
    pl.semaphore_wait(barrier, 2 * members - 1)

    unit = fronts[2][0].shape[0]

    def streams(act):
        for there, parts in ((0, fronts[2]), (1, backs[2])):

            @pl.when((role == there) & (core != role))
            def _():
                cuts = [
                    part.at[pl.ds(start, unit)]
                    for part in parts
                    for start in range(0, part.shape[0], unit)
                ]
                for i, cut in enumerate(cuts):
                    act(
                        remote(
                            cut,
                            stream_out.at[pl.ds(i * unit, unit)],
                            stream_send.at[i],
                            stream_recv.at[i],
                            me["partner"],
                        )
                    )

    streams(lambda copy: copy.start())

    def small(source, target, send, recv, device):
        return remote(source, target, send, recv, device)

    def mod_copy(peer):
        return small(
            mod, mod_all.at[mine], small_send.at[0, peer], mod_recv.at[mine], (role, peer)
        )

    def bias_copy(peer):
        return small(
            bias.at[peer], bias_all.at[mine], small_send.at[1, peer], bias_recv.at[mine],
            (role, peer),
        )

    def head_copy(peer):
        return small(
            head_sums.at[peer], head_all.at[mine], small_send.at[2, peer], head_recv.at[mine],
            (peer // members, lax.rem(peer, members)),
        )

    own_mod = pltpu.make_async_copy(mod, mod_all.at[mine], keep_sem.at[0])
    own_bias = pltpu.make_async_copy(bias.at[index], bias_all.at[mine], keep_sem.at[1])
    own_head = pltpu.make_async_copy(
        head_sums.at[core * members + index], head_all.at[mine], keep_sem.at[2]
    )

    def smalls(act_mod, act_head, act_own):
        def to_section(peer):
            @pl.when((core != role) | (peer != index))
            def _():
                act_mod(mod_copy(peer))
                act_mod(bias_copy(peer))

        each(0, members, to_section)

        @pl.when(core == role)
        def _():
            act_own(own_mod)
            act_own(own_bias)

        @pl.when(role == 0)
        def _():
            def to_all(peer):
                @pl.when(peer != core * members + index)
                def _():
                    act_head(head_copy(peer))

            each(0, 2 * members, to_all)
            act_own(own_head)

    def start(copy):
        copy.start()

    def gather_sums(entries):
        lows = [low[i] for low, *_ in entries for i in range(low.shape[0])]
        highs = [high[i] for _, high, *_ in entries for i in range(high.shape[0])]
        channels = lows[0].shape[1]
        for piece in range(6):
            rows = [v[piece : piece + 1] for v in (lows if piece < 2 else highs)]
            mod[:, piece * channels : (piece + 1) * channels] = narrow(jnp.concatenate(rows, 0))

        def total(read):
            return sum(read(entry) for entry in entries)

        wide_pre = entries[0][3].shape[1]
        bias_line[:, 0:channels] = total(lambda e: e[2][0:1, 0:channels])
        bias_line[:, channels : 2 * channels] = total(lambda e: e[2][0:1, 2 * channels :])
        bias_line[:, 2 * channels : 3 * channels] = total(lambda e: e[4][1, 0:1])
        bias_line[:, 3 * channels : 3 * channels + wide_pre] = total(lambda e: e[3][0:1])
        bias_line[:, 3 * channels + wide_pre :] = total(lambda e: e[4][0, 0:1])

    def early():
        @pl.when(role == 0)
        def _():
            gather_sums(fronts[3])

        @pl.when(role == 1)
        def _():
            gather_sums(backs[3])

        for shard in range(members):
            line, start_at = 0, 0
            for width in widths:
                for offset in range(0, width, 128):
                    size = min(128, width - offset)
                    first = start_at + shard * width + offset
                    bias[shard, line : line + 1, 0:size] = bias_line[:, first : first + size]
                    line += 1
                start_at += members * width
        smalls(start, start, start)

    def part(layer, half):
        rows = head_outs[layer].shape[0]
        return head_parts[layer].at[pl.ds(half * rows, rows)]

    def kept(layer):
        return pltpu.make_async_copy(part(layer, 0), head_outs[layer], part_send.at[layer, 0])

    def handed(layer, half, device):
        return remote(
            part(layer, half), head_outs[layer], part_send.at[layer, half], part_recv.at[layer],
            device,
        )

    @pl.when((role == 0) & (core == 0))
    def _():
        for layer in range(heads):
            kept(layer).start()
            handed(layer, 1, me["sibling"]).start()

    @pl.when((role == 0) & (core == 1))
    def _():
        for layer in range(heads):
            handed(layer, 0, (0, 2 * place + 1)).start()
            handed(layer, 1, (1, 2 * place + 1)).start()

    variants = [(role == 0,) + tuple(fronts[:2]), (role == 1,) + tuple(backs[:2])]
    ring = Ring(me, length, variants, scratch[:-11])

    def local_last(layer, slot):
        return pltpu.make_async_copy(ring.leaving[layer].at[slot], outs[layer], last_send.at[layer])

    def remote_last(layer, slot):
        return remote(
            ring.leaving[layer].at[slot], outs[layer], last_send.at[layer], last_recv.at[layer],
            me["partner"],
        )

    def finish(layer, slot):
        @pl.when(core == role)
        def _():
            local_last(layer, slot).start()

        @pl.when(core != role)
        def _():
            remote_last(layer, slot).start()

    def silu_copy(peer):
        return remote(
            silu_own, silu_all.at[core, index], silu_send.at[peer], silu_recv.at[index],
            (core, peer),
        )

    silu_kept = pltpu.make_async_copy(silu_own, silu_all.at[core, index], silu_keep)

    def others(act):
        def body(peer):
            @pl.when(peer != index)
            def _():
                act(peer)

        each(0, members, body)

    def midway():
        def mod_came(source):
            @pl.when((core != role) | (source != mine))
            def _():
                small(
                    mod, mod_all.at[source], small_send.at[0, 0], mod_recv.at[source],
                    me["sibling"],
                ).wait_recv()

        each(0, members, mod_came)

        @pl.when(core == role)
        def _():
            own_mod.wait()

        images, depth = mod.shape[0], mod_weight.shape[0]
        for source in range(members):
            mod_rows[source * images : (source + 1) * images, :] = wide(mod_all[source])
        silu_own[...] = jnp.zeros_like(silu_own)
        silu_own[:, 0:depth] = product_right_t(narrow(mod_rows[...]), mod_weight[...])
        silu_kept.start()
        others(lambda peer: silu_copy(peer).start())

    across = remote(
        silu_all.at[core], silu_all.at[core], silu_side.at[0], silu_side.at[1], me["sibling"]
    )

    def late():
        others(
            lambda peer: remote(
                silu_own, silu_all.at[core, peer], silu_send.at[peer], silu_recv.at[peer],
                (core, peer),
            ).wait_recv()
        )
        silu_kept.wait()
        across.start()

    ring.run(finish, early, midway, late)
    others(lambda peer: silu_copy(peer).wait_send())
    across.wait_send()
    remote(
        silu_all.at[1 - core], silu_all.at[1 - core], silu_side.at[0], silu_side.at[1],
        me["sibling"],
    ).wait_recv()

    @pl.when((role == 0) & (core == 0))
    def _():
        for layer in range(heads):
            kept(layer).wait()
            handed(layer, 1, me["sibling"]).wait_send()

    @pl.when((role == 0) & (core == 1))
    def _():
        for layer in range(heads):
            handed(layer, 0, (0, 2 * place + 1)).wait_send()
            handed(layer, 1, (1, 2 * place + 1)).wait_send()

    @pl.when((role == 1) | (core == 1))
    def _():
        for layer in range(heads):
            handed(layer, 0, me["sibling"]).wait_recv()

    streams(lambda copy: copy.wait())
    smalls(
        lambda copy: copy.wait_send(),
        lambda copy: copy.wait_send(),
        lambda copy: None if copy is own_mod else copy.wait(),
    )

    def came(source):
        @pl.when((core != role) | (source != mine))
        def _():
            small(
                bias.at[0], bias_all.at[source], small_send.at[1, 0], bias_recv.at[source],
                me["sibling"],
            ).wait_recv()

        @pl.when((role != 0) | (source != mine))
        def _():
            small(
                head_sums.at[0], head_all.at[source], small_send.at[2, 0], head_recv.at[source],
                me["sibling"],
            ).wait_recv()

    each(0, members, came)
    slot = (length - 1) % 2
    for layer in ring.layers:

        @pl.when(core == role)
        def _():
            local_last(layer, slot).wait()

        @pl.when(core != role)
        def _():
            remote_last(layer, slot).wait()


def reduce(fronts, backs, head_parts, head_sums, mod_weight, widths, collective_id):
    members = lax.axis_size("dp")
    lefts, rights, streams, image_sums = fronts
    length, count, heads = members // 2, len(lefts), len(head_parts)
    rows = [left[0].shape[2] for left in lefts]
    columns = [right[0].shape[1] for right in rights]
    parts = len(rights[0])
    tokens = parts * rights[0][0].shape[0]
    bf16 = jnp.bfloat16
    inside = pl.BlockSpec(memory_space=pltpu.VMEM)
    stream_shape = (tokens, streams[0].shape[1])
    operands, form = jax.tree.flatten((fronts, backs, head_parts, head_sums, mod_weight))

    def side_specs(side):
        return jax.tree.map(lambda _: ANY, side[:3]) + (jax.tree.map(lambda _: inside, side[3]),)

    specs = side_specs(fronts) + side_specs(backs)
    specs = jax.tree.leaves(specs, is_leaf=lambda leaf: isinstance(leaf, pl.BlockSpec))
    images = sum(sums_of[0].shape[0] for sums_of in image_sums)
    mod_shape = (images, 6 * image_sums[0][0].shape[2])
    bias_shape = (members, 8, 128)
    f32 = jnp.float32
    lines = members * images
    results = pl.pallas_call(
        functools.partial(reduce_kernel, length, form, count, heads, widths),
        name="reduce",
        out_shape=[jax.ShapeDtypeStruct((r, c), bf16) for r, c in zip(rows, columns)]
        + [jax.ShapeDtypeStruct((h.shape[0] // 2, h.shape[1]), bf16) for h in head_parts]
        + [jax.ShapeDtypeStruct(stream_shape, bf16)]
        + [
            jax.ShapeDtypeStruct(bias_shape, f32),
            jax.ShapeDtypeStruct((members,) + head_sums.shape[1:], f32),
        ]
        + [
            jax.ShapeDtypeStruct((lines, mod_shape[1]), f32),
            jax.ShapeDtypeStruct((2, members, lines, 128), f32),
        ],
        in_specs=specs + [inside] * (heads + 2),
        out_specs=[ANY] * (count + heads + 3) + [inside, ANY],
        scratch_shapes=Ring.scratch(length, rows, columns, tokens, parts)
        + [
            DMA((count,)),
            DMA((count,)),
            DMA((heads, 2)),
            DMA((heads,)),
            DMA((parts,)),
            DMA((parts,)),
            DMA((3, 2 * members)),
            DMA((members,)),
            DMA((members,)),
            DMA((members,)),
            DMA((3,)),
            pltpu.VMEM(mod_shape, bf16),
            pltpu.VMEM(bias_shape, f32),
            pltpu.VMEM((1, members * sum(widths)), f32),
            pltpu.VMEM((members,) + mod_shape, bf16),
            pltpu.VMEM((lines, 128), f32),
            DMA(()),
            DMA((members,)),
            DMA((members,)),
            DMA((2,)),
        ],
        compiler_params=pltpu.CompilerParams(
            collective_id=collective_id, has_side_effects=True, vmem_limit_bytes=VMEM_BYTES
        ),
        cost_estimate=ring_cost(length, rows, columns, tokens),
    )(*operands)
    return (results[:count], results[count : count + heads]) + tuple(results[count + heads :])


def local_grad(function, primal, cotangent_in):
    return jax.vjp(function, primal)[1](cotangent_in)[0]


def column_sums(values):
    return jnp.sum(wide(values), 0)


def normed_of(values):
    center = values - jnp.mean(values, -1, keepdims=True)
    inverse = lax.rsqrt(jnp.mean(center * center, -1, keepdims=True) + EPSILON)
    return center * inverse, inverse


def lane_window(head, head_size):
    start = head * head_size
    base = start // 128 * 128
    width = -(-(start + head_size - base) // 128) * 128
    return base, width, start - base


def head_only(block, inside, head_size):
    lanes = lax.broadcasted_iota(jnp.int32, block.shape, 1)
    keep = (lanes >= inside) & (lanes < inside + head_size)
    return jnp.where(keep, block, jnp.zeros_like(block))


def lay_shards(left, values):
    rows = left.shape[2]
    turned = values.T
    for shard in range(values.shape[1] // rows):
        left[shard // 2, shard % 2] = turned[shard * rows : (shard + 1) * rows]


def attend_kernel(
    head_count, hidden, pieces, pack_w, pack_b, out_w, out_b,
    input_left, packed_out, probs_out, mixed_left, attn_out, after_out, mixed_acc,
):
    channels = hidden.shape[1]
    head_size = channels // head_count
    scaling = head_size ** (-0.5)
    residual = wide(hidden[...])
    normed, _ = normed_of(residual)
    attn_input = narrow(normed * (1.0 + pieces[0, 1:2]) + pieces[0, 0:1])
    lay_shards(input_left, attn_input)
    packed_out[...] = narrow(product(attn_input, pack_w[...]) + pack_b[...])
    mixed_acc[...] = jnp.zeros_like(mixed_acc)
    for head in range(head_count):
        base, width, inside = lane_window(head, head_size)
        queries = packed_out[:, base : base + width]
        keys = head_only(packed_out[:, channels + base : channels + base + width], inside, head_size)
        values = head_only(
            packed_out[:, 2 * channels + base : 2 * channels + base + width], inside, head_size
        )
        scores = product_right_t(queries, keys) * scaling
        exponent = jnp.exp(scores - jnp.max(scores, -1, keepdims=True))
        probs = narrow(exponent * (1.0 / jnp.sum(exponent, -1, keepdims=True)))
        probs_out[0, head] = probs
        mixed_acc[:, base : base + width] += product(probs, values)
    mixed = narrow(mixed_acc[...])
    lay_shards(mixed_left, mixed)
    out = product(mixed, out_w[...]) + out_b[...]
    attn_out[...] = narrow(out)
    after_out[...] = residual + pieces[0, 2:3] * out


def rows_spec(seq_len, columns):
    return pl.BlockSpec((seq_len, columns), lambda i: (i, 0))


def block_at(shape, index):
    return pl.BlockSpec(shape, lambda i: index, pipeline_mode=pl.Buffered(1))


def fixed_spec(shape):
    return block_at(shape, (0,) * len(shape))


def image_rows(array, image):
    if image is None:
        return fixed_spec(array.shape)
    return block_at((SEQ, array.shape[1]), (image if array.shape[0] > SEQ else 0, 0))


def image_steps(array, image):
    base = 0 if image is None or array.shape[0] <= SEQ else image
    return pl.BlockSpec((SEQ, array.shape[1]), lambda i: (base + i, 0))


def attend(hidden, pieces, pack_w, out_w, bias, members, image):
    tokens, channels = hidden.shape
    left = (members // 2, 2, channels // members)
    images, seq = tokens // SEQ, SEQ
    lowest = image or 0
    bf16, f32 = jnp.bfloat16, jnp.float32
    work = tokens * channels * (4 * channels + 2 * seq)
    return pl.pallas_call(
        functools.partial(attend_kernel, HEADS),
        grid=(images,),
        name="attend",
        in_specs=[
            rows_spec(seq, channels),
            pl.BlockSpec((1,) + pieces.shape[1:], lambda i: (lowest + i, 0, 0)),
            fixed_spec(pack_w.shape),
            block_at((1, 3 * channels), (0, 0)),
            fixed_spec(out_w.shape),
            block_at((1, channels), (0, 3)),
        ],
        out_specs=[
            pl.BlockSpec(left + (seq,), lambda i: (0, 0, 0, i)),
            rows_spec(seq, 3 * channels),
            pl.BlockSpec((1, HEADS, seq, seq), lambda i: (i, 0, 0, 0)),
            pl.BlockSpec(left + (seq,), lambda i: (0, 0, 0, i)),
            rows_spec(seq, channels),
            rows_spec(seq, channels),
        ],
        out_shape=[
            jax.ShapeDtypeStruct(left + (tokens,), bf16),
            jax.ShapeDtypeStruct((tokens, 3 * channels), bf16),
            jax.ShapeDtypeStruct((images, HEADS, seq, seq), bf16),
            jax.ShapeDtypeStruct(left + (tokens,), bf16),
            jax.ShapeDtypeStruct((tokens, channels), bf16),
            jax.ShapeDtypeStruct((tokens, channels), f32),
        ],
        scratch_shapes=[pltpu.VMEM((seq, channels), f32)],
        compiler_params=pltpu.CompilerParams(vmem_limit_bytes=VMEM_BYTES),
        cost_estimate=pl.CostEstimate(
            flops=2 * work, bytes_accessed=40 * 2**20, transcendentals=0
        ),
    )(hidden, pieces, pack_w, bias, out_w, bias)


def per_image(values, images):
    return values.reshape(images, values.shape[0] // images, values.shape[1])


GELU_A, GELU_B = 0.7978845608028654, 0.044715


def mlp_kernel(
    after, pieces, up_w, up_b, down_w, down_b,
    input_left, act_left, slope_out, mlp_out, final_out, input_keep, total,
):
    step, steps = pl.program_id(0), pl.num_programs(0)
    images = pieces.shape[0]

    @pl.when(step == 0)
    def _():
        normed, _ = normed_of(per_image(after[...], images))
        rows = narrow(normed * (1.0 + pieces[:, 4:5]) + pieces[:, 3:4]).reshape(after.shape)
        input_keep[...] = rows
        lay_shards(input_left, rows)
        total[...] = jnp.zeros_like(total)

    pre = product(input_keep[...], up_w[...]) + up_b[...]
    square = pre * pre
    tanh = jnp.tanh(GELU_A * pre * (1.0 + GELU_B * square))
    half = 0.5 + 0.5 * tanh
    act = narrow(pre * half)
    lay_shards(act_left, act)
    slope_out[...] = narrow(
        half + pre * (0.5 - 0.5 * tanh * tanh) * (GELU_A + (3.0 * GELU_A * GELU_B) * square)
    )
    total[...] += product(act, down_w[...])

    @pl.when(step == steps - 1)
    def _():
        out = total[...] + down_b[...]
        mlp_out[...] = narrow(out)
        final = per_image(after[...], images) + pieces[:, 5:6] * per_image(out, images)
        final_out[...] = narrow(final * pieces[:, 6:7]).reshape(after.shape)


def feed_tile(width):
    return 1152 if width % 1152 == 0 else width


def mlp(after, pieces, up_w, down_w, bias, members, image):
    tokens, channels = after.shape
    width = up_w.shape[1]
    tile = feed_tile(width)
    bf16, f32 = jnp.bfloat16, jnp.float32
    columns = pl.BlockSpec((tokens, tile), lambda i: (0, i))
    left = (members // 2, 2, channels // members, tokens)
    rows = width // members
    act_block = (tile // (2 * rows), 2, rows, tokens)
    return pl.pallas_call(
        mlp_kernel,
        grid=(width // tile,),
        name="mlp",
        in_specs=[
            fixed_spec(after.shape),
            block_at((tokens // SEQ,) + pieces.shape[1:], (image or 0, 0, 0)),
            pl.BlockSpec((channels, tile), lambda i: (0, i)),
            pl.BlockSpec((1, tile), lambda i: (0, 4 * channels // tile + i)),
            pl.BlockSpec((tile, channels), lambda i: (i, 0)),
            block_at((1, channels), (0, 4 + width // channels)),
        ],
        out_specs=[
            fixed_spec(left),
            pl.BlockSpec(act_block, lambda i: (i, 0, 0, 0)),
            columns,
            fixed_spec((tokens, channels)),
            fixed_spec((tokens, channels)),
        ],
        out_shape=[
            jax.ShapeDtypeStruct(left, bf16),
            jax.ShapeDtypeStruct((members // 2, 2, rows, tokens), bf16),
            jax.ShapeDtypeStruct((tokens, width), bf16),
            jax.ShapeDtypeStruct((tokens, channels), bf16),
            jax.ShapeDtypeStruct((tokens, channels), bf16),
        ],
        scratch_shapes=[pltpu.VMEM((tokens, channels), bf16), pltpu.VMEM((tokens, channels), f32)],
        compiler_params=pltpu.CompilerParams(vmem_limit_bytes=VMEM_BYTES),
        cost_estimate=pl.CostEstimate(
            flops=4 * tokens * channels * width, bytes_accessed=40 * 2**20, transcendentals=0
        ),
    )(after, pieces, up_w, bias, down_w, bias)


def sum_rows(values):
    return product(jnp.ones((8, values.shape[0]), jnp.bfloat16), values)


def layer_norm_back(grad_in, normed, inverse):
    return inverse * (
        grad_in
        - jnp.mean(grad_in, -1, keepdims=True)
        - normed * jnp.mean(grad_in * normed, -1, keepdims=True)
    )


def added_grad(grad, extra, pieces):
    return per_image(wide(grad[...]) + extra[...], pieces.shape[0])


def scaled_grad(grad, extra, pieces):
    return per_image(wide(grad[...]), pieces.shape[0]) * pieces[:, 6:7]


def mlp_back_kernel(
    given_grad, grad, extra, after, pieces, slope, mlp_out, attn_out, up_w, down_w,
    grad_mlp_out, grad_pre_out, grad_after_out, grad_attn_out, sums_out, pre_sums, out_sums,
    total,
):
    step, steps = pl.program_id(0), pl.num_programs(0)
    images = pieces.shape[0]

    @pl.when(step == 0)
    def _():
        given = given_grad(grad, extra, pieces)
        rows = narrow(pieces[:, 5:6] * given).reshape(grad.shape)
        grad_mlp_out[...] = rows
        sums_out[:, 5] = jnp.sum(given * per_image(wide(mlp_out[...]), images), 1)
        out_sums[0] = sum_rows(rows)
        total[...] = jnp.zeros_like(total)

    grad_pre = narrow(wide(slope[...]) * product_right_t(grad_mlp_out[...], down_w[...]))
    grad_pre_out[...] = grad_pre
    pre_sums[...] = sum_rows(grad_pre)
    total[...] += product_right_t(grad_pre, up_w[...])

    @pl.when(step == steps - 1)
    def _():
        normed, inverse = normed_of(per_image(after[...], images))
        grad_min = per_image(total[...], images)
        sums_out[:, 3] = jnp.sum(grad_min, 1)
        sums_out[:, 4] = jnp.sum(grad_min * normed, 1)
        grad_after = given_grad(grad, extra, pieces) + layer_norm_back(
            grad_min * (1.0 + pieces[:, 4:5]), normed, inverse
        )
        grad_after_out[...] = grad_after.reshape(grad.shape)
        rows = narrow(pieces[:, 2:3] * grad_after).reshape(grad.shape)
        grad_attn_out[...] = rows
        sums_out[:, 2] = jnp.sum(grad_after * per_image(wide(attn_out[...]), images), 1)
        out_sums[1] = sum_rows(rows)


def mlp_back(given_grad, grad, extra, after, pieces, slope, mlp_out, attn_out, up_w, down_w, image):
    tokens = after.shape[0] if image is None else SEQ
    images, channels, width = tokens // SEQ, after.shape[1], up_w.shape[1]
    tile = feed_tile(width)
    bf16, f32 = jnp.bfloat16, jnp.float32
    columns = pl.BlockSpec((tokens, tile), lambda i: (0, i))
    slope_row = image if image and slope.shape[0] > SEQ else 0
    rows = fixed_spec((tokens, channels))
    return pl.pallas_call(
        functools.partial(mlp_back_kernel, given_grad),
        grid=(width // tile,),
        name="mlp_back",
        in_specs=[
            image_rows(grad, image),
            image_rows(extra, image),
            image_rows(after, image),
            block_at((images,) + pieces.shape[1:], (image or 0, 0, 0)),
            pl.BlockSpec((tokens, tile), lambda i: (slope_row, i)),
            image_rows(mlp_out, image),
            image_rows(attn_out, image),
            pl.BlockSpec((channels, tile), lambda i: (0, i)),
            pl.BlockSpec((tile, channels), lambda i: (i, 0)),
        ],
        out_specs=[
            rows,
            columns,
            rows,
            rows,
            fixed_spec((images, 8, channels)),
            pl.BlockSpec((8, tile), lambda i: (0, i)),
            fixed_spec((2, 8, channels)),
        ],
        out_shape=[
            jax.ShapeDtypeStruct((tokens, channels), bf16),
            jax.ShapeDtypeStruct((tokens, width), bf16),
            jax.ShapeDtypeStruct((tokens, channels), f32),
            jax.ShapeDtypeStruct((tokens, channels), bf16),
            jax.ShapeDtypeStruct((images, 8, channels), f32),
            jax.ShapeDtypeStruct((8, width), f32),
            jax.ShapeDtypeStruct((2, 8, channels), f32),
        ],
        scratch_shapes=[pltpu.VMEM((tokens, channels), f32)],
        compiler_params=pltpu.CompilerParams(vmem_limit_bytes=VMEM_BYTES),
        cost_estimate=pl.CostEstimate(
            flops=4 * tokens * channels * width, bytes_accessed=40 * 2**20, transcendentals=0
        ),
    )(grad, extra, after, pieces, slope, mlp_out, attn_out, up_w, down_w)


def attend_back_kernel(
    head_count, hidden, pieces, packed, probs_in, grad_attn, grad_after, pack_w, out_w,
    grad_packed_out, grad_hidden_out, sums_out, pack_sums, acc, grad_mixed_keep,
):
    channels = hidden.shape[1]
    head_size = channels // head_count
    scaling = head_size ** (-0.5)
    grad_mixed_keep[...] = narrow(product_right_t(grad_attn[...], out_w[...]))
    acc[...] = jnp.zeros_like(acc)
    for head in range(head_count):
        base, width, inside = lane_window(head, head_size)
        q_at, k_at, v_at = (slice(j * channels + base, j * channels + base + width) for j in range(3))
        queries = head_only(packed[:, q_at], inside, head_size)
        keys = head_only(packed[:, k_at], inside, head_size)
        grad_mixed = head_only(grad_mixed_keep[:, q_at], inside, head_size)
        probs = probs_in[0, head]
        grad_probs = product_right_t(grad_mixed, packed[:, v_at])
        probs_wide = wide(probs)
        weighted = probs_wide * grad_probs
        grad_scores = narrow(weighted - probs_wide * jnp.sum(weighted, -1, keepdims=True))
        acc[:, v_at] += product_left_t(probs, grad_mixed)
        acc[:, q_at] += product(grad_scores, keys) * scaling
        acc[:, k_at] += product_left_t(grad_scores, queries) * scaling
    grad_packed = narrow(acc[...])
    grad_packed_out[...] = grad_packed
    column_totals = sum_rows(grad_packed)

    @pl.when(pl.program_id(0) == 0)
    def _():
        pack_sums[...] = column_totals

    @pl.when(pl.program_id(0) > 0)
    def _():
        pack_sums[...] += column_totals

    grad_ain = product_right_t(grad_packed, pack_w[...])
    normed, inverse = normed_of(wide(hidden[...]))
    sums_out[0, 0:1] = jnp.sum(grad_ain, 0, keepdims=True)
    sums_out[0, 1:2] = jnp.sum(grad_ain * normed, 0, keepdims=True)
    grad_hidden_out[...] = narrow(
        grad_after[...] + layer_norm_back(grad_ain * (1.0 + pieces[0, 1:2]), normed, inverse)
    )


def attend_back(hidden, pieces, packed, probs, grad_attn, grad_after, pack_w, out_w, image):
    tokens = hidden.shape[0] if image is None else SEQ
    images, channels, seq = tokens // SEQ, hidden.shape[1], SEQ
    lowest = image or 0
    probs_at = lowest if probs.shape[0] > 1 else 0
    bf16, f32 = jnp.bfloat16, jnp.float32
    work = tokens * channels * (4 * channels + 5 * seq)
    return pl.pallas_call(
        functools.partial(attend_back_kernel, HEADS),
        grid=(images,),
        name="attend_back",
        in_specs=[
            image_steps(hidden, image),
            pl.BlockSpec((1,) + pieces.shape[1:], lambda i: (lowest + i, 0, 0)),
            image_steps(packed, image),
            pl.BlockSpec((1, HEADS, seq, seq), lambda i: (probs_at + i, 0, 0, 0)),
            image_steps(grad_attn, image),
            image_steps(grad_after, image),
            fixed_spec(pack_w.shape),
            fixed_spec(out_w.shape),
        ],
        out_specs=[
            rows_spec(seq, 3 * channels),
            rows_spec(seq, channels),
            pl.BlockSpec((1, 8, channels), lambda i: (i, 0, 0)),
            fixed_spec((8, 3 * channels)),
        ],
        out_shape=[
            jax.ShapeDtypeStruct((tokens, 3 * channels), bf16),
            jax.ShapeDtypeStruct((tokens, channels), bf16),
            jax.ShapeDtypeStruct((images, 8, channels), f32),
            jax.ShapeDtypeStruct((8, 3 * channels), f32),
        ],
        scratch_shapes=[
            pltpu.VMEM((seq, 3 * channels), f32),
            pltpu.VMEM((seq, channels), bf16),
        ],
        compiler_params=pltpu.CompilerParams(vmem_limit_bytes=VMEM_BYTES),
        cost_estimate=pl.CostEstimate(
            flops=2 * work, bytes_accessed=40 * 2**20, transcendentals=0
        ),
    )(hidden, pieces, packed, probs, grad_attn, grad_after, pack_w, out_w)


def block_forward(hidden, pieces, weights, members, image=None):
    pack_w, out_w, up_w, down_w, bias = weights
    input_left, packed, probs, mixed_left, attn_out, after = attend(
        hidden, pieces, pack_w, out_w, bias, members, image
    )
    rows_left, act_left, slope, mlp_out, final = mlp(
        after, pieces, up_w, down_w, bias, members, image
    )
    return (
        final,
        (packed, probs, attn_out, after, slope, mlp_out),
        (act_left, rows_left, input_left, mixed_left),
    )


def block_backward(hidden, saved_state, pieces, weights, given_grad, grad, extra, image):
    pack_w, out_w, up_w, down_w, _ = weights
    packed, probs, attn_out, after, slope, mlp_out = saved_state
    grad_mlp, grad_pre, grad_after, grad_attn, high_sums, pre_sums, out_sums = mlp_back(
        given_grad, grad, extra, after, pieces, slope, mlp_out, attn_out, up_w, down_w, image
    )
    grad_packed, grad_hidden, low_sums, pack_sums = attend_back(
        hidden, pieces, packed, probs, grad_attn, grad_after, pack_w, out_w, image
    )
    rights = (grad_mlp, grad_pre, grad_packed, grad_attn)
    return grad_hidden, rights, (low_sums, high_sums, pack_sums, pre_sums, out_sums)


def silu_parts(values):
    gate = 0.5 + 0.5 * jnp.tanh(0.5 * values)
    return values * gate, gate * (1.0 + values * (1.0 - gate))


def head_kernel(
    members, hidden_at, target_at, live, in_w_at, in_b, mid_w_at, mid_b, out_w_at, out_b,
    grad_hidden_at, last_left_at, mid_left_at, in_left_at, grad_feature_at, grad_second_at,
    device_rows,
    hidden, target, in_w, mid_w, out_w,
    grad_hidden_out, last_left, mid_left, in_left, grad_feature_out, grad_second_out,
    act_first, slope_first, act_second, slope_second, grad_first_keep, in_sums, mid_sums,
    come_sem, go_sem,
):
    width = in_w.shape[1]
    tile = 512 if width % 512 == 0 else width
    tiles = [slice(start, start + tile) for start in range(0, width, tile)]
    rows = width // (2 * members)
    pairs_in = ((hidden_at, hidden), (in_w_at, in_w), (mid_w_at, mid_w), (out_w_at, out_w), (target_at, target))
    come = [
        pltpu.make_async_copy(there, here, come_sem.at[i]) for i, (there, here) in enumerate(pairs_in)
    ]
    pairs_out = (
        (grad_hidden_out, grad_hidden_at),
        (last_left, last_left_at),
        (mid_left, mid_left_at),
        (in_left, in_left_at),
        (grad_feature_out, grad_feature_at),
        (grad_second_out, grad_second_at),
    )
    go = [
        pltpu.make_async_copy(here, there, go_sem.at[i]) for i, (here, there) in enumerate(pairs_out)
    ]

    def lay(left, values, start):
        turned = values.T
        for offset in range(0, values.shape[1], rows):
            shard = (start + offset) // rows
            half, index = shard // members, shard % members
            left[index // 2, index % 2, half * rows : (half + 1) * rows] = turned[
                offset : offset + rows
            ]

    @pl.when(lax.rem(lax.axis_index("dp"), 2) == 0)
    def _():
        for copy in come:
            copy.start()
        come[0].wait()
        come[1].wait()
        for at in tiles:
            act, slope = silu_parts(product(hidden[...], in_w[:, at]) + in_b[:, at])
            act_first[:, at] = narrow(act)
            slope_first[:, at] = narrow(slope)
        come[2].wait()
        for at in tiles:
            act, slope = silu_parts(product(act_first[...], mid_w[:, at]) + mid_b[:, at])
            act_second[:, at] = narrow(act)
            slope_second[:, at] = narrow(slope)
            lay(mid_left, act_first[:, at], at.start)
        go[2].start()
        come[3].wait()
        come[4].wait()
        feature = product(act_second[...], out_w[...]) + out_b[...]
        inverse = lax.rsqrt(jnp.sum(feature * feature, -1, keepdims=True) + EPSILON)
        unit = feature * inverse
        aim = wide(target[...])
        aim = aim * lax.rsqrt(jnp.sum(aim * aim, -1, keepdims=True) + EPSILON)
        alive = live[:, 0:1]
        cosine = jnp.sum(unit * aim, -1, keepdims=True)
        loss = 0.5 * jnp.sum(alive * (1.0 - cosine), axis=(0, 1), keepdims=True)
        grad_unit = (-0.5 * alive) * aim
        grad_feature = narrow(
            inverse * (grad_unit - unit * jnp.sum(grad_unit * unit, -1, keepdims=True))
        )
        grad_feature_out[...] = grad_feature
        go[4].start()
        out_sums = sum_rows(grad_feature)
        for at in tiles:
            grad_second = narrow(
                wide(slope_second[:, at]) * product_right_t(grad_feature, out_w[at, :])
            )
            grad_second_out[:, at] = grad_second
            mid_sums[:, at] = sum_rows(grad_second)
            lay(last_left, act_second[:, at], at.start)
        go[1].start()
        go[5].start()
        for at in tiles:
            grad_first = narrow(
                wide(slope_first[:, at]) * product_right_t(grad_second_out[...], mid_w[at, :])
            )
            grad_first_keep[:, at] = grad_first
            in_sums[:, at] = sum_rows(grad_first)
            part = product_right_t(grad_first, in_w[:, at])
            if at.start == 0:
                grad_hidden_out[...] = part
            else:
                grad_hidden_out[...] += part
            lay(in_left, grad_first_keep[:, at], at.start)
        go[0].start()
        go[3].start()
        share, devices = width // (2 * members), 2 * members
        device_rows[...] = jnp.zeros_like(device_rows)
        for device in range(devices):
            lanes = slice(device * share, (device + 1) * share)
            device_rows[device, 0:1, 0:share] = in_sums[0:1, lanes]
            device_rows[device, 0:1, share : 2 * share] = mid_sums[0:1, lanes]
        count = out_sums.shape[1] // 128
        for line in range(count):
            device_rows[:, 1 + line, :] = jnp.broadcast_to(
                out_sums[0:1, line * 128 : (line + 1) * 128], (devices, 128)
            )
        device_rows[:, 1 + count, :] = jnp.broadcast_to(loss, (devices, 128))
        for copy in go:
            copy.wait()


def head_pass(hidden, target, live, head_weights, members):
    tokens, channels = hidden.shape
    width, features = head_weights[2].shape[0], target.shape[1]
    bf16, f32 = jnp.bfloat16, jnp.float32
    left = ((members // 2, 2, width // members, tokens), bf16)
    live_lanes = jnp.broadcast_to(live[:, None], (tokens, 128))
    in_w, in_b, mid_w, mid_b, out_w, out_b = head_weights
    inside = pl.BlockSpec(memory_space=pltpu.VMEM)
    work = tokens * (channels * width + width * width + width * features)
    big = [
        ((tokens, channels), f32),
        left,
        left,
        left,
        ((tokens, features), bf16),
        ((tokens, width), bf16),
    ]
    small = [((2 * members, 2 + features // 128, 128), f32)]
    results = pl.pallas_call(
        functools.partial(head_kernel, members),
        name="head",
        in_specs=[ANY, ANY, inside, ANY, inside, ANY, inside, ANY, inside],
        out_specs=[ANY] * 6 + [inside],
        out_shape=[jax.ShapeDtypeStruct(*leaf) for leaf in big + small],
        scratch_shapes=[
            pltpu.VMEM(array.shape, array.dtype) for array in (hidden, target, in_w, mid_w, out_w)
        ]
        + [pltpu.VMEM(*leaf) for leaf in big]
        + [pltpu.VMEM((tokens, width), bf16)] * 5
        + [pltpu.VMEM((8, width), f32)] * 2
        + [DMA((5,)), DMA((6,))],
        compiler_params=pltpu.CompilerParams(vmem_limit_bytes=VMEM_BYTES),
        cost_estimate=pl.CostEstimate(
            flops=4 * work, bytes_accessed=40 * 2**20, transcendentals=0
        ),
    )(hidden, target, live_lanes, in_w, in_b[None], mid_w, mid_b[None], out_w, out_b[None])
    grad_hidden, last_left, mid_left, in_left, grad_feature, grad_second, device_rows = results
    return (
        grad_hidden,
        (last_left, mid_left, in_left),
        (grad_feature, grad_second),
        device_rows,
    )


def trade_kernel(members, given, taken, send_sem, recv_sem):
    core, index = lax.axis_index("section"), lax.axis_index("dp")
    barrier = pltpu.get_barrier_semaphore()

    def others(act):
        def body(peer):
            @pl.when(peer != index)
            def _():
                act(peer)

        each(0, members, body)

    def copy(peer):
        return remote(given, taken.at[index], send_sem.at[peer], recv_sem.at[index], (core, peer))

    others(
        lambda peer: pl.semaphore_signal(
            barrier, inc=1, device_id=(core, peer), device_id_type=MESH
        )
    )
    pl.semaphore_wait(barrier, members - 1)
    others(lambda peer: copy(peer).start())
    taken[index] = given[...]
    others(
        lambda peer: remote(
            given, taken.at[peer], send_sem.at[peer], recv_sem.at[peer], (core, peer)
        ).wait_recv()
    )
    others(lambda peer: copy(peer).wait_send())


def trade(block, collective_id):
    members = lax.axis_size("dp")
    inside = pl.BlockSpec(memory_space=pltpu.VMEM)
    return pl.pallas_call(
        functools.partial(trade_kernel, members),
        name="trade",
        out_shape=jax.ShapeDtypeStruct((members,) + block.shape, block.dtype),
        in_specs=[inside],
        out_specs=inside,
        scratch_shapes=[DMA((members,)), DMA((members,))],
        compiler_params=pltpu.CompilerParams(collective_id=collective_id, has_side_effects=True),
    )(block)


def hollow(shapes):
    leaves, form = jax.tree.flatten(shapes)
    results = pl.pallas_call(
        lambda *refs: None,
        name="hollow",
        out_shape=[jax.ShapeDtypeStruct(leaf.shape, leaf.dtype) for leaf in leaves],
        out_specs=[ANY if leaf.ndim else pl.BlockSpec(memory_space=pltpu.SMEM) for leaf in leaves],
    )()
    return jax.tree.unflatten(form, list(results))


def on_device(
    tokens_in,
    cotangent,
    targets,
    buckets,
    counts,
    time_table,
    modulate_weight,
    modulate_bias,
    qkv_weight,
    qv_bias,
    attn_weight,
    attn_bias,
    up_weight,
    up_bias,
    down_weight,
    down_bias,
    project_in_weight,
    project_in_bias,
    project_mid_weight,
    project_mid_bias,
    project_out_weight,
    project_out_bias,
):
    members = lax.axis_size("dp")
    core = lax.axis_index("section")
    index = lax.axis_index("dp")
    place, role = index // 2, index % 2
    is_first = role == 0
    own = 2 * place + core
    channels = tokens_in.shape[1]
    images = tokens_in.shape[0] // SEQ
    pairs_up, pairs_back, pairs_swap = [], [], []
    for pair in range(members // 2):
        low, high = 2 * pair, 2 * pair + 1
        pairs_swap += [(high, members + low)]
        pairs_up += [(low, high), (members + low, members + high)]
        pairs_back += [(high, low), (members + high, members + low)]
    axes = ("section", "dp")

    bucket_block = jnp.broadcast_to(jnp.pad(buckets, (0, 128 - images))[None], (8, 128))
    all_buckets = trade(bucket_block, 1)[:, 0, :images].reshape(-1)
    one_hot = (
        all_buckets[:, None] == jnp.arange(time_table.shape[0], dtype=jnp.int32)[None, :]
    ).astype(jnp.float32)
    conditioning = jnp.dot(one_hot, time_table, precision=HIGHEST)
    silu_all = narrow(jax.nn.silu(conditioning))
    depth = modulate_weight.shape[1]
    silu_depth = lax.dynamic_slice_in_dim(silu_all, index * depth, depth, 1)
    mod_part = product(silu_depth, modulate_weight[0])
    share = modulate_bias.shape[1]
    bias_row = lax.dynamic_update_slice_in_dim(
        jnp.zeros((mod_part.shape[1],), jnp.float32), wide(modulate_bias[0]), index * share, 0
    )
    mod_part = (mod_part + bias_row[None]).reshape(members, images, 6 * channels)

    section_biases = (qv_bias[0], attn_bias[0], up_bias[0], down_bias[0])
    biases = section_biases + (project_in_bias, project_mid_bias, project_out_bias)
    widths = [part.shape[0] for part in biases]
    lines = [
        jnp.pad(part, (0, -part.shape[0] % 128)).reshape(-1, 128) for part in biases
    ]
    bias_block = jnp.concatenate(lines)
    bias_block = jnp.pad(bias_block, ((0, -bias_block.shape[0] % 16), (0, 0)))
    block_full, head_full, mod_all, rows_in, block_bias, head_bias = gather(
        (
            bias_block,
            qkv_weight[0],
            attn_weight[0],
            up_weight[0],
            down_weight[0],
            project_out_weight,
        ),
        (project_in_weight, project_mid_weight),
        mod_part,
        tokens_in,
        cotangent,
        widths,
        0,
    )
    _, pack_weight, out_weight, first_weight, second_weight, head_last = block_full
    head_ends = [members * width for width in widths[4:]]
    head_bias = [
        head_bias[0, sum(head_ends[:i]) : sum(head_ends[: i + 1])] for i in range(len(head_ends))
    ]

    def whole(values):
        return values.reshape(-1, values.shape[-1])

    block_weights = (
        whole(pack_weight),
        whole(out_weight),
        whole(first_weight),
        whole(second_weight),
        block_bias,
    )
    head_weights = (
        whole(head_full[0]),
        head_bias[0],
        whole(head_full[1]),
        head_bias[1],
        whole(head_last),
        head_bias[2],
    )
    pieces = jnp.sum(mod_all, 0).reshape(images, 6, channels)

    own_counts = counts[own]
    image_live = (jnp.arange(images, dtype=jnp.int32) < own_counts).astype(jnp.float32)
    token_live = jnp.repeat(image_live, SEQ)
    out_scale = jnp.where(is_first, 1.0, image_live)
    scale_rows = jnp.broadcast_to(out_scale[:, None, None], (images, 2, channels))
    pieces = jnp.concatenate([pieces, scale_rows], 1)
    total_live = wide(jnp.sum(counts)) * SEQ
    crossed = core != role
    targets_out, rows_in = lax.optimization_barrier((targets, rows_in))
    hidden_first = jnp.where(crossed, rows_in, tokens_in)
    own_targets = jnp.where(crossed, lax.ppermute(targets_out, axes, pairs_swap), targets)

    def unused(function, *operands_in):
        return hollow(jax.eval_shape(function, *operands_in))

    def forward(hidden, mod, block):
        return block_forward(hidden, mod, block, members)

    first_out, saved_state, first_lefts = lax.cond(
        is_first,
        forward,
        lambda *operands_in: unused(forward, *operands_in),
        hidden_first,
        pieces,
        block_weights,
    )
    hidden_second = lax.ppermute(first_out, axes, pairs_up)

    rows_late, _ = lax.optimization_barrier((rows_in, first_out))
    outer = lax.optimization_barrier(jnp.where(crossed, rows_late, cotangent))
    head_result = head_pass(first_out, own_targets, token_live, head_weights, members)
    hidden_second, head_result = lax.optimization_barrier((hidden_second, head_result))
    grad_hidden, head_lefts, head_rights, head_rows = head_result

    def do_second(rows, mod, grad, block):
        final, state, lefts = block_forward(rows, mod, block, members)
        grad_rows, rights, sums_of = block_backward(
            rows, state, mod, block, scaled_grad, grad, grad, None
        )
        cut = tuple(grad_rows[i * SEQ : (i + 1) * SEQ] for i in range(images))
        return cut, final, rights, sums_of, lefts

    second = lax.cond(
        is_first,
        lambda *operands_in: unused(do_second, *operands_in),
        do_second,
        hidden_second,
        pieces,
        outer,
        block_weights,
    )
    grad_rows = second[0]
    returning = [lax.ppermute(grad_rows[0], axes, pairs_back)]
    head_lefts, head_rights, kept = lax.optimization_barrier((head_lefts, head_rights, second[1]))
    second = (second[0], kept) + second[2:]
    head_parts = head_reduce(head_lefts, head_rights + (first_out,), 2)
    returning[0], head_parts, grad_rows = lax.optimization_barrier(
        (returning[0], head_parts, grad_rows)
    )
    for i in range(1, images):
        returning.append(lax.ppermute(grad_rows[i], axes, pairs_back))
    first = []
    for i in range(images):

        def do_first(rows, state, mod, extra, grad, block, i=i):
            return block_backward(rows, state, mod, block, added_grad, grad, extra, i)

        if i:
            returning[i], gone = lax.optimization_barrier((returning[i], first[i - 1][0]))
            first[i - 1] = (gone,) + first[i - 1][1:]
        first.append(
            lax.cond(
                is_first,
                do_first,
                lambda *operands_in: unused(do_first, *operands_in),
                hidden_first,
                saved_state,
                pieces,
                grad_hidden,
                returning[i],
                block_weights,
            )
        )
    def by_layer(results):
        return [list(parts_of) for parts_of in zip(*results)]

    fronts = (
        [[left] for left in first_lefts],
        by_layer([result[1] for result in first]),
        [result[0] for result in first],
        [result[2] for result in first],
    )
    backs = (
        [[left] for left in second[4]],
        [[right] for right in second[2]],
        [second[1]],
        [second[3]],
    )
    block_grads, head_grads, stream_in, bias_all, head_all, mod_wide, silu_all_terms = reduce(
        fronts,
        backs,
        head_parts,
        head_rows,
        modulate_weight[0],
        widths[:4],
        3,
    )
    down_grad, up_grad, qkv_grad, attn_grad = block_grads
    stream = jnp.where(is_first, jnp.concatenate(fronts[2]), jnp.concatenate(backs[2]))
    stream_own = jnp.where(crossed, stream_in, stream)
    mod_w_grad = product_left_t(silu_depth, narrow(mod_wide))
    mod_b_grad = lax.dynamic_slice_in_dim(jnp.sum(mod_wide, 0), index * share, share, 0)
    silu_total = jnp.sum(silu_all_terms[:, :, :, :depth], 0)
    silu_total = jnp.swapaxes(silu_total, 0, 1).reshape(-1, channels)
    cond_grad = local_grad(jax.nn.silu, conditioning, silu_total)
    table_grad = jnp.dot(one_hot.T, cond_grad, precision=HIGHEST)

    bias_sums = jnp.sum(bias_all, 0)
    bias_outs, line = [], 0
    for width in widths[:4]:
        count = -(-width // 128)
        bias_outs.append(bias_sums[line : line + count].reshape(1, -1)[:, :width])
        line += count
    sums = jnp.sum(head_all, 0)
    head_share = head_grads[1].shape[0]
    loss_value = sums[-1, 0] / total_live
    return (
        stream_own[None],
        loss_value,
        table_grad,
        mod_w_grad[None],
        mod_b_grad[None],
        wide(qkv_grad)[None],
        bias_outs[0],
        wide(attn_grad)[None],
        bias_outs[1],
        wide(up_grad)[None],
        bias_outs[2],
        wide(down_grad)[None],
        bias_outs[3],
        wide(head_grads[2]).T,
        sums[0, :head_share],
        wide(head_grads[1]),
        sums[0, head_share : 2 * head_share],
        wide(head_grads[0]),
        sums[1:-1].reshape(-1),
    )


def solution(mesh):
    in_specs = (
        P("dp", None),
        P("dp", None),
        P("dp", None),
        P("dp"),
        P(),
        P(),
        P("section", "dp", None),
        P("section", "dp"),
        P("section", "dp", None),
        P("section", "dp"),
        P("section", "dp", None),
        P("section", "dp"),
        P("section", "dp", None),
        P("section", "dp"),
        P("section", "dp", None),
        P("section", "dp"),
        P("dp", None),
        P("dp"),
        P("dp", None),
        P("dp"),
        P("dp", None),
        P("dp"),
    )
    out_specs = (
        P("section", "dp", None),
        P(),
        P(),
        P("section", "dp", None),
        P("section", "dp"),
        P("section", "dp", None),
        P("section", "dp"),
        P("section", "dp", None),
        P("section", "dp"),
        P("section", "dp", None),
        P("section", "dp"),
        P("section", "dp", None),
        P("section", "dp"),
        P(None, ("section", "dp")),
        P(("section", "dp")),
        P(("section", "dp"), None),
        P(("section", "dp")),
        P(("section", "dp"), None),
        P(),
    )
    return jax.shard_map(
        on_device, mesh=mesh, in_specs=in_specs, out_specs=out_specs, check_vma=False
    )
```

```python
import functools
import jax
import jax.numpy as jnp
from jax import lax
from jax.experimental import pallas as pl
from jax.experimental.pallas import tpu as pltpu
from jax.sharding import PartitionSpec as P

HEADS = 16
SEQ = 256
EPSILON = 1e-06
HIGHEST = lax.Precision.HIGHEST
MESH = pl.DeviceIdType.MESH
ANY = pl.BlockSpec(memory_space=pl.ANY)
DMA = pltpu.SemaphoreType.DMA
VMEM_BYTES = 60 * 2**20


def narrow(values):
    return values.astype(jnp.bfloat16)


def wide(values):
    return values.astype(jnp.float32)


def product(left_side, right_side):
    return jnp.dot(left_side, right_side, preferred_element_type=jnp.float32)


def product_left_t(left_side, right_side):
    return lax.dot_general(
        left_side, right_side, (((0,), (0,)), ((), ())), preferred_element_type=jnp.float32
    )


def product_right_t(left_side, right_side):
    return lax.dot_general(
        left_side, right_side, (((1,), (1,)), ((), ())), preferred_element_type=jnp.float32
    )


def ring_of(place, length):
    half, side = place // 2, place % 2
    return side * (length - 1 - half) + (1 - side) * half


def place_of(spot, length):
    side = spot // (length // 2)
    half = side * (length - 1 - spot) + (1 - side) * spot
    return 2 * half + side


def whereabouts(length):
    core = lax.axis_index("section")
    index = lax.axis_index("dp")
    place, role = index // 2, index % 2
    spot = ring_of(place, length)
    step = 1 - 2 * core

    def at(offset):
        return place_of(lax.rem(spot + step * offset + 4 * length, length), length)

    return dict(
        core=core,
        place=place,
        role=role,
        at=at,
        onward=(core, 2 * at(1) + role),
        before=(core, 2 * at(-1) + role),
        sibling=(1 - core, index),
        partner=(1 - core, 2 * place + 1 - role),
    )


def greet(devices):
    barrier = pltpu.get_barrier_semaphore()
    for device in devices:
        pl.semaphore_signal(barrier, inc=1, device_id=device, device_id_type=MESH)
    pl.semaphore_wait(barrier, len(devices))


def remote(source, target, send_sem, recv_sem, device):
    return pltpu.make_async_remote_copy(
        src_ref=source,
        dst_ref=target,
        send_sem=send_sem,
        recv_sem=recv_sem,
        device_id=device,
        device_id_type=MESH,
    )


def each(first, last, body):
    def step(index, carry):
        body(index)
        return carry

    lax.fori_loop(first, last, step, 0)


def gather_kernel(length, count, heads, widths, *refs):
    total = count + heads
    shards, (mod_part, tokens, cotangent) = refs[:total], refs[total : total + 3]
    refs = refs[total + 3 :]
    full, (mod_all, rows_in, block_bias, head_bias) = refs[:total], refs[total : total + 4]
    (
        own_sem, swap_send, swap_recv, ring_send, ring_recv, side_send, side_recv,
        cross_send, cross_recv, mod_send, mod_recv, mod_sem, rows_send, rows_recv, mod_pair, mod_in,
        mod_sum,
        bias_in, bias_sem,
    ) = refs[total + 4 :]
    me = whereabouts(length)
    core, role, place, at = me["core"], me["role"], me["place"], me["at"]
    members = 2 * length
    index = 2 * place + role
    neighbour = (core, 2 * place + 1 - role)
    mine = 2 * place + core
    layers, shared, head_layers = range(count), range(count - 1), range(count, total)

    barrier = pltpu.get_barrier_semaphore()

    def signal(device):
        pl.semaphore_signal(barrier, inc=1, device_id=device, device_id_type=MESH)

    def greet_all(peer):
        other = (peer // members, lax.rem(peer, members))

        @pl.when((other[0] != core) | (other[1] != index))
        def _():
            signal(other)

    each(0, 2 * members, greet_all)
    pl.semaphore_wait(barrier, 2 * members - 1)

    def block(layer, turn):
        return full[layer].at[2 * at(-turn) + core]

    def onward(layer, turn):
        part = block(layer, turn)
        return remote(
            part, part, ring_send.at[layer, turn], ring_recv.at[layer, turn], me["onward"]
        )

    def across(layer, turn):
        part = block(layer, turn)
        return remote(
            part, part, side_send.at[layer, turn], side_recv.at[layer, turn], me["sibling"]
        )

    def from_sibling(layer, turn):
        part = full[layer].at[2 * at(turn) + 1 - core]
        return remote(
            part, part, side_send.at[layer, turn], side_recv.at[layer, turn], me["sibling"]
        )

    def own(layer):
        return pltpu.make_async_copy(shards[layer], full[layer].at[mine], own_sem.at[layer])

    def swap_out(layer):
        return remote(
            shards[layer], full[layer].at[index], swap_send.at[layer], swap_recv.at[layer],
            me["partner"],
        )

    def swap_in(layer):
        return remote(
            shards[layer], full[layer].at[mine], swap_send.at[layer], swap_recv.at[layer],
            me["partner"],
        )

    def lend(layer):
        return remote(
            shards[layer], full[layer].at[2 * place], swap_send.at[layer], swap_recv.at[layer],
            neighbour,
        )

    def cross(layer, turn):
        part = block(layer, turn)
        return remote(
            part, part, cross_send.at[layer - count, turn], cross_recv.at[layer - count, turn],
            neighbour,
        )

    @pl.when(core == role)
    def _():
        for layer in shared:
            own(layer).start()

    @pl.when((core == 0) & (role == 0))
    def _():
        own(count - 1).start()

    def rows_move(source):
        return remote(source, rows_in, rows_send, rows_recv, me["partner"])

    @pl.when(core != role)
    def _():
        for layer in shared:
            swap_out(layer).start()

    @pl.when((core == 0) & (role == 1))
    def _():
        swap_out(count - 1).start()

    @pl.when(core == role)
    def _():
        for layer in head_layers:
            own(layer).start()

    @pl.when((core == 0) & (role == 0))
    def _():
        for layer in head_layers:
            lend(layer).start()

    mod_move = remote(mod_part, mod_in, mod_pair.at[0], mod_pair.at[1], neighbour)

    def mod_copy(peer):
        return remote(
            mod_sum.at[peer], mod_all.at[place], mod_send.at[peer], mod_recv.at[place],
            (lax.rem(peer, 2), 2 * (peer // 2) + core),
        )

    mod_own = pltpu.make_async_copy(mod_sum.at[mine], mod_all.at[place], mod_sem)

    def others(act):
        def body(peer):
            @pl.when(peer != mine)
            def _():
                act(mod_copy(peer))

        each(0, members, body)

    @pl.when(core != role)
    def _():
        mod_move.start()

    def spread_mod():
        @pl.when(core == role)
        def _():
            mod_move.wait_recv()
            mod_sum[...] = mod_part[...] + mod_in[...]
            others(lambda copy: copy.start())
            mod_own.start()

    def gathered_mod():
        @pl.when(core == role)
        def _():
            mod_own.wait()
            others(lambda copy: copy.wait_send())

        @pl.when(core != role)
        def _():
            mod_move.wait_send()

        def came(source):
            @pl.when(jnp.logical_not((core == role) & (source == place)))
            def _():
                remote(
                    mod_sum.at[0], mod_all.at[source], mod_send.at[0], mod_recv.at[source],
                    me["sibling"],
                ).wait_recv()

        each(0, length, came)

    def begin(layer):
        @pl.when(core == role)
        def _():
            own(layer).wait()

        @pl.when(core != role)
        def _():
            swap_in(layer).wait_recv()

        onward(layer, 0).start()
        across(layer, 0).start()

    def ring_turn(turn, more, which):
        for layer in which:
            onward(layer, turn - 1).wait_recv()
            if more:
                onward(layer, turn).start()
            across(layer, turn).start()

    def ring_end(which):
        def end(turn):
            for layer in which:
                onward(layer, turn).wait_send()
                across(layer, turn).wait_send()
                from_sibling(layer, turn).wait_recv()

        each(0, length - 1, end)
        for layer in which:
            across(layer, length - 1).wait_send()
            from_sibling(layer, length - 1).wait_recv()

    def front_head(turn, first):
        for layer in head_layers:
            if first:

                @pl.when(core == 0)
                def _():
                    own(layer).wait()

                @pl.when(core == 1)
                def _():
                    cross(layer, turn).wait_recv()

            else:
                cross(layer, turn).wait_recv()
            across(layer, turn).start()

    @pl.when(role == 0)
    def _():
        for layer in layers:
            begin(layer)

        @pl.when(core == 1)
        def _():
            rows_move(cotangent).start()

        front_head(0, True)
        ring_turn(1, True, layers)
        spread_mod()
        late = 2

        def turn_body(turn):
            ring_turn(turn, True, layers)

            @pl.when(turn > late)
            def _():
                front_head(turn - late, False)

        each(2, length - 1, turn_body)
        ring_turn(length - 1, False, layers)
        each(length - 1 - late, length, lambda turn: front_head(turn, False))
        ring_end(layers)
        gathered_mod()

        def head_end(turn):
            for layer in head_layers:
                across(layer, turn).wait_send()
                from_sibling(layer, turn).wait_recv()

        each(0, length, head_end)

        @pl.when(core == 0)
        def _():
            for layer in head_layers:
                lend(layer).wait_send()

    @pl.when(role == 1)
    def _():
        lag = 3

        def cross_start(turn):
            @pl.when((turn > 0) | (core == 1))
            def _():
                for layer in head_layers:
                    cross(layer, turn).start()

        for layer in head_layers:

            @pl.when(core == 1)
            def _():
                own(layer).wait()

            @pl.when(core == 0)
            def _():
                lend(layer).wait_recv()

            onward(layer, 0).start()

        def head_turn(turn):
            for layer in head_layers:
                onward(layer, turn - 1).wait_recv()

                @pl.when(turn < length - 1)
                def _():
                    onward(layer, turn).start()

            @pl.when(turn >= lag)
            def _():
                cross_start(turn - lag)

        each(1, length, head_turn)
        @pl.when(core == 0)
        def _():
            rows_move(tokens).start()

        each(length - lag, length, cross_start)
        spread_mod()
        for layer in shared:
            begin(layer)
        each(1, length - 1, lambda turn: ring_turn(turn, True, shared))
        ring_turn(length - 1, False, shared)
        ring_end(shared)
        gathered_mod()

        def head_end(turn):
            for layer in head_layers:

                @pl.when(turn < length - 1)
                def _():
                    onward(layer, turn).wait_send()

                @pl.when((turn > 0) | (core == 1))
                def _():
                    cross(layer, turn).wait_send()

        each(0, length, head_end)

    fetch = pltpu.make_async_copy(full[0], bias_in, bias_sem)
    fetch.start()
    fetch.wait()
    block_bias[...] = jnp.zeros_like(block_bias)
    channels = tokens.shape[1]
    for shard in range(members):
        block = wide(bias_in[shard])
        line, start = 0, 0
        for part, width in enumerate(widths):
            if part == 4:
                start = 0
            target = block_bias if part < 4 else head_bias
            first = start + shard * width
            if part == 0 and first >= channels:
                first += channels
            for offset in range(0, width, 128):
                size = min(128, width - offset)
                target[:, first + offset : first + offset + size] = block[line : line + 1, :size]
                line += 1
            start += members * width + (channels if part == 0 else 0)

    @pl.when((core == 0) & (role == 1))
    def _():
        swap_out(count - 1).wait_send()

    @pl.when(core != role)
    def _():
        for layer in shared:
            swap_out(layer).wait_send()
        rows_move(tokens).wait()


def gather(shards, head_shards, mod_part, tokens, cotangent, widths, collective_id):
    members = lax.axis_size("dp")
    length, count, heads = members // 2, len(shards), len(head_shards)
    total = count + heads
    everything = list(shards) + list(head_shards)
    moved = sum(shard.size * 2 for shard in everything) * members
    inside = pl.BlockSpec(memory_space=pltpu.VMEM)
    results = pl.pallas_call(
        functools.partial(gather_kernel, length, count, heads, widths),
        name="gather",
        out_shape=[jax.ShapeDtypeStruct((members,) + s.shape, s.dtype) for s in everything]
        + [jax.ShapeDtypeStruct((length,) + mod_part.shape[1:], mod_part.dtype)]
        + [
            jax.ShapeDtypeStruct(tokens.shape, tokens.dtype),
            jax.ShapeDtypeStruct((1, members * sum(widths[:4]) + tokens.shape[1]), jnp.float32),
            jax.ShapeDtypeStruct((1, members * sum(widths[4:])), jnp.float32),
        ],
        in_specs=[inside] * (total + 1) + [ANY] * 2,
        out_specs=[ANY] * (total + 2) + [inside] * 2,
        scratch_shapes=[
            DMA((total,)),
            DMA((total,)),
            DMA((total,)),
            DMA((total, length)),
            DMA((total, length)),
            DMA((total, length)),
            DMA((total, length)),
            DMA((heads, length)),
            DMA((heads, length)),
            DMA((members,)),
            DMA((members,)),
            DMA(()),
            DMA(()),
            DMA(()),
            DMA((2,)),
            pltpu.VMEM(mod_part.shape, mod_part.dtype),
            pltpu.VMEM(mod_part.shape, mod_part.dtype),
            pltpu.VMEM((members,) + shards[0].shape, shards[0].dtype),
            DMA(()),
        ],
        compiler_params=pltpu.CompilerParams(
            collective_id=collective_id, has_side_effects=True, vmem_limit_bytes=VMEM_BYTES
        ),
        cost_estimate=pl.CostEstimate(flops=0, bytes_accessed=16 * moved, transcendentals=0),
    )(*everything, mod_part, tokens, cotangent)
    return (results[:count], results[count:total]) + tuple(results[total:])


def tile_of(columns):
    for tile in (512, 384, 256, 128):
        if columns % tile == 0:
            return tile
    return columns


class Ring:
    def __init__(self, me, length, variants, scratch):
        count = len(variants[0][1])
        self.me, self.length, self.layers = me, length, range(count)
        self.variants = variants
        self.left_all, self.right_all = scratch[:count], scratch[count : 2 * count]
        self.arrived, self.leaving = scratch[2 * count : 3 * count], scratch[3 * count : 4 * count]
        (
            self.own_sem, self.side_send, self.side_recv, self.ring_send, self.ring_recv,
        ) = scratch[4 * count : 4 * count + 5]

    @staticmethod
    def scratch(length, rows, columns, tokens, parts):
        bf16, count = jnp.bfloat16, len(rows)
        return (
            [pltpu.VMEM((2, length, r, tokens), bf16) for r in rows]
            + [pltpu.VMEM((2, tokens, c), bf16) for c in columns]
            + [pltpu.VMEM((length - 1, r, c), bf16) for r, c in zip(rows, columns)]
            + [pltpu.VMEM((2, r, c), bf16) for r, c in zip(rows, columns)]
            + [
                DMA((count, 2 * parts)),
                DMA((count, 2 * parts)),
                DMA((count, 2 * parts)),
                DMA((count, 2)),
                DMA((count, length)),
            ]
        )

    def chunk(self, layer, slot, turn, add):
        spot = self.me["at"](-(turn + 1))
        left, right = self.left_all[layer], self.right_all[layer]
        columns = right.shape[2]
        tile = tile_of(columns)

        def body(index):
            start = pl.multiple_of(index * tile, tile)
            total = product(left[0, spot], right[0, :, pl.ds(start, tile)]) + product(
                left[1, spot], right[1, :, pl.ds(start, tile)]
            )
            if add:
                total = total + wide(self.arrived[layer][turn - 1, :, pl.ds(start, tile)])
            self.leaving[layer][slot, :, pl.ds(start, tile)] = narrow(total)

        each(0, columns // tile, body)

    def onward(self, layer, slot, turn):
        return remote(
            self.leaving[layer].at[slot],
            self.arrived[layer].at[turn],
            self.ring_send.at[layer, slot],
            self.ring_recv.at[layer, turn],
            self.me["onward"],
        )

    def inputs(self, layer, lefts, rights):
        core, sibling = self.me["core"], self.me["sibling"]
        left_all, right_all = self.left_all[layer], self.right_all[layer]
        copies, sem, start = [], 0, 0

        def both(mine, own_to, other, other_to):
            nonlocal sem
            at = (layer, sem)
            sem += 1
            copies.append(pltpu.make_async_copy(mine, own_to, self.own_sem.at[at]))
            copies.append(
                remote(other, other_to, self.side_send.at[at], self.side_recv.at[at], sibling)
            )

        for part in lefts[layer]:
            lanes = pl.ds(start, part.shape[3])
            both(
                part.at[:, core],
                left_all.at[0, :, :, lanes],
                part.at[:, 1 - core],
                left_all.at[1, :, :, lanes],
            )
            start += part.shape[3]
        start = 0
        for part in rights[layer]:
            rows = pl.ds(start, part.shape[0])
            both(part, right_all.at[0, rows], part, right_all.at[1, rows])
            start += part.shape[0]
        return copies

    def fetch(self, layer, act):
        for predicate, lefts, rights in self.variants:

            def body():
                for copy in self.inputs(layer, lefts, rights):
                    act(copy)

            if predicate is None:
                body()
            else:
                pl.when(predicate)(body)

    def run(self, finish, early=None, midway=None, late=None):
        length = self.length
        ahead = 2
        for layer in self.layers[:ahead]:
            self.fetch(layer, lambda copy: copy.start())
        if early:
            early()
        for layer in self.layers:
            self.fetch(layer, lambda copy: copy.wait())
            for later in self.layers[layer + ahead : layer + ahead + 1]:
                self.fetch(later, lambda copy: copy.start())
            self.chunk(layer, 0, 0, False)
            self.onward(layer, 0, 0).start()

        def turn_body(turn):
            slot = lax.rem(turn, 2)
            for layer in self.layers:
                self.onward(layer, slot, turn - 1).wait_recv()

                @pl.when(turn >= 2)
                def _():
                    self.onward(layer, slot, turn).wait_send()

                self.chunk(layer, slot, turn, True)
                self.onward(layer, slot, turn).start()

        first, second = min(3, length - 1), max(min(3, length - 1), length - 2)
        each(1, first, turn_body)
        if midway:
            midway()
        each(first, second, turn_body)
        if late:
            late()
        each(second, length - 1, turn_body)
        slot = (length - 1) % 2
        for layer in self.layers:
            self.onward(layer, slot, length - 2).wait_recv()
            if length >= 3:
                self.onward(layer, slot, length - 2).wait_send()
            self.chunk(layer, slot, length - 1, True)
            finish(layer, slot)
        for layer in self.layers:
            self.onward(layer, 1 - slot, length - 2).wait_send()


def ring_cost(length, rows, columns, tokens):
    work = sum(r * c for r, c in zip(rows, columns)) * length
    return pl.CostEstimate(flops=4 * work * tokens, bytes_accessed=64 * work, transcendentals=0)


def head_reduce_kernel(length, count, *refs):
    lefts, rights, outs = refs[:count], refs[count : 2 * count], refs[2 * count : 3 * count]
    scratch = refs[3 * count :]
    last_sem = scratch[-1]
    me = whereabouts(length)

    @pl.when(me["role"] == 0)
    def _():
        greet([me["onward"], me["before"], me["sibling"]])
        ring = Ring(me, length, [(None, [[v] for v in lefts], [[v] for v in rights])], scratch[:-1])

        def last(layer, slot):
            return pltpu.make_async_copy(
                ring.leaving[layer].at[slot], outs[layer], last_sem.at[layer]
            )

        ring.run(lambda layer, slot: last(layer, slot).start())
        for layer in ring.layers:
            last(layer, (length - 1) % 2).wait()


def head_reduce(lefts, rights, collective_id):
    length, count = lax.axis_size("dp") // 2, len(lefts)
    rows = [left.shape[2] for left in lefts]
    columns = [right.shape[1] for right in rights]
    tokens = rights[0].shape[0]
    return pl.pallas_call(
        functools.partial(head_reduce_kernel, length, count),
        name="head_reduce",
        out_shape=[jax.ShapeDtypeStruct((r, c), jnp.bfloat16) for r, c in zip(rows, columns)],
        in_specs=[ANY] * (2 * count),
        out_specs=[ANY] * count,
        scratch_shapes=Ring.scratch(length, rows, columns, tokens, 1) + [DMA((count,))],
        compiler_params=pltpu.CompilerParams(
            collective_id=collective_id, has_side_effects=True, vmem_limit_bytes=VMEM_BYTES
        ),
        cost_estimate=ring_cost(length, rows, columns, tokens),
    )(*lefts, *rights)


def reduce_kernel(length, form, count, heads, widths, *refs):
    operands = form.num_leaves
    fronts, backs, head_parts, head_sums, mod_weight = jax.tree.unflatten(form, refs[:operands])
    refs = refs[operands:]
    outs, head_outs = refs[:count], refs[count : count + heads]
    stream_out, bias_all, head_all, mod_rows, silu_all = refs[count + heads : count + heads + 5]
    scratch = refs[count + heads + 5 :]
    mod_all, silu_own, silu_keep, silu_send, silu_recv, silu_side = scratch[-6:]
    mod, bias, bias_line = scratch[-9:-6]
    scratch = scratch[:-9]
    (
        last_send, last_recv, part_send, part_recv, stream_send, stream_recv, small_send,
        mod_recv, bias_recv, head_recv, keep_sem,
    ) = scratch[-11:]
    me = whereabouts(length)
    core, role, place = me["core"], me["role"], me["place"]
    members = 2 * length
    index, mine = 2 * place + role, 2 * place + core
    barrier = pltpu.get_barrier_semaphore()

    def greet_all(peer):
        other = (peer // members, lax.rem(peer, members))

        @pl.when((other[0] != core) | (other[1] != index))
        def _():
            pl.semaphore_signal(barrier, inc=1, device_id=other, device_id_type=MESH)

    each(0, 2 * members, greet_all)
    pl.semaphore_wait(barrier, 2 * members - 1)

    unit = fronts[2][0].shape[0]

    def streams(act):
        for there, parts in ((0, fronts[2]), (1, backs[2])):

            @pl.when((role == there) & (core != role))
            def _():
                cuts = [
                    part.at[pl.ds(start, unit)]
                    for part in parts
                    for start in range(0, part.shape[0], unit)
                ]
                for i, cut in enumerate(cuts):
                    act(
                        remote(
                            cut,
                            stream_out.at[pl.ds(i * unit, unit)],
                            stream_send.at[i],
                            stream_recv.at[i],
                            me["partner"],
                        )
                    )

    streams(lambda copy: copy.start())

    def small(source, target, send, recv, device):
        return remote(source, target, send, recv, device)

    def mod_copy(peer):
        return small(
            mod, mod_all.at[mine], small_send.at[0, peer], mod_recv.at[mine], (role, peer)
        )

    def bias_copy(peer):
        return small(
            bias.at[peer], bias_all.at[mine], small_send.at[1, peer], bias_recv.at[mine],
            (role, peer),
        )

    def head_copy(peer):
        return small(
            head_sums.at[peer], head_all.at[mine], small_send.at[2, peer], head_recv.at[mine],
            (peer // members, lax.rem(peer, members)),
        )

    own_mod = pltpu.make_async_copy(mod, mod_all.at[mine], keep_sem.at[0])
    own_bias = pltpu.make_async_copy(bias.at[index], bias_all.at[mine], keep_sem.at[1])
    own_head = pltpu.make_async_copy(
        head_sums.at[core * members + index], head_all.at[mine], keep_sem.at[2]
    )

    def smalls(act_mod, act_head, act_own):
        def to_section(peer):
            @pl.when((core != role) | (peer != index))
            def _():
                act_mod(mod_copy(peer))
                act_mod(bias_copy(peer))

        each(0, members, to_section)

        @pl.when(core == role)
        def _():
            act_own(own_mod)
            act_own(own_bias)

        @pl.when(role == 0)
        def _():
            def to_all(peer):
                @pl.when(peer != core * members + index)
                def _():
                    act_head(head_copy(peer))

            each(0, 2 * members, to_all)
            act_own(own_head)

    def start(copy):
        copy.start()

    def gather_sums(entries):
        lows = [low[i] for low, *_ in entries for i in range(low.shape[0])]
        highs = [high[i] for _, high, *_ in entries for i in range(high.shape[0])]
        channels = lows[0].shape[1]
        for piece in range(6):
            rows = [v[piece : piece + 1] for v in (lows if piece < 2 else highs)]
            mod[:, piece * channels : (piece + 1) * channels] = narrow(jnp.concatenate(rows, 0))

        def total(read):
            return sum(read(entry) for entry in entries)

        wide_pre = entries[0][3].shape[1]
        bias_line[:, 0:channels] = total(lambda e: e[2][0:1, 0:channels])
        bias_line[:, channels : 2 * channels] = total(lambda e: e[2][0:1, 2 * channels :])
        bias_line[:, 2 * channels : 3 * channels] = total(lambda e: e[4][1, 0:1])
        bias_line[:, 3 * channels : 3 * channels + wide_pre] = total(lambda e: e[3][0:1])
        bias_line[:, 3 * channels + wide_pre :] = total(lambda e: e[4][0, 0:1])

    def early():
        @pl.when(role == 0)
        def _():
            gather_sums(fronts[3])

        @pl.when(role == 1)
        def _():
            gather_sums(backs[3])

        for shard in range(members):
            line, start_at = 0, 0
            for width in widths:
                for offset in range(0, width, 128):
                    size = min(128, width - offset)
                    first = start_at + shard * width + offset
                    bias[shard, line : line + 1, 0:size] = bias_line[:, first : first + size]
                    line += 1
                start_at += members * width
        smalls(start, start, start)

    def part(layer, half):
        rows = head_outs[layer].shape[0]
        return head_parts[layer].at[pl.ds(half * rows, rows)]

    def kept(layer):
        return pltpu.make_async_copy(part(layer, 0), head_outs[layer], part_send.at[layer, 0])

    def handed(layer, half, device):
        return remote(
            part(layer, half), head_outs[layer], part_send.at[layer, half], part_recv.at[layer],
            device,
        )

    @pl.when((role == 0) & (core == 0))
    def _():
        for layer in range(heads):
            kept(layer).start()
            handed(layer, 1, me["sibling"]).start()

    @pl.when((role == 0) & (core == 1))
    def _():
        for layer in range(heads):
            handed(layer, 0, (0, 2 * place + 1)).start()
            handed(layer, 1, (1, 2 * place + 1)).start()

    variants = [(role == 0,) + tuple(fronts[:2]), (role == 1,) + tuple(backs[:2])]
    ring = Ring(me, length, variants, scratch[:-11])

    def local_last(layer, slot):
        return pltpu.make_async_copy(ring.leaving[layer].at[slot], outs[layer], last_send.at[layer])

    def remote_last(layer, slot):
        return remote(
            ring.leaving[layer].at[slot], outs[layer], last_send.at[layer], last_recv.at[layer],
            me["partner"],
        )

    def finish(layer, slot):
        @pl.when(core == role)
        def _():
            local_last(layer, slot).start()

        @pl.when(core != role)
        def _():
            remote_last(layer, slot).start()

    def silu_copy(peer):
        return remote(
            silu_own, silu_all.at[core, index], silu_send.at[peer], silu_recv.at[index],
            (core, peer),
        )

    silu_kept = pltpu.make_async_copy(silu_own, silu_all.at[core, index], silu_keep)

    def others(act):
        def body(peer):
            @pl.when(peer != index)
            def _():
                act(peer)

        each(0, members, body)

    def midway():
        def mod_came(source):
            @pl.when((core != role) | (source != mine))
            def _():
                small(
                    mod, mod_all.at[source], small_send.at[0, 0], mod_recv.at[source],
                    me["sibling"],
                ).wait_recv()

        each(0, members, mod_came)

        @pl.when(core == role)
        def _():
            own_mod.wait()

        images, depth = mod.shape[0], mod_weight.shape[0]
        for source in range(members):
            mod_rows[source * images : (source + 1) * images, :] = wide(mod_all[source])
        silu_own[...] = jnp.zeros_like(silu_own)
        silu_own[:, 0:depth] = product_right_t(narrow(mod_rows[...]), mod_weight[...])
        silu_kept.start()
        others(lambda peer: silu_copy(peer).start())

    across = remote(
        silu_all.at[core], silu_all.at[core], silu_side.at[0], silu_side.at[1], me["sibling"]
    )

    def late():
        others(
            lambda peer: remote(
                silu_own, silu_all.at[core, peer], silu_send.at[peer], silu_recv.at[peer],
                (core, peer),
            ).wait_recv()
        )
        silu_kept.wait()
        across.start()

    ring.run(finish, early, midway, late)
    others(lambda peer: silu_copy(peer).wait_send())
    across.wait_send()
    remote(
        silu_all.at[1 - core], silu_all.at[1 - core], silu_side.at[0], silu_side.at[1],
        me["sibling"],
    ).wait_recv()

    @pl.when((role == 0) & (core == 0))
    def _():
        for layer in range(heads):
            kept(layer).wait()
            handed(layer, 1, me["sibling"]).wait_send()

    @pl.when((role == 0) & (core == 1))
    def _():
        for layer in range(heads):
            handed(layer, 0, (0, 2 * place + 1)).wait_send()
            handed(layer, 1, (1, 2 * place + 1)).wait_send()

    @pl.when((role == 1) | (core == 1))
    def _():
        for layer in range(heads):
            handed(layer, 0, me["sibling"]).wait_recv()

    streams(lambda copy: copy.wait())
    smalls(
        lambda copy: copy.wait_send(),
        lambda copy: copy.wait_send(),
        lambda copy: None if copy is own_mod else copy.wait(),
    )

    def came(source):
        @pl.when((core != role) | (source != mine))
        def _():
            small(
                bias.at[0], bias_all.at[source], small_send.at[1, 0], bias_recv.at[source],
                me["sibling"],
            ).wait_recv()

        @pl.when((role != 0) | (source != mine))
        def _():
            small(
                head_sums.at[0], head_all.at[source], small_send.at[2, 0], head_recv.at[source],
                me["sibling"],
            ).wait_recv()

    each(0, members, came)
    slot = (length - 1) % 2
    for layer in ring.layers:

        @pl.when(core == role)
        def _():
            local_last(layer, slot).wait()

        @pl.when(core != role)
        def _():
            remote_last(layer, slot).wait()


def reduce(fronts, backs, head_parts, head_sums, mod_weight, widths, collective_id):
    members = lax.axis_size("dp")
    lefts, rights, streams, image_sums = fronts
    length, count, heads = members // 2, len(lefts), len(head_parts)
    rows = [left[0].shape[2] for left in lefts]
    columns = [right[0].shape[1] for right in rights]
    parts = len(rights[0])
    tokens = parts * rights[0][0].shape[0]
    bf16 = jnp.bfloat16
    inside = pl.BlockSpec(memory_space=pltpu.VMEM)
    stream_shape = (tokens, streams[0].shape[1])
    operands, form = jax.tree.flatten((fronts, backs, head_parts, head_sums, mod_weight))

    def side_specs(side):
        return jax.tree.map(lambda _: ANY, side[:3]) + (jax.tree.map(lambda _: inside, side[3]),)

    specs = side_specs(fronts) + side_specs(backs)
    specs = jax.tree.leaves(specs, is_leaf=lambda leaf: isinstance(leaf, pl.BlockSpec))
    images = sum(sums_of[0].shape[0] for sums_of in image_sums)
    mod_shape = (images, 6 * image_sums[0][0].shape[2])
    bias_shape = (members, 8, 128)
    f32 = jnp.float32
    lines = members * images
    results = pl.pallas_call(
        functools.partial(reduce_kernel, length, form, count, heads, widths),
        name="reduce",
        out_shape=[jax.ShapeDtypeStruct((r, c), bf16) for r, c in zip(rows, columns)]
        + [jax.ShapeDtypeStruct((h.shape[0] // 2, h.shape[1]), bf16) for h in head_parts]
        + [jax.ShapeDtypeStruct(stream_shape, bf16)]
        + [
            jax.ShapeDtypeStruct(bias_shape, f32),
            jax.ShapeDtypeStruct((members,) + head_sums.shape[1:], f32),
        ]
        + [
            jax.ShapeDtypeStruct((lines, mod_shape[1]), f32),
            jax.ShapeDtypeStruct((2, members, lines, 128), f32),
        ],
        in_specs=specs + [inside] * (heads + 2),
        out_specs=[ANY] * (count + heads + 3) + [inside, ANY],
        scratch_shapes=Ring.scratch(length, rows, columns, tokens, parts)
        + [
            DMA((count,)),
            DMA((count,)),
            DMA((heads, 2)),
            DMA((heads,)),
            DMA((parts,)),
            DMA((parts,)),
            DMA((3, 2 * members)),
            DMA((members,)),
            DMA((members,)),
            DMA((members,)),
            DMA((3,)),
            pltpu.VMEM(mod_shape, bf16),
            pltpu.VMEM(bias_shape, f32),
            pltpu.VMEM((1, members * sum(widths)), f32),
            pltpu.VMEM((members,) + mod_shape, bf16),
            pltpu.VMEM((lines, 128), f32),
            DMA(()),
            DMA((members,)),
            DMA((members,)),
            DMA((2,)),
        ],
        compiler_params=pltpu.CompilerParams(
            collective_id=collective_id, has_side_effects=True, vmem_limit_bytes=VMEM_BYTES
        ),
        cost_estimate=ring_cost(length, rows, columns, tokens),
    )(*operands)
    return (results[:count], results[count : count + heads]) + tuple(results[count + heads :])


def local_grad(function, primal, cotangent_in):
    return jax.vjp(function, primal)[1](cotangent_in)[0]


def column_sums(values):
    return jnp.sum(wide(values), 0)


def normed_of(values):
    center = values - jnp.mean(values, -1, keepdims=True)
    inverse = lax.rsqrt(jnp.mean(center * center, -1, keepdims=True) + EPSILON)
    return center * inverse, inverse


def lane_window(head, head_size):
    start = head * head_size
    base = start // 128 * 128
    width = -(-(start + head_size - base) // 128) * 128
    return base, width, start - base


def head_only(block, inside, head_size):
    lanes = lax.broadcasted_iota(jnp.int32, block.shape, 1)
    keep = (lanes >= inside) & (lanes < inside + head_size)
    return jnp.where(keep, block, jnp.zeros_like(block))


def lay_shards(left, values):
    rows = left.shape[2]
    turned = values.T
    for shard in range(values.shape[1] // rows):
        left[shard // 2, shard % 2] = turned[shard * rows : (shard + 1) * rows]


def attend_kernel(
    head_count, hidden, pieces, pack_w, pack_b, out_w, out_b,
    input_left, packed_out, probs_out, mixed_left, attn_out, after_out, mixed_acc,
):
    channels = hidden.shape[1]
    head_size = channels // head_count
    scaling = head_size ** (-0.5)
    residual = wide(hidden[...])
    normed, _ = normed_of(residual)
    attn_input = narrow(normed * (1.0 + pieces[0, 1:2]) + pieces[0, 0:1])
    lay_shards(input_left, attn_input)
    packed_out[...] = narrow(product(attn_input, pack_w[...]) + pack_b[...])
    mixed_acc[...] = jnp.zeros_like(mixed_acc)
    for head in range(head_count):
        base, width, inside = lane_window(head, head_size)
        queries = packed_out[:, base : base + width]
        keys = head_only(packed_out[:, channels + base : channels + base + width], inside, head_size)
        values = head_only(
            packed_out[:, 2 * channels + base : 2 * channels + base + width], inside, head_size
        )
        scores = product_right_t(queries, keys) * scaling
        exponent = jnp.exp(scores - jnp.max(scores, -1, keepdims=True))
        probs = narrow(exponent * (1.0 / jnp.sum(exponent, -1, keepdims=True)))
        probs_out[0, head] = probs
        mixed_acc[:, base : base + width] += product(probs, values)
    mixed = narrow(mixed_acc[...])
    lay_shards(mixed_left, mixed)
    out = product(mixed, out_w[...]) + out_b[...]
    attn_out[...] = narrow(out)
    after_out[...] = residual + pieces[0, 2:3] * out


def rows_spec(seq_len, columns):
    return pl.BlockSpec((seq_len, columns), lambda i: (i, 0))


def block_at(shape, index):
    return pl.BlockSpec(shape, lambda i: index, pipeline_mode=pl.Buffered(1))


def fixed_spec(shape):
    return block_at(shape, (0,) * len(shape))


def image_rows(array, image):
    if image is None:
        return fixed_spec(array.shape)
    return block_at((SEQ, array.shape[1]), (image if array.shape[0] > SEQ else 0, 0))


def image_steps(array, image):
    base = 0 if image is None or array.shape[0] <= SEQ else image
    return pl.BlockSpec((SEQ, array.shape[1]), lambda i: (base + i, 0))


def attend(hidden, pieces, pack_w, out_w, bias, members, image):
    tokens, channels = hidden.shape
    left = (members // 2, 2, channels // members)
    images, seq = tokens // SEQ, SEQ
    lowest = image or 0
    bf16, f32 = jnp.bfloat16, jnp.float32
    work = tokens * channels * (4 * channels + 2 * seq)
    return pl.pallas_call(
        functools.partial(attend_kernel, HEADS),
        grid=(images,),
        name="attend",
        in_specs=[
            rows_spec(seq, channels),
            pl.BlockSpec((1,) + pieces.shape[1:], lambda i: (lowest + i, 0, 0)),
            fixed_spec(pack_w.shape),
            block_at((1, 3 * channels), (0, 0)),
            fixed_spec(out_w.shape),
            block_at((1, channels), (0, 3)),
        ],
        out_specs=[
            pl.BlockSpec(left + (seq,), lambda i: (0, 0, 0, i)),
            rows_spec(seq, 3 * channels),
            pl.BlockSpec((1, HEADS, seq, seq), lambda i: (i, 0, 0, 0)),
            pl.BlockSpec(left + (seq,), lambda i: (0, 0, 0, i)),
            rows_spec(seq, channels),
            rows_spec(seq, channels),
        ],
        out_shape=[
            jax.ShapeDtypeStruct(left + (tokens,), bf16),
            jax.ShapeDtypeStruct((tokens, 3 * channels), bf16),
            jax.ShapeDtypeStruct((images, HEADS, seq, seq), bf16),
            jax.ShapeDtypeStruct(left + (tokens,), bf16),
            jax.ShapeDtypeStruct((tokens, channels), bf16),
            jax.ShapeDtypeStruct((tokens, channels), f32),
        ],
        scratch_shapes=[pltpu.VMEM((seq, channels), f32)],
        compiler_params=pltpu.CompilerParams(vmem_limit_bytes=VMEM_BYTES),
        cost_estimate=pl.CostEstimate(
            flops=2 * work, bytes_accessed=40 * 2**20, transcendentals=0
        ),
    )(hidden, pieces, pack_w, bias, out_w, bias)


def per_image(values, images):
    return values.reshape(images, values.shape[0] // images, values.shape[1])


GELU_A, GELU_B = 0.7978845608028654, 0.044715


def mlp_kernel(
    after, pieces, up_w, up_b, down_w, down_b,
    input_left, act_left, slope_out, mlp_out, final_out, input_keep, total,
):
    step, steps = pl.program_id(0), pl.num_programs(0)
    images = pieces.shape[0]

    @pl.when(step == 0)
    def _():
        normed, _ = normed_of(per_image(after[...], images))
        rows = narrow(normed * (1.0 + pieces[:, 4:5]) + pieces[:, 3:4]).reshape(after.shape)
        input_keep[...] = rows
        lay_shards(input_left, rows)
        total[...] = jnp.zeros_like(total)

    pre = product(input_keep[...], up_w[...]) + up_b[...]
    square = pre * pre
    tanh = jnp.tanh(GELU_A * pre * (1.0 + GELU_B * square))
    half = 0.5 + 0.5 * tanh
    act = narrow(pre * half)
    lay_shards(act_left, act)
    slope_out[...] = narrow(
        half + pre * (0.5 - 0.5 * tanh * tanh) * (GELU_A + (3.0 * GELU_A * GELU_B) * square)
    )
    total[...] += product(act, down_w[...])

    @pl.when(step == steps - 1)
    def _():
        out = total[...] + down_b[...]
        mlp_out[...] = narrow(out)
        final = per_image(after[...], images) + pieces[:, 5:6] * per_image(out, images)
        final_out[...] = narrow(final * pieces[:, 6:7]).reshape(after.shape)


def feed_tile(width):
    return 1152 if width % 1152 == 0 else width


def mlp(after, pieces, up_w, down_w, bias, members, image):
    tokens, channels = after.shape
    width = up_w.shape[1]
    tile = feed_tile(width)
    bf16, f32 = jnp.bfloat16, jnp.float32
    columns = pl.BlockSpec((tokens, tile), lambda i: (0, i))
    left = (members // 2, 2, channels // members, tokens)
    rows = width // members
    act_block = (tile // (2 * rows), 2, rows, tokens)
    return pl.pallas_call(
        mlp_kernel,
        grid=(width // tile,),
        name="mlp",
        in_specs=[
            fixed_spec(after.shape),
            block_at((tokens // SEQ,) + pieces.shape[1:], (image or 0, 0, 0)),
            pl.BlockSpec((channels, tile), lambda i: (0, i)),
            pl.BlockSpec((1, tile), lambda i: (0, 4 * channels // tile + i)),
            pl.BlockSpec((tile, channels), lambda i: (i, 0)),
            block_at((1, channels), (0, 4 + width // channels)),
        ],
        out_specs=[
            fixed_spec(left),
            pl.BlockSpec(act_block, lambda i: (i, 0, 0, 0)),
            columns,
            fixed_spec((tokens, channels)),
            fixed_spec((tokens, channels)),
        ],
        out_shape=[
            jax.ShapeDtypeStruct(left, bf16),
            jax.ShapeDtypeStruct((members // 2, 2, rows, tokens), bf16),
            jax.ShapeDtypeStruct((tokens, width), bf16),
            jax.ShapeDtypeStruct((tokens, channels), bf16),
            jax.ShapeDtypeStruct((tokens, channels), bf16),
        ],
        scratch_shapes=[pltpu.VMEM((tokens, channels), bf16), pltpu.VMEM((tokens, channels), f32)],
        compiler_params=pltpu.CompilerParams(vmem_limit_bytes=VMEM_BYTES),
        cost_estimate=pl.CostEstimate(
            flops=4 * tokens * channels * width, bytes_accessed=40 * 2**20, transcendentals=0
        ),
    )(after, pieces, up_w, bias, down_w, bias)


def sum_rows(values):
    return product(jnp.ones((8, values.shape[0]), jnp.bfloat16), values)


def layer_norm_back(grad_in, normed, inverse):
    return inverse * (
        grad_in
        - jnp.mean(grad_in, -1, keepdims=True)
        - normed * jnp.mean(grad_in * normed, -1, keepdims=True)
    )


def added_grad(grad, extra, pieces):
    return per_image(wide(grad[...]) + extra[...], pieces.shape[0])


def scaled_grad(grad, extra, pieces):
    return per_image(wide(grad[...]), pieces.shape[0]) * pieces[:, 6:7]


def mlp_back_kernel(
    given_grad, grad, extra, after, pieces, slope, mlp_out, attn_out, up_w, down_w,
    grad_mlp_out, grad_pre_out, grad_after_out, grad_attn_out, sums_out, pre_sums, out_sums,
    total,
):
    step, steps = pl.program_id(0), pl.num_programs(0)
    images = pieces.shape[0]

    @pl.when(step == 0)
    def _():
        given = given_grad(grad, extra, pieces)
        rows = narrow(pieces[:, 5:6] * given).reshape(grad.shape)
        grad_mlp_out[...] = rows
        sums_out[:, 5] = jnp.sum(given * per_image(wide(mlp_out[...]), images), 1)
        out_sums[0] = sum_rows(rows)
        total[...] = jnp.zeros_like(total)

    grad_pre = narrow(wide(slope[...]) * product_right_t(grad_mlp_out[...], down_w[...]))
    grad_pre_out[...] = grad_pre
    pre_sums[...] = sum_rows(grad_pre)
    total[...] += product_right_t(grad_pre, up_w[...])

    @pl.when(step == steps - 1)
    def _():
        normed, inverse = normed_of(per_image(after[...], images))
        grad_min = per_image(total[...], images)
        sums_out[:, 3] = jnp.sum(grad_min, 1)
        sums_out[:, 4] = jnp.sum(grad_min * normed, 1)
        grad_after = given_grad(grad, extra, pieces) + layer_norm_back(
            grad_min * (1.0 + pieces[:, 4:5]), normed, inverse
        )
        grad_after_out[...] = grad_after.reshape(grad.shape)
        rows = narrow(pieces[:, 2:3] * grad_after).reshape(grad.shape)
        grad_attn_out[...] = rows
        sums_out[:, 2] = jnp.sum(grad_after * per_image(wide(attn_out[...]), images), 1)
        out_sums[1] = sum_rows(rows)


def mlp_back(given_grad, grad, extra, after, pieces, slope, mlp_out, attn_out, up_w, down_w, image):
    tokens = after.shape[0] if image is None else SEQ
    images, channels, width = tokens // SEQ, after.shape[1], up_w.shape[1]
    tile = feed_tile(width)
    bf16, f32 = jnp.bfloat16, jnp.float32
    columns = pl.BlockSpec((tokens, tile), lambda i: (0, i))
    slope_row = image if image and slope.shape[0] > SEQ else 0
    rows = fixed_spec((tokens, channels))
    return pl.pallas_call(
        functools.partial(mlp_back_kernel, given_grad),
        grid=(width // tile,),
        name="mlp_back",
        in_specs=[
            image_rows(grad, image),
            image_rows(extra, image),
            image_rows(after, image),
            block_at((images,) + pieces.shape[1:], (image or 0, 0, 0)),
            pl.BlockSpec((tokens, tile), lambda i: (slope_row, i)),
            image_rows(mlp_out, image),
            image_rows(attn_out, image),
            pl.BlockSpec((channels, tile), lambda i: (0, i)),
            pl.BlockSpec((tile, channels), lambda i: (i, 0)),
        ],
        out_specs=[
            rows,
            columns,
            rows,
            rows,
            fixed_spec((images, 8, channels)),
            pl.BlockSpec((8, tile), lambda i: (0, i)),
            fixed_spec((2, 8, channels)),
        ],
        out_shape=[
            jax.ShapeDtypeStruct((tokens, channels), bf16),
            jax.ShapeDtypeStruct((tokens, width), bf16),
            jax.ShapeDtypeStruct((tokens, channels), f32),
            jax.ShapeDtypeStruct((tokens, channels), bf16),
            jax.ShapeDtypeStruct((images, 8, channels), f32),
            jax.ShapeDtypeStruct((8, width), f32),
            jax.ShapeDtypeStruct((2, 8, channels), f32),
        ],
        scratch_shapes=[pltpu.VMEM((tokens, channels), f32)],
        compiler_params=pltpu.CompilerParams(vmem_limit_bytes=VMEM_BYTES),
        cost_estimate=pl.CostEstimate(
            flops=4 * tokens * channels * width, bytes_accessed=40 * 2**20, transcendentals=0
        ),
    )(grad, extra, after, pieces, slope, mlp_out, attn_out, up_w, down_w)


def attend_back_kernel(
    head_count, hidden, pieces, packed, probs_in, grad_attn, grad_after, pack_w, out_w,
    grad_packed_out, grad_hidden_out, sums_out, pack_sums, acc, grad_mixed_keep,
):
    channels = hidden.shape[1]
    head_size = channels // head_count
    scaling = head_size ** (-0.5)
    grad_mixed_keep[...] = narrow(product_right_t(grad_attn[...], out_w[...]))
    acc[...] = jnp.zeros_like(acc)
    for head in range(head_count):
        base, width, inside = lane_window(head, head_size)
        q_at, k_at, v_at = (slice(j * channels + base, j * channels + base + width) for j in range(3))
        queries = head_only(packed[:, q_at], inside, head_size)
        keys = head_only(packed[:, k_at], inside, head_size)
        grad_mixed = head_only(grad_mixed_keep[:, q_at], inside, head_size)
        probs = probs_in[0, head]
        grad_probs = product_right_t(grad_mixed, packed[:, v_at])
        probs_wide = wide(probs)
        weighted = probs_wide * grad_probs
        grad_scores = narrow(weighted - probs_wide * jnp.sum(weighted, -1, keepdims=True))
        acc[:, v_at] += product_left_t(probs, grad_mixed)
        acc[:, q_at] += product(grad_scores, keys) * scaling
        acc[:, k_at] += product_left_t(grad_scores, queries) * scaling
    grad_packed = narrow(acc[...])
    grad_packed_out[...] = grad_packed
    column_totals = sum_rows(grad_packed)

    @pl.when(pl.program_id(0) == 0)
    def _():
        pack_sums[...] = column_totals

    @pl.when(pl.program_id(0) > 0)
    def _():
        pack_sums[...] += column_totals

    grad_ain = product_right_t(grad_packed, pack_w[...])
    normed, inverse = normed_of(wide(hidden[...]))
    sums_out[0, 0:1] = jnp.sum(grad_ain, 0, keepdims=True)
    sums_out[0, 1:2] = jnp.sum(grad_ain * normed, 0, keepdims=True)
    grad_hidden_out[...] = narrow(
        grad_after[...] + layer_norm_back(grad_ain * (1.0 + pieces[0, 1:2]), normed, inverse)
    )


def attend_back(hidden, pieces, packed, probs, grad_attn, grad_after, pack_w, out_w, image):
    tokens = hidden.shape[0] if image is None else SEQ
    images, channels, seq = tokens // SEQ, hidden.shape[1], SEQ
    lowest = image or 0
    probs_at = lowest if probs.shape[0] > 1 else 0
    bf16, f32 = jnp.bfloat16, jnp.float32
    work = tokens * channels * (4 * channels + 5 * seq)
    return pl.pallas_call(
        functools.partial(attend_back_kernel, HEADS),
        grid=(images,),
        name="attend_back",
        in_specs=[
            image_steps(hidden, image),
            pl.BlockSpec((1,) + pieces.shape[1:], lambda i: (lowest + i, 0, 0)),
            image_steps(packed, image),
            pl.BlockSpec((1, HEADS, seq, seq), lambda i: (probs_at + i, 0, 0, 0)),
            image_steps(grad_attn, image),
            image_steps(grad_after, image),
            fixed_spec(pack_w.shape),
            fixed_spec(out_w.shape),
        ],
        out_specs=[
            rows_spec(seq, 3 * channels),
            rows_spec(seq, channels),
            pl.BlockSpec((1, 8, channels), lambda i: (i, 0, 0)),
            fixed_spec((8, 3 * channels)),
        ],
        out_shape=[
            jax.ShapeDtypeStruct((tokens, 3 * channels), bf16),
            jax.ShapeDtypeStruct((tokens, channels), bf16),
            jax.ShapeDtypeStruct((images, 8, channels), f32),
            jax.ShapeDtypeStruct((8, 3 * channels), f32),
        ],
        scratch_shapes=[
            pltpu.VMEM((seq, 3 * channels), f32),
            pltpu.VMEM((seq, channels), bf16),
        ],
        compiler_params=pltpu.CompilerParams(vmem_limit_bytes=VMEM_BYTES),
        cost_estimate=pl.CostEstimate(
            flops=2 * work, bytes_accessed=40 * 2**20, transcendentals=0
        ),
    )(hidden, pieces, packed, probs, grad_attn, grad_after, pack_w, out_w)


def block_forward(hidden, pieces, weights, members, image=None):
    pack_w, out_w, up_w, down_w, bias = weights
    input_left, packed, probs, mixed_left, attn_out, after = attend(
        hidden, pieces, pack_w, out_w, bias, members, image
    )
    rows_left, act_left, slope, mlp_out, final = mlp(
        after, pieces, up_w, down_w, bias, members, image
    )
    return (
        final,
        (packed, probs, attn_out, after, slope, mlp_out),
        (act_left, rows_left, input_left, mixed_left),
    )


def block_backward(hidden, saved_state, pieces, weights, given_grad, grad, extra, image):
    pack_w, out_w, up_w, down_w, _ = weights
    packed, probs, attn_out, after, slope, mlp_out = saved_state
    grad_mlp, grad_pre, grad_after, grad_attn, high_sums, pre_sums, out_sums = mlp_back(
        given_grad, grad, extra, after, pieces, slope, mlp_out, attn_out, up_w, down_w, image
    )
    grad_packed, grad_hidden, low_sums, pack_sums = attend_back(
        hidden, pieces, packed, probs, grad_attn, grad_after, pack_w, out_w, image
    )
    rights = (grad_mlp, grad_pre, grad_packed, grad_attn)
    return grad_hidden, rights, (low_sums, high_sums, pack_sums, pre_sums, out_sums)


def silu_parts(values):
    gate = 0.5 + 0.5 * jnp.tanh(0.5 * values)
    return values * gate, gate * (1.0 + values * (1.0 - gate))


def head_kernel(
    members, hidden_at, target_at, live, in_w_at, in_b, mid_w_at, mid_b, out_w_at, out_b,
    grad_hidden_at, last_left_at, mid_left_at, in_left_at, grad_feature_at, grad_second_at,
    device_rows,
    hidden, target, in_w, mid_w, out_w,
    grad_hidden_out, last_left, mid_left, in_left, grad_feature_out, grad_second_out,
    act_first, slope_first, act_second, slope_second, grad_first_keep, in_sums, mid_sums,
    come_sem, go_sem,
):
    width = in_w.shape[1]
    tile = 512 if width % 512 == 0 else width
    tiles = [slice(start, start + tile) for start in range(0, width, tile)]
    rows = width // (2 * members)
    pairs_in = ((hidden_at, hidden), (in_w_at, in_w), (mid_w_at, mid_w), (out_w_at, out_w), (target_at, target))
    come = [
        pltpu.make_async_copy(there, here, come_sem.at[i]) for i, (there, here) in enumerate(pairs_in)
    ]
    pairs_out = (
        (grad_hidden_out, grad_hidden_at),
        (last_left, last_left_at),
        (mid_left, mid_left_at),
        (in_left, in_left_at),
        (grad_feature_out, grad_feature_at),
        (grad_second_out, grad_second_at),
    )
    go = [
        pltpu.make_async_copy(here, there, go_sem.at[i]) for i, (here, there) in enumerate(pairs_out)
    ]

    def lay(left, values, start):
        turned = values.T
        for offset in range(0, values.shape[1], rows):
            shard = (start + offset) // rows
            half, index = shard // members, shard % members
            left[index // 2, index % 2, half * rows : (half + 1) * rows] = turned[
                offset : offset + rows
            ]

    @pl.when(lax.rem(lax.axis_index("dp"), 2) == 0)
    def _():
        for copy in come:
            copy.start()
        come[0].wait()
        come[1].wait()
        for at in tiles:
            act, slope = silu_parts(product(hidden[...], in_w[:, at]) + in_b[:, at])
            act_first[:, at] = narrow(act)
            slope_first[:, at] = narrow(slope)
        come[2].wait()
        for at in tiles:
            act, slope = silu_parts(product(act_first[...], mid_w[:, at]) + mid_b[:, at])
            act_second[:, at] = narrow(act)
            slope_second[:, at] = narrow(slope)
            lay(mid_left, act_first[:, at], at.start)
        go[2].start()
        come[3].wait()
        come[4].wait()
        feature = product(act_second[...], out_w[...]) + out_b[...]
        inverse = lax.rsqrt(jnp.sum(feature * feature, -1, keepdims=True) + EPSILON)
        unit = feature * inverse
        aim = wide(target[...])
        aim = aim * lax.rsqrt(jnp.sum(aim * aim, -1, keepdims=True) + EPSILON)
        alive = live[:, 0:1]
        cosine = jnp.sum(unit * aim, -1, keepdims=True)
        loss = 0.5 * jnp.sum(alive * (1.0 - cosine), axis=(0, 1), keepdims=True)
        grad_unit = (-0.5 * alive) * aim
        grad_feature = narrow(
            inverse * (grad_unit - unit * jnp.sum(grad_unit * unit, -1, keepdims=True))
        )
        grad_feature_out[...] = grad_feature
        go[4].start()
        out_sums = sum_rows(grad_feature)
        for at in tiles:
            grad_second = narrow(
                wide(slope_second[:, at]) * product_right_t(grad_feature, out_w[at, :])
            )
            grad_second_out[:, at] = grad_second
            mid_sums[:, at] = sum_rows(grad_second)
            lay(last_left, act_second[:, at], at.start)
        go[1].start()
        go[5].start()
        for at in tiles:
            grad_first = narrow(
                wide(slope_first[:, at]) * product_right_t(grad_second_out[...], mid_w[at, :])
            )
            grad_first_keep[:, at] = grad_first
            in_sums[:, at] = sum_rows(grad_first)
            part = product_right_t(grad_first, in_w[:, at])
            if at.start == 0:
                grad_hidden_out[...] = part
            else:
                grad_hidden_out[...] += part
            lay(in_left, grad_first_keep[:, at], at.start)
        go[0].start()
        go[3].start()
        share, devices = width // (2 * members), 2 * members
        device_rows[...] = jnp.zeros_like(device_rows)
        for device in range(devices):
            lanes = slice(device * share, (device + 1) * share)
            device_rows[device, 0:1, 0:share] = in_sums[0:1, lanes]
            device_rows[device, 0:1, share : 2 * share] = mid_sums[0:1, lanes]
        count = out_sums.shape[1] // 128
        for line in range(count):
            device_rows[:, 1 + line, :] = jnp.broadcast_to(
                out_sums[0:1, line * 128 : (line + 1) * 128], (devices, 128)
            )
        device_rows[:, 1 + count, :] = jnp.broadcast_to(loss, (devices, 128))
        for copy in go:
            copy.wait()


def head_pass(hidden, target, live, head_weights, members):
    tokens, channels = hidden.shape
    width, features = head_weights[2].shape[0], target.shape[1]
    bf16, f32 = jnp.bfloat16, jnp.float32
    left = ((members // 2, 2, width // members, tokens), bf16)
    live_lanes = jnp.broadcast_to(live[:, None], (tokens, 128))
    in_w, in_b, mid_w, mid_b, out_w, out_b = head_weights
    inside = pl.BlockSpec(memory_space=pltpu.VMEM)
    work = tokens * (channels * width + width * width + width * features)
    big = [
        ((tokens, channels), f32),
        left,
        left,
        left,
        ((tokens, features), bf16),
        ((tokens, width), bf16),
    ]
    small = [((2 * members, 2 + features // 128, 128), f32)]
    results = pl.pallas_call(
        functools.partial(head_kernel, members),
        name="head",
        in_specs=[ANY, ANY, inside, ANY, inside, ANY, inside, ANY, inside],
        out_specs=[ANY] * 6 + [inside],
        out_shape=[jax.ShapeDtypeStruct(*leaf) for leaf in big + small],
        scratch_shapes=[
            pltpu.VMEM(array.shape, array.dtype) for array in (hidden, target, in_w, mid_w, out_w)
        ]
        + [pltpu.VMEM(*leaf) for leaf in big]
        + [pltpu.VMEM((tokens, width), bf16)] * 5
        + [pltpu.VMEM((8, width), f32)] * 2
        + [DMA((5,)), DMA((6,))],
        compiler_params=pltpu.CompilerParams(vmem_limit_bytes=VMEM_BYTES),
        cost_estimate=pl.CostEstimate(
            flops=4 * work, bytes_accessed=40 * 2**20, transcendentals=0
        ),
    )(hidden, target, live_lanes, in_w, in_b[None], mid_w, mid_b[None], out_w, out_b[None])
    grad_hidden, last_left, mid_left, in_left, grad_feature, grad_second, device_rows = results
    return (
        grad_hidden,
        (last_left, mid_left, in_left),
        (grad_feature, grad_second),
        device_rows,
    )


def trade_kernel(members, given, taken, send_sem, recv_sem):
    core, index = lax.axis_index("section"), lax.axis_index("dp")
    barrier = pltpu.get_barrier_semaphore()

    def others(act):
        def body(peer):
            @pl.when(peer != index)
            def _():
                act(peer)

        each(0, members, body)

    def copy(peer):
        return remote(given, taken.at[index], send_sem.at[peer], recv_sem.at[index], (core, peer))

    others(
        lambda peer: pl.semaphore_signal(
            barrier, inc=1, device_id=(core, peer), device_id_type=MESH
        )
    )
    pl.semaphore_wait(barrier, members - 1)
    others(lambda peer: copy(peer).start())
    taken[index] = given[...]
    others(
        lambda peer: remote(
            given, taken.at[peer], send_sem.at[peer], recv_sem.at[peer], (core, peer)
        ).wait_recv()
    )
    others(lambda peer: copy(peer).wait_send())


def trade(block, collective_id):
    members = lax.axis_size("dp")
    inside = pl.BlockSpec(memory_space=pltpu.VMEM)
    return pl.pallas_call(
        functools.partial(trade_kernel, members),
        name="trade",
        out_shape=jax.ShapeDtypeStruct((members,) + block.shape, block.dtype),
        in_specs=[inside],
        out_specs=inside,
        scratch_shapes=[DMA((members,)), DMA((members,))],
        compiler_params=pltpu.CompilerParams(collective_id=collective_id, has_side_effects=True),
    )(block)


def hollow(shapes):
    leaves, form = jax.tree.flatten(shapes)
    results = pl.pallas_call(
        lambda *refs: None,
        name="hollow",
        out_shape=[jax.ShapeDtypeStruct(leaf.shape, leaf.dtype) for leaf in leaves],
        out_specs=[ANY if leaf.ndim else pl.BlockSpec(memory_space=pltpu.SMEM) for leaf in leaves],
    )()
    return jax.tree.unflatten(form, list(results))


def on_device(
    tokens_in,
    cotangent,
    targets,
    buckets,
    counts,
    time_table,
    modulate_weight,
    modulate_bias,
    qkv_weight,
    qv_bias,
    attn_weight,
    attn_bias,
    up_weight,
    up_bias,
    down_weight,
    down_bias,
    project_in_weight,
    project_in_bias,
    project_mid_weight,
    project_mid_bias,
    project_out_weight,
    project_out_bias,
):
    members = lax.axis_size("dp")
    core = lax.axis_index("section")
    index = lax.axis_index("dp")
    place, role = index // 2, index % 2
    is_first = role == 0
    own = 2 * place + core
    channels = tokens_in.shape[1]
    images = tokens_in.shape[0] // SEQ
    pairs_up, pairs_back, pairs_swap = [], [], []
    for pair in range(members // 2):
        low, high = 2 * pair, 2 * pair + 1
        pairs_swap += [(high, members + low)]
        pairs_up += [(low, high), (members + low, members + high)]
        pairs_back += [(high, low), (members + high, members + low)]
    axes = ("section", "dp")

    bucket_block = jnp.broadcast_to(jnp.pad(buckets, (0, 128 - images))[None], (8, 128))
    all_buckets = trade(bucket_block, 1)[:, 0, :images].reshape(-1)
    one_hot = (
        all_buckets[:, None] == jnp.arange(time_table.shape[0], dtype=jnp.int32)[None, :]
    ).astype(jnp.float32)
    conditioning = jnp.dot(one_hot, time_table, precision=HIGHEST)
    silu_all = narrow(jax.nn.silu(conditioning))
    depth = modulate_weight.shape[1]
    silu_depth = lax.dynamic_slice_in_dim(silu_all, index * depth, depth, 1)
    mod_part = product(silu_depth, modulate_weight[0])
    share = modulate_bias.shape[1]
    bias_row = lax.dynamic_update_slice_in_dim(
        jnp.zeros((mod_part.shape[1],), jnp.float32), wide(modulate_bias[0]), index * share, 0
    )
    mod_part = (mod_part + bias_row[None]).reshape(members, images, 6 * channels)

    section_biases = (qv_bias[0], attn_bias[0], up_bias[0], down_bias[0])
    biases = section_biases + (project_in_bias, project_mid_bias, project_out_bias)
    widths = [part.shape[0] for part in biases]
    lines = [
        jnp.pad(part, (0, -part.shape[0] % 128)).reshape(-1, 128) for part in biases
    ]
    bias_block = jnp.concatenate(lines)
    bias_block = jnp.pad(bias_block, ((0, -bias_block.shape[0] % 16), (0, 0)))
    block_full, head_full, mod_all, rows_in, block_bias, head_bias = gather(
        (
            bias_block,
            qkv_weight[0],
            attn_weight[0],
            up_weight[0],
            down_weight[0],
            project_out_weight,
        ),
        (project_in_weight, project_mid_weight),
        mod_part,
        tokens_in,
        cotangent,
        widths,
        0,
    )
    _, pack_weight, out_weight, first_weight, second_weight, head_last = block_full
    head_ends = [members * width for width in widths[4:]]
    head_bias = [
        head_bias[0, sum(head_ends[:i]) : sum(head_ends[: i + 1])] for i in range(len(head_ends))
    ]

    def whole(values):
        return values.reshape(-1, values.shape[-1])

    block_weights = (
        whole(pack_weight),
        whole(out_weight),
        whole(first_weight),
        whole(second_weight),
        block_bias,
    )
    head_weights = (
        whole(head_full[0]),
        head_bias[0],
        whole(head_full[1]),
        head_bias[1],
        whole(head_last),
        head_bias[2],
    )
    pieces = jnp.sum(mod_all, 0).reshape(images, 6, channels)

    own_counts = counts[own]
    image_live = (jnp.arange(images, dtype=jnp.int32) < own_counts).astype(jnp.float32)
    token_live = jnp.repeat(image_live, SEQ)
    out_scale = jnp.where(is_first, 1.0, image_live)
    scale_rows = jnp.broadcast_to(out_scale[:, None, None], (images, 2, channels))
    pieces = jnp.concatenate([pieces, scale_rows], 1)
    total_live = wide(jnp.sum(counts)) * SEQ
    crossed = core != role
    targets_out, rows_in = lax.optimization_barrier((targets, rows_in))
    hidden_first = jnp.where(crossed, rows_in, tokens_in)
    own_targets = jnp.where(crossed, lax.ppermute(targets_out, axes, pairs_swap), targets)

    def unused(function, *operands_in):
        return hollow(jax.eval_shape(function, *operands_in))

    def forward(hidden, mod, block):
        return block_forward(hidden, mod, block, members)

    first_out, saved_state, first_lefts = lax.cond(
        is_first,
        forward,
        lambda *operands_in: unused(forward, *operands_in),
        hidden_first,
        pieces,
        block_weights,
    )
    hidden_second = lax.ppermute(first_out, axes, pairs_up)

    rows_late, _ = lax.optimization_barrier((rows_in, first_out))
    outer = lax.optimization_barrier(jnp.where(crossed, rows_late, cotangent))
    head_result = head_pass(first_out, own_targets, token_live, head_weights, members)
    hidden_second, head_result = lax.optimization_barrier((hidden_second, head_result))
    grad_hidden, head_lefts, head_rights, head_rows = head_result

    def do_second(rows, mod, grad, block):
        final, state, lefts = block_forward(rows, mod, block, members)
        grad_rows, rights, sums_of = block_backward(
            rows, state, mod, block, scaled_grad, grad, grad, None
        )
        cut = tuple(grad_rows[i * SEQ : (i + 1) * SEQ] for i in range(images))
        return cut, final, rights, sums_of, lefts

    second = lax.cond(
        is_first,
        lambda *operands_in: unused(do_second, *operands_in),
        do_second,
        hidden_second,
        pieces,
        outer,
        block_weights,
    )
    grad_rows = second[0]
    returning = [lax.ppermute(grad_rows[0], axes, pairs_back)]
    head_lefts, head_rights, kept = lax.optimization_barrier((head_lefts, head_rights, second[1]))
    second = (second[0], kept) + second[2:]
    head_parts = head_reduce(head_lefts, head_rights + (first_out,), 2)
    returning[0], head_parts, grad_rows = lax.optimization_barrier(
        (returning[0], head_parts, grad_rows)
    )
    for i in range(1, images):
        returning.append(lax.ppermute(grad_rows[i], axes, pairs_back))
    first = []
    for i in range(images):

        def do_first(rows, state, mod, extra, grad, block, i=i):
            return block_backward(rows, state, mod, block, added_grad, grad, extra, i)

        if i:
            returning[i], gone = lax.optimization_barrier((returning[i], first[i - 1][0]))
            first[i - 1] = (gone,) + first[i - 1][1:]
        first.append(
            lax.cond(
                is_first,
                do_first,
                lambda *operands_in: unused(do_first, *operands_in),
                hidden_first,
                saved_state,
                pieces,
                grad_hidden,
                returning[i],
                block_weights,
            )
        )
    def by_layer(results):
        return [list(parts_of) for parts_of in zip(*results)]

    fronts = (
        [[left] for left in first_lefts],
        by_layer([result[1] for result in first]),
        [result[0] for result in first],
        [result[2] for result in first],
    )
    backs = (
        [[left] for left in second[4]],
        [[right] for right in second[2]],
        [second[1]],
        [second[3]],
    )
    block_grads, head_grads, stream_in, bias_all, head_all, mod_wide, silu_all_terms = reduce(
        fronts,
        backs,
        head_parts,
        head_rows,
        modulate_weight[0],
        widths[:4],
        3,
    )
    down_grad, up_grad, qkv_grad, attn_grad = block_grads
    stream = jnp.where(is_first, jnp.concatenate(fronts[2]), jnp.concatenate(backs[2]))
    stream_own = jnp.where(crossed, stream_in, stream)
    mod_w_grad = product_left_t(silu_depth, narrow(mod_wide))
    mod_b_grad = lax.dynamic_slice_in_dim(jnp.sum(mod_wide, 0), index * share, share, 0)
    silu_total = jnp.sum(silu_all_terms[:, :, :, :depth], 0)
    silu_total = jnp.swapaxes(silu_total, 0, 1).reshape(-1, channels)
    cond_grad = local_grad(jax.nn.silu, conditioning, silu_total)
    table_grad = jnp.dot(one_hot.T, cond_grad, precision=HIGHEST)

    bias_sums = jnp.sum(bias_all, 0)
    bias_outs, line = [], 0
    for width in widths[:4]:
        count = -(-width // 128)
        bias_outs.append(bias_sums[line : line + count].reshape(1, -1)[:, :width])
        line += count
    sums = jnp.sum(head_all, 0)
    head_share = head_grads[1].shape[0]
    loss_value = sums[-1, 0] / total_live
    return (
        stream_own[None],
        loss_value,
        table_grad,
        mod_w_grad[None],
        mod_b_grad[None],
        wide(qkv_grad)[None],
        bias_outs[0],
        wide(attn_grad)[None],
        bias_outs[1],
        wide(up_grad)[None],
        bias_outs[2],
        wide(down_grad)[None],
        bias_outs[3],
        wide(head_grads[2]).T,
        sums[0, :head_share],
        wide(head_grads[1]),
        sums[0, head_share : 2 * head_share],
        wide(head_grads[0]),
        sums[1:-1].reshape(-1),
    )


def solution(mesh):
    in_specs = (
        P("dp", None),
        P("dp", None),
        P("dp", None),
        P("dp"),
        P(),
        P(),
        P("section", "dp", None),
        P("section", "dp"),
        P("section", "dp", None),
        P("section", "dp"),
        P("section", "dp", None),
        P("section", "dp"),
        P("section", "dp", None),
        P("section", "dp"),
        P("section", "dp", None),
        P("section", "dp"),
        P("dp", None),
        P("dp"),
        P("dp", None),
        P("dp"),
        P("dp", None),
        P("dp"),
    )
    out_specs = (
        P("section", "dp", None),
        P(),
        P(),
        P("section", "dp", None),
        P("section", "dp"),
        P("section", "dp", None),
        P("section", "dp"),
        P("section", "dp", None),
        P("section", "dp"),
        P("section", "dp", None),
        P("section", "dp"),
        P("section", "dp", None),
        P("section", "dp"),
        P(None, ("section", "dp")),
        P(("section", "dp")),
        P(("section", "dp"), None),
        P(("section", "dp")),
        P(("section", "dp"), None),
        P(),
    )
    return jax.shard_map(
        on_device, mesh=mesh, in_specs=in_specs, out_specs=out_specs, check_vma=False
    )
```
